32 devices in a mesh: dp: 4 (over y, x), expert: 8 (over z, core).
Axes of the slice: x: 2, y: 2, z: 4, core: 2. Of those that a mesh axis runs over, the one named last changes fastest.
Arguments:
- hidden: bfloat16 [4, 16, 384, 1024], P('dp', 'expert'), may hold values from -6 to 6
- down_weight: bfloat16 [16, 1024, 3584], P('expert'), may hold values from -0.1875 to 0.1875
- cotangent: bfloat16 [2048, 3584], P('dp', 'expert'), may hold values from -6 to 6
- expert_ids: int32 [2048, 8], P('dp'), may hold values from 0 to 15, as said below
- gate_weights: bfloat16 [2048, 8], P('dp'), may hold values from 0.049804688 to 0.5
- row_token: int32 [4, 16, 384], P('dp', 'expert'), may hold values from -1 to 511, as said below
- tile_count: int32 [4, 16], P('dp', 'expert'), may hold values from 1 to 3, as said below
Outputs:
- mixed_out: bfloat16 [2048, 3584], P('dp', 'expert')
- hidden_grad: bfloat16 [4, 16, 384, 1024], P('dp', 'expert')
- weight_grad: float32 [16, 1024, 3584], P('expert', 'dp')
The draws below stay inside these ranges and needn't reach their ends.
Inputs may be any that keep to these rules, and one draw needn't show every extreme that they name: `expert_ids`: each token names 8 different experts; every expert is named by some token of every group. row_token[i, e, r] is the index within group i (0 to 511) of a token that names expert e, or -1 for an empty slot; each token of a group stands exactly once in the rows of each expert it names and nowhere else; an expert's filled rows come first. tile_count[i, e] is the number of 128-row tiles that hold expert e's filled rows in group i, except for one expert of every group whose count is one tile less; the busiest expert of every group has 384 filled rows, all of them counted.
All inputs are finite; a program needn't handle non-finite values.
Results may differ from the reference program's by a relative error of at most 0.013.
Values may be sent and summed in bfloat16 or wider, within the bound.
No kernel may reach another device: no remote copies, remote signals or barrier semaphores. Data moves between devices by JAX's collectives and lax.ppermute only.
A program may use at most 128 MiB of HBM per device.

```python
import math
import jax
import jax.numpy as jnp
from jax import lax

D = 3584
H = 1024
TOPK = 8
EXPERTS = 16
TILE = 128
GROUP_TOK = 512
TOKENS = 2048
MEAN_ROWS = 256
ROWS_CAP = 384
N_DP = 4


def group_plan(group_key):
    pair_order = jax.random.permutation(jax.random.fold_in(group_key, 11), EXPERTS)
    half_mean = MEAN_ROWS // 2
    shifts = jax.random.randint(jax.random.fold_in(group_key, 12), (EXPERTS // 2,), 0, half_mean + 1)
    shifts = shifts.at[0].set(half_mean)
    signed = jnp.stack([shifts, -shifts], axis=1).reshape(EXPERTS)
    loads = jnp.zeros((EXPERTS,), jnp.int32).at[pair_order].set(MEAN_ROWS + signed)
    ends = jnp.cumsum(loads)
    starts = ends - loads
    positions = jnp.arange(GROUP_TOK * TOPK, dtype=jnp.int32)
    owner_expert = jnp.sum((positions[:, None] >= ends[None, :]).astype(jnp.int32), axis=1)
    token_perm = jax.random.permutation(jax.random.fold_in(group_key, 13), GROUP_TOK).astype(jnp.int32)
    by_column = owner_expert.reshape(TOPK, GROUP_TOK).T
    ids_group = jnp.zeros((GROUP_TOK, TOPK), jnp.int32).at[token_perm].set(by_column)
    slot_index = jnp.arange(ROWS_CAP, dtype=jnp.int32)
    flat_pos = starts[:, None] + slot_index[None, :]
    rows_group = jnp.where(slot_index[None, :] < loads[:, None], token_perm[flat_pos % GROUP_TOK], -1)
    needed = (loads + TILE - 1) // TILE
    last_fill = loads - TILE * (needed - 1)
    expert_index = jnp.arange(EXPERTS, dtype=jnp.int32)
    eligible = (needed >= 2) & (expert_index != pair_order[0])
    score = jnp.where(eligible, last_fill * EXPERTS + expert_index, -1)
    short_expert = jnp.argmax(score)
    counts_group = needed - (expert_index == short_expert).astype(jnp.int32)
    return (ids_group, rows_group.astype(jnp.int32), counts_group.astype(jnp.int32))


def all_groups(key):
    base_key = jax.random.fold_in(key, 5)
    group_keys = jax.vmap(lambda index: jax.random.fold_in(base_key, index))(jnp.arange(N_DP))
    return jax.vmap(group_plan)(group_keys)


def draw_expert_ids(key, part):
    return all_groups(key)[0].reshape(TOKENS, TOPK)


def draw_row_token(key, part):
    return all_groups(key)[1]


def draw_tile_count(key, part):
    return all_groups(key)[2]


def level_of(stream_key, extent, cuts, smallest, largest):
    gain = 1.0
    for dim, shards_of in cuts:
        draws = jax.random.uniform(jax.random.fold_in(jax.random.fold_in(stream_key, 6), dim), (shards_of,), jnp.float32, smallest / len(cuts), largest / len(cuts))
        gain = gain * jnp.repeat(jnp.exp(draws), extent[dim] // shards_of).reshape((-1,) + (1,) * (len(extent) - 1 - dim))
    return gain


def scatter_about(rng, shape, spread, bound, shards=(), kind=jnp.bfloat16):
    gain = level_of(rng, shape, shards, -0.22, 0.18) if shards else 1.0
    array = jax.random.normal(rng, shape, jnp.float32) * spread * gain
    return jnp.minimum(jnp.maximum(array, -bound), bound).astype(kind)


def setup_inputs(seed: int = 0) -> dict:
    key_list = jax.random.split(jax.random.key(seed), 8)
    hidden = scatter_about(key_list[0], (N_DP, EXPERTS, ROWS_CAP, H), 1.0, 6.0, ((0, 4), (1, 8)))
    down_weight = scatter_about(key_list[1], (EXPERTS, H, D), H ** -0.5, 0.1875, ((0, 8),))
    cotangent = scatter_about(key_list[2], (TOKENS, D), 1.0, 6.0, ((0, 4), (1, 8)))
    expert_ids = draw_expert_ids(jax.random.fold_in(key_list[7], 71), 0)
    gate_weights = jnp.clip(jnp.exp(math.log(0.5) - 2.306499 * jax.random.uniform(key_list[4], (TOKENS, TOPK), jnp.float32) ** level_of(key_list[4], (TOKENS, TOPK), ((0, 4),), -0.2, 0.2)), 0.049804688, 0.5).astype(jnp.bfloat16)
    row_token = draw_row_token(jax.random.fold_in(key_list[7], 71), 0)
    tile_count = draw_tile_count(jax.random.fold_in(key_list[7], 71), 0)
    return dict(hidden=hidden, down_weight=down_weight, cotangent=cotangent, expert_ids=expert_ids, gate_weights=gate_weights, row_token=row_token, tile_count=tile_count)


def group_terms(hidden_rows, down_weight, token_rows, counts, group_ids, group_gates, group_cotangent):
    slot_index = jnp.arange(ROWS_CAP, dtype=jnp.int32)
    expert_index = jnp.arange(EXPERTS, dtype=jnp.int32)
    live_rows = (token_rows >= 0) & (slot_index[None, :] < counts[:, None] * TILE)
    safe_rows = jnp.where(live_rows, token_rows, 0).astype(jnp.int32)
    named_here = group_ids[safe_rows] == expert_index[:, None, None]
    row_gate = jnp.sum(jnp.where(named_here, group_gates[safe_rows].astype(jnp.float32), 0.0), axis=-1)
    row_gate = jnp.where(live_rows, row_gate, 0.0)
    weight_full = down_weight.astype(jnp.float32)
    hidden_full = hidden_rows.astype(jnp.float32)
    out_rows = jnp.einsum("erh,ehd->erd", hidden_full, weight_full).astype(jnp.bfloat16)
    contrib = row_gate[:, :, None] * out_rows.astype(jnp.float32)
    target = jnp.where(live_rows, token_rows, GROUP_TOK).astype(jnp.int32).reshape(-1)
    mixed_group = jnp.zeros((GROUP_TOK, D), jnp.float32).at[target].add(contrib.reshape(-1, D), mode="drop")
    routed = (row_gate[:, :, None] * group_cotangent[safe_rows].astype(jnp.float32)).astype(jnp.bfloat16)
    routed_full = routed.astype(jnp.float32)
    hidden_grad = jnp.einsum("erd,ehd->erh", routed_full, weight_full).astype(jnp.bfloat16)
    weight_part = jnp.einsum("erh,erd->ehd", hidden_full, routed_full).astype(jnp.bfloat16)
    return mixed_group.astype(jnp.bfloat16), hidden_grad, weight_part


def reference(hidden, down_weight, cotangent, expert_ids, gate_weights, row_token, tile_count):
    ids_groups = expert_ids.reshape(N_DP, GROUP_TOK, TOPK)
    gate_groups = gate_weights.reshape(N_DP, GROUP_TOK, TOPK)
    cot_groups = cotangent.reshape(N_DP, GROUP_TOK, D)

    def scan_group(grad_total, inputs):
        mixed_group, hidden_grad, weight_part = group_terms(inputs[0], down_weight, inputs[1], inputs[2], inputs[3], inputs[4], inputs[5])
        return grad_total + weight_part.astype(jnp.float32), (mixed_group, hidden_grad)

    grad_total, outputs = lax.scan(scan_group, jnp.zeros((EXPERTS, H, D), jnp.float32), (hidden, row_token, tile_count, ids_groups, gate_groups, cot_groups))
    return outputs[0].reshape(TOKENS, D), outputs[1], grad_total
```

```python
import functools

import jax
import jax.numpy as jnp
from jax import lax
from jax.experimental import pallas as pl
from jax.experimental.pallas import tpu as pltpu
from jax.sharding import PartitionSpec as P

EXPERTS = 16
TILE = 128
LANES = 128
CORES = 2
EXTRA_ROWS = 16
VMEM_BYTES = 56 * 1024 * 1024


def swapped(shard, axis, bit):
    return lax.ppermute(shard, axis, [(i, i ^ 1 << bit) for i in range(lax.axis_size(axis))])


def across_dp(shard, mask):
    return lax.ppermute(shard, "dp", [(i, i ^ mask) for i in range(lax.axis_size("dp"))])


def across_cores(shard):
    return swapped(shard, "expert", 0)


def along_z(shard, step, senders):
    pairs = [
        (CORES * z + core, CORES * (z + step) + core) for z in senders for core in range(CORES)
    ]
    return lax.ppermute(shard, "expert", pairs)


def dot(lhs, rhs, lhs_dim, rhs_dim):
    return lax.dot_general(
        lhs, rhs, (((lhs_dim,), (rhs_dim,)), ((), ())), preferred_element_type=jnp.float32
    )


def hot_rows(token_row, gate_row, first_token, tokens):
    slots = token_row.shape[1]
    token_index = lax.broadcasted_iota(jnp.int32, (tokens, slots), 0) + first_token
    spread = jnp.broadcast_to(gate_row, (tokens, slots))
    return jnp.where(token_index == token_row, spread, 0.0).astype(jnp.bfloat16)


def whole(shape):
    return pl.BlockSpec(shape, lambda *_: (0,) * len(shape))


def call(kernel, scalars, grid, in_specs, out_specs, out_shape, scratch, operands, aliases=None):
    return pl.pallas_call(
        kernel,
        grid_spec=pltpu.PrefetchScalarGridSpec(
            num_scalar_prefetch=1,
            grid=grid,
            in_specs=in_specs,
            out_specs=out_specs,
            scratch_shapes=scratch,
        ),
        out_shape=out_shape,
        input_output_aliases=aliases or {},
        compiler_params=pltpu.CompilerParams(
            dimension_semantics=("arbitrary",) * len(grid), vmem_limit_bytes=VMEM_BYTES
        ),
    )(scalars, *operands)


def expert_sums(chip, core, token_rows, row_gate, hidden_rows, weight, tokens):
    local_count, slots, width_in = hidden_rows.shape
    chips = lax.axis_size("expert") // CORES
    cols = weight.shape[2] // chips
    half = tokens // CORES

    def kernel(where, token_ref, gate_ref, hidden_ref, weight_ref, keep_ref, send_ref, by_token, total):
        local = pl.program_id(1)

        @pl.when(pl.program_id(0) == 0)
        def _():
            hot = hot_rows(token_ref[local], gate_ref[local], 0, tokens)
            by_token[local] = dot(hot, hidden_ref[local], 1, 0).astype(jnp.bfloat16)

        product = dot(by_token[local], weight_ref[0], 1, 0)

        @pl.when(local == 0)
        def _():
            total[...] = product

        @pl.when(local > 0)
        def _():
            total[...] += product

        @pl.when(local == local_count - 1)
        def _():
            mine = pl.multiple_of(where[1] * half, half)
            other = pl.multiple_of((1 - where[1]) * half, half)
            keep_ref[0] = total[pl.ds(mine, half), :].astype(jnp.bfloat16)
            send_ref[0] = total[pl.ds(other, half), :].astype(jnp.bfloat16)

    shape = jax.ShapeDtypeStruct((chips, half, cols), jnp.bfloat16)
    out_spec = pl.BlockSpec((1, half, cols), lambda k, e, where: (k, 0, 0))
    return call(
        kernel,
        jnp.stack([chip, core]),
        (chips, local_count),
        [
            whole((local_count, 1, slots)),
            whole((local_count, 1, slots)),
            whole(hidden_rows.shape),
            pl.BlockSpec((1, width_in, cols), lambda k, e, where: (e, 0, k)),
        ],
        (out_spec, out_spec),
        (shape, shape),
        [
            pltpu.VMEM((local_count, tokens, width_in), jnp.bfloat16),
            pltpu.VMEM((tokens, cols), jnp.float32),
        ],
        (token_rows[:, None], row_gate[:, None], hidden_rows, weight),
    )


def shares_by_token(payloads, slots, tokens):
    local_count, _, share = payloads[0].shape
    groups = len(payloads)

    def kernel(*refs):
        out_ref = refs[-1]

        def row(ref, local, first, count):
            wide = [ref[local, slots + first + i : slots + first + i + 1, :] for i in range(2)]
            return jnp.concatenate(wide, axis=1)[:, :count].astype(jnp.float32)

        for group in range(groups):
            ref = refs[group]
            for local in range(local_count):
                high = row(ref, local, 0, slots)
                low = row(ref, local, 2, slots)
                gate = row(ref, local, 4, slots)
                token = (high * 2.0 + low).astype(jnp.int32)
                hot = hot_rows(token, gate, 0, tokens)
                by_token = dot(hot, ref[local, :slots, :], 1, 0)
                out_ref[group, local] = by_token.T.astype(jnp.bfloat16)

    return pl.pallas_call(
        kernel,
        out_shape=jax.ShapeDtypeStruct((groups, local_count, share, tokens), jnp.bfloat16),
        compiler_params=pltpu.CompilerParams(vmem_limit_bytes=VMEM_BYTES),
    )(*payloads)


def hidden_grads(chip_order, core, token_rows, row_gate, mine, other, weight, tokens):
    local_count, width_in, width = weight.shape
    slots = token_rows.shape[1]
    chips = len(mine)
    half, cols = mine[0].shape
    depth = width_in // 2

    def kernel(where, token_ref, gate_ref, *refs):
        mine_refs, other_refs = refs[:chips], refs[chips : 2 * chips]
        weight_ref, out_ref = refs[2 * chips], refs[2 * chips + 1]
        local = pl.program_id(0)
        total = None
        for side, side_refs in enumerate((mine_refs, other_refs)):
            sums = None
            for place in range(chips):
                start = pl.multiple_of(where[1 + place] * cols, LANES)
                product = dot(side_refs[place][...], weight_ref[0, :, pl.ds(start, cols)], 1, 1)
                sums = product if sums is None else sums + product
            first = jnp.where(side == 0, where[0], 1 - where[0]) * half
            hot = hot_rows(token_ref[local], gate_ref[local], first, half)
            part = dot(hot, sums.astype(jnp.bfloat16), 0, 0)
            total = part if total is None else total + part
        out_ref[0] = total.astype(jnp.bfloat16)

    return call(
        kernel,
        jnp.concatenate([core[None], chip_order]),
        (local_count, width_in // depth),
        [whole((local_count, 1, slots))] * 2
        + [whole((half, cols))] * (2 * chips)
        + [pl.BlockSpec((1, depth, width), lambda e, h, where: (e, h, 0))],
        pl.BlockSpec((1, slots, depth), lambda e, h, where: (e, 0, h)),
        jax.ShapeDtypeStruct((local_count, slots, width_in), jnp.bfloat16),
        [],
        (token_rows[:, None], row_gate[:, None], *mine, *other, weight),
    )


def weight_cols(chip, core, shares, mine, other, width, so_far):
    groups, local_count, share, tokens = shares.shape
    half = tokens // CORES
    cols = mine[0][0].shape[1]
    flat_mine = [block for blocks in mine for block in blocks]
    flat_other = [block for blocks in other for block in blocks]
    count = len(flat_mine)
    given = () if so_far is None else (so_far,)
    layout = []
    for group, blocks in enumerate(mine):
        first = 0
        for block in blocks:
            layout.append((group, first, block.shape[0]))
            first += block.shape[0]

    def kernel(where, shares_ref, *refs):
        out_ref = refs[-1]
        total = None
        for side in range(CORES):
            start = jnp.where(side == 0, where[1], 1 - where[1]) * half
            for place, (group, first, rows) in enumerate(layout):
                ref = refs[side * count + place]
                at = pl.multiple_of(start + first, LANES)
                product = dot(shares_ref[group, 0, :, pl.ds(at, rows)], ref[...], 1, 0)
                total = product if total is None else total + product
        out_ref[0] = total

    return call(
        kernel,
        jnp.stack([chip, core]),
        (local_count,),
        [pl.BlockSpec((groups, 1, share, tokens), lambda e, where: (0, e, 0, 0))]
        + [whole(block.shape) for block in flat_mine + flat_other]
        + [pl.BlockSpec(memory_space=pl.ANY)] * len(given),
        pl.BlockSpec((1, share, cols), lambda e, where: (e, 0, where[0])),
        jax.ShapeDtypeStruct((local_count, share, width), jnp.float32),
        [],
        (shares, *flat_mine, *flat_other, *given),
        {2 + 2 * count: 0} if given else None,
    )


def planned_body(hidden, down_weight, cotangent, expert_ids, gate_weights, row_token, tile_count):
    local_count, width_in, width = down_weight.shape
    tokens, own_cols = cotangent.shape
    slots = hidden.shape[2]
    groups = lax.axis_size("dp")
    chips = lax.axis_size("expert") // CORES
    half = tokens // CORES
    quarter = half // 2
    share = width_in // groups
    group = lax.axis_index("dp")
    expert_place = lax.axis_index("expert")
    chip = expert_place // CORES
    core = expert_place % CORES

    kept = lax.dynamic_slice_in_dim(cotangent, core * half, half, 0)
    sent = lax.dynamic_slice_in_dim(cotangent, (1 - core) * half, half, 0)
    got = across_cores(sent)
    low = jnp.where(core == 0, kept, got)
    high = jnp.where(core == 0, got, kept)
    own = jnp.concatenate([low, high], axis=1)

    from_low, from_high = [own], [own]
    for step in range(1, chips):
        from_low.append(along_z(from_low[-1], 1, range(step - 1, chips - 1)))
        from_high.append(along_z(from_high[-1], -1, range(1, chips - step + 1)))
    blocks = [own]
    origins = [chip]
    for slot in range(1, chips):
        below, above = chip, chips - 1 - chip
        both = jnp.minimum(below, above)
        in_pairs = slot <= 2 * both
        take_low = jnp.where(in_pairs, slot % 2 == 1, below > above)
        distance = jnp.where(in_pairs, (slot + 1) // 2, slot - both)
        origins.append(jnp.where(take_low, chip - distance, chip + distance))
        block = from_high[1]
        for away in range(1, chips):
            for taking, source in ((True, from_low[away]), (False, from_high[away])):
                if (away, taking) != (1, False):
                    block = jnp.where((take_low == taking) & (distance == away), source, block)
        blocks.append(block)
    blocks_other = [across_cores(block) for block in blocks]

    slot_index = jnp.arange(slots, dtype=jnp.int32)
    token_index = jnp.arange(tokens, dtype=jnp.int32)
    live = (row_token[0] >= 0) & (slot_index[None] < tile_count[0][:, None] * TILE)
    token_rows = jnp.where(live, row_token[0], -1)
    experts = expert_place * local_count + jnp.arange(local_count, dtype=jnp.int32)
    named = expert_ids[None] == experts[:, None, None]
    token_gate = jnp.sum(jnp.where(named, gate_weights[None].astype(jnp.float32), 0.0), axis=2)
    at_token = token_rows[:, :, None] == token_index[None, None, :]
    row_gate = jnp.sum(jnp.where(at_token, token_gate[:, None, :], 0.0), axis=2)

    def as_rows(values):
        padded = jnp.pad(values.astype(jnp.bfloat16), ((0, 0), (0, 2 * share - slots)))
        return padded.reshape(local_count, 2, share)

    extra = jnp.concatenate(
        [as_rows(token_rows >> 1), as_rows(token_rows & 1), as_rows(row_gate)], axis=1
    )
    extra = jnp.pad(extra, ((0, 0), (0, EXTRA_ROWS - extra.shape[1]), (0, 0)))
    payloads = []
    for mask in range(groups):
        rows = lax.dynamic_slice_in_dim(hidden[0], (group ^ mask) * share, share, 2)
        payload = jnp.concatenate([rows, extra], axis=1)
        payloads.append(across_dp(payload, mask) if mask else payload)
    shares = shares_by_token(payloads, slots, tokens)

    keep, send = expert_sums(chip, core, token_rows, row_gate, hidden[0], down_weight, tokens)
    sums = keep.astype(jnp.float32) + across_cores(send).astype(jnp.float32)

    def toward(place):
        return lax.dynamic_index_in_dim(sums, place % chips, 0, keepdims=False)

    up, down = 0.0, 0.0
    for step in range(1, chips):
        up_out = (toward(chip + chips - step) + up).astype(jnp.bfloat16)
        down_out = (toward(chip + step) + down).astype(jnp.bfloat16)
        up = along_z(up_out, 1, range(0, step)).astype(jnp.float32)
        down = along_z(down_out, -1, range(chips - step, chips)).astype(jnp.float32)
    mixed = (toward(chip) + up + down).astype(jnp.bfloat16)
    mixed_low, mixed_high = mixed[:, :own_cols], mixed[:, own_cols:]
    mixed_mine = jnp.where(core == 0, mixed_low, mixed_high)
    mixed_got = across_cores(jnp.where(core == 0, mixed_high, mixed_low))
    mixed_out = jnp.where(
        core == 0,
        jnp.concatenate([mixed_mine, mixed_got], axis=0),
        jnp.concatenate([mixed_got, mixed_mine], axis=0),
    )

    hidden_grad = hidden_grads(
        jnp.stack(origins), core, token_rows, row_gate, blocks, blocks_other, down_weight, tokens
    )

    weight_grad = None
    for place in range(chips):
        own_block, own_other = blocks[place], blocks_other[place]
        by_x = across_dp(own_block, 1)
        by_y = across_dp(own_block, 2)
        far_top = across_dp(by_x[:quarter], 2)
        far_end = across_dp(by_y[quarter:], 1)
        mine = [[own_block], [by_x], [by_y], [far_top, far_end]]
        other = [[own_other]] + [[across_cores(block) for block in far] for far in mine[1:]]
        weight_grad = weight_cols(origins[place], core, shares, mine, other, width, weight_grad)
    return (mixed_out, hidden_grad[None], weight_grad)


def tile_products(rows_in, weight_mat, count, contract_dim):
    rows_cap = rows_in.shape[0]
    width_out = weight_mat.shape[1 - contract_dim]

    def one_tile(tile_index, outputs):
        block = lax.dynamic_slice_in_dim(rows_in, tile_index * TILE, TILE, 0)
        product = lax.dot_general(
            block,
            weight_mat,
            (((1,), (contract_dim,)), ((), ())),
            preferred_element_type=jnp.float32,
        )
        return lax.dynamic_update_slice_in_dim(
            outputs, product.astype(jnp.bfloat16), tile_index * TILE, 0
        )

    return lax.fori_loop(0, count, one_tile, jnp.zeros((rows_cap, width_out), jnp.bfloat16))


def general_body(hidden, down_weight, cotangent, expert_ids, gate_weights, row_token, tile_count):
    local_count = down_weight.shape[0]
    group_size = cotangent.shape[0]
    expert_index = jnp.arange(EXPERTS, dtype=jnp.int32)
    named_cols = expert_ids[:, :, None] == expert_index[None, None, :]
    gate_cols = jnp.sum(
        jnp.where(named_cols, gate_weights[:, :, None].astype(jnp.float32), 0.0), axis=1
    ).astype(jnp.bfloat16)
    group_cot = lax.all_gather(cotangent, "expert", axis=1, tiled=True)
    width = group_cot.shape[1]
    first_expert = lax.axis_index("expert") * local_count
    slot_index = jnp.arange(hidden.shape[2], dtype=jnp.int32)
    share_rows = down_weight.shape[1] // lax.axis_size("dp")
    partial_value = jnp.zeros((group_size, width), jnp.float32)
    grad_list = []
    weight_list = []
    for local in range(local_count):
        token_rows = row_token[0, local]
        count = tile_count[0, local]
        live_rows = (token_rows >= 0) & (slot_index < count * TILE)
        safe_rows = jnp.where(live_rows, token_rows, 0)
        column = lax.dynamic_index_in_dim(gate_cols, first_expert + local, 1, keepdims=False)
        row_gate = jnp.where(live_rows, column[safe_rows].astype(jnp.float32), 0.0)
        target = jnp.where(live_rows, token_rows, group_size)
        hidden_rows = hidden[0, local]
        weight_mat = down_weight[local]
        out_rows = tile_products(hidden_rows, weight_mat, count, 0)
        partial_value = partial_value.at[target].add(
            row_gate[:, None] * out_rows.astype(jnp.float32), mode="drop"
        )
        routed = (row_gate[:, None] * group_cot[safe_rows].astype(jnp.float32)).astype(jnp.bfloat16)
        grad_list.append(tile_products(routed, weight_mat, count, 1))

        def weight_rows(start, rows_count, hidden_rows=hidden_rows, routed_rows=routed):
            return lax.dot_general(
                hidden_rows,
                routed_rows,
                (((0,), (0,)), ((), ())),
                preferred_element_type=jnp.float32,
            )

        weight_list.append(
            lax.psum_scatter(
                weight_rows(jnp.int32(0), share_rows * lax.axis_size("dp")).astype(jnp.bfloat16),
                "dp",
                scatter_dimension=0,
                tiled=True,
            ).astype(jnp.float32)
        )
    merged = partial_value
    top_bit = lax.axis_size("expert").bit_length() - 1
    axis_index = lax.axis_index("expert")
    for bit_index in reversed(range(top_bit)):
        half_cols = merged.shape[1] // 2
        lower_half = merged[:, :half_cols]
        upper_half = merged[:, half_cols:]
        high_side = axis_index // 2**bit_index % 2 == 1
        sending = jnp.where(high_side, lower_half, upper_half)
        keeping = jnp.where(high_side, upper_half, lower_half)
        merged = keeping + swapped(sending.astype(jnp.bfloat16), "expert", bit_index).astype(
            sending.dtype
        )
    mixed_out = merged.astype(jnp.bfloat16)
    hidden_grad = jnp.stack(grad_list, axis=0)[None]
    weight_grad = jnp.stack(weight_list, axis=0)
    return (mixed_out, hidden_grad, weight_grad)


def solution(mesh):
    placed = (
        P("dp", "expert", None, None),
        P("expert", None, None),
        P("dp", "expert"),
        P("dp", None),
        P("dp", None),
        P("dp", "expert", None),
        P("dp", "expert"),
    )

    def body(*shards):
        width = shards[1].shape[2]
        chips = mesh.shape["expert"] // CORES
        fits = mesh.shape["dp"] == 4 and chips > 1 and width % (chips * LANES) == 0
        return planned_body(*shards) if fits else general_body(*shards)

    return jax.shard_map(
        body,
        mesh=mesh,
        in_specs=placed,
        out_specs=(P("dp", "expert"), P("dp", "expert", None, None), P("expert", "dp", None)),
        check_vma=False,
    )
```

```python
import jax
import jax.numpy as jnp
from jax import lax
from jax.experimental import pallas as pl
from jax.experimental.pallas import tpu as pltpu
from jax.sharding import PartitionSpec as P

EXPERTS = 16
TILE = 128
LANES = 128
CORES = 2
EXTRA_ROWS = 16
VMEM_BYTES = 56 * 1024 * 1024


def swapped(shard, axis, bit):
    return lax.ppermute(shard, axis, [(i, i ^ 1 << bit) for i in range(lax.axis_size(axis))])


def across_dp(shard, mask):
    return lax.ppermute(shard, "dp", [(i, i ^ mask) for i in range(lax.axis_size("dp"))])


def across_cores(shard):
    return swapped(shard, "expert", 0)


def z_lines():
    size = lax.axis_size("expert")
    return [list(range(core, size, CORES)) for core in range(CORES)]


def dot(lhs, rhs, lhs_dim, rhs_dim):
    return lax.dot_general(
        lhs, rhs, (((lhs_dim,), (rhs_dim,)), ((), ())), preferred_element_type=jnp.float32
    )


def hot_rows(token_row, gate_row, first_token, tokens):
    slots = token_row.shape[1]
    token_index = lax.broadcasted_iota(jnp.int32, (tokens, slots), 0) + first_token
    spread = jnp.broadcast_to(gate_row, (tokens, slots))
    return jnp.where(token_index == token_row, spread, 0.0).astype(jnp.bfloat16)


def whole(shape):
    return pl.BlockSpec(shape, lambda *_: (0,) * len(shape))


def call(kernel, scalars, grid, in_specs, out_specs, out_shape, scratch, operands, flops, aliases=None):
    outputs = jax.tree.leaves(out_shape)
    moved = sum(a.size * a.dtype.itemsize for a in [*operands, *outputs])
    return pl.pallas_call(
        kernel,
        grid_spec=pltpu.PrefetchScalarGridSpec(
            num_scalar_prefetch=1,
            grid=grid,
            in_specs=in_specs,
            out_specs=out_specs,
            scratch_shapes=scratch,
        ),
        out_shape=out_shape,
        input_output_aliases=aliases or {},
        cost_estimate=pl.CostEstimate(flops=flops, bytes_accessed=moved, transcendentals=0),
        compiler_params=pltpu.CompilerParams(
            dimension_semantics=("arbitrary",) * len(grid), vmem_limit_bytes=VMEM_BYTES
        ),
    )(scalars, *operands)


def expert_sums(where, token_rows, row_gate, hidden_rows, weight, tokens):
    local_count, slots, width_in = hidden_rows.shape
    chips = lax.axis_size("expert") // CORES
    cols = weight.shape[2] // chips
    half = tokens // CORES

    def kernel(where, token_ref, gate_ref, hidden_ref, weight_ref, keep_ref, send_ref, by_token):
        @pl.when(pl.program_id(0) == 0)
        def _():
            for local in range(local_count):
                for side in range(CORES):
                    first = jnp.bitwise_xor(where[1], side) * half
                    hot = hot_rows(token_ref[local], gate_ref[local], first, half)
                    rows = dot(hot, hidden_ref[local], 1, 0).astype(jnp.bfloat16)
                    by_token[side * half : (side + 1) * half, local * width_in : (local + 1) * width_in] = rows

        stacked = weight_ref[...].reshape(local_count * width_in, cols)
        total = dot(by_token[...], stacked, 1, 0).astype(jnp.bfloat16)
        keep_ref[0] = total[:half]
        send_ref[0] = total[half:]

    shape = jax.ShapeDtypeStruct((chips, half, cols), jnp.bfloat16)
    out_spec = pl.BlockSpec((1, half, cols), lambda k, where: (k, 0, 0))
    return call(
        kernel,
        where,
        (chips,),
        [
            whole((local_count, 1, slots)),
            whole((local_count, 1, slots)),
            whole(hidden_rows.shape),
            pl.BlockSpec((local_count, width_in, cols), lambda k, where: (0, 0, k)),
        ],
        (out_spec, out_spec),
        (shape, shape),
        [pltpu.VMEM((tokens, local_count * width_in), jnp.bfloat16)],
        (token_rows[:, None], row_gate[:, None], hidden_rows, weight),
        2 * tokens * weight.size,
    )


def shares_by_token(where, payloads, slots, tokens):
    local_count, _, share = payloads[0].shape
    groups = len(payloads)
    half = tokens // CORES

    def kernel(where, *refs):
        out_ref = refs[-1]

        def row(ref, local, first):
            wide = [ref[local, slots + first + i : slots + first + i + 1, :] for i in range(2)]
            return jnp.concatenate(wide, axis=1)[:, :slots].astype(jnp.float32)

        for group in range(groups):
            ref = refs[group]
            for local in range(local_count):
                token = (row(ref, local, 0) * 2.0 + row(ref, local, 2)).astype(jnp.int32)
                gate = row(ref, local, 4)
                for side in range(CORES):
                    first = jnp.bitwise_xor(where[1], side) * half
                    hot = hot_rows(token, gate, first, half)
                    by_token = dot(hot, ref[local, :slots, :], 1, 0)
                    start = group * tokens + side * half
                    out_ref[local * share : (local + 1) * share, start : start + half] = by_token.T.astype(
                        jnp.bfloat16
                    )

    shape = (local_count * share, groups * tokens)
    return call(
        kernel,
        where,
        (1,),
        [whole(payload.shape) for payload in payloads],
        whole(shape),
        jax.ShapeDtypeStruct(shape, jnp.bfloat16),
        [],
        payloads,
        2 * shape[0] * shape[1] * slots,
    )


def hidden_grads(where, token_rows, row_gate, mine, other, weight, tokens):
    local_count, width_in, width = weight.shape
    slots = token_rows.shape[1]
    chips, half, cols = mine.shape
    depth = width_in // 2

    def kernel(where, token_ref, gate_ref, mine_ref, other_ref, weight_ref, out_ref, group_cot):
        local = pl.program_id(0)

        @pl.when((local == 0) & (pl.program_id(1) == 0))
        def _():
            for side, ref in enumerate((mine_ref, other_ref)):
                for chip in range(chips):
                    group_cot[side * half : (side + 1) * half, chip * cols : (chip + 1) * cols] = ref[chip]

        sums = dot(group_cot[...], weight_ref[0], 1, 1).astype(jnp.bfloat16)
        hot = [
            hot_rows(token_ref[local], gate_ref[local], jnp.bitwise_xor(where[1], side) * half, half)
            for side in range(CORES)
        ]
        out_ref[0] = dot(jnp.concatenate(hot, axis=0), sums, 0, 0).astype(jnp.bfloat16)

    return call(
        kernel,
        where,
        (local_count, width_in // depth),
        [whole((local_count, 1, slots))] * 2
        + [whole(mine.shape)] * 2
        + [pl.BlockSpec((1, depth, width), lambda e, h, where: (e, h, 0))],
        pl.BlockSpec((1, slots, depth), lambda e, h, where: (e, 0, h)),
        jax.ShapeDtypeStruct((local_count, slots, width_in), jnp.bfloat16),
        [pltpu.VMEM((tokens, width), jnp.bfloat16)],
        (token_rows[:, None], row_gate[:, None], mine, other, weight),
        2 * tokens * weight.size,
    )


def weight_cols(where, first, count, shares, near, far, local_count, width, so_far):
    share = shares.shape[0] // local_count
    chips, half, cols = near[0].shape
    flat = [block for group in far for side in group for block in side]
    given = () if so_far is None else (so_far,)

    def chip_at(place, where):
        return lax.rem(where[0] + first + place, chips)

    def kernel(where, shares_ref, *refs):
        out_ref = refs[-1]
        blocks = [ref[0] for ref in refs[: CORES + len(flat)]]
        total = dot(shares_ref[...], jnp.concatenate(blocks, axis=0), 1, 0)
        for local in range(local_count):
            out_ref[local] = total[local * share : (local + 1) * share]

    return call(
        kernel,
        where,
        (count,),
        [whole(shares.shape)]
        + [pl.BlockSpec((1, half, cols), lambda s, where: (chip_at(s, where), 0, 0))] * CORES
        + [pl.BlockSpec((1, *block.shape[1:]), lambda s, where: (s, 0, 0)) for block in flat]
        + [pl.BlockSpec(memory_space=pl.ANY)] * len(given),
        pl.BlockSpec((local_count, share, cols), lambda s, where: (0, 0, chip_at(s, where))),
        jax.ShapeDtypeStruct((local_count, share, width), jnp.float32),
        [],
        (shares, *near, *flat, *given),
        2 * shares.size * cols * count,
        {2 + CORES + len(flat): 0} if given else None,
    )


def planned_body(hidden, down_weight, cotangent, expert_ids, gate_weights, row_token, tile_count):
    local_count, width_in, width = down_weight.shape
    tokens, own_cols = cotangent.shape
    slots = hidden.shape[2]
    groups = lax.axis_size("dp")
    chips = lax.axis_size("expert") // CORES
    half = tokens // CORES
    quarter = half // 2
    share = width_in // groups
    group = lax.axis_index("dp")
    expert_place = lax.axis_index("expert")
    chip = expert_place // CORES
    core = expert_place % CORES
    where = jnp.stack([chip, core])

    kept = lax.dynamic_slice_in_dim(cotangent, core * half, half, 0)
    sent = lax.dynamic_slice_in_dim(cotangent, (1 - core) * half, half, 0)
    got = across_cores(sent)
    low = jnp.where(core == 0, kept, got)
    high = jnp.where(core == 0, got, kept)
    own = jnp.concatenate([low, high], axis=1)

    near = lax.all_gather(own, "expert", axis_index_groups=z_lines())
    near = (near, across_cores(near))

    slot_index = jnp.arange(slots, dtype=jnp.int32)
    token_index = jnp.arange(tokens, dtype=jnp.int32)
    live = (row_token[0] >= 0) & (slot_index[None] < tile_count[0][:, None] * TILE)
    token_rows = jnp.where(live, row_token[0], -1)
    experts = expert_place * local_count + jnp.arange(local_count, dtype=jnp.int32)
    named = expert_ids[None] == experts[:, None, None]
    token_gate = jnp.sum(jnp.where(named, gate_weights[None].astype(jnp.float32), 0.0), axis=2)
    at_token = token_rows[:, :, None] == token_index[None, None, :]
    row_gate = jnp.sum(jnp.where(at_token, token_gate[:, None, :], 0.0), axis=2)

    def as_rows(values):
        padded = jnp.pad(values.astype(jnp.bfloat16), ((0, 0), (0, 2 * share - slots)))
        return padded.reshape(local_count, 2, share)

    extra = jnp.concatenate(
        [as_rows(token_rows >> 1), as_rows(token_rows & 1), as_rows(row_gate)], axis=1
    )
    extra = jnp.pad(extra, ((0, 0), (0, EXTRA_ROWS - extra.shape[1]), (0, 0)))
    payloads = []
    for mask in range(groups):
        rows = lax.dynamic_slice_in_dim(hidden[0], (group ^ mask) * share, share, 2)
        payload = jnp.concatenate([rows, extra], axis=1)
        payloads.append(across_dp(payload, mask) if mask else payload)
    shares = shares_by_token(where, payloads, slots, tokens)

    keep, send = expert_sums(where, token_rows, row_gate, hidden[0], down_weight, tokens)
    sums = keep.astype(jnp.float32) + across_cores(send).astype(jnp.float32)
    mixed = lax.psum_scatter(
        sums.astype(jnp.bfloat16), "expert", scatter_dimension=0, axis_index_groups=z_lines()
    )
    mixed_low, mixed_high = mixed[:, :own_cols], mixed[:, own_cols:]
    mixed_mine = jnp.where(core == 0, mixed_low, mixed_high)
    mixed_got = across_cores(jnp.where(core == 0, mixed_high, mixed_low))
    mixed_out = jnp.where(
        core == 0,
        jnp.concatenate([mixed_mine, mixed_got], axis=0),
        jnp.concatenate([mixed_got, mixed_mine], axis=0),
    )

    hidden_grad = hidden_grads(where, token_rows, row_gate, *near, down_weight, tokens)

    weight_grad = None
    first = 0
    for count in (1, chips - 2, 1):
        if first == 0:
            block = own[None]
        else:
            block = jnp.stack(
                [
                    lax.dynamic_index_in_dim(near[0], (chip + first + s) % chips, 0, keepdims=False)
                    for s in range(count)
                ]
            )
        by_x = across_dp(block, 1)
        by_y = across_dp(block, 2)
        far_top = across_dp(by_x[:, :quarter], 2)
        far_end = across_dp(by_y[:, quarter:], 1)
        far = []
        for blocks in ([by_x], [by_y], [far_top, far_end]):
            far.append((blocks, [across_cores(block) for block in blocks]))
        weight_grad = weight_cols(
            where, first, count, shares, near, far, local_count, width, weight_grad
        )
        first += count
    return (mixed_out, hidden_grad[None], weight_grad)


def tile_products(rows_in, weight_mat, count, contract_dim):
    rows_cap = rows_in.shape[0]
    width_out = weight_mat.shape[1 - contract_dim]

    def one_tile(tile_index, outputs):
        block = lax.dynamic_slice_in_dim(rows_in, tile_index * TILE, TILE, 0)
        product = lax.dot_general(
            block,
            weight_mat,
            (((1,), (contract_dim,)), ((), ())),
            preferred_element_type=jnp.float32,
        )
        return lax.dynamic_update_slice_in_dim(
            outputs, product.astype(jnp.bfloat16), tile_index * TILE, 0
        )

    return lax.fori_loop(0, count, one_tile, jnp.zeros((rows_cap, width_out), jnp.bfloat16))


def general_body(hidden, down_weight, cotangent, expert_ids, gate_weights, row_token, tile_count):
    local_count = down_weight.shape[0]
    group_size = cotangent.shape[0]
    expert_index = jnp.arange(EXPERTS, dtype=jnp.int32)
    named_cols = expert_ids[:, :, None] == expert_index[None, None, :]
    gate_cols = jnp.sum(
        jnp.where(named_cols, gate_weights[:, :, None].astype(jnp.float32), 0.0), axis=1
    ).astype(jnp.bfloat16)
    group_cot = lax.all_gather(cotangent, "expert", axis=1, tiled=True)
    width = group_cot.shape[1]
    first_expert = lax.axis_index("expert") * local_count
    slot_index = jnp.arange(hidden.shape[2], dtype=jnp.int32)
    share_rows = down_weight.shape[1] // lax.axis_size("dp")
    partial_value = jnp.zeros((group_size, width), jnp.float32)
    grad_list = []
    weight_list = []
    for local in range(local_count):
        token_rows = row_token[0, local]
        count = tile_count[0, local]
        live_rows = (token_rows >= 0) & (slot_index < count * TILE)
        safe_rows = jnp.where(live_rows, token_rows, 0)
        column = lax.dynamic_index_in_dim(gate_cols, first_expert + local, 1, keepdims=False)
        row_gate = jnp.where(live_rows, column[safe_rows].astype(jnp.float32), 0.0)
        target = jnp.where(live_rows, token_rows, group_size)
        hidden_rows = hidden[0, local]
        weight_mat = down_weight[local]
        out_rows = tile_products(hidden_rows, weight_mat, count, 0)
        partial_value = partial_value.at[target].add(
            row_gate[:, None] * out_rows.astype(jnp.float32), mode="drop"
        )
        routed = (row_gate[:, None] * group_cot[safe_rows].astype(jnp.float32)).astype(jnp.bfloat16)
        grad_list.append(tile_products(routed, weight_mat, count, 1))

        def weight_rows(start, rows_count, hidden_rows=hidden_rows, routed_rows=routed):
            return lax.dot_general(
                hidden_rows,
                routed_rows,
                (((0,), (0,)), ((), ())),
                preferred_element_type=jnp.float32,
            )

        weight_list.append(
            lax.psum_scatter(
                weight_rows(jnp.int32(0), share_rows * lax.axis_size("dp")).astype(jnp.bfloat16),
                "dp",
                scatter_dimension=0,
                tiled=True,
            ).astype(jnp.float32)
        )
    merged = partial_value
    top_bit = lax.axis_size("expert").bit_length() - 1
    axis_index = lax.axis_index("expert")
    for bit_index in reversed(range(top_bit)):
        half_cols = merged.shape[1] // 2
        lower_half = merged[:, :half_cols]
        upper_half = merged[:, half_cols:]
        high_side = axis_index // 2**bit_index % 2 == 1
        sending = jnp.where(high_side, lower_half, upper_half)
        keeping = jnp.where(high_side, upper_half, lower_half)
        merged = keeping + swapped(sending.astype(jnp.bfloat16), "expert", bit_index).astype(
            sending.dtype
        )
    mixed_out = merged.astype(jnp.bfloat16)
    hidden_grad = jnp.stack(grad_list, axis=0)[None]
    weight_grad = jnp.stack(weight_list, axis=0)
    return (mixed_out, hidden_grad, weight_grad)


def solution(mesh):
    placed = (
        P("dp", "expert", None, None),
        P("expert", None, None),
        P("dp", "expert"),
        P("dp", None),
        P("dp", None),
        P("dp", "expert", None),
        P("dp", "expert"),
    )

    def body(*shards):
        width = shards[1].shape[2]
        chips = mesh.shape["expert"] // CORES
        fits = mesh.shape["dp"] == 4 and chips > 1 and width % (chips * LANES) == 0
        return planned_body(*shards) if fits else general_body(*shards)

    return jax.shard_map(
        body,
        mesh=mesh,
        in_specs=placed,
        out_specs=(P("dp", "expert"), P("dp", "expert", None, None), P("expert", "dp", None)),
        check_vma=False,
    )
```

```python
import jax
import jax.numpy as jnp
from jax import lax
from jax.experimental import pallas as pl
from jax.experimental.pallas import tpu as pltpu
from jax.sharding import PartitionSpec as P

EXPERTS = 16
TILE = 128
LANES = 128
CORES = 2
EXTRA_ROWS = 16
VMEM_BYTES = 56 * 1024 * 1024


def swapped(shard, axis, bit):
    return lax.ppermute(shard, axis, [(i, i ^ 1 << bit) for i in range(lax.axis_size(axis))])


def across_dp(shard, mask):
    return lax.ppermute(shard, "dp", [(i, i ^ mask) for i in range(lax.axis_size("dp"))])


def across_cores(shard):
    return swapped(shard, "expert", 0)


def z_lines():
    size = lax.axis_size("expert")
    return [list(range(core, size, CORES)) for core in range(CORES)]


def joined(*values):
    return lax.optimization_barrier(values)


def dot(lhs, rhs, lhs_dim, rhs_dim):
    return lax.dot_general(
        lhs, rhs, (((lhs_dim,), (rhs_dim,)), ((), ())), preferred_element_type=jnp.float32
    )


def hot_rows(token_row, gate_row, first_token, tokens):
    slots = token_row.shape[1]
    token_index = lax.broadcasted_iota(jnp.int32, (tokens, slots), 0) + first_token
    spread = jnp.broadcast_to(gate_row, (tokens, slots))
    return jnp.where(token_index == token_row, spread, 0.0).astype(jnp.bfloat16)


def whole(shape):
    return pl.BlockSpec(shape, lambda *_: (0,) * len(shape))


def call(kernel, scalars, grid, in_specs, out_specs, out_shape, scratch, operands, flops, aliases=None):
    outputs = jax.tree.leaves(out_shape)
    moved = sum(a.size * a.dtype.itemsize for a in [*operands, *outputs])
    return pl.pallas_call(
        kernel,
        grid_spec=pltpu.PrefetchScalarGridSpec(
            num_scalar_prefetch=1,
            grid=grid,
            in_specs=in_specs,
            out_specs=out_specs,
            scratch_shapes=scratch,
        ),
        out_shape=out_shape,
        input_output_aliases=aliases or {},
        cost_estimate=pl.CostEstimate(flops=flops, bytes_accessed=moved, transcendentals=0),
        compiler_params=pltpu.CompilerParams(
            dimension_semantics=("arbitrary",) * len(grid), vmem_limit_bytes=VMEM_BYTES
        ),
    )(scalars, *operands)


def expert_sums(where, token_rows, row_gate, hidden_rows, weight, tokens):
    local_count, slots, width_in = hidden_rows.shape
    chips = lax.axis_size("expert") // CORES
    cols = weight.shape[2] // chips
    half = tokens // CORES

    def kernel(where, token_ref, gate_ref, hidden_ref, weight_ref, keep_ref, send_ref, by_token):
        @pl.when(pl.program_id(0) == 0)
        def _():
            for local in range(local_count):
                for side in range(CORES):
                    first = jnp.bitwise_xor(where[1], side) * half
                    hot = hot_rows(token_ref[local], gate_ref[local], first, half)
                    rows = dot(hot, hidden_ref[local], 1, 0).astype(jnp.bfloat16)
                    by_token[side * half : (side + 1) * half, local * width_in : (local + 1) * width_in] = rows

        stacked = weight_ref[...].reshape(local_count * width_in, cols)
        total = dot(by_token[...], stacked, 1, 0)
        keep_ref[0] = total[:half].T.astype(jnp.bfloat16)
        send_ref[0] = total[half:].T.astype(jnp.bfloat16)

    shape = jax.ShapeDtypeStruct((chips, cols, half), jnp.bfloat16)
    out_spec = pl.BlockSpec((1, cols, half), lambda k, where: (k, 0, 0))
    return call(
        kernel,
        where,
        (chips,),
        [
            whole((local_count, 1, slots)),
            whole((local_count, 1, slots)),
            whole(hidden_rows.shape),
            pl.BlockSpec((local_count, width_in, cols), lambda k, where: (0, 0, k)),
        ],
        (out_spec, out_spec),
        (shape, shape),
        [pltpu.VMEM((tokens, local_count * width_in), jnp.bfloat16)],
        (token_rows[:, None], row_gate[:, None], hidden_rows, weight),
        2 * tokens * weight.size,
    )


def shares_by_token(where, payloads, slots, tokens):
    local_count, _, share = payloads[0].shape
    groups = len(payloads)
    half = tokens // CORES

    def kernel(where, *refs):
        out_ref = refs[-1]

        def row(ref, local, first):
            wide = [ref[local, slots + first + i : slots + first + i + 1, :] for i in range(2)]
            return jnp.concatenate(wide, axis=1)[:, :slots].astype(jnp.float32)

        for group in range(groups):
            ref = refs[group]
            for local in range(local_count):
                token = (row(ref, local, 0) * 2.0 + row(ref, local, 2)).astype(jnp.int32)
                gate = row(ref, local, 4)
                for side in range(CORES):
                    first = jnp.bitwise_xor(where[1], side) * half
                    hot = hot_rows(token, gate, first, half)
                    by_token = dot(hot, ref[local, :slots, :], 1, 0)
                    start = group * tokens + side * half
                    out_ref[start : start + half, local * share : (local + 1) * share] = by_token.astype(
                        jnp.bfloat16
                    )

    shape = (groups * tokens, local_count * share)
    return call(
        kernel,
        where,
        (1,),
        [whole(payload.shape) for payload in payloads],
        whole(shape),
        jax.ShapeDtypeStruct(shape, jnp.bfloat16),
        [],
        payloads,
        2 * shape[0] * shape[1] * slots,
    )


def hidden_grads(where, token_rows, row_gate, mine, other, weight, tokens):
    local_count, width_in, width = weight.shape
    slots = token_rows.shape[1]
    chips, cols, half = mine.shape

    def kernel(where, token_ref, gate_ref, mine_ref, other_ref, weight_ref, out_ref, group_cot):
        local = pl.program_id(0)

        @pl.when(local == 0)
        def _():
            for side, ref in enumerate((mine_ref, other_ref)):
                for chip in range(chips):
                    group_cot[chip * cols : (chip + 1) * cols, side * half : (side + 1) * half] = ref[chip]

        sums = dot(weight_ref[0], group_cot[...], 1, 0).astype(jnp.bfloat16)
        hot = [
            hot_rows(token_ref[local], gate_ref[local], jnp.bitwise_xor(where[1], side) * half, half)
            for side in range(CORES)
        ]
        grads = dot(sums, jnp.concatenate(hot, axis=0), 1, 0)
        out_ref[0] = grads.T.astype(jnp.bfloat16)

    return call(
        kernel,
        where,
        (local_count,),
        [whole((local_count, 1, slots))] * 2
        + [whole(mine.shape)] * 2
        + [pl.BlockSpec((1, width_in, width), lambda e, where: (e, 0, 0))],
        pl.BlockSpec((1, slots, width_in), lambda e, where: (e, 0, 0)),
        jax.ShapeDtypeStruct((local_count, slots, width_in), jnp.bfloat16),
        [pltpu.VMEM((width, tokens), jnp.bfloat16)],
        (token_rows[:, None], row_gate[:, None], mine, other, weight),
        2 * tokens * weight.size,
    )


def weight_cols(where, first, shares, groups, from_group, chips, local_count, width, so_far, add):
    share = shares.shape[1] // local_count
    flat = [block for group in groups for side in group for block in side]
    count = min(block.shape[0] for block in flat)
    cols = sum(block.shape[1] for block in groups[0][0])
    rows = shares.shape[0] // 4 * len(groups)
    given = () if so_far is None else (so_far,)

    def chip_at(place, where):
        return lax.rem(where[0] + first + place, chips)

    def kernel(where, shares_ref, *refs):
        out_ref = refs[-1]
        blocks = []
        place = 0
        for group in groups:
            for side in group:
                pieces = [ref[0] for ref in refs[place : place + len(side)]]
                blocks.append(pieces[0] if len(pieces) == 1 else jnp.concatenate(pieces, axis=0))
                place += len(side)
        total = dot(jnp.concatenate(blocks, axis=1), shares_ref[...], 1, 0).T
        for local in range(local_count):
            part = total[local * share : (local + 1) * share]
            out_ref[local] = part + refs[-2][local] if add else part

    def block_spec(block):
        if block.shape[0] == count:
            return pl.BlockSpec((1, *block.shape[1:]), lambda s, where: (s, 0, 0))
        return pl.BlockSpec((1, *block.shape[1:]), lambda s, where: (chip_at(s, where), 0, 0))

    out_spec = pl.BlockSpec((local_count, share, cols), lambda s, where: (0, 0, chip_at(s, where)))
    first_rows = from_group * (shares.shape[0] // 4) // rows
    return call(
        kernel,
        where,
        (count,),
        [pl.BlockSpec((rows, shares.shape[1]), lambda s, where: (first_rows, 0))]
        + [block_spec(block) for block in flat]
        + [out_spec if add else pl.BlockSpec(memory_space=pl.ANY)] * len(given),
        out_spec,
        jax.ShapeDtypeStruct((local_count, share, width), jnp.float32),
        [],
        (shares, *flat, *given),
        2 * rows * shares.shape[1] * cols * count,
        {2 + len(flat): 0} if given else None,
    )


def planned_body(hidden, down_weight, cotangent, expert_ids, gate_weights, row_token, tile_count):
    local_count, width_in, width = down_weight.shape
    tokens, own_cols = cotangent.shape
    slots = hidden.shape[2]
    groups = lax.axis_size("dp")
    chips = lax.axis_size("expert") // CORES
    half = tokens // CORES
    share = width_in // groups
    group = lax.axis_index("dp")
    expert_place = lax.axis_index("expert")
    chip = expert_place // CORES
    core = expert_place % CORES
    where = jnp.stack([chip, core])

    own_rows = cotangent.T
    kept = lax.dynamic_slice_in_dim(own_rows, core * half, half, 1)
    sent = lax.dynamic_slice_in_dim(own_rows, (1 - core) * half, half, 1)
    got = across_cores(sent)
    own = jnp.where(
        core == 0, jnp.concatenate([kept, got], axis=0), jnp.concatenate([got, kept], axis=0)
    )[None]
    middle = own.shape[1] // 2

    near = lax.all_gather(own[0], "expert", axis_index_groups=z_lines())
    x_own, y_own = across_dp(own, 1), across_dp(own, 2)
    own_other = across_cores(own)

    own, expert_ids, row_token = joined(own, expert_ids, row_token)
    slot_index = jnp.arange(slots, dtype=jnp.int32)
    token_index = jnp.arange(tokens, dtype=jnp.int32)
    live = (row_token[0] >= 0) & (slot_index[None] < tile_count[0][:, None] * TILE)
    token_rows = jnp.where(live, row_token[0], -1)
    experts = expert_place * local_count + jnp.arange(local_count, dtype=jnp.int32)
    named = expert_ids[None] == experts[:, None, None]
    token_gate = jnp.sum(jnp.where(named, gate_weights[None].astype(jnp.float32), 0.0), axis=2)
    at_token = token_rows[:, :, None] == token_index[None, None, :]
    row_gate = jnp.sum(jnp.where(at_token, token_gate[:, None, :], 0.0), axis=2)

    def as_rows(values):
        padded = jnp.pad(values.astype(jnp.bfloat16), ((0, 0), (0, 2 * share - slots)))
        return padded.reshape(local_count, 2, share)

    extra = jnp.concatenate(
        [as_rows(token_rows >> 1), as_rows(token_rows & 1), as_rows(row_gate)], axis=1
    )
    extra = jnp.pad(extra, ((0, 0), (0, EXTRA_ROWS - extra.shape[1]), (0, 0)))
    payloads = []
    for mask in range(groups):
        rows = lax.dynamic_slice_in_dim(hidden[0], (group ^ mask) * share, share, 2)
        payloads.append(jnp.concatenate([rows, extra], axis=1))
    x_own, y_own, own_other, token_rows, row_gate, *payloads = joined(
        x_own, y_own, own_other, token_rows, row_gate, *payloads
    )

    payloads = [across_dp(payload, mask) if mask else payload for mask, payload in enumerate(payloads)]
    far_own = [across_dp(x_own[:, :middle], 2), across_dp(y_own[:, middle:], 1)]

    keep, send = expert_sums(where, token_rows, row_gate, hidden[0], down_weight, tokens)
    x_own, y_own, keep, send, *sent = joined(x_own, y_own, keep, send, *payloads, *far_own)
    payloads, far_own = sent[:groups], sent[groups:]

    from_other, x_own_other, y_own_other = across_cores(send), across_cores(x_own), across_cores(y_own)
    far_own_other = [across_cores(piece) for piece in far_own]

    sums = (keep.astype(jnp.float32) + from_other.astype(jnp.float32)).astype(jnp.bfloat16)
    mixed = lax.psum_scatter(sums, "expert", scatter_dimension=0, axis_index_groups=z_lines())

    rest = jnp.stack(
        [
            lax.dynamic_index_in_dim(near, (chip + place) % chips, 0, keepdims=False)
            for place in range(1, chips)
        ]
    )
    x_rest, y_rest = across_dp(rest, 1), across_dp(rest, 2)
    near_other = across_cores(near)
    shares = shares_by_token(where, payloads, slots, tokens)
    sizes = (chips, local_count, width)
    weight_grad = weight_cols(
        where,
        0,
        shares,
        [
            ([own], [own_other]),
            ([x_own], [x_own_other]),
            ([y_own], [y_own_other]),
            (far_own, far_own_other),
        ],
        0,
        *sizes,
        None,
        False,
    )
    weight_grad, near_other = joined(weight_grad, near_other)
    hidden_grad = hidden_grads(where, token_rows, row_gate, near, near_other, down_weight, tokens)
    hidden_grad, x_rest, y_rest = joined(hidden_grad, x_rest, y_rest)
    far_rest = [across_dp(x_rest[:, :middle], 2), across_dp(y_rest[:, middle:], 1)]
    x_rest_other, y_rest_other = across_cores(x_rest), across_cores(y_rest)
    weight_grad = weight_cols(
        where,
        1,
        shares,
        [([near], [near_other]), ([x_rest], [x_rest_other]), ([y_rest], [y_rest_other])],
        0,
        *sizes,
        weight_grad,
        False,
    )
    weight_grad, mixed, *far_rest = joined(weight_grad, mixed, *far_rest)
    far_rest_other = [across_cores(piece) for piece in far_rest]

    mixed_low, mixed_high = mixed[:own_cols], mixed[own_cols:]
    mixed_mine = jnp.where(core == 0, mixed_low, mixed_high)
    mixed_got = across_cores(jnp.where(core == 0, mixed_high, mixed_low))
    mixed_out = jnp.where(
        core == 0,
        jnp.concatenate([mixed_mine, mixed_got], axis=1),
        jnp.concatenate([mixed_got, mixed_mine], axis=1),
    ).T
    weight_grad = weight_cols(
        where, 1, shares, [(far_rest, far_rest_other)], groups - 1, *sizes, weight_grad, True
    )
    return (mixed_out, hidden_grad[None], weight_grad)


def tile_products(rows_in, weight_mat, count, contract_dim):
    rows_cap = rows_in.shape[0]
    width_out = weight_mat.shape[1 - contract_dim]

    def one_tile(tile_index, outputs):
        block = lax.dynamic_slice_in_dim(rows_in, tile_index * TILE, TILE, 0)
        product = lax.dot_general(
            block,
            weight_mat,
            (((1,), (contract_dim,)), ((), ())),
            preferred_element_type=jnp.float32,
        )
        return lax.dynamic_update_slice_in_dim(
            outputs, product.astype(jnp.bfloat16), tile_index * TILE, 0
        )

    return lax.fori_loop(0, count, one_tile, jnp.zeros((rows_cap, width_out), jnp.bfloat16))


def general_body(hidden, down_weight, cotangent, expert_ids, gate_weights, row_token, tile_count):
    local_count = down_weight.shape[0]
    group_size = cotangent.shape[0]
    expert_index = jnp.arange(EXPERTS, dtype=jnp.int32)
    named_cols = expert_ids[:, :, None] == expert_index[None, None, :]
    gate_cols = jnp.sum(
        jnp.where(named_cols, gate_weights[:, :, None].astype(jnp.float32), 0.0), axis=1
    ).astype(jnp.bfloat16)
    group_cot = lax.all_gather(cotangent, "expert", axis=1, tiled=True)
    width = group_cot.shape[1]
    first_expert = lax.axis_index("expert") * local_count
    slot_index = jnp.arange(hidden.shape[2], dtype=jnp.int32)
    share_rows = down_weight.shape[1] // lax.axis_size("dp")
    partial_value = jnp.zeros((group_size, width), jnp.float32)
    grad_list = []
    weight_list = []
    for local in range(local_count):
        token_rows = row_token[0, local]
        count = tile_count[0, local]
        live_rows = (token_rows >= 0) & (slot_index < count * TILE)
        safe_rows = jnp.where(live_rows, token_rows, 0)
        column = lax.dynamic_index_in_dim(gate_cols, first_expert + local, 1, keepdims=False)
        row_gate = jnp.where(live_rows, column[safe_rows].astype(jnp.float32), 0.0)
        target = jnp.where(live_rows, token_rows, group_size)
        hidden_rows = hidden[0, local]
        weight_mat = down_weight[local]
        out_rows = tile_products(hidden_rows, weight_mat, count, 0)
        partial_value = partial_value.at[target].add(
            row_gate[:, None] * out_rows.astype(jnp.float32), mode="drop"
        )
        routed = (row_gate[:, None] * group_cot[safe_rows].astype(jnp.float32)).astype(jnp.bfloat16)
        grad_list.append(tile_products(routed, weight_mat, count, 1))

        def weight_rows(start, rows_count, hidden_rows=hidden_rows, routed_rows=routed):
            return lax.dot_general(
                hidden_rows,
                routed_rows,
                (((0,), (0,)), ((), ())),
                preferred_element_type=jnp.float32,
            )

        weight_list.append(
            lax.psum_scatter(
                weight_rows(jnp.int32(0), share_rows * lax.axis_size("dp")).astype(jnp.bfloat16),
                "dp",
                scatter_dimension=0,
                tiled=True,
            ).astype(jnp.float32)
        )
    merged = partial_value
    top_bit = lax.axis_size("expert").bit_length() - 1
    axis_index = lax.axis_index("expert")
    for bit_index in reversed(range(top_bit)):
        half_cols = merged.shape[1] // 2
        lower_half = merged[:, :half_cols]
        upper_half = merged[:, half_cols:]
        high_side = axis_index // 2**bit_index % 2 == 1
        sending = jnp.where(high_side, lower_half, upper_half)
        keeping = jnp.where(high_side, upper_half, lower_half)
        merged = keeping + swapped(sending.astype(jnp.bfloat16), "expert", bit_index).astype(
            sending.dtype
        )
    mixed_out = merged.astype(jnp.bfloat16)
    hidden_grad = jnp.stack(grad_list, axis=0)[None]
    weight_grad = jnp.stack(weight_list, axis=0)
    return (mixed_out, hidden_grad, weight_grad)


def solution(mesh):
    placed = (
        P("dp", "expert", None, None),
        P("expert", None, None),
        P("dp", "expert"),
        P("dp", None),
        P("dp", None),
        P("dp", "expert", None),
        P("dp", "expert"),
    )

    def body(*shards):
        width = shards[1].shape[2]
        chips = mesh.shape["expert"] // CORES
        fits = mesh.shape["dp"] == 4 and chips > 2 and width % (chips * LANES) == 0
        return planned_body(*shards) if fits else general_body(*shards)

    return jax.shard_map(
        body,
        mesh=mesh,
        in_specs=placed,
        out_specs=(P("dp", "expert"), P("dp", "expert", None, None), P("expert", "dp", None)),
        check_vma=False,
    )
```

```python
import jax
import jax.numpy as jnp
from jax import lax
from jax.experimental import pallas as pl
from jax.experimental.pallas import tpu as pltpu
from jax.sharding import PartitionSpec as P

EXPERTS = 16
TILE = 128
LANES = 128
CORES = 2
EXTRA_ROWS = 16
VMEM_BYTES = 56 * 1024 * 1024


def swapped(shard, axis, bit):
    return lax.ppermute(shard, axis, [(i, i ^ 1 << bit) for i in range(lax.axis_size(axis))])


def across_dp(shard, mask):
    return lax.ppermute(shard, "dp", [(i, i ^ mask) for i in range(lax.axis_size("dp"))])


def across_cores(shard):
    return swapped(shard, "expert", 0)


def along_z(shard, step, senders):
    pairs = [
        (CORES * z + core, CORES * (z + step) + core) for z in senders for core in range(CORES)
    ]
    return lax.ppermute(shard, "expert", pairs)


def z_lines():
    size = lax.axis_size("expert")
    return [list(range(core, size, CORES)) for core in range(CORES)]


def joined(*values):
    return lax.optimization_barrier(values)


def dot(lhs, rhs, lhs_dim, rhs_dim):
    return lax.dot_general(
        lhs, rhs, (((lhs_dim,), (rhs_dim,)), ((), ())), preferred_element_type=jnp.float32
    )


def hot_rows(token_row, gate_row, tokens):
    slots = token_row.shape[1]
    token_index = lax.broadcasted_iota(jnp.int32, (tokens, slots), 0)
    spread = jnp.broadcast_to(gate_row, (tokens, slots))
    return jnp.where(token_index == token_row, spread, 0.0).astype(jnp.bfloat16)


def whole(shape):
    return pl.BlockSpec(shape, lambda *_: (0,) * len(shape))


def call(kernel, scalars, grid, in_specs, out_specs, out_shape, scratch, operands, flops, aliases=None):
    outputs = jax.tree.leaves(out_shape)
    moved = sum(a.size * a.dtype.itemsize for a in [*operands, *outputs])
    return pl.pallas_call(
        kernel,
        grid_spec=pltpu.PrefetchScalarGridSpec(
            num_scalar_prefetch=1,
            grid=grid,
            in_specs=in_specs,
            out_specs=out_specs,
            scratch_shapes=scratch,
        ),
        out_shape=out_shape,
        input_output_aliases=aliases or {},
        cost_estimate=pl.CostEstimate(flops=flops, bytes_accessed=moved, transcendentals=0),
        compiler_params=pltpu.CompilerParams(
            dimension_semantics=("arbitrary",) * len(grid), vmem_limit_bytes=VMEM_BYTES
        ),
    )(scalars, *operands)


def expert_sums(where, weight, first, count, rows):
    local_count, width_in, width = weight.shape
    cols = width // (lax.axis_size("expert") // CORES)
    half = cols // CORES
    making = len(rows) > 1
    tokens = rows[3] if making else rows[0].shape[0]
    rows = rows[:3]
    by_token = (tokens, local_count * width_in)

    def kernel(where, *refs):
        weight_ref, keep_ref, send_ref = refs[len(rows) : len(rows) + 3]
        turned = refs[-1]
        rows_ref = refs[-2] if making else refs[0]

        if making:
            token_ref, gate_ref, hidden_ref = refs[:3]

            @pl.when(pl.program_id(0) == 0)
            def _():
                for local in range(local_count):
                    hot = hot_rows(token_ref[local], gate_ref[local], tokens)
                    made = dot(hot, hidden_ref[local], 1, 0).astype(jnp.bfloat16)
                    rows_ref[:, local * width_in : (local + 1) * width_in] = made

        stacked = weight_ref[...].reshape(local_count * width_in, cols)
        turned[...] = dot(rows_ref[...], stacked, 1, 0).astype(jnp.bfloat16).T
        keep_ref[0] = turned[pl.ds(pl.multiple_of(where[1] * half, half), half), :]
        send_ref[0] = turned[pl.ds(pl.multiple_of((1 - where[1]) * half, half), half), :]

    shape = jax.ShapeDtypeStruct((count, half, tokens), jnp.bfloat16)
    out_spec = pl.BlockSpec((1, half, tokens), lambda k, where: (k, 0, 0))
    out_shapes, out_specs = [shape, shape], [out_spec, out_spec]
    if making:
        out_shapes.append(jax.ShapeDtypeStruct(by_token, jnp.bfloat16))
        out_specs.append(whole(by_token))
    return call(
        kernel,
        where,
        (count,),
        [whole(array.shape) for array in rows]
        + [pl.BlockSpec((local_count, width_in, cols), lambda k, where: (0, 0, first + k))],
        out_specs,
        out_shapes,
        [pltpu.VMEM((cols, tokens), jnp.bfloat16)],
        (*rows, weight),
        2 * tokens * local_count * width_in * cols * count,
    )


def shares_by_token(where, payloads, slots, tokens):
    local_count, _, share = payloads[0].shape
    groups = len(payloads)

    def kernel(where, *refs):
        out_ref = refs[-1]

        def row(ref, local, first):
            wide = [ref[local, slots + first + i : slots + first + i + 1, :] for i in range(2)]
            return jnp.concatenate(wide, axis=1)[:, :slots].astype(jnp.float32)

        for group in range(groups):
            ref = refs[group]
            for local in range(local_count):
                token = (row(ref, local, 0) * 2.0 + row(ref, local, 2)).astype(jnp.int32)
                hot = hot_rows(token, row(ref, local, 4), tokens)
                by_token = dot(hot, ref[local, :slots, :], 1, 0).astype(jnp.bfloat16)
                out_ref[local * share : (local + 1) * share, group * tokens : (group + 1) * tokens] = by_token.T

    shape = (local_count * share, groups * tokens)
    return call(
        kernel,
        where,
        (1,),
        [whole(payload.shape) for payload in payloads],
        whole(shape),
        jax.ShapeDtypeStruct(shape, jnp.bfloat16),
        [],
        payloads,
        2 * shape[0] * shape[1] * slots,
    )


def hidden_grads(where, token_rows, row_gate, mine, other, weight):
    local_count, width_in, width = weight.shape
    slots = token_rows.shape[1]
    half, tokens = mine[0].shape[1:]
    flat = [*mine, *other]

    def kernel(where, token_ref, gate_ref, *refs):
        weight_ref, out_ref, group_cot = refs[len(flat) :]
        local = pl.program_id(0)

        @pl.when(local == 0)
        def _():
            for side in range(CORES):
                core = jnp.bitwise_xor(where[1], side)
                place = 0
                for ref in refs[side * len(mine) : (side + 1) * len(mine)]:
                    for row in range(ref.shape[0]):
                        start = (where[CORES + place] * CORES + core) * half
                        group_cot[pl.ds(pl.multiple_of(start, half), half), :] = ref[row]
                        place += 1

        sums = dot(weight_ref[0], group_cot[...], 1, 0).astype(jnp.bfloat16)
        hot = hot_rows(token_ref[local], gate_ref[local], tokens)
        out_ref[0] = dot(hot, sums, 0, 1).astype(jnp.bfloat16)

    return call(
        kernel,
        where,
        (local_count,),
        [whole((local_count, 1, slots))] * 2
        + [whole(block.shape) for block in flat]
        + [pl.BlockSpec((1, width_in, width), lambda e, where: (e, 0, 0))],
        pl.BlockSpec((1, slots, width_in), lambda e, where: (e, 0, 0)),
        jax.ShapeDtypeStruct((local_count, slots, width_in), jnp.bfloat16),
        [pltpu.VMEM((width, tokens), jnp.bfloat16)],
        (token_rows[:, None], row_gate[:, None], *flat, weight),
        2 * tokens * weight.size,
    )


def weight_cols(where, first, shares, groups, from_group, local_count, width, so_far, add):
    share = shares.shape[0] // local_count
    flat = [block for group in groups for side in group for block in side]
    count, _, tokens = flat[0].shape
    cols = CORES * sum(block.shape[1] for block in groups[0][0])
    depth = tokens * len(groups)
    given = () if so_far is None else (so_far,)

    def kernel(where, shares_ref, *refs):
        out_ref = refs[-1]
        sides = [[], []]
        place = 0
        for group in groups:
            for side, pieces in zip(sides, group):
                loaded = [ref[0] for ref in refs[place : place + len(pieces)]]
                side.append(loaded[0] if len(loaded) == 1 else jnp.concatenate(loaded, axis=0))
                place += len(pieces)
        mine, other = [side[0] if len(side) == 1 else jnp.concatenate(side, axis=1) for side in sides]
        low = jnp.where(where[1] == 0, mine, other)
        high = jnp.where(where[1] == 0, other, mine)
        total = dot(shares_ref[...], jnp.concatenate([low, high], axis=0), 1, 1)
        for local in range(local_count):
            part = total[local * share : (local + 1) * share]
            out_ref[local] = part + refs[-2][local] if add else part

    out_spec = pl.BlockSpec(
        (local_count, share, cols), lambda s, where: (0, 0, where[CORES + first + s])
    )
    return call(
        kernel,
        where,
        (count,),
        [pl.BlockSpec((shares.shape[0], depth), lambda s, where: (0, from_group * tokens // depth))]
        + [pl.BlockSpec((1, *block.shape[1:]), lambda s, where: (s, 0, 0)) for block in flat]
        + [out_spec if add else pl.BlockSpec(memory_space=pl.ANY)] * len(given),
        out_spec,
        jax.ShapeDtypeStruct((local_count, share, width), jnp.float32),
        [],
        (shares, *flat, *given),
        2 * depth * shares.shape[0] * cols * count,
        {2 + len(flat): 0} if given else None,
    )


def planned_body(hidden, down_weight, cotangent, expert_ids, gate_weights, row_token, tile_count):
    local_count, width_in, width = down_weight.shape
    tokens = cotangent.shape[0]
    slots = hidden.shape[2]
    groups = lax.axis_size("dp")
    chips = lax.axis_size("expert") // CORES
    share = width_in // groups
    group = lax.axis_index("dp")
    expert_place = lax.axis_index("expert")
    chip = expert_place // CORES
    core = expert_place % CORES
    rest = (local_count, width)

    at_low, at_high = chip == 0, chip == chips - 1
    low_half = chip < chips // 2
    where = jnp.stack(
        [
            chip,
            core,
            chip,
            jnp.where(at_low, chip + 1, chip - 1),
            jnp.where(at_low, chip + 2, jnp.where(at_high, chip - 2, chip + 1)),
            jnp.where(at_low, chip + 3, jnp.where(at_high, chip - 3, jnp.where(low_half, chip + 2, chip - 2))),
        ]
    )

    own = cotangent.T
    middle = own.shape[0] // 2
    low_1, high_1 = along_z(own, 1, range(chips - 1)), along_z(own, -1, range(1, chips))
    x_own, y_own = across_dp(own, 1), across_dp(own, 2)
    own_other = across_cores(own)

    slot_index = jnp.arange(slots, dtype=jnp.int32)
    token_index = jnp.arange(tokens, dtype=jnp.int32)
    live = (row_token[0] >= 0) & (slot_index[None] < tile_count[0][:, None] * TILE)
    token_rows = jnp.where(live, row_token[0], -1)
    experts = expert_place * local_count + jnp.arange(local_count, dtype=jnp.int32)
    named = expert_ids[None] == experts[:, None, None]
    token_gate = jnp.sum(jnp.where(named, gate_weights[None].astype(jnp.float32), 0.0), axis=2)
    at_token = token_rows[:, :, None] == token_index[None, None, :]
    row_gate = jnp.sum(jnp.where(at_token, token_gate[:, None, :], 0.0), axis=2)

    def as_rows(values):
        padded = jnp.pad(values.astype(jnp.bfloat16), ((0, 0), (0, 2 * share - slots)))
        return padded.reshape(local_count, 2, share)

    extra = jnp.concatenate(
        [as_rows(token_rows >> 1), as_rows(token_rows & 1), as_rows(row_gate)], axis=1
    )
    extra = jnp.pad(extra, ((0, 0), (0, EXTRA_ROWS - extra.shape[1]), (0, 0)))
    payloads = []
    for mask in range(groups):
        rows = lax.dynamic_slice_in_dim(hidden[0], (group ^ mask) * share, share, 2)
        payloads.append(jnp.concatenate([rows, extra], axis=1))
    low_1, high_1, x_own, y_own, own_other, token_rows, row_gate, *payloads = joined(
        low_1, high_1, x_own, y_own, own_other, token_rows, row_gate, *payloads
    )

    x_payload, y_payload = across_dp(payloads[1], 1), across_dp(payloads[2], 2)
    low_2, high_2 = along_z(low_1, 1, range(1, chips - 1)), along_z(high_1, -1, range(1, chips - 1))
    x_own_other = across_cores(x_own)
    making = (token_rows[:, None], row_gate[:, None], hidden[0], tokens)
    keep_low, send_low, by_token = expert_sums(where, down_weight, 0, chips // 2, making)
    x_payload, y_payload, low_2, high_2, x_own_other, keep_low, send_low, by_token = joined(
        x_payload, y_payload, low_2, high_2, x_own_other, keep_low, send_low, by_token
    )

    far_payload = across_dp(payloads[3], 3)
    low_3, high_3 = along_z(low_2, 1, range(2, chips - 1)), along_z(high_2, -1, range(1, chips - 2))
    far_own = [across_dp(x_own[:middle], 2), across_dp(y_own[middle:], 1)]
    keep_high, send_high = expert_sums(where, down_weight, chips // 2, chips - chips // 2, (by_token,))
    far_payload, low_3, high_3, keep_high, send_high, x_own, y_own, *far_own = joined(
        far_payload, low_3, high_3, keep_high, send_high, x_own, y_own, *far_own
    )

    near = jnp.stack(
        [
            jnp.where(at_low, high_1, low_1),
            jnp.where(at_low, high_2, jnp.where(at_high, low_2, high_1)),
            jnp.where(at_low, high_3, jnp.where(at_high, low_3, jnp.where(low_half, high_2, low_2))),
        ]
    )
    low_other, high_other, y_own_other = [across_cores(block) for block in (send_low, send_high, y_own)]
    payloads = (payloads[0], x_payload, y_payload, far_payload)
    low_other, high_other, y_own_other, near, *sent = joined(
        low_other, high_other, y_own_other, near, *far_own, *payloads
    )
    far_own, payloads = sent[: len(far_own)], sent[len(far_own) :]
    x_near, y_near = across_dp(near, 1), across_dp(near, 2)
    shares = shares_by_token(where, payloads, slots, tokens)

    far_own_other = [across_cores(block) for block in far_own]
    near_other = across_cores(near)
    keep = jnp.concatenate([keep_low, keep_high], axis=0).astype(jnp.float32)
    other = jnp.concatenate([low_other, high_other], axis=0).astype(jnp.float32)
    sums = (keep + other).astype(jnp.bfloat16)
    mixed = lax.psum_scatter(sums, "expert", scatter_dimension=0, axis_index_groups=z_lines())

    def by_chip(*blocks):
        return [block[None] for block in blocks]

    weight_grad = weight_cols(
        where,
        0,
        shares,
        [
            (by_chip(own), by_chip(own_other)),
            (by_chip(x_own), by_chip(x_own_other)),
            (by_chip(y_own), by_chip(y_own_other)),
            (by_chip(*far_own), by_chip(*far_own_other)),
        ],
        0,
        *rest,
        None,
        False,
    )
    weight_grad, near_other = joined(weight_grad, near_other)
    hidden_grad = hidden_grads(
        where, token_rows, row_gate, [own[None], near], [own_other[None], near_other], down_weight
    )
    hidden_grad, x_near, y_near = joined(hidden_grad, x_near, y_near)

    far_near = [across_dp(x_near[:, :middle], 2), across_dp(y_near[:, middle:], 1)]
    x_other, y_other = across_cores(x_near), across_cores(y_near)
    weight_grad = weight_cols(
        where,
        1,
        shares,
        [([near], [near_other]), ([x_near], [x_other]), ([y_near], [y_other])],
        0,
        *rest,
        weight_grad,
        False,
    )
    weight_grad, mixed, *far_near = joined(weight_grad, mixed, *far_near)
    far_other = [across_cores(piece) for piece in far_near]
    weight_grad = weight_cols(
        where, 1, shares, [(far_near, far_other)], groups - 1, *rest, weight_grad, True
    )
    return (mixed.T, hidden_grad[None], weight_grad)


def tile_products(rows_in, weight_mat, count, contract_dim):
    rows_cap = rows_in.shape[0]
    width_out = weight_mat.shape[1 - contract_dim]

    def one_tile(tile_index, outputs):
        block = lax.dynamic_slice_in_dim(rows_in, tile_index * TILE, TILE, 0)
        product = lax.dot_general(
            block,
            weight_mat,
            (((1,), (contract_dim,)), ((), ())),
            preferred_element_type=jnp.float32,
        )
        return lax.dynamic_update_slice_in_dim(
            outputs, product.astype(jnp.bfloat16), tile_index * TILE, 0
        )

    return lax.fori_loop(0, count, one_tile, jnp.zeros((rows_cap, width_out), jnp.bfloat16))


def general_body(hidden, down_weight, cotangent, expert_ids, gate_weights, row_token, tile_count):
    local_count = down_weight.shape[0]
    group_size = cotangent.shape[0]
    expert_index = jnp.arange(EXPERTS, dtype=jnp.int32)
    named_cols = expert_ids[:, :, None] == expert_index[None, None, :]
    gate_cols = jnp.sum(
        jnp.where(named_cols, gate_weights[:, :, None].astype(jnp.float32), 0.0), axis=1
    ).astype(jnp.bfloat16)
    group_cot = lax.all_gather(cotangent, "expert", axis=1, tiled=True)
    width = group_cot.shape[1]
    first_expert = lax.axis_index("expert") * local_count
    slot_index = jnp.arange(hidden.shape[2], dtype=jnp.int32)
    share_rows = down_weight.shape[1] // lax.axis_size("dp")
    partial_value = jnp.zeros((group_size, width), jnp.float32)
    grad_list = []
    weight_list = []
    for local in range(local_count):
        token_rows = row_token[0, local]
        count = tile_count[0, local]
        live_rows = (token_rows >= 0) & (slot_index < count * TILE)
        safe_rows = jnp.where(live_rows, token_rows, 0)
        column = lax.dynamic_index_in_dim(gate_cols, first_expert + local, 1, keepdims=False)
        row_gate = jnp.where(live_rows, column[safe_rows].astype(jnp.float32), 0.0)
        target = jnp.where(live_rows, token_rows, group_size)
        hidden_rows = hidden[0, local]
        weight_mat = down_weight[local]
        out_rows = tile_products(hidden_rows, weight_mat, count, 0)
        partial_value = partial_value.at[target].add(
            row_gate[:, None] * out_rows.astype(jnp.float32), mode="drop"
        )
        routed = (row_gate[:, None] * group_cot[safe_rows].astype(jnp.float32)).astype(jnp.bfloat16)
        grad_list.append(tile_products(routed, weight_mat, count, 1))

        def weight_rows(start, rows_count, hidden_rows=hidden_rows, routed_rows=routed):
            return lax.dot_general(
                hidden_rows,
                routed_rows,
                (((0,), (0,)), ((), ())),
                preferred_element_type=jnp.float32,
            )

        weight_list.append(
            lax.psum_scatter(
                weight_rows(jnp.int32(0), share_rows * lax.axis_size("dp")).astype(jnp.bfloat16),
                "dp",
                scatter_dimension=0,
                tiled=True,
            ).astype(jnp.float32)
        )
    merged = partial_value
    top_bit = lax.axis_size("expert").bit_length() - 1
    axis_index = lax.axis_index("expert")
    for bit_index in reversed(range(top_bit)):
        half_cols = merged.shape[1] // 2
        lower_half = merged[:, :half_cols]
        upper_half = merged[:, half_cols:]
        high_side = axis_index // 2**bit_index % 2 == 1
        sending = jnp.where(high_side, lower_half, upper_half)
        keeping = jnp.where(high_side, upper_half, lower_half)
        merged = keeping + swapped(sending.astype(jnp.bfloat16), "expert", bit_index).astype(
            sending.dtype
        )
    mixed_out = merged.astype(jnp.bfloat16)
    hidden_grad = jnp.stack(grad_list, axis=0)[None]
    weight_grad = jnp.stack(weight_list, axis=0)
    return (mixed_out, hidden_grad, weight_grad)


def solution(mesh):
    placed = (
        P("dp", "expert", None, None),
        P("expert", None, None),
        P("dp", "expert"),
        P("dp", None),
        P("dp", None),
        P("dp", "expert", None),
        P("dp", "expert"),
    )

    def body(*shards):
        width = shards[1].shape[2]
        chips = mesh.shape["expert"] // CORES
        fits = mesh.shape["dp"] == 4 and chips == 4 and width % (chips * LANES) == 0
        return planned_body(*shards) if fits else general_body(*shards)

    return jax.shard_map(
        body,
        mesh=mesh,
        in_specs=placed,
        out_specs=(P("dp", "expert"), P("dp", "expert", None, None), P("expert", "dp", None)),
        check_vma=False,
    )
```

```python
import jax
import jax.numpy as jnp
from jax import lax
from jax.experimental import pallas as pl
from jax.experimental.pallas import tpu as pltpu
from jax.sharding import PartitionSpec as P

EXPERTS = 16
TILE = 128
LANES = 128
CORES = 2
EXTRA_ROWS = 16
VMEM_BYTES = 56 * 1024 * 1024


def swapped(shard, axis, bit):
    return lax.ppermute(shard, axis, [(i, i ^ 1 << bit) for i in range(lax.axis_size(axis))])


def across_dp(shard, mask):
    return lax.ppermute(shard, "dp", [(i, i ^ mask) for i in range(lax.axis_size("dp"))])


def across_cores(shard):
    return swapped(shard, "expert", 0)


def z_lines():
    size = lax.axis_size("expert")
    return [list(range(core, size, CORES)) for core in range(CORES)]


def joined(*values):
    return lax.optimization_barrier(values)


def dot(lhs, rhs, lhs_dim, rhs_dim):
    return lax.dot_general(
        lhs, rhs, (((lhs_dim,), (rhs_dim,)), ((), ())), preferred_element_type=jnp.float32
    )


def hot_rows(token_row, gate_row, tokens):
    slots = token_row.shape[1]
    token_index = lax.broadcasted_iota(jnp.int32, (tokens, slots), 0)
    spread = jnp.broadcast_to(gate_row, (tokens, slots))
    return jnp.where(token_index == token_row, spread, 0.0).astype(jnp.bfloat16)


def whole(shape):
    return pl.BlockSpec(shape, lambda *_: (0,) * len(shape))


def call(kernel, scalars, grid, in_specs, out_specs, out_shape, scratch, operands, flops, aliases=None):
    outputs = jax.tree.leaves(out_shape)
    moved = sum(a.size * a.dtype.itemsize for a in [*operands, *outputs])
    return pl.pallas_call(
        kernel,
        grid_spec=pltpu.PrefetchScalarGridSpec(
            num_scalar_prefetch=1,
            grid=grid,
            in_specs=in_specs,
            out_specs=out_specs,
            scratch_shapes=scratch,
        ),
        out_shape=out_shape,
        input_output_aliases=aliases or {},
        cost_estimate=pl.CostEstimate(flops=flops, bytes_accessed=moved, transcendentals=0),
        compiler_params=pltpu.CompilerParams(
            dimension_semantics=("arbitrary",) * len(grid), vmem_limit_bytes=VMEM_BYTES
        ),
    )(scalars, *operands)


def expert_sums(where, token_rows, row_gate, hidden_rows, weight, tokens):
    local_count, slots, width_in = hidden_rows.shape
    chips = lax.axis_size("expert") // CORES
    cols = weight.shape[2] // chips
    half = cols // CORES

    def kernel(where, token_ref, gate_ref, hidden_ref, weight_ref, keep_ref, send_ref, by_token, turned):
        @pl.when(pl.program_id(0) == 0)
        def _():
            for local in range(local_count):
                hot = hot_rows(token_ref[local], gate_ref[local], tokens)
                made = dot(hot, hidden_ref[local], 1, 0).astype(jnp.bfloat16)
                by_token[:, local * width_in : (local + 1) * width_in] = made

        stacked = weight_ref[...].reshape(local_count * width_in, cols)
        turned[...] = dot(by_token[...], stacked, 1, 0).astype(jnp.bfloat16).T
        keep_ref[0] = turned[pl.ds(pl.multiple_of(where[1] * half, half), half), :]
        send_ref[0] = turned[pl.ds(pl.multiple_of((1 - where[1]) * half, half), half), :]

    shape = jax.ShapeDtypeStruct((chips, half, tokens), jnp.bfloat16)
    out_spec = pl.BlockSpec((1, half, tokens), lambda k, where: (k, 0, 0))
    return call(
        kernel,
        where,
        (chips,),
        [
            whole((local_count, 1, slots)),
            whole((local_count, 1, slots)),
            whole(hidden_rows.shape),
            pl.BlockSpec((local_count, width_in, cols), lambda k, where: (0, 0, k)),
        ],
        (out_spec, out_spec),
        (shape, shape),
        [
            pltpu.VMEM((tokens, local_count * width_in), jnp.bfloat16),
            pltpu.VMEM((cols, tokens), jnp.bfloat16),
        ],
        (token_rows[:, None], row_gate[:, None], hidden_rows, weight),
        2 * tokens * weight.size,
    )


def shares_by_token(where, payloads, slots, tokens):
    local_count, _, share = payloads[0].shape
    groups = len(payloads)

    def kernel(where, *refs):
        out_ref = refs[-1]

        def row(ref, local, first):
            wide = [ref[local, slots + first + i : slots + first + i + 1, :] for i in range(2)]
            return jnp.concatenate(wide, axis=1)[:, :slots].astype(jnp.float32)

        for group in range(groups):
            ref = refs[group]
            for local in range(local_count):
                token = (row(ref, local, 0) * 2.0 + row(ref, local, 2)).astype(jnp.int32)
                hot = hot_rows(token, row(ref, local, 4), tokens)
                by_token = dot(hot, ref[local, :slots, :], 1, 0).astype(jnp.bfloat16)
                out_ref[local * share : (local + 1) * share, group * tokens : (group + 1) * tokens] = by_token.T

    shape = (local_count * share, groups * tokens)
    return call(
        kernel,
        where,
        (1,),
        [whole(payload.shape) for payload in payloads],
        whole(shape),
        jax.ShapeDtypeStruct(shape, jnp.bfloat16),
        [],
        payloads,
        2 * shape[0] * shape[1] * slots,
    )


def hidden_grads(where, token_rows, row_gate, group_cot, weight):
    local_count, width_in, width = weight.shape
    slots = token_rows.shape[1]
    tokens = group_cot.shape[1]
    depth = width_in // 2

    def kernel(where, token_ref, gate_ref, cot_ref, weight_ref, out_ref):
        local = pl.program_id(0)
        sums = dot(weight_ref[0], cot_ref[...], 1, 0).astype(jnp.bfloat16)
        hot = hot_rows(token_ref[local], gate_ref[local], tokens)
        out_ref[0] = dot(hot, sums, 0, 1).astype(jnp.bfloat16)

    return call(
        kernel,
        where,
        (local_count, width_in // depth),
        [whole((local_count, 1, slots))] * 2
        + [whole(group_cot.shape)]
        + [pl.BlockSpec((1, depth, width), lambda e, h, where: (e, h, 0))],
        pl.BlockSpec((1, slots, depth), lambda e, h, where: (e, 0, h)),
        jax.ShapeDtypeStruct((local_count, slots, width_in), jnp.bfloat16),
        [],
        (token_rows[:, None], row_gate[:, None], group_cot, weight),
        2 * tokens * weight.size,
    )


def weight_cols(where, place, shares, groups, local_count, width, so_far):
    share = shares.shape[0] // local_count
    chips = lax.axis_size("expert") // CORES
    cols = width // chips
    tokens = groups[0][0][0][0].shape[-1]
    flat = [piece for group in groups for side in group for piece in side]
    given = () if so_far is None else (so_far,)

    def kernel(where, shares_ref, *refs):
        out_ref, total_ref, sem = refs[-3:]
        sums = [None] * CORES
        at = 0
        for group, sides in enumerate(groups):
            part = shares_ref[:, group * tokens : (group + 1) * tokens]
            for side, pieces in enumerate(sides):
                loaded = [refs[at + i][index] for i, (_, index) in enumerate(pieces)]
                at += len(pieces)
                block = loaded[0] if len(loaded) == 1 else jnp.concatenate(loaded, axis=0)
                product = dot(part, block, 1, 1)
                sums[side] = product if sums[side] is None else sums[side] + product
        low = jnp.where(where[1] == 0, sums[0], sums[1])
        high = jnp.where(where[1] == 0, sums[1], sums[0])
        total = jnp.concatenate([low, high], axis=1)
        for local in range(local_count):
            total_ref[local] = total[local * share : (local + 1) * share]
        first = pl.multiple_of(lax.rem(where[0] + place, chips) * cols, LANES)
        copy = pltpu.make_async_copy(total_ref, out_ref.at[:, :, pl.ds(first, cols)], sem)
        copy.start()
        copy.wait()

    operands = [pltpu.with_memory_space_constraint(array, pltpu.VMEM) for array, _ in flat]
    shares = pltpu.with_memory_space_constraint(shares, pltpu.VMEM)
    flops = 2 * shares.size * cols
    return pl.pallas_call(
        kernel,
        in_specs=[pl.BlockSpec(memory_space=pltpu.SMEM)]
        + [pl.BlockSpec(memory_space=pltpu.VMEM)] * (1 + len(operands))
        + [pl.BlockSpec(memory_space=pl.ANY)] * len(given),
        out_specs=pl.BlockSpec(memory_space=pl.ANY),
        out_shape=jax.ShapeDtypeStruct((local_count, share, width), jnp.float32),
        scratch_shapes=[pltpu.VMEM((local_count, share, cols), jnp.float32), pltpu.SemaphoreType.DMA],
        input_output_aliases={2 + len(operands): 0} if given else {},
        cost_estimate=pl.CostEstimate(flops=flops, bytes_accessed=4 * 512 * cols, transcendentals=0),
        compiler_params=pltpu.CompilerParams(vmem_limit_bytes=VMEM_BYTES // 2),
    )(where, shares, *operands, *given)


def planned_body(hidden, down_weight, cotangent, expert_ids, gate_weights, row_token, tile_count):
    local_count, width_in, width = down_weight.shape
    tokens = cotangent.shape[0]
    slots = hidden.shape[2]
    groups = lax.axis_size("dp")
    chips = lax.axis_size("expert") // CORES
    share = width_in // groups
    group = lax.axis_index("dp")
    expert_place = lax.axis_index("expert")
    chip = expert_place // CORES
    core = expert_place % CORES
    where = jnp.stack([chip, core])
    rest = (local_count, width)

    own = cotangent.T
    middle = own.shape[0] // 2
    gathered = lax.all_gather(own, "expert")
    x_own, y_own = across_dp(own, 1), across_dp(own, 2)

    slot_index = jnp.arange(slots, dtype=jnp.int32)
    token_index = jnp.arange(tokens, dtype=jnp.int32)
    live = (row_token[0] >= 0) & (slot_index[None] < tile_count[0][:, None] * TILE)
    token_rows = jnp.where(live, row_token[0], -1)
    experts = expert_place * local_count + jnp.arange(local_count, dtype=jnp.int32)
    named = expert_ids[None] == experts[:, None, None]
    token_gate = jnp.sum(jnp.where(named, gate_weights[None].astype(jnp.float32), 0.0), axis=2)
    at_token = token_rows[:, :, None] == token_index[None, None, :]
    row_gate = jnp.sum(jnp.where(at_token, token_gate[:, None, :], 0.0), axis=2)

    def as_rows(values):
        padded = jnp.pad(values.astype(jnp.bfloat16), ((0, 0), (0, 2 * share - slots)))
        return padded.reshape(local_count, 2, share)

    extra = jnp.concatenate(
        [as_rows(token_rows >> 1), as_rows(token_rows & 1), as_rows(row_gate)], axis=1
    )
    extra = jnp.pad(extra, ((0, 0), (0, EXTRA_ROWS - extra.shape[1]), (0, 0)))
    payloads = []
    for mask in range(groups):
        rows = lax.dynamic_slice_in_dim(hidden[0], (group ^ mask) * share, share, 2)
        payloads.append(jnp.concatenate([rows, extra], axis=1))
    x_own, y_own, token_rows, row_gate, *payloads = joined(
        x_own, y_own, token_rows, row_gate, *payloads
    )

    payloads = [across_dp(payload, mask) if mask else payload for mask, payload in enumerate(payloads)]
    far_own = [across_dp(x_own[:middle], 2), across_dp(y_own[middle:], 1)]

    keep, send = expert_sums(where, token_rows, row_gate, hidden[0], down_weight, tokens)
    x_own, y_own, keep, send, *sent = joined(x_own, y_own, keep, send, *payloads, *far_own)
    payloads, far_own = sent[:groups], sent[groups:]

    from_other = across_cores(send)
    sums = (keep.astype(jnp.float32) + from_other.astype(jnp.float32)).astype(jnp.bfloat16)

    def of_chip(step, side):
        place = (chip + step) % chips * CORES + (core ^ side)
        return lax.dynamic_index_in_dim(gathered, place, 0, keepdims=False)

    near = jnp.stack([of_chip(step, 0) for step in range(1, chips)])
    near_other = jnp.stack([of_chip(step, 1) for step in range(1, chips)])
    own_other = of_chip(0, 1)
    x_near, y_near = across_dp(near, 1), across_dp(near, 2)
    own_far = [x_own, y_own, *far_own]
    own_far_other = [across_cores(block) for block in own_far]
    sums, *payloads = joined(sums, *payloads)
    mixed = lax.psum_scatter(sums, "expert", scatter_dimension=0, axis_index_groups=z_lines())
    shares = shares_by_token(where, payloads, slots, tokens)
    sides = [[(block, ...) for block in blocks] for blocks in (own_far, own_far_other)]
    weight_grad = weight_cols(
        where,
        0,
        shares,
        [([(own, ...)], [(own_other, ...)])]
        + [[side[first:last] for side in sides] for first, last in ((0, 1), (1, 2), (2, 4))],
        *rest,
        None,
    )
    hidden_grad = hidden_grads(where, token_rows, row_gate, gathered.reshape(width, tokens), down_weight)
    hidden_grad, weight_grad, x_near, y_near = joined(hidden_grad, weight_grad, x_near, y_near)

    far = [
        [across_dp(x_near[step, :middle], 2), across_dp(y_near[step, middle:], 1)]
        for step in range(chips - 1)
    ]
    x_other, y_other = across_cores(x_near), across_cores(y_near)
    for step in range(chips - 1):
        far_other = [across_cores(piece) for piece in far[step]]
        weight_grad = weight_cols(
            where,
            step + 1,
            shares,
            [
                ([(near, step)], [(near_other, step)]),
                ([(x_near, step)], [(x_other, step)]),
                ([(y_near, step)], [(y_other, step)]),
                ([(piece, ...) for piece in far[step]], [(piece, ...) for piece in far_other]),
            ],
            *rest,
            weight_grad,
        )
        if step < chips - 2:
            weight_grad, *far[step + 1] = joined(weight_grad, *far[step + 1])
        if step == 0:
            weight_grad, mixed = joined(weight_grad, mixed)
    return (mixed.T, hidden_grad[None], weight_grad)


def tile_products(rows_in, weight_mat, count, contract_dim):
    rows_cap = rows_in.shape[0]
    width_out = weight_mat.shape[1 - contract_dim]

    def one_tile(tile_index, outputs):
        block = lax.dynamic_slice_in_dim(rows_in, tile_index * TILE, TILE, 0)
        product = lax.dot_general(
            block,
            weight_mat,
            (((1,), (contract_dim,)), ((), ())),
            preferred_element_type=jnp.float32,
        )
        return lax.dynamic_update_slice_in_dim(
            outputs, product.astype(jnp.bfloat16), tile_index * TILE, 0
        )

    return lax.fori_loop(0, count, one_tile, jnp.zeros((rows_cap, width_out), jnp.bfloat16))


def general_body(hidden, down_weight, cotangent, expert_ids, gate_weights, row_token, tile_count):
    local_count = down_weight.shape[0]
    group_size = cotangent.shape[0]
    expert_index = jnp.arange(EXPERTS, dtype=jnp.int32)
    named_cols = expert_ids[:, :, None] == expert_index[None, None, :]
    gate_cols = jnp.sum(
        jnp.where(named_cols, gate_weights[:, :, None].astype(jnp.float32), 0.0), axis=1
    ).astype(jnp.bfloat16)
    group_cot = lax.all_gather(cotangent, "expert", axis=1, tiled=True)
    width = group_cot.shape[1]
    first_expert = lax.axis_index("expert") * local_count
    slot_index = jnp.arange(hidden.shape[2], dtype=jnp.int32)
    share_rows = down_weight.shape[1] // lax.axis_size("dp")
    partial_value = jnp.zeros((group_size, width), jnp.float32)
    grad_list = []
    weight_list = []
    for local in range(local_count):
        token_rows = row_token[0, local]
        count = tile_count[0, local]
        live_rows = (token_rows >= 0) & (slot_index < count * TILE)
        safe_rows = jnp.where(live_rows, token_rows, 0)
        column = lax.dynamic_index_in_dim(gate_cols, first_expert + local, 1, keepdims=False)
        row_gate = jnp.where(live_rows, column[safe_rows].astype(jnp.float32), 0.0)
        target = jnp.where(live_rows, token_rows, group_size)
        hidden_rows = hidden[0, local]
        weight_mat = down_weight[local]
        out_rows = tile_products(hidden_rows, weight_mat, count, 0)
        partial_value = partial_value.at[target].add(
            row_gate[:, None] * out_rows.astype(jnp.float32), mode="drop"
        )
        routed = (row_gate[:, None] * group_cot[safe_rows].astype(jnp.float32)).astype(jnp.bfloat16)
        grad_list.append(tile_products(routed, weight_mat, count, 1))

        def weight_rows(start, rows_count, hidden_rows=hidden_rows, routed_rows=routed):
            return lax.dot_general(
                hidden_rows,
                routed_rows,
                (((0,), (0,)), ((), ())),
                preferred_element_type=jnp.float32,
            )

        weight_list.append(
            lax.psum_scatter(
                weight_rows(jnp.int32(0), share_rows * lax.axis_size("dp")).astype(jnp.bfloat16),
                "dp",
                scatter_dimension=0,
                tiled=True,
            ).astype(jnp.float32)
        )
    merged = partial_value
    top_bit = lax.axis_size("expert").bit_length() - 1
    axis_index = lax.axis_index("expert")
    for bit_index in reversed(range(top_bit)):
        half_cols = merged.shape[1] // 2
        lower_half = merged[:, :half_cols]
        upper_half = merged[:, half_cols:]
        high_side = axis_index // 2**bit_index % 2 == 1
        sending = jnp.where(high_side, lower_half, upper_half)
        keeping = jnp.where(high_side, upper_half, lower_half)
        merged = keeping + swapped(sending.astype(jnp.bfloat16), "expert", bit_index).astype(
            sending.dtype
        )
    mixed_out = merged.astype(jnp.bfloat16)
    hidden_grad = jnp.stack(grad_list, axis=0)[None]
    weight_grad = jnp.stack(weight_list, axis=0)
    return (mixed_out, hidden_grad, weight_grad)


def solution(mesh):
    placed = (
        P("dp", "expert", None, None),
        P("expert", None, None),
        P("dp", "expert"),
        P("dp", None),
        P("dp", None),
        P("dp", "expert", None),
        P("dp", "expert"),
    )

    def body(*shards):
        width = shards[1].shape[2]
        chips = mesh.shape["expert"] // CORES
        fits = mesh.shape["dp"] == 4 and chips > 2 and width % (chips * LANES) == 0
        return planned_body(*shards) if fits else general_body(*shards)

    return jax.shard_map(
        body,
        mesh=mesh,
        in_specs=placed,
        out_specs=(P("dp", "expert"), P("dp", "expert", None, None), P("expert", "dp", None)),
        check_vma=False,
    )
```

```python
import jax
import jax.numpy as jnp
from jax import lax
from jax.experimental import pallas as pl
from jax.experimental.pallas import tpu as pltpu
from jax.sharding import PartitionSpec as P

EXPERTS = 16
TILE = 128
LANES = 128
CORES = 2
EXTRA_ROWS = 16
MIB = 1024 * 1024


def swapped(shard, axis, bit):
    return lax.ppermute(shard, axis, [(i, i ^ 1 << bit) for i in range(lax.axis_size(axis))])


def across_dp(shard, mask):
    return lax.ppermute(shard, "dp", [(i, i ^ mask) for i in range(lax.axis_size("dp"))])


def across_cores(shard):
    return swapped(shard, "expert", 0)


def z_lines():
    size = lax.axis_size("expert")
    return [list(range(core, size, CORES)) for core in range(CORES)]


def joined(*values):
    return lax.optimization_barrier(values)


def dot(lhs, rhs, lhs_dim, rhs_dim):
    return lax.dot_general(
        lhs, rhs, (((lhs_dim,), (rhs_dim,)), ((), ())), preferred_element_type=jnp.float32
    )


def hot_rows(token_row, gate_row, tokens):
    slots = token_row.shape[1]
    token_index = lax.broadcasted_iota(jnp.int32, (tokens, slots), 0)
    spread = jnp.broadcast_to(gate_row, (tokens, slots))
    return jnp.where(token_index == token_row, spread, 0.0).astype(jnp.bfloat16)


def whole(shape):
    return pl.BlockSpec(shape, lambda *_: (0,) * len(shape))


def call(kernel, scalars, grid, in_specs, out_specs, out_shape, scratch, operands, vmem):
    return pl.pallas_call(
        kernel,
        grid_spec=pltpu.PrefetchScalarGridSpec(
            num_scalar_prefetch=1,
            grid=grid,
            in_specs=in_specs,
            out_specs=out_specs,
            scratch_shapes=scratch,
        ),
        out_shape=out_shape,
        compiler_params=pltpu.CompilerParams(
            dimension_semantics=("arbitrary",) * len(grid), vmem_limit_bytes=vmem
        ),
    )(scalars, *operands)


def expert_sums(where, token_rows, row_gate, hidden_rows, weight, tokens):
    local_count, slots, width_in = hidden_rows.shape
    chips = lax.axis_size("expert") // CORES
    cols = weight.shape[2] // chips
    half = cols // CORES

    def kernel(where, token_ref, gate_ref, hidden_ref, weight_ref, keep_ref, send_ref, by_token, turned):
        @pl.when(pl.program_id(0) == 0)
        def _():
            for local in range(local_count):
                hot = hot_rows(token_ref[local], gate_ref[local], tokens)
                made = dot(hot, hidden_ref[local], 1, 0).astype(jnp.bfloat16)
                by_token[:, local * width_in : (local + 1) * width_in] = made

        stacked = weight_ref[...].reshape(local_count * width_in, cols)
        turned[...] = dot(by_token[...], stacked, 1, 0).astype(jnp.bfloat16).T
        keep_ref[0] = turned[pl.ds(pl.multiple_of(where[1] * half, half), half), :]
        send_ref[0] = turned[pl.ds(pl.multiple_of((1 - where[1]) * half, half), half), :]

    shape = jax.ShapeDtypeStruct((chips, half, tokens), jnp.bfloat16)
    out_spec = pl.BlockSpec((1, half, tokens), lambda k, where: (k, 0, 0))
    return call(
        kernel,
        where,
        (chips,),
        [
            whole((local_count, 1, slots)),
            whole((local_count, 1, slots)),
            whole(hidden_rows.shape),
            pl.BlockSpec((local_count, width_in, cols), lambda k, where: (0, 0, k)),
        ],
        (out_spec, out_spec),
        (shape, shape),
        [
            pltpu.VMEM((tokens, local_count * width_in), jnp.bfloat16),
            pltpu.VMEM((cols, tokens), jnp.bfloat16),
        ],
        (token_rows[:, None], row_gate[:, None], hidden_rows, weight),
        32 * MIB,
    )


def resident(kernel, scalars, operands, out_shapes, scratch=(), passed=None):
    held = [pltpu.with_memory_space_constraint(array, pltpu.VMEM) for array in operands]
    in_vmem, anywhere = pl.BlockSpec(memory_space=pltpu.VMEM), pl.BlockSpec(memory_space=pl.ANY)
    given = [] if passed is None else [passed]
    return pl.pallas_call(
        kernel,
        in_specs=[pl.BlockSpec(memory_space=pltpu.SMEM)] + [in_vmem] * len(held) + [anywhere] * len(given),
        out_specs=[anywhere if isinstance(shape, jax.ShapeDtypeStruct) else in_vmem for shape in out_shapes],
        out_shape=out_shapes,
        scratch_shapes=list(scratch),
        input_output_aliases={1 + len(held): 0} if given else {},
        compiler_params=pltpu.CompilerParams(vmem_limit_bytes=16 * MIB),
    )(scalars, *held, *given)


def shares_by_token(where, payloads, slots, tokens):
    local_count, _, share = payloads[0].shape
    groups = len(payloads)

    def kernel(where, *refs):
        out_ref = refs[-1]

        def row(ref, local, first):
            wide = [ref[local, slots + first + i : slots + first + i + 1, :] for i in range(2)]
            return jnp.concatenate(wide, axis=1)[:, :slots].astype(jnp.float32)

        for group in range(groups):
            ref = refs[group]
            for local in range(local_count):
                token = (row(ref, local, 0) * 2.0 + row(ref, local, 2)).astype(jnp.int32)
                hot = hot_rows(token, row(ref, local, 4), tokens)
                by_token = dot(hot, ref[local, :slots, :], 1, 0).astype(jnp.bfloat16)
                out_ref[local * share : (local + 1) * share, group * tokens : (group + 1) * tokens] = by_token.T

    shape = (local_count * share, groups * tokens)
    return resident(kernel, where, payloads, [pltpu.VMEM(shape, jnp.bfloat16)])[0]


def blocks_of(where, gathered, steps, side):
    devices, rows, tokens = gathered.shape

    def kernel(where, gathered_ref, out_ref, sem):
        copies = []
        for place, step in enumerate(steps):
            chip = lax.rem(where[0] + step, devices // CORES)
            source = gathered_ref.at[chip * CORES + jnp.bitwise_xor(where[1], side)]
            copies.append(pltpu.make_async_copy(source, out_ref.at[place], sem.at[place]))
        for copy in copies:
            copy.start()
        for copy in copies:
            copy.wait()

    return pl.pallas_call(
        kernel,
        in_specs=[pl.BlockSpec(memory_space=pltpu.SMEM), pl.BlockSpec(memory_space=pl.ANY)],
        out_specs=pl.BlockSpec(memory_space=pltpu.VMEM),
        out_shape=pltpu.VMEM((len(steps), rows, tokens), gathered.dtype),
        scratch_shapes=[pltpu.SemaphoreType.DMA((len(steps),))],
    )(where, gathered)


def hidden_grads(where, token_rows, row_gate, gathered, weight):
    local_count, width_in, width = weight.shape
    slots = token_rows.shape[1]
    devices, part, tokens = gathered[0].shape
    depth = width_in // 2

    def kernel(where, token_ref, gate_ref, *refs):
        parts = refs[: len(gathered)]
        weight_ref, out_ref, group_cot, sem = refs[len(gathered) :]
        local = pl.program_id(0)

        @pl.when((local == 0) & (pl.program_id(1) == 0))
        def _():
            copies = []
            for place, ref in enumerate(parts):
                for device in range(devices):
                    rows = pl.ds((device * len(parts) + place) * part, part)
                    copies.append(pltpu.make_async_copy(ref.at[device], group_cot.at[rows], sem.at[len(copies)]))
            for copy in copies:
                copy.start()
            for copy in copies:
                copy.wait()

        sums = dot(weight_ref[0], group_cot[...], 1, 0).astype(jnp.bfloat16)
        hot = hot_rows(token_ref[local], gate_ref[local], tokens)
        out_ref[0] = dot(hot, sums, 0, 1).astype(jnp.bfloat16)

    return call(
        kernel,
        where,
        (local_count, width_in // depth),
        [whole((local_count, 1, slots))] * 2
        + [pl.BlockSpec(memory_space=pl.ANY)] * len(gathered)
        + [pl.BlockSpec((1, depth, width), lambda e, h, where: (e, h, 0))],
        pl.BlockSpec((1, slots, depth), lambda e, h, where: (e, 0, h)),
        jax.ShapeDtypeStruct((local_count, slots, width_in), jnp.bfloat16),
        [pltpu.VMEM((width, tokens), jnp.bfloat16), pltpu.SemaphoreType.DMA((devices * len(gathered),))],
        (token_rows[:, None], row_gate[:, None], *gathered, weight),
        28 * MIB,
    )


def group_products(where, shares, groups, refs, chip):
    total, at = None, 0
    for place, sides in groups:
        loaded = []
        for pieces in sides:
            loaded.append([ref[first + chip] for ref, (_, first) in zip(refs[at:], pieces)])
            at += len(pieces)
        mine, other = [jnp.concatenate(pieces, axis=0) if len(pieces) > 1 else pieces[0] for pieces in loaded]
        low = jnp.where(where[1] == 0, mine, other)
        high = jnp.where(where[1] == 0, other, mine)
        block = jnp.concatenate([low, high], axis=0)
        tokens = block.shape[1]
        product = dot(shares[:, place * tokens : (place + 1) * tokens], block, 1, 1)
        total = product if total is None else total + product
    return total


def pieces_of(groups):
    return [array for _, sides in groups for pieces in sides for array, _ in pieces]


def part_sums(where, shares, groups, count, cols):
    flat = pieces_of(groups)
    shape = (count, shares.shape[0], cols)

    def kernel(where, shares_ref, *refs):
        for chip in range(count):
            refs[-1][chip] = group_products(where, shares_ref, groups, refs, chip)

    return resident(kernel, where, [shares, *flat], [pltpu.VMEM(shape, jnp.float32)])[0]


def weight_cols(where, first, count, shares, groups, so_far, local_count, width, passed):
    flat = pieces_of(groups)
    share = shares.shape[0] // local_count
    chips = lax.axis_size("expert") // CORES
    cols = width // chips
    added = [] if so_far is None else [so_far]

    def kernel(where, shares_ref, *refs):
        out_ref, total_ref, sem = refs[-3:]
        copies = []
        for chip in range(count):
            total = group_products(where, shares_ref, groups, refs, chip)
            if added:
                total = total + refs[len(flat)][chip]
            for local in range(local_count):
                total_ref[chip, local] = total[local * share : (local + 1) * share]
            start = pl.multiple_of(lax.rem(where[0] + first + chip, chips) * cols, LANES)
            copy = pltpu.make_async_copy(total_ref.at[chip], out_ref.at[:, :, pl.ds(start, cols)], sem.at[chip])
            copy.start()
            copies.append(copy)
        for copy in copies:
            copy.wait()

    return resident(
        kernel,
        where,
        [shares, *flat, *added],
        [jax.ShapeDtypeStruct((local_count, share, width), jnp.float32)],
        [pltpu.VMEM((count, local_count, share, cols), jnp.float32), pltpu.SemaphoreType.DMA((count,))],
        passed,
    )[0]


def planned_body(hidden, down_weight, cotangent, expert_ids, gate_weights, row_token, tile_count):
    local_count, width_in, width = down_weight.shape
    tokens = cotangent.shape[0]
    slots = hidden.shape[2]
    groups = lax.axis_size("dp")
    chips = lax.axis_size("expert") // CORES
    cols = width // chips
    share = width_in // groups
    group = lax.axis_index("dp")
    expert_place = lax.axis_index("expert")
    chip = expert_place // CORES
    core = expert_place % CORES
    where = jnp.stack([chip, core])

    own = cotangent.T
    middle = own.shape[0] // 2
    gathered = [lax.all_gather(part, "expert") for part in (own[:middle], own[middle:])]
    x_own, y_own = across_dp(own, 1), across_dp(own, 2)

    slot_index = jnp.arange(slots, dtype=jnp.int32)
    token_index = jnp.arange(tokens, dtype=jnp.int32)
    live = (row_token[0] >= 0) & (slot_index[None] < tile_count[0][:, None] * TILE)
    token_rows = jnp.where(live, row_token[0], -1)
    experts = expert_place * local_count + jnp.arange(local_count, dtype=jnp.int32)
    named = expert_ids[None] == experts[:, None, None]
    token_gate = jnp.sum(jnp.where(named, gate_weights[None].astype(jnp.float32), 0.0), axis=2)
    at_token = token_rows[:, :, None] == token_index[None, None, :]
    row_gate = jnp.sum(jnp.where(at_token, token_gate[:, None, :], 0.0), axis=2)

    def as_rows(values):
        padded = jnp.pad(values.astype(jnp.bfloat16), ((0, 0), (0, 2 * share - slots)))
        return padded.reshape(local_count, 2, share)

    extra = jnp.concatenate(
        [as_rows(token_rows >> 1), as_rows(token_rows & 1), as_rows(row_gate)], axis=1
    )
    extra = jnp.pad(extra, ((0, 0), (0, EXTRA_ROWS - extra.shape[1]), (0, 0)))
    payloads = []
    for mask in range(groups):
        rows = lax.dynamic_slice_in_dim(hidden[0], (group ^ mask) * share, share, 2)
        payloads.append(jnp.concatenate([rows, extra], axis=1))
    x_own, y_own, token_rows, row_gate, *payloads = joined(
        x_own, y_own, token_rows, row_gate, *payloads
    )

    payloads = [across_dp(payload, mask) if mask else payload for mask, payload in enumerate(payloads)]
    far_own = [across_dp(x_own[:middle], 2), across_dp(y_own[middle:], 1)]
    own_others = [across_cores(x_own), across_cores(y_own)]
    keep, send = expert_sums(where, token_rows, row_gate, hidden[0], down_weight, tokens)
    x_own, y_own, keep, send, *sent = joined(
        x_own, y_own, keep, send, *own_others, *far_own, *gathered, *payloads
    )
    own_others, far_own, gathered, payloads = sent[:2], sent[2:4], sent[4:6], sent[6:]

    steps = list(range(1, chips))
    near = [blocks_of(where, part, steps, 0) for part in gathered]
    x_near, y_near = [None, None], [None, None]
    x_near[0], y_near[1] = across_dp(near[0], 1), across_dp(near[1], 2)
    x_near[1], y_near[0] = across_dp(near[1], 1), across_dp(near[0], 2)

    from_other = across_cores(send)
    from_other, *sent = joined(from_other, *payloads, *far_own)
    payloads, far_own = sent[:groups], jnp.concatenate(sent[groups:], axis=0)
    own_others.append(across_cores(far_own))
    sums = (keep.astype(jnp.float32) + from_other.astype(jnp.float32)).astype(jnp.bfloat16)
    mixed = lax.psum_scatter(sums, "expert", scatter_dimension=0, axis_index_groups=z_lines())
    shares = shares_by_token(where, payloads, slots, tokens)
    hidden_grad = hidden_grads(where, token_rows, row_gate, gathered, down_weight)
    hidden_grad, shares, _, *sent = joined(hidden_grad, shares, sums, *own_others, *x_near, *y_near)
    own_others, x_near, y_near = sent[:3], sent[3:5], sent[5:]

    far = [across_dp(x_near[0], 2), across_dp(y_near[1], 1)]
    x_other = [across_cores(part) for part in x_near]
    y_other = [across_cores(part) for part in y_near]
    own_other = [blocks_of(where, part, [0], 1) for part in gathered]
    own_groups = [(0, ([(own[None], 0)], [(part, 0) for part in own_other]))]
    for place, pair in enumerate(zip((x_own, y_own, far_own), own_others), 1):
        own_groups.append((place, tuple([(block[None], 0)] for block in pair)))
    weight_grad = weight_cols(where, 0, 1, shares, own_groups, None, local_count, width, None)

    def halves(parts):
        return [(part, 0) for part in parts]

    near_other = [blocks_of(where, part, steps, 1) for part in gathered]
    pairs = [(near, near_other), (x_near, x_other), (y_near, y_other)]
    three = [(place, (halves(mine), halves(other))) for place, (mine, other) in enumerate(pairs)]
    so_far = part_sums(where, shares, three, chips - 1, cols)
    so_far, weight_grad, mixed, *far = joined(so_far, weight_grad, mixed, *far)
    last = [(groups - 1, (halves(far), halves([across_cores(part) for part in far])))]
    weight_grad = weight_cols(
        where, 1, chips - 1, shares, last, so_far, local_count, width, weight_grad
    )
    return (mixed.T, hidden_grad[None], weight_grad)


def tile_products(rows_in, weight_mat, count, contract_dim):
    rows_cap = rows_in.shape[0]
    width_out = weight_mat.shape[1 - contract_dim]

    def one_tile(tile_index, outputs):
        block = lax.dynamic_slice_in_dim(rows_in, tile_index * TILE, TILE, 0)
        product = lax.dot_general(
            block,
            weight_mat,
            (((1,), (contract_dim,)), ((), ())),
            preferred_element_type=jnp.float32,
        )
        return lax.dynamic_update_slice_in_dim(
            outputs, product.astype(jnp.bfloat16), tile_index * TILE, 0
        )

    return lax.fori_loop(0, count, one_tile, jnp.zeros((rows_cap, width_out), jnp.bfloat16))


def general_body(hidden, down_weight, cotangent, expert_ids, gate_weights, row_token, tile_count):
    local_count = down_weight.shape[0]
    group_size = cotangent.shape[0]
    expert_index = jnp.arange(EXPERTS, dtype=jnp.int32)
    named_cols = expert_ids[:, :, None] == expert_index[None, None, :]
    gate_cols = jnp.sum(
        jnp.where(named_cols, gate_weights[:, :, None].astype(jnp.float32), 0.0), axis=1
    ).astype(jnp.bfloat16)
    group_cot = lax.all_gather(cotangent, "expert", axis=1, tiled=True)
    width = group_cot.shape[1]
    first_expert = lax.axis_index("expert") * local_count
    slot_index = jnp.arange(hidden.shape[2], dtype=jnp.int32)
    share_rows = down_weight.shape[1] // lax.axis_size("dp")
    partial_value = jnp.zeros((group_size, width), jnp.float32)
    grad_list = []
    weight_list = []
    for local in range(local_count):
        token_rows = row_token[0, local]
        count = tile_count[0, local]
        live_rows = (token_rows >= 0) & (slot_index < count * TILE)
        safe_rows = jnp.where(live_rows, token_rows, 0)
        column = lax.dynamic_index_in_dim(gate_cols, first_expert + local, 1, keepdims=False)
        row_gate = jnp.where(live_rows, column[safe_rows].astype(jnp.float32), 0.0)
        target = jnp.where(live_rows, token_rows, group_size)
        hidden_rows = hidden[0, local]
        weight_mat = down_weight[local]
        out_rows = tile_products(hidden_rows, weight_mat, count, 0)
        partial_value = partial_value.at[target].add(
            row_gate[:, None] * out_rows.astype(jnp.float32), mode="drop"
        )
        routed = (row_gate[:, None] * group_cot[safe_rows].astype(jnp.float32)).astype(jnp.bfloat16)
        grad_list.append(tile_products(routed, weight_mat, count, 1))

        def weight_rows(start, rows_count, hidden_rows=hidden_rows, routed_rows=routed):
            return lax.dot_general(
                hidden_rows,
                routed_rows,
                (((0,), (0,)), ((), ())),
                preferred_element_type=jnp.float32,
            )

        weight_list.append(
            lax.psum_scatter(
                weight_rows(jnp.int32(0), share_rows * lax.axis_size("dp")).astype(jnp.bfloat16),
                "dp",
                scatter_dimension=0,
                tiled=True,
            ).astype(jnp.float32)
        )
    merged = partial_value
    top_bit = lax.axis_size("expert").bit_length() - 1
    axis_index = lax.axis_index("expert")
    for bit_index in reversed(range(top_bit)):
        half_cols = merged.shape[1] // 2
        lower_half = merged[:, :half_cols]
        upper_half = merged[:, half_cols:]
        high_side = axis_index // 2**bit_index % 2 == 1
        sending = jnp.where(high_side, lower_half, upper_half)
        keeping = jnp.where(high_side, upper_half, lower_half)
        merged = keeping + swapped(sending.astype(jnp.bfloat16), "expert", bit_index).astype(
            sending.dtype
        )
    mixed_out = merged.astype(jnp.bfloat16)
    hidden_grad = jnp.stack(grad_list, axis=0)[None]
    weight_grad = jnp.stack(weight_list, axis=0)
    return (mixed_out, hidden_grad, weight_grad)


def solution(mesh):
    placed = (
        P("dp", "expert", None, None),
        P("expert", None, None),
        P("dp", "expert"),
        P("dp", None),
        P("dp", None),
        P("dp", "expert", None),
        P("dp", "expert"),
    )

    def body(*shards):
        width = shards[1].shape[2]
        chips = mesh.shape["expert"] // CORES
        fits = mesh.shape["dp"] == 4 and chips > 2 and width % (chips * LANES) == 0
        return planned_body(*shards) if fits else general_body(*shards)

    return jax.shard_map(
        body,
        mesh=mesh,
        in_specs=placed,
        out_specs=(P("dp", "expert"), P("dp", "expert", None, None), P("expert", "dp", None)),
        check_vma=False,
    )
```

```python
import jax
import jax.numpy as jnp
from jax import lax
from jax.experimental import pallas as pl
from jax.experimental.pallas import tpu as pltpu
from jax.sharding import PartitionSpec as P

EXPERTS = 16
TILE = 128
LANES = 128
CORES = 2
EXTRA_ROWS = 16
MIB = 1024 * 1024


def swapped(shard, axis, bit):
    return lax.ppermute(shard, axis, [(i, i ^ 1 << bit) for i in range(lax.axis_size(axis))])


def across_dp(shard, mask):
    return lax.ppermute(shard, "dp", [(i, i ^ mask) for i in range(lax.axis_size("dp"))])


def across_cores(shard):
    return swapped(shard, "expert", 0)


def z_lines():
    size = lax.axis_size("expert")
    return [list(range(core, size, CORES)) for core in range(CORES)]


def joined(*values):
    return lax.optimization_barrier(values)


def dot(lhs, rhs, lhs_dim, rhs_dim):
    return lax.dot_general(
        lhs, rhs, (((lhs_dim,), (rhs_dim,)), ((), ())), preferred_element_type=jnp.float32
    )


def hot_rows(token_row, gate_row, tokens):
    slots = token_row.shape[1]
    token_index = lax.broadcasted_iota(jnp.int32, (tokens, slots), 0)
    spread = jnp.broadcast_to(gate_row, (tokens, slots))
    return jnp.where(token_index == token_row, spread, 0.0).astype(jnp.bfloat16)


def in_hbm(array):
    return pltpu.with_memory_space_constraint(array, pltpu.HBM)


def whole(shape):
    return pl.BlockSpec(shape, lambda *_: (0,) * len(shape))


def call(kernel, scalars, grid, in_specs, out_specs, out_shape, scratch, operands, vmem):
    return pl.pallas_call(
        kernel,
        grid_spec=pltpu.PrefetchScalarGridSpec(
            num_scalar_prefetch=1,
            grid=grid,
            in_specs=in_specs,
            out_specs=out_specs,
            scratch_shapes=scratch,
        ),
        out_shape=out_shape,
        compiler_params=pltpu.CompilerParams(
            dimension_semantics=("arbitrary",) * len(grid), vmem_limit_bytes=vmem
        ),
    )(scalars, *operands)


def expert_sums(where, token_rows, row_gate, hidden_rows, weight, tokens):
    local_count, slots, width_in = hidden_rows.shape
    chips = lax.axis_size("expert") // CORES
    cols = weight.shape[2] // chips
    half = cols // CORES

    def kernel(where, token_ref, gate_ref, hidden_ref, weight_ref, keep_ref, send_ref, by_token, turned):
        @pl.when(pl.program_id(0) == 0)
        def _():
            for local in range(local_count):
                hot = hot_rows(token_ref[local], gate_ref[local], tokens)
                made = dot(hot, hidden_ref[local], 1, 0).astype(jnp.bfloat16)
                by_token[:, local * width_in : (local + 1) * width_in] = made

        stacked = weight_ref[...].reshape(local_count * width_in, cols)
        turned[...] = dot(by_token[...], stacked, 1, 0).astype(jnp.bfloat16).T
        keep_ref[0] = turned[pl.ds(pl.multiple_of(where[1] * half, half), half), :]
        send_ref[0] = turned[pl.ds(pl.multiple_of((1 - where[1]) * half, half), half), :]

    shape = jax.ShapeDtypeStruct((chips, half, tokens), jnp.bfloat16)
    out_spec = pl.BlockSpec((1, half, tokens), lambda k, where: (k, 0, 0))
    return call(
        kernel,
        where,
        (chips,),
        [
            whole((local_count, 1, slots)),
            whole((local_count, 1, slots)),
            whole(hidden_rows.shape),
            pl.BlockSpec((local_count, width_in, cols), lambda k, where: (0, 0, k)),
        ],
        (out_spec, out_spec),
        (shape, shape),
        [
            pltpu.VMEM((tokens, local_count * width_in), jnp.bfloat16),
            pltpu.VMEM((cols, tokens), jnp.bfloat16),
        ],
        (token_rows[:, None], row_gate[:, None], hidden_rows, in_hbm(weight)),
        32 * MIB,
    )


def resident(kernel, scalars, operands, out_shapes, scratch=(), distant=(), passed=None):
    held = [pltpu.with_memory_space_constraint(array, pltpu.VMEM) for array in operands]
    in_vmem, anywhere = pl.BlockSpec(memory_space=pltpu.VMEM), pl.BlockSpec(memory_space=pl.ANY)
    far_off = [in_hbm(array) for array in distant] + ([] if passed is None else [passed])
    return pl.pallas_call(
        kernel,
        in_specs=[pl.BlockSpec(memory_space=pltpu.SMEM)] + [in_vmem] * len(held) + [anywhere] * len(far_off),
        out_specs=[anywhere if isinstance(shape, jax.ShapeDtypeStruct) else in_vmem for shape in out_shapes],
        out_shape=out_shapes,
        scratch_shapes=list(scratch),
        input_output_aliases={} if passed is None else {len(held) + len(far_off): 0},
        compiler_params=pltpu.CompilerParams(vmem_limit_bytes=20 * MIB),
    )(scalars, *held, *far_off)


def shares_by_token(where, payloads, slots, tokens):
    local_count, _, share = payloads[0].shape
    groups = len(payloads)

    def kernel(where, *refs):
        out_ref = refs[-1]

        def row(ref, local, first):
            wide = [ref[local, slots + first + i : slots + first + i + 1, :] for i in range(2)]
            return jnp.concatenate(wide, axis=1)[:, :slots].astype(jnp.float32)

        for group in range(groups):
            ref = refs[group]
            for local in range(local_count):
                token = (row(ref, local, 0) * 2.0 + row(ref, local, 2)).astype(jnp.int32)
                hot = hot_rows(token, row(ref, local, 4), tokens)
                by_token = dot(hot, ref[local, :slots, :], 1, 0).astype(jnp.bfloat16)
                out_ref[local * share : (local + 1) * share, group * tokens : (group + 1) * tokens] = by_token.T

    shape = (local_count * share, groups * tokens)
    return resident(kernel, where, payloads, [pltpu.VMEM(shape, jnp.bfloat16)])[0]


def blocks_of(where, gathered, steps, parts):
    devices, rows, tokens = gathered.shape
    part = rows // parts

    def kernel(where, gathered_ref, *refs):
        sem = refs[-1]
        copies = []
        for place, step in enumerate(steps):
            chip = lax.rem(where[0] + step, devices // CORES)
            for index, out_ref in enumerate(refs[:-1]):
                source = gathered_ref.at[chip * CORES + where[1], pl.ds(index * part, part)]
                copies.append(pltpu.make_async_copy(source, out_ref.at[place], sem.at[len(copies)]))
        for copy in copies:
            copy.start()
        for copy in copies:
            copy.wait()

    return pl.pallas_call(
        kernel,
        in_specs=[pl.BlockSpec(memory_space=pltpu.SMEM), pl.BlockSpec(memory_space=pl.ANY)],
        out_specs=[pl.BlockSpec(memory_space=pltpu.VMEM)] * parts,
        out_shape=[pltpu.VMEM((len(steps), part, tokens), gathered.dtype)] * parts,
        scratch_shapes=[pltpu.SemaphoreType.DMA((len(steps) * parts,))],
    )(where, in_hbm(gathered))


def hidden_grads(where, token_rows, row_gate, group_cot, weight):
    local_count, width_in, width = weight.shape
    slots = token_rows.shape[1]
    tokens = group_cot.shape[1]
    depth = width_in // 2

    def kernel(where, token_ref, gate_ref, cot_ref, weight_ref, out_ref):
        local = pl.program_id(0)
        sums = dot(weight_ref[0], cot_ref[...], 1, 0).astype(jnp.bfloat16)
        hot = hot_rows(token_ref[local], gate_ref[local], tokens)
        out_ref[0] = dot(hot, sums, 0, 1).astype(jnp.bfloat16)

    return call(
        kernel,
        where,
        (local_count, width_in // depth),
        [whole((local_count, 1, slots))] * 2
        + [whole(group_cot.shape)]
        + [pl.BlockSpec((1, depth, width), lambda e, h, where: (e, h, 0))],
        pl.BlockSpec((1, slots, depth), lambda e, h, where: (e, 0, h)),
        jax.ShapeDtypeStruct((local_count, slots, width_in), jnp.bfloat16),
        [],
        (token_rows[:, None], row_gate[:, None], in_hbm(group_cot), in_hbm(weight)),
        28 * MIB,
    )


def group_products(where, shares, groups, refs, chip):
    total, at = None, 0
    for place, sides in groups:
        loaded = []
        for pieces in sides:
            loaded.append([ref[first + chip] for ref, (_, first) in zip(refs[at:], pieces)])
            at += len(pieces)
        mine, other = [jnp.concatenate(pieces, axis=0) if len(pieces) > 1 else pieces[0] for pieces in loaded]
        low = jnp.where(where[1] == 0, mine, other)
        high = jnp.where(where[1] == 0, other, mine)
        block = jnp.concatenate([low, high], axis=0)
        tokens = block.shape[1]
        product = dot(shares[:, place * tokens : (place + 1) * tokens], block, 1, 1)
        total = product if total is None else total + product
    return total


def halves(parts):
    return [(part, 0) for part in parts]


def weight_cols(
    where, first, count, shares, groups, local_count, width, gathered=None, so_far=None, passed=None, keep=False
):
    chips = lax.axis_size("expert") // CORES
    cols = width // chips
    share = shares.shape[0] // local_count
    flat = [array for _, sides in groups for pieces in sides for array, _ in pieces]
    tokens = flat[0].shape[-1]
    held = [shares, *flat] + ([] if so_far is None else [so_far])
    distant = [] if gathered is None else [gathered]

    def kernel(where, shares_ref, *refs):
        refs = list(refs)
        pieces = [refs.pop(0) for _ in flat]
        added = refs.pop(0) if so_far is not None else None
        source = refs.pop(0) if distant else None
        if passed is not None:
            refs.pop(0)
        out_ref = refs.pop(0)
        place = [lax.rem(where[0] + first + chip, chips) for chip in range(count)]
        loads, stores = [], []
        if distant:
            own_ref, own_sem = refs.pop(0), refs.pop(0)
            for chip in range(count):
                block = source.at[pl.ds(place[chip] * CORES, CORES)]
                loads.append(pltpu.make_async_copy(block, own_ref.at[chip], own_sem.at[chip]))
                loads[-1].start()
        for chip in range(count):
            total = group_products(where, shares_ref, groups, pieces, chip)
            if distant:
                loads[chip].wait()
                total = total + dot(shares_ref[:, :tokens], own_ref[chip].reshape(cols, tokens), 1, 1)
            if added is not None:
                total = total + added[chip]
            if keep:
                out_ref[chip] = total
                continue
            total_ref, sem = refs
            for local in range(local_count):
                total_ref[chip, local] = total[local * share : (local + 1) * share]
            columns = pl.ds(pl.multiple_of(place[chip] * cols, LANES), cols)
            stores.append(pltpu.make_async_copy(total_ref.at[chip], out_ref.at[:, :, columns], sem.at[chip]))
            stores[-1].start()
        for store in stores:
            store.wait()

    scratch = []
    if distant:
        scratch += [pltpu.VMEM((count, CORES, cols // CORES, tokens), jnp.bfloat16), pltpu.SemaphoreType.DMA((count,))]
    if keep:
        out_shape = pltpu.VMEM((count, shares.shape[0], cols), jnp.float32)
    else:
        out_shape = jax.ShapeDtypeStruct((local_count, share, width), jnp.float32)
        scratch += [pltpu.VMEM((count, local_count, share, cols), jnp.float32), pltpu.SemaphoreType.DMA((count,))]
    return resident(kernel, where, held, [out_shape], scratch, distant, passed)[0]


def planned_body(hidden, down_weight, cotangent, expert_ids, gate_weights, row_token, tile_count):
    local_count, width_in, width = down_weight.shape
    tokens = cotangent.shape[0]
    slots = hidden.shape[2]
    groups = lax.axis_size("dp")
    chips = lax.axis_size("expert") // CORES
    share = width_in // groups
    group = lax.axis_index("dp")
    expert_place = lax.axis_index("expert")
    chip = expert_place // CORES
    core = expert_place % CORES
    where = jnp.stack([chip, core])

    own = cotangent.T
    middle = own.shape[0] // 2
    gathered = lax.all_gather(own, "expert")
    x_own, y_own = across_dp(own, 1), across_dp(own, 2)

    slot_index = jnp.arange(slots, dtype=jnp.int32)
    token_index = jnp.arange(tokens, dtype=jnp.int32)
    live = (row_token[0] >= 0) & (slot_index[None] < tile_count[0][:, None] * TILE)
    token_rows = jnp.where(live, row_token[0], -1)
    experts = expert_place * local_count + jnp.arange(local_count, dtype=jnp.int32)
    named = expert_ids[None] == experts[:, None, None]
    token_gate = jnp.sum(jnp.where(named, gate_weights[None].astype(jnp.float32), 0.0), axis=2)
    at_token = token_rows[:, :, None] == token_index[None, None, :]
    row_gate = jnp.sum(jnp.where(at_token, token_gate[:, None, :], 0.0), axis=2)

    def as_rows(values):
        padded = jnp.pad(values.astype(jnp.bfloat16), ((0, 0), (0, 2 * share - slots)))
        return padded.reshape(local_count, 2, share)

    extra = jnp.concatenate(
        [as_rows(token_rows >> 1), as_rows(token_rows & 1), as_rows(row_gate)], axis=1
    )
    extra = jnp.pad(extra, ((0, 0), (0, EXTRA_ROWS - extra.shape[1]), (0, 0)))
    payloads = []
    for mask in range(groups):
        rows = lax.dynamic_slice_in_dim(hidden[0], (group ^ mask) * share, share, 2)
        payloads.append(jnp.concatenate([rows, extra], axis=1))
    x_own, y_own, token_rows, row_gate, *payloads = joined(
        x_own, y_own, token_rows, row_gate, *payloads
    )

    payloads = [across_dp(payload, mask) if mask else payload for mask, payload in enumerate(payloads)]
    far_own = [across_dp(x_own[:middle], 2), across_dp(y_own[middle:], 1)]
    keep, send = expert_sums(where, token_rows, row_gate, hidden[0], down_weight, tokens)
    x_own, y_own, keep, send, *sent = joined(x_own, y_own, keep, send, *far_own, *payloads)
    far_own, payloads = sent[:2], sent[2:]

    steps = list(range(1, chips))
    near = blocks_of(where, gathered, steps, 2)
    x_near, y_near = [None, None], [None, None]
    x_near[0], y_near[1] = across_dp(near[0], 1), across_dp(near[1], 2)
    x_near[1], y_near[0] = across_dp(near[1], 1), across_dp(near[0], 2)

    from_other = across_cores(send)
    from_other, x_own, y_own, *sent = joined(from_other, x_own, y_own, *far_own, *payloads)
    far_own, payloads = sent[:2], sent[2:]
    own_far = jnp.stack([x_own, y_own, jnp.concatenate(far_own, axis=0)])
    own_far_other = across_cores(own_far)
    sums = (keep.astype(jnp.float32) + from_other.astype(jnp.float32)).astype(jnp.bfloat16)
    mixed = lax.psum_scatter(sums, "expert", scatter_dimension=0, axis_index_groups=z_lines())
    shares = shares_by_token(where, payloads, slots, tokens)
    hidden_grad = hidden_grads(where, token_rows, row_gate, gathered.reshape(width, tokens), down_weight)
    rest = (local_count, width)
    own_groups = [(place + 1, ([(own_far, place)], [(own_far_other, place)])) for place in range(groups - 1)]
    weight_grad = weight_cols(where, 0, 1, shares, own_groups, *rest, gathered)
    hidden_grad, shares, weight_grad, _, *sent = joined(
        hidden_grad, shares, weight_grad, sums, *x_near, *y_near
    )
    x_near, y_near = sent[:2], sent[2:]

    far = [across_dp(x_near[0], 2), across_dp(y_near[1], 1)]
    x_other = [across_cores(part) for part in x_near]
    y_other = [across_cores(part) for part in y_near]
    two = [(place, tuple(map(halves, pair))) for place, pair in ((1, (x_near, x_other)), (2, (y_near, y_other)))]
    so_far = weight_cols(where, 1, chips - 1, shares, two, *rest, gathered, keep=True)
    so_far, mixed, *far = joined(so_far, mixed, *far)
    last = [(groups - 1, (halves(far), halves([across_cores(part) for part in far])))]
    weight_grad = weight_cols(where, 1, chips - 1, shares, last, *rest, None, so_far, weight_grad)
    return (mixed.T, hidden_grad[None], weight_grad)


def tile_products(rows_in, weight_mat, count, contract_dim):
    rows_cap = rows_in.shape[0]
    width_out = weight_mat.shape[1 - contract_dim]

    def one_tile(tile_index, outputs):
        block = lax.dynamic_slice_in_dim(rows_in, tile_index * TILE, TILE, 0)
        product = lax.dot_general(
            block,
            weight_mat,
            (((1,), (contract_dim,)), ((), ())),
            preferred_element_type=jnp.float32,
        )
        return lax.dynamic_update_slice_in_dim(
            outputs, product.astype(jnp.bfloat16), tile_index * TILE, 0
        )

    return lax.fori_loop(0, count, one_tile, jnp.zeros((rows_cap, width_out), jnp.bfloat16))


def general_body(hidden, down_weight, cotangent, expert_ids, gate_weights, row_token, tile_count):
    local_count = down_weight.shape[0]
    group_size = cotangent.shape[0]
    expert_index = jnp.arange(EXPERTS, dtype=jnp.int32)
    named_cols = expert_ids[:, :, None] == expert_index[None, None, :]
    gate_cols = jnp.sum(
        jnp.where(named_cols, gate_weights[:, :, None].astype(jnp.float32), 0.0), axis=1
    ).astype(jnp.bfloat16)
    group_cot = lax.all_gather(cotangent, "expert", axis=1, tiled=True)
    width = group_cot.shape[1]
    first_expert = lax.axis_index("expert") * local_count
    slot_index = jnp.arange(hidden.shape[2], dtype=jnp.int32)
    share_rows = down_weight.shape[1] // lax.axis_size("dp")
    partial_value = jnp.zeros((group_size, width), jnp.float32)
    grad_list = []
    weight_list = []
    for local in range(local_count):
        token_rows = row_token[0, local]
        count = tile_count[0, local]
        live_rows = (token_rows >= 0) & (slot_index < count * TILE)
        safe_rows = jnp.where(live_rows, token_rows, 0)
        column = lax.dynamic_index_in_dim(gate_cols, first_expert + local, 1, keepdims=False)
        row_gate = jnp.where(live_rows, column[safe_rows].astype(jnp.float32), 0.0)
        target = jnp.where(live_rows, token_rows, group_size)
        hidden_rows = hidden[0, local]
        weight_mat = down_weight[local]
        out_rows = tile_products(hidden_rows, weight_mat, count, 0)
        partial_value = partial_value.at[target].add(
            row_gate[:, None] * out_rows.astype(jnp.float32), mode="drop"
        )
        routed = (row_gate[:, None] * group_cot[safe_rows].astype(jnp.float32)).astype(jnp.bfloat16)
        grad_list.append(tile_products(routed, weight_mat, count, 1))

        def weight_rows(start, rows_count, hidden_rows=hidden_rows, routed_rows=routed):
            return lax.dot_general(
                hidden_rows,
                routed_rows,
                (((0,), (0,)), ((), ())),
                preferred_element_type=jnp.float32,
            )

        weight_list.append(
            lax.psum_scatter(
                weight_rows(jnp.int32(0), share_rows * lax.axis_size("dp")).astype(jnp.bfloat16),
                "dp",
                scatter_dimension=0,
                tiled=True,
            ).astype(jnp.float32)
        )
    merged = partial_value
    top_bit = lax.axis_size("expert").bit_length() - 1
    axis_index = lax.axis_index("expert")
    for bit_index in reversed(range(top_bit)):
        half_cols = merged.shape[1] // 2
        lower_half = merged[:, :half_cols]
        upper_half = merged[:, half_cols:]
        high_side = axis_index // 2**bit_index % 2 == 1
        sending = jnp.where(high_side, lower_half, upper_half)
        keeping = jnp.where(high_side, upper_half, lower_half)
        merged = keeping + swapped(sending.astype(jnp.bfloat16), "expert", bit_index).astype(
            sending.dtype
        )
    mixed_out = merged.astype(jnp.bfloat16)
    hidden_grad = jnp.stack(grad_list, axis=0)[None]
    weight_grad = jnp.stack(weight_list, axis=0)
    return (mixed_out, hidden_grad, weight_grad)


def solution(mesh):
    placed = (
        P("dp", "expert", None, None),
        P("expert", None, None),
        P("dp", "expert"),
        P("dp", None),
        P("dp", None),
        P("dp", "expert", None),
        P("dp", "expert"),
    )

    def body(*shards):
        width = shards[1].shape[2]
        chips = mesh.shape["expert"] // CORES
        fits = mesh.shape["dp"] == 4 and chips > 2 and width % (chips * LANES) == 0
        return planned_body(*shards) if fits else general_body(*shards)

    return jax.shard_map(
        body,
        mesh=mesh,
        in_specs=placed,
        out_specs=(P("dp", "expert"), P("dp", "expert", None, None), P("expert", "dp", None)),
        check_vma=False,
    )
```

```python
import jax
import jax.numpy as jnp
from jax import lax
from jax.experimental import pallas as pl
from jax.experimental.pallas import tpu as pltpu
from jax.sharding import PartitionSpec as P

EXPERTS = 16
TILE = 128
LANES = 128
CORES = 2
EXTRA_ROWS = 16
MIB = 1024 * 1024


def swapped(shard, axis, bit):
    return lax.ppermute(shard, axis, [(i, i ^ 1 << bit) for i in range(lax.axis_size(axis))])


def across_dp(shard, mask):
    return lax.ppermute(shard, "dp", [(i, i ^ mask) for i in range(lax.axis_size("dp"))])


def across_cores(shard):
    return swapped(shard, "expert", 0)


def z_lines():
    size = lax.axis_size("expert")
    return [list(range(core, size, CORES)) for core in range(CORES)]


def joined(*values):
    return lax.optimization_barrier(values)


def dot(lhs, rhs, lhs_dim, rhs_dim):
    return lax.dot_general(
        lhs, rhs, (((lhs_dim,), (rhs_dim,)), ((), ())), preferred_element_type=jnp.float32
    )


def hot_rows(token_row, gate_row, tokens):
    slots = token_row.shape[1]
    token_index = lax.broadcasted_iota(jnp.int32, (tokens, slots), 0)
    spread = jnp.broadcast_to(gate_row, (tokens, slots))
    return jnp.where(token_index == token_row, spread, 0.0).astype(jnp.bfloat16)


def in_hbm(array):
    return pltpu.with_memory_space_constraint(array, pltpu.HBM)


def whole(shape):
    return pl.BlockSpec(shape, lambda *_: (0,) * len(shape))


def call(kernel, scalars, grid, in_specs, out_specs, out_shape, scratch, operands, vmem):
    return pl.pallas_call(
        kernel,
        grid_spec=pltpu.PrefetchScalarGridSpec(
            num_scalar_prefetch=1,
            grid=grid,
            in_specs=in_specs,
            out_specs=out_specs,
            scratch_shapes=scratch,
        ),
        out_shape=out_shape,
        compiler_params=pltpu.CompilerParams(
            dimension_semantics=("arbitrary",) * len(grid), vmem_limit_bytes=vmem
        ),
    )(scalars, *operands)


def expert_sums(where, token_rows, row_gate, hidden_rows, weight, tokens):
    local_count, slots, width_in = hidden_rows.shape
    chips = lax.axis_size("expert") // CORES
    cols = weight.shape[2] // chips
    half = cols // CORES

    def kernel(where, token_ref, gate_ref, hidden_ref, weight_ref, keep_ref, send_ref, by_token, turned):
        @pl.when(pl.program_id(0) == 0)
        def _():
            for local in range(local_count):
                hot = hot_rows(token_ref[local], gate_ref[local], tokens)
                made = dot(hot, hidden_ref[local], 1, 0).astype(jnp.bfloat16)
                by_token[:, local * width_in : (local + 1) * width_in] = made

        stacked = weight_ref[...].reshape(local_count * width_in, cols)
        turned[...] = dot(by_token[...], stacked, 1, 0).astype(jnp.bfloat16).T
        keep_ref[0] = turned[pl.ds(pl.multiple_of(where[1] * half, half), half), :]
        send_ref[0] = turned[pl.ds(pl.multiple_of((1 - where[1]) * half, half), half), :]

    shape = jax.ShapeDtypeStruct((chips, half, tokens), jnp.bfloat16)
    out_spec = pl.BlockSpec((1, half, tokens), lambda k, where: (k, 0, 0))
    return call(
        kernel,
        where,
        (chips,),
        [
            whole((local_count, 1, slots)),
            whole((local_count, 1, slots)),
            whole(hidden_rows.shape),
            pl.BlockSpec((local_count, width_in, cols), lambda k, where: (0, 0, k)),
        ],
        (out_spec, out_spec),
        (shape, shape),
        [
            pltpu.VMEM((tokens, local_count * width_in), jnp.bfloat16),
            pltpu.VMEM((cols, tokens), jnp.bfloat16),
        ],
        (token_rows[:, None], row_gate[:, None], hidden_rows, in_hbm(weight)),
        32 * MIB,
    )


def resident(kernel, scalars, operands, out_shapes, scratch=(), distant=(), passed=None):
    held = [pltpu.with_memory_space_constraint(array, pltpu.VMEM) for array in operands]
    in_vmem, anywhere = pl.BlockSpec(memory_space=pltpu.VMEM), pl.BlockSpec(memory_space=pl.ANY)
    far_off = [in_hbm(array) for array in distant] + ([] if passed is None else [passed])
    return pl.pallas_call(
        kernel,
        in_specs=[pl.BlockSpec(memory_space=pltpu.SMEM)] + [in_vmem] * len(held) + [anywhere] * len(far_off),
        out_specs=[anywhere if isinstance(shape, jax.ShapeDtypeStruct) else in_vmem for shape in out_shapes],
        out_shape=out_shapes,
        scratch_shapes=list(scratch),
        input_output_aliases={} if passed is None else {len(held) + len(far_off): 0},
        compiler_params=pltpu.CompilerParams(vmem_limit_bytes=20 * MIB),
    )(scalars, *held, *far_off)


def shares_by_token(where, payloads, slots, tokens):
    local_count, _, share = payloads[0].shape
    groups = len(payloads)

    def kernel(where, *refs):
        sources, (out_ref, held, sem) = refs[:groups], refs[groups:]
        loads = [pltpu.make_async_copy(ref, held.at[i], sem.at[i]) for i, ref in enumerate(sources)]
        for load in loads:
            load.start()

        def row(group, local, first):
            wide = [held[group, local, slots + first + i : slots + first + i + 1, :] for i in range(2)]
            return jnp.concatenate(wide, axis=1)[:, :slots].astype(jnp.float32)

        for group in range(groups):
            loads[group].wait()
            for local in range(local_count):
                token = (row(group, local, 0) * 2.0 + row(group, local, 2)).astype(jnp.int32)
                hot = hot_rows(token, row(group, local, 4), tokens)
                by_token = dot(hot, held[group, local, :slots, :], 1, 0).astype(jnp.bfloat16)
                out_ref[local * share : (local + 1) * share, group * tokens : (group + 1) * tokens] = by_token.T

    shape = (local_count * share, groups * tokens)
    scratch = [pltpu.VMEM((groups, *payloads[0].shape), jnp.bfloat16), pltpu.SemaphoreType.DMA((groups,))]
    return resident(kernel, where, [], [pltpu.VMEM(shape, jnp.bfloat16)], scratch, payloads)[0]


def blocks_of(where, gathered, steps, parts):
    devices, rows, tokens = gathered.shape
    part = rows // parts

    def kernel(where, gathered_ref, *refs):
        sem = refs[-1]
        copies = []
        for place, step in enumerate(steps):
            chip = lax.rem(where[0] + step, devices // CORES)
            for index, out_ref in enumerate(refs[:-1]):
                source = gathered_ref.at[chip * CORES + where[1], pl.ds(index * part, part)]
                copies.append(pltpu.make_async_copy(source, out_ref.at[place], sem.at[len(copies)]))
        for copy in copies:
            copy.start()
        for copy in copies:
            copy.wait()

    return pl.pallas_call(
        kernel,
        in_specs=[pl.BlockSpec(memory_space=pltpu.SMEM), pl.BlockSpec(memory_space=pl.ANY)],
        out_specs=[pl.BlockSpec(memory_space=pltpu.VMEM)] * parts,
        out_shape=[pltpu.VMEM((len(steps), part, tokens), gathered.dtype)] * parts,
        scratch_shapes=[pltpu.SemaphoreType.DMA((len(steps) * parts,))],
    )(where, in_hbm(gathered))


def hidden_grads(where, token_rows, row_gate, group_cot, weight):
    local_count, width_in, width = weight.shape
    slots = token_rows.shape[1]
    tokens = group_cot.shape[1]
    depth = width_in // 2

    def kernel(where, token_ref, gate_ref, cot_ref, weight_ref, out_ref):
        local = pl.program_id(0)
        sums = dot(weight_ref[0], cot_ref[...], 1, 0).astype(jnp.bfloat16)
        hot = hot_rows(token_ref[local], gate_ref[local], tokens)
        out_ref[0] = dot(hot, sums, 0, 1).astype(jnp.bfloat16)

    return call(
        kernel,
        where,
        (local_count, width_in // depth),
        [whole((local_count, 1, slots))] * 2
        + [whole(group_cot.shape)]
        + [pl.BlockSpec((1, depth, width), lambda e, h, where: (e, h, 0))],
        pl.BlockSpec((1, slots, depth), lambda e, h, where: (e, 0, h)),
        jax.ShapeDtypeStruct((local_count, slots, width_in), jnp.bfloat16),
        [],
        (token_rows[:, None], row_gate[:, None], in_hbm(group_cot), in_hbm(weight)),
        28 * MIB,
    )


def weight_cols(where, jobs, shares, local_count, width, gathered=None, passed=None, add=False):
    chips = lax.axis_size("expert") // CORES
    cols = width // chips
    share = shares.shape[0] // local_count
    held = [shares]
    for _, groups in jobs:
        for _, sides in groups:
            for array, _ in (piece for pieces in sides for piece in pieces):
                if not any(array is other for other in held):
                    held.append(array)
    tokens = held[1].shape[-1]
    distant = [] if gathered is None else [gathered]
    count = len(jobs)

    def kernel(where, *refs):
        refs = list(refs)
        held_refs = [refs.pop(0) for _ in held]
        shares_ref = held_refs[0]
        source = refs.pop(0) if distant else None
        so_far = refs.pop(0) if passed is not None else None
        out_ref, total_ref, sem = refs[:3]
        columns, loads = [], []
        for i, (step, _) in enumerate(jobs):
            place = lax.rem(where[0] + step, chips)
            columns.append(pl.ds(pl.multiple_of(place * cols, LANES), cols))
            if distant:
                block = source.at[pl.ds(place * CORES, CORES)]
                loads.append(pltpu.make_async_copy(block, refs[3].at[i], refs[4].at[i]))
            if add:
                loads.append(pltpu.make_async_copy(so_far.at[:, :, columns[i]], refs[3].at[i], refs[4].at[i]))
        for load in loads:
            load.start()

        def block_of(pieces):
            found = [held_refs[[a is array for a in held].index(True)][index] for array, index in pieces]
            return found[0] if len(found) == 1 else jnp.concatenate(found, axis=0)

        stores = []
        for i, (_, groups) in enumerate(jobs):
            total = None
            for place, sides in groups:
                mine, other = map(block_of, sides)
                low = jnp.where(where[1] == 0, mine, other)
                high = jnp.where(where[1] == 0, other, mine)
                block = jnp.concatenate([low, high], axis=0)
                product = dot(shares_ref[:, place * tokens : (place + 1) * tokens], block, 1, 1)
                total = product if total is None else total + product
            if loads:
                loads[i].wait()
            if distant:
                total = total + dot(shares_ref[:, :tokens], refs[3][i].reshape(cols, tokens), 1, 1)
            for local in range(local_count):
                part = total[local * share : (local + 1) * share]
                total_ref[i, local] = part + refs[3][i, local] if add else part
            stores.append(pltpu.make_async_copy(total_ref.at[i], out_ref.at[:, :, columns[i]], sem.at[i]))
            stores[-1].start()
        for store in stores:
            store.wait()

    by_chip = (count, local_count, share, cols)
    scratch = [pltpu.VMEM(by_chip, jnp.float32), pltpu.SemaphoreType.DMA((count,))]
    if distant:
        scratch.append(pltpu.VMEM((count, CORES, cols // CORES, tokens), jnp.bfloat16))
    if add:
        scratch.append(pltpu.VMEM(by_chip, jnp.float32))
    if distant or add:
        scratch.append(pltpu.SemaphoreType.DMA((count,)))
    out_shape = jax.ShapeDtypeStruct((local_count, share, width), jnp.float32)
    return resident(kernel, where, held, [out_shape], scratch, distant, passed)[0]


def planned_body(hidden, down_weight, cotangent, expert_ids, gate_weights, row_token, tile_count):
    local_count, width_in, width = down_weight.shape
    tokens = cotangent.shape[0]
    slots = hidden.shape[2]
    groups = lax.axis_size("dp")
    chips = lax.axis_size("expert") // CORES
    share = width_in // groups
    group = lax.axis_index("dp")
    expert_place = lax.axis_index("expert")
    chip = expert_place // CORES
    core = expert_place % CORES
    where = jnp.stack([chip, core])

    own = cotangent.T
    middle = own.shape[0] // 2
    gathered = lax.all_gather(own, "expert")
    x_own, y_own = across_dp(own, 1), across_dp(own, 2)

    slot_index = jnp.arange(slots, dtype=jnp.int32)
    token_index = jnp.arange(tokens, dtype=jnp.int32)
    live = (row_token[0] >= 0) & (slot_index[None] < tile_count[0][:, None] * TILE)
    token_rows = jnp.where(live, row_token[0], -1)
    experts = expert_place * local_count + jnp.arange(local_count, dtype=jnp.int32)
    named = expert_ids[None] == experts[:, None, None]
    token_gate = jnp.sum(jnp.where(named, gate_weights[None].astype(jnp.float32), 0.0), axis=2)
    at_token = token_rows[:, :, None] == token_index[None, None, :]
    row_gate = jnp.sum(jnp.where(at_token, token_gate[:, None, :], 0.0), axis=2)

    def as_rows(values):
        padded = jnp.pad(values.astype(jnp.bfloat16), ((0, 0), (0, 2 * share - slots)))
        return padded.reshape(local_count, 2, share)

    extra = jnp.concatenate(
        [as_rows(token_rows >> 1), as_rows(token_rows & 1), as_rows(row_gate)], axis=1
    )
    extra = jnp.pad(extra, ((0, 0), (0, EXTRA_ROWS - extra.shape[1]), (0, 0)))
    payloads = []
    for mask in range(groups):
        rows = lax.dynamic_slice_in_dim(hidden[0], (group ^ mask) * share, share, 2)
        payloads.append(jnp.concatenate([rows, extra], axis=1))
    x_own, y_own, token_rows, row_gate, *payloads = joined(
        x_own, y_own, token_rows, row_gate, *payloads
    )

    payloads = [across_dp(payload, mask) if mask else payload for mask, payload in enumerate(payloads)]
    far_own = [across_dp(x_own[:middle], 2), across_dp(y_own[middle:], 1)]
    keep, send = expert_sums(where, token_rows, row_gate, hidden[0], down_weight, tokens)
    x_own, y_own, keep, send, *sent = joined(x_own, y_own, keep, send, *far_own, *payloads)
    far_own, payloads = sent[:2], sent[2:]

    steps = list(range(1, chips))
    near = blocks_of(where, gathered, steps, 2)
    x_near, y_near = [None, None], [None, None]
    x_near[0], y_near[1] = across_dp(near[0], 1), across_dp(near[1], 2)
    x_near[1], y_near[0] = across_dp(near[1], 1), across_dp(near[0], 2)

    own_far = [x_own, y_own, *far_own]
    from_other, *own_far_other = [across_cores(block) for block in (send, *own_far)]
    shares = shares_by_token(where, payloads, slots, tokens)
    from_other, shares, *own_far_other = joined(from_other, shares, *own_far_other)
    sums = (keep.astype(jnp.float32) + from_other.astype(jnp.float32)).astype(jnp.bfloat16)
    mixed = lax.psum_scatter(sums, "expert", scatter_dimension=0, axis_index_groups=z_lines())
    hidden_grad = hidden_grads(where, token_rows, row_gate, gathered.reshape(width, tokens), down_weight)
    hidden_grad, shares, _, *sent = joined(hidden_grad, shares, sums, *x_near, *y_near)
    x_near, y_near = sent[:2], sent[2:]

    far = [across_dp(x_near[0], 2), across_dp(y_near[1], 1)]
    x_other = [across_cores(part) for part in x_near]
    y_other = [across_cores(part) for part in y_near]

    def pieces(index, *arrays):
        return [(array, index) for array in arrays]

    own_pairs = [(pieces(..., mine), pieces(..., other)) for mine, other in zip(own_far, own_far_other)]
    own_pairs[2] = tuple(a + b for a, b in zip(*own_pairs[2:]))
    jobs = [(0, list(enumerate(own_pairs[:3], 1)))]
    for step in steps:
        pairs = [(pieces(step - 1, *mine), pieces(step - 1, *other)) for mine, other in ((x_near, x_other), (y_near, y_other))]
        jobs.append((step, list(enumerate(pairs, 1))))
    weight_grad = weight_cols(where, jobs, shares, local_count, width, gathered)
    weight_grad, mixed, *far = joined(weight_grad, mixed, *far)
    far_other = [across_cores(part) for part in far]
    jobs = [(step, [(groups - 1, (pieces(step - 1, *far), pieces(step - 1, *far_other)))]) for step in steps]
    weight_grad = weight_cols(where, jobs, shares, local_count, width, None, weight_grad, True)
    return (mixed.T, hidden_grad[None], weight_grad)


def tile_products(rows_in, weight_mat, count, contract_dim):
    rows_cap = rows_in.shape[0]
    width_out = weight_mat.shape[1 - contract_dim]

    def one_tile(tile_index, outputs):
        block = lax.dynamic_slice_in_dim(rows_in, tile_index * TILE, TILE, 0)
        product = lax.dot_general(
            block,
            weight_mat,
            (((1,), (contract_dim,)), ((), ())),
            preferred_element_type=jnp.float32,
        )
        return lax.dynamic_update_slice_in_dim(
            outputs, product.astype(jnp.bfloat16), tile_index * TILE, 0
        )

    return lax.fori_loop(0, count, one_tile, jnp.zeros((rows_cap, width_out), jnp.bfloat16))


def general_body(hidden, down_weight, cotangent, expert_ids, gate_weights, row_token, tile_count):
    local_count = down_weight.shape[0]
    group_size = cotangent.shape[0]
    expert_index = jnp.arange(EXPERTS, dtype=jnp.int32)
    named_cols = expert_ids[:, :, None] == expert_index[None, None, :]
    gate_cols = jnp.sum(
        jnp.where(named_cols, gate_weights[:, :, None].astype(jnp.float32), 0.0), axis=1
    ).astype(jnp.bfloat16)
    group_cot = lax.all_gather(cotangent, "expert", axis=1, tiled=True)
    width = group_cot.shape[1]
    first_expert = lax.axis_index("expert") * local_count
    slot_index = jnp.arange(hidden.shape[2], dtype=jnp.int32)
    share_rows = down_weight.shape[1] // lax.axis_size("dp")
    partial_value = jnp.zeros((group_size, width), jnp.float32)
    grad_list = []
    weight_list = []
    for local in range(local_count):
        token_rows = row_token[0, local]
        count = tile_count[0, local]
        live_rows = (token_rows >= 0) & (slot_index < count * TILE)
        safe_rows = jnp.where(live_rows, token_rows, 0)
        column = lax.dynamic_index_in_dim(gate_cols, first_expert + local, 1, keepdims=False)
        row_gate = jnp.where(live_rows, column[safe_rows].astype(jnp.float32), 0.0)
        target = jnp.where(live_rows, token_rows, group_size)
        hidden_rows = hidden[0, local]
        weight_mat = down_weight[local]
        out_rows = tile_products(hidden_rows, weight_mat, count, 0)
        partial_value = partial_value.at[target].add(
            row_gate[:, None] * out_rows.astype(jnp.float32), mode="drop"
        )
        routed = (row_gate[:, None] * group_cot[safe_rows].astype(jnp.float32)).astype(jnp.bfloat16)
        grad_list.append(tile_products(routed, weight_mat, count, 1))

        def weight_rows(start, rows_count, hidden_rows=hidden_rows, routed_rows=routed):
            return lax.dot_general(
                hidden_rows,
                routed_rows,
                (((0,), (0,)), ((), ())),
                preferred_element_type=jnp.float32,
            )

        weight_list.append(
            lax.psum_scatter(
                weight_rows(jnp.int32(0), share_rows * lax.axis_size("dp")).astype(jnp.bfloat16),
                "dp",
                scatter_dimension=0,
                tiled=True,
            ).astype(jnp.float32)
        )
    merged = partial_value
    top_bit = lax.axis_size("expert").bit_length() - 1
    axis_index = lax.axis_index("expert")
    for bit_index in reversed(range(top_bit)):
        half_cols = merged.shape[1] // 2
        lower_half = merged[:, :half_cols]
        upper_half = merged[:, half_cols:]
        high_side = axis_index // 2**bit_index % 2 == 1
        sending = jnp.where(high_side, lower_half, upper_half)
        keeping = jnp.where(high_side, upper_half, lower_half)
        merged = keeping + swapped(sending.astype(jnp.bfloat16), "expert", bit_index).astype(
            sending.dtype
        )
    mixed_out = merged.astype(jnp.bfloat16)
    hidden_grad = jnp.stack(grad_list, axis=0)[None]
    weight_grad = jnp.stack(weight_list, axis=0)
    return (mixed_out, hidden_grad, weight_grad)


def solution(mesh):
    placed = (
        P("dp", "expert", None, None),
        P("expert", None, None),
        P("dp", "expert"),
        P("dp", None),
        P("dp", None),
        P("dp", "expert", None),
        P("dp", "expert"),
    )

    def body(*shards):
        width = shards[1].shape[2]
        chips = mesh.shape["expert"] // CORES
        fits = mesh.shape["dp"] == 4 and chips > 2 and width % (chips * LANES) == 0
        return planned_body(*shards) if fits else general_body(*shards)

    return jax.shard_map(
        body,
        mesh=mesh,
        in_specs=placed,
        out_specs=(P("dp", "expert"), P("dp", "expert", None, None), P("expert", "dp", None)),
        check_vma=False,
    )
```

```python
import jax
import jax.numpy as jnp
from jax import lax
from jax.experimental import pallas as pl
from jax.experimental.pallas import tpu as pltpu
from jax.sharding import PartitionSpec as P

EXPERTS = 16
TILE = 128
LANES = 128
CORES = 2
EXTRA_ROWS = 16
MIB = 1024 * 1024


def swapped(shard, axis, bit):
    return lax.ppermute(shard, axis, [(i, i ^ 1 << bit) for i in range(lax.axis_size(axis))])


def across_dp(shard, mask):
    return lax.ppermute(shard, "dp", [(i, i ^ mask) for i in range(lax.axis_size("dp"))])


def across_cores(shard):
    return swapped(shard, "expert", 0)


def along_z(shard, step, senders):
    pairs = [
        (CORES * z + core, CORES * (z + step) + core) for z in senders for core in range(CORES)
    ]
    return lax.ppermute(shard, "expert", pairs)


def z_lines():
    size = lax.axis_size("expert")
    return [list(range(core, size, CORES)) for core in range(CORES)]


def joined(*values):
    return lax.optimization_barrier(values)


def dot(lhs, rhs, lhs_dim, rhs_dim):
    return lax.dot_general(
        lhs, rhs, (((lhs_dim,), (rhs_dim,)), ((), ())), preferred_element_type=jnp.float32
    )


def hot_rows(token_row, gate_row, tokens):
    slots = token_row.shape[1]
    token_index = lax.broadcasted_iota(jnp.int32, (tokens, slots), 0)
    spread = jnp.broadcast_to(gate_row, (tokens, slots))
    return jnp.where(token_index == token_row, spread, 0.0).astype(jnp.bfloat16)


def in_hbm(array):
    return pltpu.with_memory_space_constraint(array, pltpu.HBM)


def whole(shape):
    return pl.BlockSpec(shape, lambda *_: (0,) * len(shape))


def call(kernel, scalars, grid, in_specs, out_specs, out_shape, scratch, operands, vmem):
    return pl.pallas_call(
        kernel,
        grid_spec=pltpu.PrefetchScalarGridSpec(
            num_scalar_prefetch=1,
            grid=grid,
            in_specs=in_specs,
            out_specs=out_specs,
            scratch_shapes=scratch,
        ),
        out_shape=out_shape,
        compiler_params=pltpu.CompilerParams(
            dimension_semantics=("arbitrary",) * len(grid), vmem_limit_bytes=vmem
        ),
    )(scalars, *operands)


def expert_sums(where, token_rows, row_gate, hidden_rows, weight, tokens):
    local_count, slots, width_in = hidden_rows.shape
    chips = lax.axis_size("expert") // CORES
    cols = weight.shape[2] // chips
    half = cols // CORES

    def kernel(where, token_ref, gate_ref, hidden_ref, weight_ref, keep_ref, send_ref, by_token, turned):
        @pl.when(pl.program_id(0) == 0)
        def _():
            for local in range(local_count):
                hot = hot_rows(token_ref[local], gate_ref[local], tokens)
                made = dot(hot, hidden_ref[local], 1, 0).astype(jnp.bfloat16)
                by_token[:, local * width_in : (local + 1) * width_in] = made

        stacked = weight_ref[...].reshape(local_count * width_in, cols)
        turned[...] = dot(by_token[...], stacked, 1, 0).astype(jnp.bfloat16).T
        keep_ref[0] = turned[pl.ds(pl.multiple_of(where[1] * half, half), half), :]
        send_ref[0] = turned[pl.ds(pl.multiple_of((1 - where[1]) * half, half), half), :]

    shape = jax.ShapeDtypeStruct((chips, half, tokens), jnp.bfloat16)
    out_spec = pl.BlockSpec((1, half, tokens), lambda k, where: (k, 0, 0))
    return call(
        kernel,
        where,
        (chips,),
        [
            whole((local_count, 1, slots)),
            whole((local_count, 1, slots)),
            whole(hidden_rows.shape),
            pl.BlockSpec((local_count, width_in, cols), lambda k, where: (0, 0, k)),
        ],
        (out_spec, out_spec),
        (shape, shape),
        [
            pltpu.VMEM((tokens, local_count * width_in), jnp.bfloat16),
            pltpu.VMEM((cols, tokens), jnp.bfloat16),
        ],
        (token_rows[:, None], row_gate[:, None], hidden_rows, in_hbm(weight)),
        32 * MIB,
    )


def resident(kernel, scalars, operands, out_shapes, scratch=(), distant=(), passed=None):
    held = [pltpu.with_memory_space_constraint(array, pltpu.VMEM) for array in operands]
    in_vmem, anywhere = pl.BlockSpec(memory_space=pltpu.VMEM), pl.BlockSpec(memory_space=pl.ANY)
    far_off = [in_hbm(array) for array in distant] + ([] if passed is None else [passed])
    return pl.pallas_call(
        kernel,
        in_specs=[pl.BlockSpec(memory_space=pltpu.SMEM)] + [in_vmem] * len(held) + [anywhere] * len(far_off),
        out_specs=[anywhere if isinstance(shape, jax.ShapeDtypeStruct) else in_vmem for shape in out_shapes],
        out_shape=out_shapes,
        scratch_shapes=list(scratch),
        input_output_aliases={} if passed is None else {len(held) + len(far_off): 0},
        compiler_params=pltpu.CompilerParams(vmem_limit_bytes=20 * MIB),
    )(scalars, *held, *far_off)


def shares_by_token(where, payloads, slots, tokens):
    local_count, _, share = payloads[0].shape
    groups = len(payloads)

    def kernel(where, *refs):
        sources, (out_ref, held, sem) = refs[:groups], refs[groups:]
        loads = [pltpu.make_async_copy(ref, held.at[i], sem.at[i]) for i, ref in enumerate(sources)]
        for load in loads:
            load.start()

        def row(group, local, first):
            wide = [held[group, local, slots + first + i : slots + first + i + 1, :] for i in range(2)]
            return jnp.concatenate(wide, axis=1)[:, :slots].astype(jnp.float32)

        for group in range(groups):
            loads[group].wait()
            for local in range(local_count):
                token = (row(group, local, 0) * 2.0 + row(group, local, 2)).astype(jnp.int32)
                hot = hot_rows(token, row(group, local, 4), tokens)
                by_token = dot(hot, held[group, local, :slots, :], 1, 0).astype(jnp.bfloat16)
                out_ref[local * share : (local + 1) * share, group * tokens : (group + 1) * tokens] = by_token.T

    shape = (local_count * share, groups * tokens)
    scratch = [pltpu.VMEM((groups, *payloads[0].shape), jnp.bfloat16), pltpu.SemaphoreType.DMA((groups,))]
    return resident(kernel, where, [], [pltpu.VMEM(shape, jnp.bfloat16)], scratch, payloads)[0]


def blocks_of(where, gathered, places):
    _, rows, tokens = gathered.shape

    def kernel(where, gathered_ref, *refs):
        sem = refs[-1]
        copies = []
        for place, out_ref in zip(places, refs):
            source = gathered_ref.at[where[place] * CORES + where[1]]
            copies.append(pltpu.make_async_copy(source, out_ref, sem.at[len(copies)]))
        for copy in copies:
            copy.start()
        for copy in copies:
            copy.wait()

    return pl.pallas_call(
        kernel,
        in_specs=[pl.BlockSpec(memory_space=pltpu.SMEM), pl.BlockSpec(memory_space=pl.ANY)],
        out_specs=[pl.BlockSpec(memory_space=pltpu.VMEM)] * len(places),
        out_shape=[pltpu.VMEM((rows, tokens), gathered.dtype)] * len(places),
        scratch_shapes=[pltpu.SemaphoreType.DMA((len(places),))],
    )(where, in_hbm(gathered))


def hidden_grads(where, token_rows, row_gate, group_cot, weight):
    local_count, width_in, width = weight.shape
    slots = token_rows.shape[1]
    tokens = group_cot.shape[1]
    depth = width_in // 2

    def kernel(where, token_ref, gate_ref, cot_ref, weight_ref, out_ref):
        local = pl.program_id(0)
        sums = dot(weight_ref[0], cot_ref[...], 1, 0).astype(jnp.bfloat16)
        hot = hot_rows(token_ref[local], gate_ref[local], tokens)
        out_ref[0] = dot(hot, sums, 0, 1).astype(jnp.bfloat16)

    return call(
        kernel,
        where,
        (local_count, width_in // depth),
        [whole((local_count, 1, slots))] * 2
        + [whole(group_cot.shape)]
        + [pl.BlockSpec((1, depth, width), lambda e, h, where: (e, h, 0))],
        pl.BlockSpec((1, slots, depth), lambda e, h, where: (e, 0, h)),
        jax.ShapeDtypeStruct((local_count, slots, width_in), jnp.bfloat16),
        [],
        (token_rows[:, None], row_gate[:, None], in_hbm(group_cot), in_hbm(weight)),
        28 * MIB,
    )


def weight_cols(where, jobs, shares, gathered, local_count, width, passed, loading):
    chips = lax.axis_size("expert") // CORES
    cols = width // chips
    half = cols // CORES
    share = shares.shape[0] // local_count
    tokens = gathered.shape[-1]
    count = len(jobs)
    blocks = [block for _, pairs in jobs for pair in pairs for block in pair]
    held, distant = ([shares], [gathered, *blocks]) if loading else ([shares, *blocks], [gathered])

    def kernel(where, *refs):
        refs = list(refs)
        shares_ref = refs.pop(0)
        block_refs = [] if loading else [refs.pop(0) for _ in blocks]
        source = refs.pop(0)
        load_refs = [refs.pop(0) for _ in blocks] if loading else []
        if passed is not None:
            refs.pop(0)
        out_ref, total_ref, sem, own_ref, own_sem = refs[:5]
        loads = []
        for i, (place, _) in enumerate(jobs):
            own = source.at[pl.ds(where[place] * CORES, CORES)]
            loads.append(pltpu.make_async_copy(own, own_ref.at[i], own_sem.at[i]))
        for i, ref in enumerate(load_refs):
            loads.append(pltpu.make_async_copy(ref, refs[5].at[i], refs[6].at[i]))
        for load in loads:
            load.start()

        stores, at = [], 0
        for i, (place, pairs) in enumerate(jobs):
            loads[i].wait()
            total = dot(shares_ref[:, :tokens], own_ref[i].reshape(cols, tokens), 1, 1)
            for group in range(1, len(pairs) + 1):
                if loading:
                    loads[count + at].wait()
                    loads[count + at + 1].wait()
                    mine, other = refs[5][at], refs[5][at + 1]
                else:
                    mine, other = block_refs[at][...], block_refs[at + 1][...]
                at += 2
                low = jnp.where(where[1] == 0, mine, other)
                high = jnp.where(where[1] == 0, other, mine)
                part = shares_ref[:, group * tokens : (group + 1) * tokens]
                total = total + dot(part, jnp.concatenate([low, high], axis=0), 1, 1)
            for local in range(local_count):
                total_ref[i, local] = total[local * share : (local + 1) * share]
            columns = pl.ds(pl.multiple_of(where[place] * cols, LANES), cols)
            stores.append(pltpu.make_async_copy(total_ref.at[i], out_ref.at[:, :, columns], sem.at[i]))
            stores[-1].start()
        for store in stores:
            store.wait()

    scratch = [
        pltpu.VMEM((count, local_count, share, cols), jnp.float32),
        pltpu.SemaphoreType.DMA((count,)),
        pltpu.VMEM((count, CORES, half, tokens), jnp.bfloat16),
        pltpu.SemaphoreType.DMA((count,)),
    ]
    if loading:
        scratch += [pltpu.VMEM((len(blocks), half, tokens), jnp.bfloat16), pltpu.SemaphoreType.DMA((len(blocks),))]
    out_shape = jax.ShapeDtypeStruct((local_count, share, width), jnp.float32)
    return resident(kernel, where, held, [out_shape], scratch, distant, passed)[0]


def planned_body(hidden, down_weight, cotangent, expert_ids, gate_weights, row_token, tile_count):
    local_count, width_in, width = down_weight.shape
    tokens = cotangent.shape[0]
    slots = hidden.shape[2]
    groups = lax.axis_size("dp")
    chips = lax.axis_size("expert") // CORES
    share = width_in // groups
    group = lax.axis_index("dp")
    expert_place = lax.axis_index("expert")
    chip = expert_place // CORES
    core = expert_place % CORES

    at_low = chip == 0
    next_chip = jnp.where(at_low, 1, chip - 1)
    others = [jnp.where(chip > 1, jnp.where(chip == 2, 3, 0), 2), jnp.where(chip > 1, jnp.where(chip == 2, 0, 1), 3)]
    where = jnp.stack([chip, core, chip, next_chip, *others])

    own = cotangent.T
    gathered = lax.all_gather(own, "expert")
    x_0, y_0 = across_dp(own, 1), across_dp(own, 2)
    low, high = along_z(own, 1, range(chips - 1)), along_z(own, -1, range(1, chips))

    slot_index = jnp.arange(slots, dtype=jnp.int32)
    token_index = jnp.arange(tokens, dtype=jnp.int32)
    live = (row_token[0] >= 0) & (slot_index[None] < tile_count[0][:, None] * TILE)
    token_rows = jnp.where(live, row_token[0], -1)
    experts = expert_place * local_count + jnp.arange(local_count, dtype=jnp.int32)
    named = expert_ids[None] == experts[:, None, None]
    token_gate = jnp.sum(jnp.where(named, gate_weights[None].astype(jnp.float32), 0.0), axis=2)
    at_token = token_rows[:, :, None] == token_index[None, None, :]
    row_gate = jnp.sum(jnp.where(at_token, token_gate[:, None, :], 0.0), axis=2)

    def as_rows(values):
        padded = jnp.pad(values.astype(jnp.bfloat16), ((0, 0), (0, 2 * share - slots)))
        return padded.reshape(local_count, 2, share)

    extra = jnp.concatenate(
        [as_rows(token_rows >> 1), as_rows(token_rows & 1), as_rows(row_gate)], axis=1
    )
    extra = jnp.pad(extra, ((0, 0), (0, EXTRA_ROWS - extra.shape[1]), (0, 0)))
    payloads = []
    for mask in range(groups):
        rows = lax.dynamic_slice_in_dim(hidden[0], (group ^ mask) * share, share, 2)
        payloads.append(jnp.concatenate([rows, extra], axis=1))
    x_0, y_0, low, high, token_rows, row_gate, *payloads = joined(
        x_0, y_0, low, high, token_rows, row_gate, *payloads
    )

    payloads = [across_dp(payload, mask) if mask else payload for mask, payload in enumerate(payloads)]
    keep, send = expert_sums(where, token_rows, row_gate, hidden[0], down_weight, tokens)
    block_1 = jnp.where(at_low, high, low)
    x_0, y_0, block_1, keep, send, *payloads = joined(x_0, y_0, block_1, keep, send, *payloads)

    far_0, x_1 = across_dp(x_0, 2), across_dp(block_1, 1)
    from_other, x_0_other, y_0_other = [across_cores(block) for block in (send, x_0, y_0)]
    shares = shares_by_token(where, payloads, slots, tokens)
    sums = (keep.astype(jnp.float32) + from_other.astype(jnp.float32)).astype(jnp.bfloat16)
    shares, _, far_0, x_1, x_0_other, y_0_other, block_1 = joined(
        shares, sums, far_0, x_1, x_0_other, y_0_other, block_1
    )
    mixed = lax.psum_scatter(sums, "expert", scatter_dimension=0, axis_index_groups=z_lines())

    y_1 = across_dp(block_1, 2)
    block_2, block_3 = blocks_of(where, gathered, (4, 5))
    x_2, y_2 = across_dp(block_2, 1), across_dp(block_2, 2)
    x_3, y_3 = across_dp(block_3, 1), across_dp(block_3, 2)
    hidden_grad = hidden_grads(where, token_rows, row_gate, gathered.reshape(width, tokens), down_weight)
    hidden_grad, shares, far_0, y_1, x_2, x_3, y_3 = joined(hidden_grad, shares, far_0, y_1, x_2, x_3, y_3)

    rest = (local_count, width)
    far_1, far_2, far_3 = across_dp(y_1, 1), across_dp(x_2, 2), across_dp(y_3, 1)
    far_0_other = across_cores(far_0)
    pairs = [(x_0, x_0_other), (y_0, y_0_other), (far_0, far_0_other)]
    weight_grad = weight_cols(where, [(2, pairs)], shares, gathered, *rest, None, True)
    weight_grad, y_2, far_1 = joined(weight_grad, y_2, far_1)
    pairs = [(block, across_cores(block)) for block in (x_1, y_1, far_1)]
    weight_grad = weight_cols(where, [(3, pairs)], shares, gathered, *rest, weight_grad, False)
    weight_grad, far_2, far_3, mixed = joined(weight_grad, far_2, far_3, mixed)
    pairs = [[(block, across_cores(block)) for block in blocks] for blocks in ((x_2, y_2, far_2), (x_3, y_3, far_3))]
    weight_grad = weight_cols(where, [*zip((4, 5), pairs)], shares, gathered, *rest, weight_grad, False)
    return (mixed.T, hidden_grad[None], weight_grad)


def tile_products(rows_in, weight_mat, count, contract_dim):
    rows_cap = rows_in.shape[0]
    width_out = weight_mat.shape[1 - contract_dim]

    def one_tile(tile_index, outputs):
        block = lax.dynamic_slice_in_dim(rows_in, tile_index * TILE, TILE, 0)
        product = lax.dot_general(
            block,
            weight_mat,
            (((1,), (contract_dim,)), ((), ())),
            preferred_element_type=jnp.float32,
        )
        return lax.dynamic_update_slice_in_dim(
            outputs, product.astype(jnp.bfloat16), tile_index * TILE, 0
        )

    return lax.fori_loop(0, count, one_tile, jnp.zeros((rows_cap, width_out), jnp.bfloat16))


def general_body(hidden, down_weight, cotangent, expert_ids, gate_weights, row_token, tile_count):
    local_count = down_weight.shape[0]
    group_size = cotangent.shape[0]
    expert_index = jnp.arange(EXPERTS, dtype=jnp.int32)
    named_cols = expert_ids[:, :, None] == expert_index[None, None, :]
    gate_cols = jnp.sum(
        jnp.where(named_cols, gate_weights[:, :, None].astype(jnp.float32), 0.0), axis=1
    ).astype(jnp.bfloat16)
    group_cot = lax.all_gather(cotangent, "expert", axis=1, tiled=True)
    width = group_cot.shape[1]
    first_expert = lax.axis_index("expert") * local_count
    slot_index = jnp.arange(hidden.shape[2], dtype=jnp.int32)
    share_rows = down_weight.shape[1] // lax.axis_size("dp")
    partial_value = jnp.zeros((group_size, width), jnp.float32)
    grad_list = []
    weight_list = []
    for local in range(local_count):
        token_rows = row_token[0, local]
        count = tile_count[0, local]
        live_rows = (token_rows >= 0) & (slot_index < count * TILE)
        safe_rows = jnp.where(live_rows, token_rows, 0)
        column = lax.dynamic_index_in_dim(gate_cols, first_expert + local, 1, keepdims=False)
        row_gate = jnp.where(live_rows, column[safe_rows].astype(jnp.float32), 0.0)
        target = jnp.where(live_rows, token_rows, group_size)
        hidden_rows = hidden[0, local]
        weight_mat = down_weight[local]
        out_rows = tile_products(hidden_rows, weight_mat, count, 0)
        partial_value = partial_value.at[target].add(
            row_gate[:, None] * out_rows.astype(jnp.float32), mode="drop"
        )
        routed = (row_gate[:, None] * group_cot[safe_rows].astype(jnp.float32)).astype(jnp.bfloat16)
        grad_list.append(tile_products(routed, weight_mat, count, 1))

        def weight_rows(start, rows_count, hidden_rows=hidden_rows, routed_rows=routed):
            return lax.dot_general(
                hidden_rows,
                routed_rows,
                (((0,), (0,)), ((), ())),
                preferred_element_type=jnp.float32,
            )

        weight_list.append(
            lax.psum_scatter(
                weight_rows(jnp.int32(0), share_rows * lax.axis_size("dp")).astype(jnp.bfloat16),
                "dp",
                scatter_dimension=0,
                tiled=True,
            ).astype(jnp.float32)
        )
    merged = partial_value
    top_bit = lax.axis_size("expert").bit_length() - 1
    axis_index = lax.axis_index("expert")
    for bit_index in reversed(range(top_bit)):
        half_cols = merged.shape[1] // 2
        lower_half = merged[:, :half_cols]
        upper_half = merged[:, half_cols:]
        high_side = axis_index // 2**bit_index % 2 == 1
        sending = jnp.where(high_side, lower_half, upper_half)
        keeping = jnp.where(high_side, upper_half, lower_half)
        merged = keeping + swapped(sending.astype(jnp.bfloat16), "expert", bit_index).astype(
            sending.dtype
        )
    mixed_out = merged.astype(jnp.bfloat16)
    hidden_grad = jnp.stack(grad_list, axis=0)[None]
    weight_grad = jnp.stack(weight_list, axis=0)
    return (mixed_out, hidden_grad, weight_grad)


def solution(mesh):
    placed = (
        P("dp", "expert", None, None),
        P("expert", None, None),
        P("dp", "expert"),
        P("dp", None),
        P("dp", None),
        P("dp", "expert", None),
        P("dp", "expert"),
    )

    def body(*shards):
        width = shards[1].shape[2]
        chips = mesh.shape["expert"] // CORES
        fits = mesh.shape["dp"] == 4 and chips == 4 and width % (chips * LANES) == 0
        return planned_body(*shards) if fits else general_body(*shards)

    return jax.shard_map(
        body,
        mesh=mesh,
        in_specs=placed,
        out_specs=(P("dp", "expert"), P("dp", "expert", None, None), P("expert", "dp", None)),
        check_vma=False,
    )
```

```python
import jax
import jax.numpy as jnp
from jax import lax
from jax.experimental import pallas as pl
from jax.experimental.pallas import tpu as pltpu
from jax.sharding import PartitionSpec as P

EXPERTS = 16
TILE = 128
LANES = 128
CORES = 2
EXTRA_ROWS = 16
MIB = 1024 * 1024


def swapped(shard, axis, bit):
    return lax.ppermute(shard, axis, [(i, i ^ 1 << bit) for i in range(lax.axis_size(axis))])


def across_dp(shard, mask):
    return lax.ppermute(shard, "dp", [(i, i ^ mask) for i in range(lax.axis_size("dp"))])


def across_cores(shard):
    return swapped(shard, "expert", 0)


def z_lines():
    size = lax.axis_size("expert")
    return [list(range(core, size, CORES)) for core in range(CORES)]


def joined(*values):
    return lax.optimization_barrier(values)


def dot(lhs, rhs, lhs_dim, rhs_dim):
    return lax.dot_general(
        lhs, rhs, (((lhs_dim,), (rhs_dim,)), ((), ())), preferred_element_type=jnp.float32
    )


def hot_rows(token_row, gate_row, tokens):
    slots = token_row.shape[1]
    token_index = lax.broadcasted_iota(jnp.int32, (tokens, slots), 0)
    spread = jnp.broadcast_to(gate_row, (tokens, slots))
    return jnp.where(token_index == token_row, spread, 0.0).astype(jnp.bfloat16)


def in_hbm(array):
    return pltpu.with_memory_space_constraint(array, pltpu.HBM)


def whole(shape):
    return pl.BlockSpec(shape, lambda *_: (0,) * len(shape))


def call(kernel, scalars, grid, in_specs, out_specs, out_shape, scratch, operands, vmem):
    return pl.pallas_call(
        kernel,
        grid_spec=pltpu.PrefetchScalarGridSpec(
            num_scalar_prefetch=1,
            grid=grid,
            in_specs=in_specs,
            out_specs=out_specs,
            scratch_shapes=scratch,
        ),
        out_shape=out_shape,
        compiler_params=pltpu.CompilerParams(
            dimension_semantics=("arbitrary",) * len(grid), vmem_limit_bytes=vmem
        ),
    )(scalars, *operands)


def expert_sums(where, token_rows, row_gate, hidden_rows, weight, tokens):
    local_count, slots, width_in = hidden_rows.shape
    chips = lax.axis_size("expert") // CORES
    cols = weight.shape[2] // chips
    half = cols // CORES

    def kernel(where, token_ref, gate_ref, hidden_ref, weight_ref, keep_ref, send_ref, by_token, turned):
        @pl.when(pl.program_id(0) == 0)
        def _():
            for local in range(local_count):
                hot = hot_rows(token_ref[local], gate_ref[local], tokens)
                made = dot(hot, hidden_ref[local], 1, 0).astype(jnp.bfloat16)
                by_token[:, local * width_in : (local + 1) * width_in] = made

        stacked = weight_ref[...].reshape(local_count * width_in, cols)
        turned[...] = dot(by_token[...], stacked, 1, 0).astype(jnp.bfloat16).T
        keep_ref[0] = turned[pl.ds(pl.multiple_of(where[1] * half, half), half), :]
        send_ref[0] = turned[pl.ds(pl.multiple_of((1 - where[1]) * half, half), half), :]

    shape = jax.ShapeDtypeStruct((chips, half, tokens), jnp.bfloat16)
    out_spec = pl.BlockSpec((1, half, tokens), lambda k, where: (k, 0, 0))
    return call(
        kernel,
        where,
        (chips,),
        [
            whole((local_count, 1, slots)),
            whole((local_count, 1, slots)),
            whole(hidden_rows.shape),
            pl.BlockSpec((local_count, width_in, cols), lambda k, where: (0, 0, k)),
        ],
        (out_spec, out_spec),
        (shape, shape),
        [
            pltpu.VMEM((tokens, local_count * width_in), jnp.bfloat16),
            pltpu.VMEM((cols, tokens), jnp.bfloat16),
        ],
        (token_rows[:, None], row_gate[:, None], hidden_rows, in_hbm(weight)),
        32 * MIB,
    )


def resident(kernel, scalars, operands, out_shapes, scratch=(), distant=(), passed=None):
    held = [pltpu.with_memory_space_constraint(array, pltpu.VMEM) for array in operands]
    in_vmem, anywhere = pl.BlockSpec(memory_space=pltpu.VMEM), pl.BlockSpec(memory_space=pl.ANY)
    far_off = [in_hbm(array) for array in distant] + ([] if passed is None else [passed])
    return pl.pallas_call(
        kernel,
        in_specs=[pl.BlockSpec(memory_space=pltpu.SMEM)] + [in_vmem] * len(held) + [anywhere] * len(far_off),
        out_specs=[anywhere if isinstance(shape, jax.ShapeDtypeStruct) else in_vmem for shape in out_shapes],
        out_shape=out_shapes,
        scratch_shapes=list(scratch),
        input_output_aliases={} if passed is None else {len(held) + len(far_off): 0},
        compiler_params=pltpu.CompilerParams(vmem_limit_bytes=20 * MIB),
    )(scalars, *held, *far_off)


def shares_by_token(where, payloads, slots, tokens):
    local_count, _, share = payloads[0].shape
    groups = len(payloads)

    def kernel(where, *refs):
        sources, (out_ref, held, sem) = refs[:groups], refs[groups:]
        loads = [pltpu.make_async_copy(ref, held.at[i], sem.at[i]) for i, ref in enumerate(sources)]
        for load in loads:
            load.start()

        def row(group, local, first):
            wide = [held[group, local, slots + first + i : slots + first + i + 1, :] for i in range(2)]
            return jnp.concatenate(wide, axis=1)[:, :slots].astype(jnp.float32)

        for group in range(groups):
            loads[group].wait()
            for local in range(local_count):
                token = (row(group, local, 0) * 2.0 + row(group, local, 2)).astype(jnp.int32)
                hot = hot_rows(token, row(group, local, 4), tokens)
                by_token = dot(hot, held[group, local, :slots, :], 1, 0).astype(jnp.bfloat16)
                out_ref[local * share : (local + 1) * share, group * tokens : (group + 1) * tokens] = by_token.T

    shape = (local_count * share, groups * tokens)
    scratch = [pltpu.VMEM((groups, *payloads[0].shape), jnp.bfloat16), pltpu.SemaphoreType.DMA((groups,))]
    return resident(kernel, where, [], [pltpu.VMEM(shape, jnp.bfloat16)], scratch, payloads)[0]


def blocks_of(where, gathered, steps, part, parts):
    devices, rows, tokens = gathered.shape
    rows //= parts

    def kernel(where, gathered_ref, out_ref, sem):
        copies = []
        for place, step in enumerate(steps):
            chip = lax.rem(where[0] + step, devices // CORES)
            source = gathered_ref.at[chip * CORES + where[1], pl.ds(part * rows, rows)]
            copies.append(pltpu.make_async_copy(source, out_ref.at[place], sem.at[place]))
        for copy in copies:
            copy.start()
        for copy in copies:
            copy.wait()

    return pl.pallas_call(
        kernel,
        in_specs=[pl.BlockSpec(memory_space=pltpu.SMEM), pl.BlockSpec(memory_space=pl.ANY)],
        out_specs=pl.BlockSpec(memory_space=pltpu.VMEM),
        out_shape=pltpu.VMEM((len(steps), rows, tokens), gathered.dtype),
        scratch_shapes=[pltpu.SemaphoreType.DMA((len(steps),))],
    )(where, in_hbm(gathered))


def hidden_grads(where, token_rows, row_gate, group_cot, weight):
    local_count, width_in, width = weight.shape
    slots = token_rows.shape[1]
    tokens = group_cot.shape[1]
    depth = width_in // 2

    def kernel(where, token_ref, gate_ref, cot_ref, weight_ref, out_ref):
        local = pl.program_id(0)
        sums = dot(weight_ref[0], cot_ref[...], 1, 0).astype(jnp.bfloat16)
        hot = hot_rows(token_ref[local], gate_ref[local], tokens)
        out_ref[0] = dot(hot, sums, 0, 1).astype(jnp.bfloat16)

    return call(
        kernel,
        where,
        (local_count, width_in // depth),
        [whole((local_count, 1, slots))] * 2
        + [whole(group_cot.shape)]
        + [pl.BlockSpec((1, depth, width), lambda e, h, where: (e, h, 0))],
        pl.BlockSpec((1, slots, depth), lambda e, h, where: (e, 0, h)),
        jax.ShapeDtypeStruct((local_count, slots, width_in), jnp.bfloat16),
        [],
        (token_rows[:, None], row_gate[:, None], in_hbm(group_cot), in_hbm(weight)),
        28 * MIB,
    )


def group_products(where, shares, groups, refs, chip):
    total, at = None, 0
    for place, sides in groups:
        loaded = []
        for pieces in sides:
            loaded.append([ref[first + chip] for ref, (_, first) in zip(refs[at:], pieces)])
            at += len(pieces)
        mine, other = [jnp.concatenate(pieces, axis=0) if len(pieces) > 1 else pieces[0] for pieces in loaded]
        low = jnp.where(where[1] == 0, mine, other)
        high = jnp.where(where[1] == 0, other, mine)
        block = jnp.concatenate([low, high], axis=0)
        tokens = block.shape[1]
        product = dot(shares[:, place * tokens : (place + 1) * tokens], block, 1, 1)
        total = product if total is None else total + product
    return total


def halves(parts):
    return [(part, 0) for part in parts]


def weight_cols(
    where, first, count, shares, groups, local_count, width, gathered=None, so_far=None, passed=None, keep=False
):
    chips = lax.axis_size("expert") // CORES
    cols = width // chips
    share = shares.shape[0] // local_count
    flat = [array for _, sides in groups for pieces in sides for array, _ in pieces]
    tokens = flat[0].shape[-1]
    kept = (count, shares.shape[0], cols)
    distant = [array for array in (gathered, so_far) if array is not None]

    def kernel(where, shares_ref, *refs):
        refs = list(refs)
        pieces = [refs.pop(0) for _ in flat]
        source = refs.pop(0) if gathered is not None else None
        added = refs.pop(0) if so_far is not None else None
        if passed is not None:
            refs.pop(0)
        out_ref, total_ref, sem = refs[:3]
        refs = refs[3:]
        place = [lax.rem(where[0] + first + chip, chips) for chip in range(count)]
        loads, stores = [], []
        for chip in range(count):
            loads.append([])
            if source is not None:
                block = source.at[pl.ds(place[chip] * CORES, CORES)]
                loads[chip].append(pltpu.make_async_copy(block, refs[0].at[chip], refs[1].at[chip]))
            if added is not None:
                loads[chip].append(pltpu.make_async_copy(added.at[chip], refs[-2].at[chip], refs[-1].at[chip]))
            for load in loads[chip]:
                load.start()
        for chip in range(count):
            total = group_products(where, shares_ref, groups, pieces, chip)
            for load in loads[chip]:
                load.wait()
            if source is not None:
                total = total + dot(shares_ref[:, :tokens], refs[0][chip].reshape(cols, tokens), 1, 1)
            if added is not None:
                total = total + refs[-2][chip].astype(jnp.float32)
            if keep:
                total_ref[chip] = total.astype(jnp.bfloat16)
                target = out_ref.at[chip]
            else:
                for local in range(local_count):
                    total_ref[chip, local] = total[local * share : (local + 1) * share]
                target = out_ref.at[:, :, pl.ds(pl.multiple_of(place[chip] * cols, LANES), cols)]
            stores.append(pltpu.make_async_copy(total_ref.at[chip], target, sem.at[chip]))
            stores[-1].start()
        for store in stores:
            store.wait()

    if keep:
        scratch = [pltpu.VMEM(kept, jnp.bfloat16)]
        out_shape = jax.ShapeDtypeStruct(kept, jnp.bfloat16)
    else:
        scratch = [pltpu.VMEM((count, local_count, share, cols), jnp.float32)]
        out_shape = jax.ShapeDtypeStruct((local_count, share, width), jnp.float32)
    scratch.append(pltpu.SemaphoreType.DMA((count,)))
    if gathered is not None:
        scratch += [pltpu.VMEM((count, CORES, cols // CORES, tokens), jnp.bfloat16), pltpu.SemaphoreType.DMA((count,))]
    if so_far is not None:
        scratch += [pltpu.VMEM(kept, jnp.bfloat16), pltpu.SemaphoreType.DMA((count,))]
    return resident(kernel, where, [shares, *flat], [out_shape], scratch, distant, passed)[0]


def planned_body(hidden, down_weight, cotangent, expert_ids, gate_weights, row_token, tile_count):
    local_count, width_in, width = down_weight.shape
    tokens = cotangent.shape[0]
    slots = hidden.shape[2]
    groups = lax.axis_size("dp")
    chips = lax.axis_size("expert") // CORES
    share = width_in // groups
    group = lax.axis_index("dp")
    expert_place = lax.axis_index("expert")
    chip = expert_place // CORES
    core = expert_place % CORES
    where = jnp.stack([chip, core])

    own = cotangent.T
    middle = own.shape[0] // 2
    gathered = lax.all_gather(own, "expert")
    x_own, y_own = across_dp(own, 1), across_dp(own, 2)

    slot_index = jnp.arange(slots, dtype=jnp.int32)
    token_index = jnp.arange(tokens, dtype=jnp.int32)
    live = (row_token[0] >= 0) & (slot_index[None] < tile_count[0][:, None] * TILE)
    token_rows = jnp.where(live, row_token[0], -1)
    experts = expert_place * local_count + jnp.arange(local_count, dtype=jnp.int32)
    named = expert_ids[None] == experts[:, None, None]
    token_gate = jnp.sum(jnp.where(named, gate_weights[None].astype(jnp.float32), 0.0), axis=2)
    at_token = token_rows[:, :, None] == token_index[None, None, :]
    row_gate = jnp.sum(jnp.where(at_token, token_gate[:, None, :], 0.0), axis=2)

    def as_rows(values):
        padded = jnp.pad(values.astype(jnp.bfloat16), ((0, 0), (0, 2 * share - slots)))
        return padded.reshape(local_count, 2, share)

    extra = jnp.concatenate(
        [as_rows(token_rows >> 1), as_rows(token_rows & 1), as_rows(row_gate)], axis=1
    )
    extra = jnp.pad(extra, ((0, 0), (0, EXTRA_ROWS - extra.shape[1]), (0, 0)))
    payloads = []
    for mask in range(groups):
        rows = lax.dynamic_slice_in_dim(hidden[0], (group ^ mask) * share, share, 2)
        payloads.append(jnp.concatenate([rows, extra], axis=1))
    x_own, y_own, token_rows, row_gate, *payloads = joined(
        x_own, y_own, token_rows, row_gate, *payloads
    )

    payloads = [across_dp(payload, mask) if mask else payload for mask, payload in enumerate(payloads)]
    far_own = [across_dp(x_own[:middle], 2), across_dp(y_own[middle:], 1)]
    keep, send = expert_sums(where, token_rows, row_gate, hidden[0], down_weight, tokens)
    x_own, y_own, keep, send, *sent = joined(x_own, y_own, keep, send, *far_own, *payloads)
    far_own, payloads = sent[:2], sent[2:]

    steps = list(range(1, chips))
    near = [blocks_of(where, gathered, steps, part, 2) for part in range(2)]
    x_near, y_near = [None, None], [None, None]
    x_near[0], y_near[1] = across_dp(near[0], 1), across_dp(near[1], 2)
    x_near[1], y_near[0] = across_dp(near[1], 1), across_dp(near[0], 2)

    from_other = across_cores(send)
    from_other, *payloads = joined(from_other, *payloads)
    own_far = jnp.stack([x_own, y_own, jnp.concatenate(far_own, axis=0)])
    own_far_other = across_cores(own_far)
    sums = (keep.astype(jnp.float32) + from_other.astype(jnp.float32)).astype(jnp.bfloat16)
    mixed = lax.psum_scatter(sums, "expert", scatter_dimension=0, axis_index_groups=z_lines())
    shares = shares_by_token(where, payloads, slots, tokens)
    hidden_grad = hidden_grads(where, token_rows, row_gate, gathered.reshape(width, tokens), down_weight)
    rest = (local_count, width)
    own_groups = [(place + 1, ([(own_far, place)], [(own_far_other, place)])) for place in range(groups - 1)]
    weight_grad = weight_cols(where, 0, 1, shares, own_groups, *rest, gathered)
    hidden_grad, shares, weight_grad, _, *sent = joined(
        hidden_grad, shares, weight_grad, sums, *x_near, *y_near
    )
    x_near, y_near = sent[:2], sent[2:]

    far = [across_dp(x_near[0], 2), across_dp(y_near[1], 1)]
    x_other = [across_cores(part) for part in x_near]
    y_other = [across_cores(part) for part in y_near]
    two = [(place, tuple(map(halves, pair))) for place, pair in ((1, (x_near, x_other)), (2, (y_near, y_other)))]
    so_far = weight_cols(where, 1, chips - 1, shares, two, *rest, gathered, keep=True)
    so_far, mixed, *far = joined(so_far, mixed, *far)
    last = [(groups - 1, (halves(far), halves([across_cores(part) for part in far])))]
    weight_grad = weight_cols(where, 1, chips - 1, shares, last, *rest, None, so_far, weight_grad)
    return (mixed.T, hidden_grad[None], weight_grad)


def tile_products(rows_in, weight_mat, count, contract_dim):
    rows_cap = rows_in.shape[0]
    width_out = weight_mat.shape[1 - contract_dim]

    def one_tile(tile_index, outputs):
        block = lax.dynamic_slice_in_dim(rows_in, tile_index * TILE, TILE, 0)
        product = lax.dot_general(
            block,
            weight_mat,
            (((1,), (contract_dim,)), ((), ())),
            preferred_element_type=jnp.float32,
        )
        return lax.dynamic_update_slice_in_dim(
            outputs, product.astype(jnp.bfloat16), tile_index * TILE, 0
        )

    return lax.fori_loop(0, count, one_tile, jnp.zeros((rows_cap, width_out), jnp.bfloat16))


def general_body(hidden, down_weight, cotangent, expert_ids, gate_weights, row_token, tile_count):
    local_count = down_weight.shape[0]
    group_size = cotangent.shape[0]
    expert_index = jnp.arange(EXPERTS, dtype=jnp.int32)
    named_cols = expert_ids[:, :, None] == expert_index[None, None, :]
    gate_cols = jnp.sum(
        jnp.where(named_cols, gate_weights[:, :, None].astype(jnp.float32), 0.0), axis=1
    ).astype(jnp.bfloat16)
    group_cot = lax.all_gather(cotangent, "expert", axis=1, tiled=True)
    width = group_cot.shape[1]
    first_expert = lax.axis_index("expert") * local_count
    slot_index = jnp.arange(hidden.shape[2], dtype=jnp.int32)
    share_rows = down_weight.shape[1] // lax.axis_size("dp")
    partial_value = jnp.zeros((group_size, width), jnp.float32)
    grad_list = []
    weight_list = []
    for local in range(local_count):
        token_rows = row_token[0, local]
        count = tile_count[0, local]
        live_rows = (token_rows >= 0) & (slot_index < count * TILE)
        safe_rows = jnp.where(live_rows, token_rows, 0)
        column = lax.dynamic_index_in_dim(gate_cols, first_expert + local, 1, keepdims=False)
        row_gate = jnp.where(live_rows, column[safe_rows].astype(jnp.float32), 0.0)
        target = jnp.where(live_rows, token_rows, group_size)
        hidden_rows = hidden[0, local]
        weight_mat = down_weight[local]
        out_rows = tile_products(hidden_rows, weight_mat, count, 0)
        partial_value = partial_value.at[target].add(
            row_gate[:, None] * out_rows.astype(jnp.float32), mode="drop"
        )
        routed = (row_gate[:, None] * group_cot[safe_rows].astype(jnp.float32)).astype(jnp.bfloat16)
        grad_list.append(tile_products(routed, weight_mat, count, 1))

        def weight_rows(start, rows_count, hidden_rows=hidden_rows, routed_rows=routed):
            return lax.dot_general(
                hidden_rows,
                routed_rows,
                (((0,), (0,)), ((), ())),
                preferred_element_type=jnp.float32,
            )

        weight_list.append(
            lax.psum_scatter(
                weight_rows(jnp.int32(0), share_rows * lax.axis_size("dp")).astype(jnp.bfloat16),
                "dp",
                scatter_dimension=0,
                tiled=True,
            ).astype(jnp.float32)
        )
    merged = partial_value
    top_bit = lax.axis_size("expert").bit_length() - 1
    axis_index = lax.axis_index("expert")
    for bit_index in reversed(range(top_bit)):
        half_cols = merged.shape[1] // 2
        lower_half = merged[:, :half_cols]
        upper_half = merged[:, half_cols:]
        high_side = axis_index // 2**bit_index % 2 == 1
        sending = jnp.where(high_side, lower_half, upper_half)
        keeping = jnp.where(high_side, upper_half, lower_half)
        merged = keeping + swapped(sending.astype(jnp.bfloat16), "expert", bit_index).astype(
            sending.dtype
        )
    mixed_out = merged.astype(jnp.bfloat16)
    hidden_grad = jnp.stack(grad_list, axis=0)[None]
    weight_grad = jnp.stack(weight_list, axis=0)
    return (mixed_out, hidden_grad, weight_grad)


def solution(mesh):
    placed = (
        P("dp", "expert", None, None),
        P("expert", None, None),
        P("dp", "expert"),
        P("dp", None),
        P("dp", None),
        P("dp", "expert", None),
        P("dp", "expert"),
    )

    def body(*shards):
        width = shards[1].shape[2]
        chips = mesh.shape["expert"] // CORES
        fits = mesh.shape["dp"] == 4 and chips > 2 and width % (chips * LANES) == 0
        return planned_body(*shards) if fits else general_body(*shards)

    return jax.shard_map(
        body,
        mesh=mesh,
        in_specs=placed,
        out_specs=(P("dp", "expert"), P("dp", "expert", None, None), P("expert", "dp", None)),
        check_vma=False,
    )
```

```python
import jax
import jax.numpy as jnp
from jax import lax
from jax.experimental import pallas as pl
from jax.experimental.pallas import tpu as pltpu
from jax.sharding import PartitionSpec as P

EXPERTS = 16
TILE = 128
LANES = 128
CORES = 2
EXTRA_ROWS = 16
MIB = 1024 * 1024


def swapped(shard, axis, bit):
    return lax.ppermute(shard, axis, [(i, i ^ 1 << bit) for i in range(lax.axis_size(axis))])


def across_dp(shard, mask):
    return lax.ppermute(shard, "dp", [(i, i ^ mask) for i in range(lax.axis_size("dp"))])


def across_cores(shard):
    return swapped(shard, "expert", 0)


def z_lines():
    size = lax.axis_size("expert")
    return [list(range(core, size, CORES)) for core in range(CORES)]


def joined(*values):
    return lax.optimization_barrier(values)


def dot(lhs, rhs, lhs_dim, rhs_dim):
    return lax.dot_general(
        lhs, rhs, (((lhs_dim,), (rhs_dim,)), ((), ())), preferred_element_type=jnp.float32
    )


def hot_rows(token_row, gate_row, tokens):
    slots = token_row.shape[1]
    token_index = lax.broadcasted_iota(jnp.int32, (tokens, slots), 0)
    spread = jnp.broadcast_to(gate_row, (tokens, slots))
    return jnp.where(token_index == token_row, spread, 0.0).astype(jnp.bfloat16)


def in_hbm(array):
    return pltpu.with_memory_space_constraint(array, pltpu.HBM)


def whole(shape):
    return pl.BlockSpec(shape, lambda *_: (0,) * len(shape))


def call(kernel, scalars, grid, in_specs, out_specs, out_shape, scratch, operands, vmem):
    return pl.pallas_call(
        kernel,
        grid_spec=pltpu.PrefetchScalarGridSpec(
            num_scalar_prefetch=1,
            grid=grid,
            in_specs=in_specs,
            out_specs=out_specs,
            scratch_shapes=scratch,
        ),
        out_shape=out_shape,
        compiler_params=pltpu.CompilerParams(
            dimension_semantics=("arbitrary",) * len(grid), vmem_limit_bytes=vmem
        ),
    )(scalars, *operands)


def expert_sums(where, token_rows, row_gate, hidden_rows, weight, tokens):
    local_count, slots, width_in = hidden_rows.shape
    chips = lax.axis_size("expert") // CORES
    cols = weight.shape[2] // chips
    half = cols // CORES

    def kernel(where, token_ref, gate_ref, hidden_ref, weight_ref, keep_ref, send_ref, by_token, turned):
        @pl.when(pl.program_id(0) == 0)
        def _():
            for local in range(local_count):
                hot = hot_rows(token_ref[local], gate_ref[local], tokens)
                made = dot(hot, hidden_ref[local], 1, 0).astype(jnp.bfloat16)
                by_token[:, local * width_in : (local + 1) * width_in] = made

        stacked = weight_ref[...].reshape(local_count * width_in, cols)
        turned[...] = dot(by_token[...], stacked, 1, 0).astype(jnp.bfloat16).T
        keep_ref[0] = turned[pl.ds(pl.multiple_of(where[1] * half, half), half), :]
        send_ref[0] = turned[pl.ds(pl.multiple_of((1 - where[1]) * half, half), half), :]

    shape = jax.ShapeDtypeStruct((chips, half, tokens), jnp.bfloat16)
    out_spec = pl.BlockSpec((1, half, tokens), lambda k, where: (k, 0, 0))
    return call(
        kernel,
        where,
        (chips,),
        [
            whole((local_count, 1, slots)),
            whole((local_count, 1, slots)),
            whole(hidden_rows.shape),
            pl.BlockSpec((local_count, width_in, cols), lambda k, where: (0, 0, k)),
        ],
        (out_spec, out_spec),
        (shape, shape),
        [
            pltpu.VMEM((tokens, local_count * width_in), jnp.bfloat16),
            pltpu.VMEM((cols, tokens), jnp.bfloat16),
        ],
        (token_rows[:, None], row_gate[:, None], hidden_rows, in_hbm(weight)),
        32 * MIB,
    )


def resident(kernel, scalars, operands, out_shapes, scratch=(), distant=(), passed=None):
    held = [pltpu.with_memory_space_constraint(array, pltpu.VMEM) for array in operands]
    in_vmem, anywhere = pl.BlockSpec(memory_space=pltpu.VMEM), pl.BlockSpec(memory_space=pl.ANY)
    far_off = [in_hbm(array) for array in distant] + ([] if passed is None else [passed])
    return pl.pallas_call(
        kernel,
        in_specs=[pl.BlockSpec(memory_space=pltpu.SMEM)] + [in_vmem] * len(held) + [anywhere] * len(far_off),
        out_specs=[anywhere if isinstance(shape, jax.ShapeDtypeStruct) else in_vmem for shape in out_shapes],
        out_shape=out_shapes,
        scratch_shapes=list(scratch),
        input_output_aliases={} if passed is None else {len(held) + len(far_off): 0},
        compiler_params=pltpu.CompilerParams(vmem_limit_bytes=20 * MIB),
    )(scalars, *held, *far_off)


def shares_by_token(where, payloads, slots, tokens):
    local_count, _, share = payloads[0].shape
    groups = len(payloads)

    def kernel(where, *refs):
        sources, (out_ref, held, sem) = refs[:groups], refs[groups:]
        loads = [pltpu.make_async_copy(ref, held.at[i], sem.at[i]) for i, ref in enumerate(sources)]
        for load in loads:
            load.start()

        def row(group, local, first):
            wide = [held[group, local, slots + first + i : slots + first + i + 1, :] for i in range(2)]
            return jnp.concatenate(wide, axis=1)[:, :slots].astype(jnp.float32)

        for group in range(groups):
            loads[group].wait()
            for local in range(local_count):
                token = (row(group, local, 0) * 2.0 + row(group, local, 2)).astype(jnp.int32)
                hot = hot_rows(token, row(group, local, 4), tokens)
                by_token = dot(hot, held[group, local, :slots, :], 1, 0).astype(jnp.bfloat16)
                out_ref[local * share : (local + 1) * share, group * tokens : (group + 1) * tokens] = by_token.T

    shape = (local_count * share, groups * tokens)
    scratch = [pltpu.VMEM((groups, *payloads[0].shape), jnp.bfloat16), pltpu.SemaphoreType.DMA((groups,))]
    return resident(kernel, where, [], [pltpu.VMEM(shape, jnp.bfloat16)], scratch, payloads)[0]


def blocks_of(where, gathered, steps, parts):
    devices, rows, tokens = gathered.shape
    part = rows // parts

    def kernel(where, gathered_ref, *refs):
        sem = refs[-1]
        copies = []
        for place, step in enumerate(steps):
            chip = lax.rem(where[0] + step, devices // CORES)
            for index, out_ref in enumerate(refs[:-1]):
                source = gathered_ref.at[chip * CORES + where[1], pl.ds(index * part, part)]
                copies.append(pltpu.make_async_copy(source, out_ref.at[place], sem.at[len(copies)]))
        for copy in copies:
            copy.start()
        for copy in copies:
            copy.wait()

    return pl.pallas_call(
        kernel,
        in_specs=[pl.BlockSpec(memory_space=pltpu.SMEM), pl.BlockSpec(memory_space=pl.ANY)],
        out_specs=[pl.BlockSpec(memory_space=pltpu.VMEM)] * parts,
        out_shape=[pltpu.VMEM((len(steps), part, tokens), gathered.dtype)] * parts,
        scratch_shapes=[pltpu.SemaphoreType.DMA((len(steps) * parts,))],
    )(where, in_hbm(gathered))


def hidden_grads(where, token_rows, row_gate, group_cot, weight):
    local_count, width_in, width = weight.shape
    slots = token_rows.shape[1]
    tokens = group_cot.shape[1]
    depth = width_in // 2

    def kernel(where, token_ref, gate_ref, cot_ref, weight_ref, out_ref):
        local = pl.program_id(0)
        sums = dot(weight_ref[0], cot_ref[...], 1, 0).astype(jnp.bfloat16)
        hot = hot_rows(token_ref[local], gate_ref[local], tokens)
        out_ref[0] = dot(hot, sums, 0, 1).astype(jnp.bfloat16)

    return call(
        kernel,
        where,
        (local_count, width_in // depth),
        [whole((local_count, 1, slots))] * 2
        + [whole(group_cot.shape)]
        + [pl.BlockSpec((1, depth, width), lambda e, h, where: (e, h, 0))],
        pl.BlockSpec((1, slots, depth), lambda e, h, where: (e, 0, h)),
        jax.ShapeDtypeStruct((local_count, slots, width_in), jnp.bfloat16),
        [],
        (token_rows[:, None], row_gate[:, None], in_hbm(group_cot), in_hbm(weight)),
        28 * MIB,
    )


def group_products(where, shares, groups, refs, chip):
    total, at = None, 0
    for place, sides in groups:
        loaded = []
        for pieces in sides:
            loaded.append([ref[first + chip] for ref, (_, first) in zip(refs[at:], pieces)])
            at += len(pieces)
        mine, other = [jnp.concatenate(pieces, axis=0) if len(pieces) > 1 else pieces[0] for pieces in loaded]
        low = jnp.where(where[1] == 0, mine, other)
        high = jnp.where(where[1] == 0, other, mine)
        block = jnp.concatenate([low, high], axis=0)
        tokens = block.shape[1]
        product = dot(shares[:, place * tokens : (place + 1) * tokens], block, 1, 1)
        total = product if total is None else total + product
    return total


def halves(parts):
    return [(part, 0) for part in parts]


def weight_cols(
    where, first, count, shares, groups, local_count, width, gathered=None, so_far=None, passed=None, keep=False
):
    chips = lax.axis_size("expert") // CORES
    cols = width // chips
    share = shares.shape[0] // local_count
    flat = [array for _, sides in groups for pieces in sides for array, _ in pieces]
    tokens = flat[0].shape[-1]
    kept = (count, shares.shape[0], cols)
    distant = [array for array in (gathered, so_far) if array is not None]

    def kernel(where, shares_ref, *refs):
        refs = list(refs)
        pieces = [refs.pop(0) for _ in flat]
        source = refs.pop(0) if gathered is not None else None
        added = refs.pop(0) if so_far is not None else None
        if passed is not None:
            refs.pop(0)
        out_ref, total_ref, sem = refs[:3]
        refs = refs[3:]
        place = [lax.rem(where[0] + first + chip, chips) for chip in range(count)]
        loads, stores = [], []
        for chip in range(count):
            loads.append([])
            if source is not None:
                block = source.at[pl.ds(place[chip] * CORES, CORES)]
                loads[chip].append(pltpu.make_async_copy(block, refs[0].at[chip], refs[1].at[chip]))
            if added is not None:
                loads[chip].append(pltpu.make_async_copy(added.at[first - 1 + chip], refs[-2].at[chip], refs[-1].at[chip]))
            for load in loads[chip]:
                load.start()
        for chip in range(count):
            total = group_products(where, shares_ref, groups, pieces, chip)
            for load in loads[chip]:
                load.wait()
            if source is not None:
                total = total + dot(shares_ref[:, :tokens], refs[0][chip].reshape(cols, tokens), 1, 1)
            if added is not None:
                total = total + refs[-2][chip].astype(jnp.float32)
            if keep:
                total_ref[chip] = total.astype(jnp.bfloat16)
                target = out_ref.at[chip]
            else:
                for local in range(local_count):
                    total_ref[chip, local] = total[local * share : (local + 1) * share]
                target = out_ref.at[:, :, pl.ds(pl.multiple_of(place[chip] * cols, LANES), cols)]
            stores.append(pltpu.make_async_copy(total_ref.at[chip], target, sem.at[chip]))
            stores[-1].start()
        for store in stores:
            store.wait()

    if keep:
        scratch = [pltpu.VMEM(kept, jnp.bfloat16)]
        out_shape = jax.ShapeDtypeStruct(kept, jnp.bfloat16)
    else:
        scratch = [pltpu.VMEM((count, local_count, share, cols), jnp.float32)]
        out_shape = jax.ShapeDtypeStruct((local_count, share, width), jnp.float32)
    scratch.append(pltpu.SemaphoreType.DMA((count,)))
    if gathered is not None:
        scratch += [pltpu.VMEM((count, CORES, cols // CORES, tokens), jnp.bfloat16), pltpu.SemaphoreType.DMA((count,))]
    if so_far is not None:
        scratch += [pltpu.VMEM(kept, jnp.bfloat16), pltpu.SemaphoreType.DMA((count,))]
    return resident(kernel, where, [shares, *flat], [out_shape], scratch, distant, passed)[0]


def planned_body(hidden, down_weight, cotangent, expert_ids, gate_weights, row_token, tile_count):
    local_count, width_in, width = down_weight.shape
    tokens = cotangent.shape[0]
    slots = hidden.shape[2]
    groups = lax.axis_size("dp")
    chips = lax.axis_size("expert") // CORES
    share = width_in // groups
    group = lax.axis_index("dp")
    expert_place = lax.axis_index("expert")
    chip = expert_place // CORES
    core = expert_place % CORES
    where = jnp.stack([chip, core])

    own = cotangent.T
    middle = own.shape[0] // 2
    gathered = lax.all_gather(own, "expert")
    x_own, y_own = across_dp(own, 1), across_dp(own, 2)

    slot_index = jnp.arange(slots, dtype=jnp.int32)
    token_index = jnp.arange(tokens, dtype=jnp.int32)
    live = (row_token[0] >= 0) & (slot_index[None] < tile_count[0][:, None] * TILE)
    token_rows = jnp.where(live, row_token[0], -1)
    experts = expert_place * local_count + jnp.arange(local_count, dtype=jnp.int32)
    named = expert_ids[None] == experts[:, None, None]
    token_gate = jnp.sum(jnp.where(named, gate_weights[None].astype(jnp.float32), 0.0), axis=2)
    at_token = token_rows[:, :, None] == token_index[None, None, :]
    row_gate = jnp.sum(jnp.where(at_token, token_gate[:, None, :], 0.0), axis=2)

    def as_rows(values):
        padded = jnp.pad(values.astype(jnp.bfloat16), ((0, 0), (0, 2 * share - slots)))
        return padded.reshape(local_count, 2, share)

    extra = jnp.concatenate(
        [as_rows(token_rows >> 1), as_rows(token_rows & 1), as_rows(row_gate)], axis=1
    )
    extra = jnp.pad(extra, ((0, 0), (0, EXTRA_ROWS - extra.shape[1]), (0, 0)))
    payloads = []
    for mask in range(groups):
        rows = lax.dynamic_slice_in_dim(hidden[0], (group ^ mask) * share, share, 2)
        payloads.append(jnp.concatenate([rows, extra], axis=1))
    x_own, y_own, token_rows, row_gate, *payloads = joined(
        x_own, y_own, token_rows, row_gate, *payloads
    )

    payloads = [across_dp(payload, mask) if mask else payload for mask, payload in enumerate(payloads)]
    far_own = [across_dp(x_own[:middle], 2), across_dp(y_own[middle:], 1)]
    keep, send = expert_sums(where, token_rows, row_gate, hidden[0], down_weight, tokens)
    x_own, y_own, keep, send, *sent = joined(x_own, y_own, keep, send, *far_own, *payloads)
    far_own, payloads = sent[:2], sent[2:]

    steps = list(range(1, chips))
    near = blocks_of(where, gathered, steps, 2)
    x_near, y_near = [None, None], [None, None]
    x_near[0], y_near[1] = across_dp(near[0], 1), across_dp(near[1], 2)
    x_near[1], y_near[0] = across_dp(near[1], 1), across_dp(near[0], 2)

    from_other = across_cores(send)
    own_far = jnp.stack([x_own, y_own, jnp.concatenate(far_own, axis=0)])
    from_other, own_far, *payloads = joined(from_other, own_far, *payloads)
    own_far_other = across_cores(own_far)
    sums = (keep.astype(jnp.float32) + from_other.astype(jnp.float32)).astype(jnp.bfloat16)
    mixed = lax.psum_scatter(sums, "expert", scatter_dimension=0, axis_index_groups=z_lines())
    shares = shares_by_token(where, payloads, slots, tokens)
    hidden_grad = hidden_grads(where, token_rows, row_gate, gathered.reshape(width, tokens), down_weight)
    rest = (local_count, width)
    own_groups = [(place + 1, ([(own_far, place)], [(own_far_other, place)])) for place in range(groups - 1)]
    weight_grad = weight_cols(where, 0, 1, shares, own_groups, *rest, gathered)
    hidden_grad, shares, weight_grad, _, *sent = joined(
        hidden_grad, shares, weight_grad, sums, *x_near, *y_near
    )
    x_near, y_near = sent[:2], sent[2:]

    early = chips - 2
    spans = [slice(0, early), slice(early, early + 1)]
    far = [[across_dp(x_near[0][span], 2), across_dp(y_near[1][span], 1)] for span in spans]
    x_other = [across_cores(part) for part in x_near]
    y_other = [across_cores(part) for part in y_near]
    two = [(place, tuple(map(halves, pair))) for place, pair in ((1, (x_near, x_other)), (2, (y_near, y_other)))]
    so_far = weight_cols(where, 1, chips - 1, shares, two, *rest, gathered, keep=True)
    for first, count, pieces in ((1, early, far[0]), (1 + early, 1, far[1])):
        if first == 1:
            so_far, *pieces = joined(so_far, *pieces)
        else:
            weight_grad, mixed, *pieces = joined(weight_grad, mixed, *pieces)
        last = [(groups - 1, (halves(pieces), halves([across_cores(part) for part in pieces])))]
        weight_grad = weight_cols(where, first, count, shares, last, *rest, None, so_far, weight_grad)
    return (mixed.T, hidden_grad[None], weight_grad)


def tile_products(rows_in, weight_mat, count, contract_dim):
    rows_cap = rows_in.shape[0]
    width_out = weight_mat.shape[1 - contract_dim]

    def one_tile(tile_index, outputs):
        block = lax.dynamic_slice_in_dim(rows_in, tile_index * TILE, TILE, 0)
        product = lax.dot_general(
            block,
            weight_mat,
            (((1,), (contract_dim,)), ((), ())),
            preferred_element_type=jnp.float32,
        )
        return lax.dynamic_update_slice_in_dim(
            outputs, product.astype(jnp.bfloat16), tile_index * TILE, 0
        )

    return lax.fori_loop(0, count, one_tile, jnp.zeros((rows_cap, width_out), jnp.bfloat16))


def general_body(hidden, down_weight, cotangent, expert_ids, gate_weights, row_token, tile_count):
    local_count = down_weight.shape[0]
    group_size = cotangent.shape[0]
    expert_index = jnp.arange(EXPERTS, dtype=jnp.int32)
    named_cols = expert_ids[:, :, None] == expert_index[None, None, :]
    gate_cols = jnp.sum(
        jnp.where(named_cols, gate_weights[:, :, None].astype(jnp.float32), 0.0), axis=1
    ).astype(jnp.bfloat16)
    group_cot = lax.all_gather(cotangent, "expert", axis=1, tiled=True)
    width = group_cot.shape[1]
    first_expert = lax.axis_index("expert") * local_count
    slot_index = jnp.arange(hidden.shape[2], dtype=jnp.int32)
    share_rows = down_weight.shape[1] // lax.axis_size("dp")
    partial_value = jnp.zeros((group_size, width), jnp.float32)
    grad_list = []
    weight_list = []
    for local in range(local_count):
        token_rows = row_token[0, local]
        count = tile_count[0, local]
        live_rows = (token_rows >= 0) & (slot_index < count * TILE)
        safe_rows = jnp.where(live_rows, token_rows, 0)
        column = lax.dynamic_index_in_dim(gate_cols, first_expert + local, 1, keepdims=False)
        row_gate = jnp.where(live_rows, column[safe_rows].astype(jnp.float32), 0.0)
        target = jnp.where(live_rows, token_rows, group_size)
        hidden_rows = hidden[0, local]
        weight_mat = down_weight[local]
        out_rows = tile_products(hidden_rows, weight_mat, count, 0)
        partial_value = partial_value.at[target].add(
            row_gate[:, None] * out_rows.astype(jnp.float32), mode="drop"
        )
        routed = (row_gate[:, None] * group_cot[safe_rows].astype(jnp.float32)).astype(jnp.bfloat16)
        grad_list.append(tile_products(routed, weight_mat, count, 1))

        def weight_rows(start, rows_count, hidden_rows=hidden_rows, routed_rows=routed):
            return lax.dot_general(
                hidden_rows,
                routed_rows,
                (((0,), (0,)), ((), ())),
                preferred_element_type=jnp.float32,
            )

        weight_list.append(
            lax.psum_scatter(
                weight_rows(jnp.int32(0), share_rows * lax.axis_size("dp")).astype(jnp.bfloat16),
                "dp",
                scatter_dimension=0,
                tiled=True,
            ).astype(jnp.float32)
        )
    merged = partial_value
    top_bit = lax.axis_size("expert").bit_length() - 1
    axis_index = lax.axis_index("expert")
    for bit_index in reversed(range(top_bit)):
        half_cols = merged.shape[1] // 2
        lower_half = merged[:, :half_cols]
        upper_half = merged[:, half_cols:]
        high_side = axis_index // 2**bit_index % 2 == 1
        sending = jnp.where(high_side, lower_half, upper_half)
        keeping = jnp.where(high_side, upper_half, lower_half)
        merged = keeping + swapped(sending.astype(jnp.bfloat16), "expert", bit_index).astype(
            sending.dtype
        )
    mixed_out = merged.astype(jnp.bfloat16)
    hidden_grad = jnp.stack(grad_list, axis=0)[None]
    weight_grad = jnp.stack(weight_list, axis=0)
    return (mixed_out, hidden_grad, weight_grad)


def solution(mesh):
    placed = (
        P("dp", "expert", None, None),
        P("expert", None, None),
        P("dp", "expert"),
        P("dp", None),
        P("dp", None),
        P("dp", "expert", None),
        P("dp", "expert"),
    )

    def body(*shards):
        width = shards[1].shape[2]
        chips = mesh.shape["expert"] // CORES
        fits = mesh.shape["dp"] == 4 and chips > 2 and width % (chips * LANES) == 0
        return planned_body(*shards) if fits else general_body(*shards)

    return jax.shard_map(
        body,
        mesh=mesh,
        in_specs=placed,
        out_specs=(P("dp", "expert"), P("dp", "expert", None, None), P("expert", "dp", None)),
        check_vma=False,
    )
```

```python
import jax
import jax.numpy as jnp
from jax import lax
from jax.experimental import pallas as pl
from jax.experimental.pallas import tpu as pltpu
from jax.sharding import PartitionSpec as P

EXPERTS = 16
TILE = 128
LANES = 128
CORES = 2
EXTRA_ROWS = 16
MIB = 1024 * 1024


def swapped(shard, axis, bit):
    return lax.ppermute(shard, axis, [(i, i ^ 1 << bit) for i in range(lax.axis_size(axis))])


def across_dp(shard, mask):
    return lax.ppermute(shard, "dp", [(i, i ^ mask) for i in range(lax.axis_size("dp"))])


def across_cores(shard):
    return swapped(shard, "expert", 0)


def along_z(shard, step, senders):
    pairs = [
        (CORES * z + core, CORES * (z + step) + core) for z in senders for core in range(CORES)
    ]
    return lax.ppermute(shard, "expert", pairs)


def joined(*values):
    return lax.optimization_barrier(values)


def dot(lhs, rhs, lhs_dim, rhs_dim):
    return lax.dot_general(
        lhs, rhs, (((lhs_dim,), (rhs_dim,)), ((), ())), preferred_element_type=jnp.float32
    )


def hot_rows(token_row, gate_row, tokens):
    slots = token_row.shape[1]
    token_index = lax.broadcasted_iota(jnp.int32, (tokens, slots), 0)
    spread = jnp.broadcast_to(gate_row, (tokens, slots))
    return jnp.where(token_index == token_row, spread, 0.0).astype(jnp.bfloat16)


def in_hbm(array):
    return pltpu.with_memory_space_constraint(array, pltpu.HBM)


def whole(shape):
    return pl.BlockSpec(shape, lambda *_: (0,) * len(shape))


def call(kernel, scalars, grid, in_specs, out_specs, out_shape, scratch, operands, vmem):
    return pl.pallas_call(
        kernel,
        grid_spec=pltpu.PrefetchScalarGridSpec(
            num_scalar_prefetch=1,
            grid=grid,
            in_specs=in_specs,
            out_specs=out_specs,
            scratch_shapes=scratch,
        ),
        out_shape=out_shape,
        compiler_params=pltpu.CompilerParams(
            dimension_semantics=("arbitrary",) * len(grid), vmem_limit_bytes=vmem
        ),
    )(scalars, *operands)


def expert_sums(where, weight, first, count, rows):
    local_count, width_in, width = weight.shape
    cols = width // (lax.axis_size("expert") // CORES)
    half = cols // CORES
    making = len(rows) > 1
    tokens = rows[3] if making else rows[0].shape[0]
    rows = rows[:3]
    by_token = (tokens, local_count * width_in)

    def kernel(where, *refs):
        weight_ref, keep_ref, send_ref = refs[len(rows) : len(rows) + 3]
        turned = refs[-1]
        rows_ref = refs[-2] if making else refs[0]

        if making:
            token_ref, gate_ref, hidden_ref = refs[:3]

            @pl.when(pl.program_id(0) == 0)
            def _():
                for local in range(local_count):
                    hot = hot_rows(token_ref[local], gate_ref[local], tokens)
                    made = dot(hot, hidden_ref[local], 1, 0).astype(jnp.bfloat16)
                    rows_ref[:, local * width_in : (local + 1) * width_in] = made

        stacked = weight_ref[...].reshape(local_count * width_in, cols)
        turned[...] = dot(rows_ref[...], stacked, 1, 0).astype(jnp.bfloat16).T
        keep_ref[0] = turned[pl.ds(pl.multiple_of(where[1] * half, half), half), :]
        send_ref[0] = turned[pl.ds(pl.multiple_of((1 - where[1]) * half, half), half), :]

    shape = jax.ShapeDtypeStruct((count, half, tokens), jnp.bfloat16)
    out_spec = pl.BlockSpec((1, half, tokens), lambda k, where: (k, 0, 0))
    out_shapes, out_specs = [shape, shape], [out_spec, out_spec]
    if making:
        out_shapes.append(jax.ShapeDtypeStruct(by_token, jnp.bfloat16))
        out_specs.append(whole(by_token))
    return call(
        kernel,
        where,
        (count,),
        [whole(array.shape) for array in rows]
        + [pl.BlockSpec((local_count, width_in, cols), lambda k, where: (0, 0, first + k))],
        out_specs,
        out_shapes,
        [pltpu.VMEM((cols, tokens), jnp.bfloat16)],
        (*rows, in_hbm(weight)),
        32 * MIB,
    )


def resident(kernel, scalars, operands, out_shapes, scratch=(), distant=(), passed=None):
    held = [pltpu.with_memory_space_constraint(array, pltpu.VMEM) for array in operands]
    in_vmem, anywhere = pl.BlockSpec(memory_space=pltpu.VMEM), pl.BlockSpec(memory_space=pl.ANY)
    far_off = [in_hbm(array) for array in distant] + ([] if passed is None else [passed])
    return pl.pallas_call(
        kernel,
        in_specs=[pl.BlockSpec(memory_space=pltpu.SMEM)] + [in_vmem] * len(held) + [anywhere] * len(far_off),
        out_specs=[anywhere if isinstance(shape, jax.ShapeDtypeStruct) else in_vmem for shape in out_shapes],
        out_shape=out_shapes,
        scratch_shapes=list(scratch),
        input_output_aliases={} if passed is None else {len(held) + len(far_off): 0},
        compiler_params=pltpu.CompilerParams(vmem_limit_bytes=20 * MIB),
    )(scalars, *held, *far_off)


def shares_by_token(where, payloads, slots, tokens):
    local_count, _, share = payloads[0].shape
    groups = len(payloads)

    def kernel(where, *refs):
        sources, (out_ref, held, sem) = refs[:groups], refs[groups:]
        loads = [pltpu.make_async_copy(ref, held.at[i], sem.at[i]) for i, ref in enumerate(sources)]
        for load in loads:
            load.start()

        def row(group, local, first):
            wide = [held[group, local, slots + first + i : slots + first + i + 1, :] for i in range(2)]
            return jnp.concatenate(wide, axis=1)[:, :slots].astype(jnp.float32)

        for group in range(groups):
            loads[group].wait()
            for local in range(local_count):
                token = (row(group, local, 0) * 2.0 + row(group, local, 2)).astype(jnp.int32)
                hot = hot_rows(token, row(group, local, 4), tokens)
                by_token = dot(hot, held[group, local, :slots, :], 1, 0).astype(jnp.bfloat16)
                out_ref[local * share : (local + 1) * share, group * tokens : (group + 1) * tokens] = by_token.T

    shape = (local_count * share, groups * tokens)
    scratch = [pltpu.VMEM((groups, *payloads[0].shape), jnp.bfloat16), pltpu.SemaphoreType.DMA((groups,))]
    return resident(kernel, where, [], [pltpu.VMEM(shape, jnp.bfloat16)], scratch, payloads)[0]


def hidden_grads(where, token_rows, row_gate, mine, other, weight):
    local_count, width_in, width = weight.shape
    slots = token_rows.shape[1]
    half, tokens = mine[0].shape[1:]
    flat = [*mine, *other]
    depth = width_in // 2

    def kernel(where, token_ref, gate_ref, *refs):
        weight_ref, out_ref, group_cot = refs[len(flat) :]
        local = pl.program_id(0)

        @pl.when((local == 0) & (pl.program_id(1) == 0))
        def _():
            for side in range(CORES):
                core = jnp.bitwise_xor(where[1], side)
                place = 0
                for ref in refs[side * len(mine) : (side + 1) * len(mine)]:
                    for row in range(ref.shape[0]):
                        start = (where[CORES + place] * CORES + core) * half
                        group_cot[pl.ds(pl.multiple_of(start, half), half), :] = ref[row]
                        place += 1

        sums = dot(weight_ref[0], group_cot[...], 1, 0).astype(jnp.bfloat16)
        hot = hot_rows(token_ref[local], gate_ref[local], tokens)
        out_ref[0] = dot(hot, sums, 0, 1).astype(jnp.bfloat16)

    return call(
        kernel,
        where,
        (local_count, width_in // depth),
        [whole((local_count, 1, slots))] * 2
        + [whole(block.shape) for block in flat]
        + [pl.BlockSpec((1, depth, width), lambda e, h, where: (e, h, 0))],
        pl.BlockSpec((1, slots, depth), lambda e, h, where: (e, 0, h)),
        jax.ShapeDtypeStruct((local_count, slots, width_in), jnp.bfloat16),
        [pltpu.VMEM((width, tokens), jnp.bfloat16)],
        (token_rows[:, None], row_gate[:, None], *flat, in_hbm(weight)),
        32 * MIB,
    )


def group_products(where, shares, groups, refs, chip):
    total, at = None, 0
    for place, sides in groups:
        loaded = []
        for pieces in sides:
            loaded.append([ref[first + chip] for ref, (_, first) in zip(refs[at:], pieces)])
            at += len(pieces)
        mine, other = [jnp.concatenate(pieces, axis=0) if len(pieces) > 1 else pieces[0] for pieces in loaded]
        low = jnp.where(where[1] == 0, mine, other)
        high = jnp.where(where[1] == 0, other, mine)
        block = jnp.concatenate([low, high], axis=0)
        tokens = block.shape[1]
        product = dot(shares[:, place * tokens : (place + 1) * tokens], block, 1, 1)
        total = product if total is None else total + product
    return total


def halves(parts):
    return [(part, 0) for part in parts]


def weight_cols(
    where, first, count, shares, groups, local_count, width, so_far=None, passed=None, keep=False
):
    chips = lax.axis_size("expert") // CORES
    cols = width // chips
    share = shares.shape[0] // local_count
    flat = [array for _, sides in groups for pieces in sides for array, _ in pieces]
    kept = (count, shares.shape[0], cols)
    distant = [] if so_far is None else [so_far]

    def kernel(where, shares_ref, *refs):
        refs = list(refs)
        pieces = [refs.pop(0) for _ in flat]
        added = refs.pop(0) if so_far is not None else None
        if passed is not None:
            refs.pop(0)
        out_ref, total_ref, sem = refs[:3]
        refs = refs[3:]
        place = [where[CORES + first + chip] for chip in range(count)]
        loads, stores = [], []
        for chip in range(count):
            loads.append([])
            if added is not None:
                loads[chip].append(pltpu.make_async_copy(added.at[first - 1 + chip], refs[-2].at[chip], refs[-1].at[chip]))
            for load in loads[chip]:
                load.start()
        for chip in range(count):
            total = group_products(where, shares_ref, groups, pieces, chip)
            for load in loads[chip]:
                load.wait()
            if added is not None:
                total = total + refs[-2][chip].astype(jnp.float32)
            if keep:
                total_ref[chip] = total.astype(jnp.bfloat16)
                target = out_ref.at[chip]
            else:
                for local in range(local_count):
                    total_ref[chip, local] = total[local * share : (local + 1) * share]
                target = out_ref.at[:, :, pl.ds(pl.multiple_of(place[chip] * cols, LANES), cols)]
            stores.append(pltpu.make_async_copy(total_ref.at[chip], target, sem.at[chip]))
            stores[-1].start()
        for store in stores:
            store.wait()

    if keep:
        scratch = [pltpu.VMEM(kept, jnp.bfloat16)]
        out_shape = jax.ShapeDtypeStruct(kept, jnp.bfloat16)
    else:
        scratch = [pltpu.VMEM((count, local_count, share, cols), jnp.float32)]
        out_shape = jax.ShapeDtypeStruct((local_count, share, width), jnp.float32)
    scratch.append(pltpu.SemaphoreType.DMA((count,)))
    if so_far is not None:
        scratch += [pltpu.VMEM(kept, jnp.bfloat16), pltpu.SemaphoreType.DMA((count,))]
    return resident(kernel, where, [shares, *flat], [out_shape], scratch, distant, passed)[0]


def planned_body(hidden, down_weight, cotangent, expert_ids, gate_weights, row_token, tile_count):
    local_count, width_in, width = down_weight.shape
    tokens = cotangent.shape[0]
    slots = hidden.shape[2]
    groups = lax.axis_size("dp")
    chips = lax.axis_size("expert") // CORES
    share = width_in // groups
    group = lax.axis_index("dp")
    expert_place = lax.axis_index("expert")
    chip = expert_place // CORES
    core = expert_place % CORES
    rest = (local_count, width)

    at_low, at_high = chip == 0, chip == chips - 1
    low_half = chip < chips // 2
    where = jnp.stack(
        [
            chip,
            core,
            chip,
            jnp.where(at_low, chip + 1, chip - 1),
            jnp.where(at_low, chip + 2, jnp.where(at_high, chip - 2, chip + 1)),
            jnp.where(at_low, chip + 3, jnp.where(at_high, chip - 3, jnp.where(low_half, chip + 2, chip - 2))),
        ]
    )

    own = cotangent.T
    middle = own.shape[0] // 2
    low_1, high_1 = along_z(own, 1, range(chips - 1)), along_z(own, -1, range(1, chips))
    x_own, y_own = across_dp(own, 1), across_dp(own, 2)
    own_other = across_cores(own)

    slot_index = jnp.arange(slots, dtype=jnp.int32)
    token_index = jnp.arange(tokens, dtype=jnp.int32)
    live = (row_token[0] >= 0) & (slot_index[None] < tile_count[0][:, None] * TILE)
    token_rows = jnp.where(live, row_token[0], -1)
    experts = expert_place * local_count + jnp.arange(local_count, dtype=jnp.int32)
    named = expert_ids[None] == experts[:, None, None]
    token_gate = jnp.sum(jnp.where(named, gate_weights[None].astype(jnp.float32), 0.0), axis=2)
    at_token = token_rows[:, :, None] == token_index[None, None, :]
    row_gate = jnp.sum(jnp.where(at_token, token_gate[:, None, :], 0.0), axis=2)

    def as_rows(values):
        padded = jnp.pad(values.astype(jnp.bfloat16), ((0, 0), (0, 2 * share - slots)))
        return padded.reshape(local_count, 2, share)

    extra = jnp.concatenate(
        [as_rows(token_rows >> 1), as_rows(token_rows & 1), as_rows(row_gate)], axis=1
    )
    extra = jnp.pad(extra, ((0, 0), (0, EXTRA_ROWS - extra.shape[1]), (0, 0)))
    payloads = []
    for mask in range(groups):
        rows = lax.dynamic_slice_in_dim(hidden[0], (group ^ mask) * share, share, 2)
        payloads.append(jnp.concatenate([rows, extra], axis=1))
    low_1, high_1, x_own, y_own, own_other, token_rows, row_gate, *payloads = joined(
        low_1, high_1, x_own, y_own, own_other, token_rows, row_gate, *payloads
    )

    x_payload, y_payload = across_dp(payloads[1], 1), across_dp(payloads[2], 2)
    low_2, high_2 = along_z(low_1, 1, range(1, chips - 1)), along_z(high_1, -1, range(1, chips - 1))
    x_own_other = across_cores(x_own)
    making = (token_rows[:, None], row_gate[:, None], hidden[0], tokens)
    keep_low, send_low, by_token = expert_sums(where, down_weight, 0, chips // 2, making)
    x_payload, y_payload, low_2, high_2, x_own_other, keep_low, send_low, by_token = joined(
        x_payload, y_payload, low_2, high_2, x_own_other, keep_low, send_low, by_token
    )

    far_payload = across_dp(payloads[3], 3)
    low_3, high_3 = along_z(low_2, 1, range(2, chips - 1)), along_z(high_2, -1, range(1, chips - 2))
    far_own = [across_dp(x_own[:middle], 2), across_dp(y_own[middle:], 1)]
    keep_high, send_high = expert_sums(where, down_weight, chips // 2, chips - chips // 2, (by_token,))
    far_payload, low_3, high_3, keep_high, send_high, x_own, y_own, *far_own = joined(
        far_payload, low_3, high_3, keep_high, send_high, x_own, y_own, *far_own
    )

    near = jnp.stack(
        [
            jnp.where(at_low, high_1, low_1),
            jnp.where(at_low, high_2, jnp.where(at_high, low_2, high_1)),
            jnp.where(at_low, high_3, jnp.where(at_high, low_3, jnp.where(low_half, high_2, low_2))),
        ]
    )
    x_near, y_near = across_dp(near, 1), across_dp(near, 2)

    low_other, high_other, y_own_other = [across_cores(block) for block in (send_low, send_high, y_own)]
    payloads = (payloads[0], x_payload, y_payload, far_payload)
    low_other, high_other, y_own_other, near, *payloads = joined(
        low_other, high_other, y_own_other, near, *payloads
    )
    near_other = across_cores(near)
    keep = jnp.concatenate([keep_low, keep_high], axis=0).astype(jnp.float32)
    other = jnp.concatenate([low_other, high_other], axis=0).astype(jnp.float32)
    sums = (keep + other).astype(jnp.bfloat16)

    def toward(place):
        return lax.dynamic_index_in_dim(sums, place % chips, 0, keepdims=False).astype(jnp.float32)

    def combine(step, up, down):
        up_out = (toward(chip + chips - step) + up).astype(jnp.bfloat16)
        down_out = (toward(chip + step) + down).astype(jnp.bfloat16)
        up = along_z(up_out, 1, range(0, step))
        return up, along_z(down_out, -1, range(chips - step, chips))

    up, down = combine(1, 0.0, 0.0)
    shares = shares_by_token(where, payloads, slots, tokens)
    near_other, shares, *far_own = joined(near_other, shares, *far_own)
    far_own = jnp.concatenate(far_own, axis=0)
    far_own_other = across_cores(far_own)
    hidden_grad = hidden_grads(
        where, token_rows, row_gate, [own[None], near], [own_other[None], near_other], down_weight
    )
    hidden_grad, shares, far_own_other, up, down = joined(hidden_grad, shares, far_own_other, up, down)
    up, down = combine(2, up.astype(jnp.float32), down.astype(jnp.float32))
    x_near, y_near, shares = joined(x_near, y_near, shares)

    far = [across_dp(x_near[:, :middle], 2), across_dp(y_near[:, middle:], 1)]
    x_other = across_cores(x_near)
    own_pairs = ((own, own_other), (x_own, x_own_other), (y_own, y_own_other), (far_own, far_own_other))
    own_groups = [(place, tuple(halves([block[None]]) for block in pair)) for place, pair in enumerate(own_pairs)]
    weight_grad = weight_cols(where, 0, 1, shares, own_groups, *rest)
    up, down, y_near = joined(up, down, y_near)
    y_other = across_cores(y_near)
    up, down = combine(3, up.astype(jnp.float32), down.astype(jnp.float32))
    three = [
        (place, (halves([mine]), halves([other])))
        for place, (mine, other) in enumerate(((near, near_other), (x_near, x_other), (y_near, y_other)))
    ]
    so_far = weight_cols(where, 1, chips - 1, shares, three, *rest, keep=True)
    so_far, weight_grad, up, down, *far = joined(so_far, weight_grad, up, down, *far)
    far_other = [across_cores(part) for part in far]
    mixed = (toward(chip) + up.astype(jnp.float32) + down.astype(jnp.float32)).astype(jnp.bfloat16)
    mixed, *far_other = joined(mixed, *far_other)
    last = [(groups - 1, (halves(far), halves(far_other)))]
    weight_grad = weight_cols(where, 1, chips - 1, shares, last, *rest, so_far, weight_grad)
    return (mixed.T, hidden_grad[None], weight_grad)


def tile_products(rows_in, weight_mat, count, contract_dim):
    rows_cap = rows_in.shape[0]
    width_out = weight_mat.shape[1 - contract_dim]

    def one_tile(tile_index, outputs):
        block = lax.dynamic_slice_in_dim(rows_in, tile_index * TILE, TILE, 0)
        product = lax.dot_general(
            block,
            weight_mat,
            (((1,), (contract_dim,)), ((), ())),
            preferred_element_type=jnp.float32,
        )
        return lax.dynamic_update_slice_in_dim(
            outputs, product.astype(jnp.bfloat16), tile_index * TILE, 0
        )

    return lax.fori_loop(0, count, one_tile, jnp.zeros((rows_cap, width_out), jnp.bfloat16))


def general_body(hidden, down_weight, cotangent, expert_ids, gate_weights, row_token, tile_count):
    local_count = down_weight.shape[0]
    group_size = cotangent.shape[0]
    expert_index = jnp.arange(EXPERTS, dtype=jnp.int32)
    named_cols = expert_ids[:, :, None] == expert_index[None, None, :]
    gate_cols = jnp.sum(
        jnp.where(named_cols, gate_weights[:, :, None].astype(jnp.float32), 0.0), axis=1
    ).astype(jnp.bfloat16)
    group_cot = lax.all_gather(cotangent, "expert", axis=1, tiled=True)
    width = group_cot.shape[1]
    first_expert = lax.axis_index("expert") * local_count
    slot_index = jnp.arange(hidden.shape[2], dtype=jnp.int32)
    share_rows = down_weight.shape[1] // lax.axis_size("dp")
    partial_value = jnp.zeros((group_size, width), jnp.float32)
    grad_list = []
    weight_list = []
    for local in range(local_count):
        token_rows = row_token[0, local]
        count = tile_count[0, local]
        live_rows = (token_rows >= 0) & (slot_index < count * TILE)
        safe_rows = jnp.where(live_rows, token_rows, 0)
        column = lax.dynamic_index_in_dim(gate_cols, first_expert + local, 1, keepdims=False)
        row_gate = jnp.where(live_rows, column[safe_rows].astype(jnp.float32), 0.0)
        target = jnp.where(live_rows, token_rows, group_size)
        hidden_rows = hidden[0, local]
        weight_mat = down_weight[local]
        out_rows = tile_products(hidden_rows, weight_mat, count, 0)
        partial_value = partial_value.at[target].add(
            row_gate[:, None] * out_rows.astype(jnp.float32), mode="drop"
        )
        routed = (row_gate[:, None] * group_cot[safe_rows].astype(jnp.float32)).astype(jnp.bfloat16)
        grad_list.append(tile_products(routed, weight_mat, count, 1))

        def weight_rows(start, rows_count, hidden_rows=hidden_rows, routed_rows=routed):
            return lax.dot_general(
                hidden_rows,
                routed_rows,
                (((0,), (0,)), ((), ())),
                preferred_element_type=jnp.float32,
            )

        weight_list.append(
            lax.psum_scatter(
                weight_rows(jnp.int32(0), share_rows * lax.axis_size("dp")).astype(jnp.bfloat16),
                "dp",
                scatter_dimension=0,
                tiled=True,
            ).astype(jnp.float32)
        )
    merged = partial_value
    top_bit = lax.axis_size("expert").bit_length() - 1
    axis_index = lax.axis_index("expert")
    for bit_index in reversed(range(top_bit)):
        half_cols = merged.shape[1] // 2
        lower_half = merged[:, :half_cols]
        upper_half = merged[:, half_cols:]
        high_side = axis_index // 2**bit_index % 2 == 1
        sending = jnp.where(high_side, lower_half, upper_half)
        keeping = jnp.where(high_side, upper_half, lower_half)
        merged = keeping + swapped(sending.astype(jnp.bfloat16), "expert", bit_index).astype(
            sending.dtype
        )
    mixed_out = merged.astype(jnp.bfloat16)
    hidden_grad = jnp.stack(grad_list, axis=0)[None]
    weight_grad = jnp.stack(weight_list, axis=0)
    return (mixed_out, hidden_grad, weight_grad)


def solution(mesh):
    placed = (
        P("dp", "expert", None, None),
        P("expert", None, None),
        P("dp", "expert"),
        P("dp", None),
        P("dp", None),
        P("dp", "expert", None),
        P("dp", "expert"),
    )

    def body(*shards):
        width = shards[1].shape[2]
        chips = mesh.shape["expert"] // CORES
        fits = mesh.shape["dp"] == 4 and chips == 4 and width % (chips * LANES) == 0
        return planned_body(*shards) if fits else general_body(*shards)

    return jax.shard_map(
        body,
        mesh=mesh,
        in_specs=placed,
        out_specs=(P("dp", "expert"), P("dp", "expert", None, None), P("expert", "dp", None)),
        check_vma=False,
    )
```

```python
import jax
import jax.numpy as jnp
from jax import lax
from jax.experimental import pallas as pl
from jax.experimental.pallas import tpu as pltpu
from jax.sharding import PartitionSpec as P

EXPERTS = 16
TILE = 128
LANES = 128
CORES = 2
EXTRA_ROWS = 16
MIB = 1024 * 1024


def swapped(shard, axis, bit):
    return lax.ppermute(shard, axis, [(i, i ^ 1 << bit) for i in range(lax.axis_size(axis))])


def across_dp(shard, mask):
    return lax.ppermute(shard, "dp", [(i, i ^ mask) for i in range(lax.axis_size("dp"))])


def across_cores(shard):
    return swapped(shard, "expert", 0)


def z_lines():
    size = lax.axis_size("expert")
    return [list(range(core, size, CORES)) for core in range(CORES)]


def exchanged(parts):
    return lax.all_to_all(parts, "expert", 0, 0, axis_index_groups=z_lines(), tiled=True)


def joined(*values):
    return lax.optimization_barrier(values)


def dot(lhs, rhs, lhs_dim, rhs_dim):
    return lax.dot_general(
        lhs, rhs, (((lhs_dim,), (rhs_dim,)), ((), ())), preferred_element_type=jnp.float32
    )


def hot_rows(token_row, gate_row, tokens):
    slots = token_row.shape[1]
    token_index = lax.broadcasted_iota(jnp.int32, (tokens, slots), 0)
    spread = jnp.broadcast_to(gate_row, (tokens, slots))
    return jnp.where(token_index == token_row, spread, 0.0).astype(jnp.bfloat16)


def in_hbm(array):
    return pltpu.with_memory_space_constraint(array, pltpu.HBM)


def whole(shape):
    return pl.BlockSpec(shape, lambda *_: (0,) * len(shape))


def call(kernel, scalars, grid, in_specs, out_specs, out_shape, scratch, operands, vmem):
    return pl.pallas_call(
        kernel,
        grid_spec=pltpu.PrefetchScalarGridSpec(
            num_scalar_prefetch=1,
            grid=grid,
            in_specs=in_specs,
            out_specs=out_specs,
            scratch_shapes=scratch,
        ),
        out_shape=out_shape,
        compiler_params=pltpu.CompilerParams(
            dimension_semantics=("arbitrary",) * len(grid), vmem_limit_bytes=vmem
        ),
    )(scalars, *operands)


def expert_sums(where, token_rows, row_gate, hidden_rows, weight, tokens):
    local_count, slots, width_in = hidden_rows.shape
    chips = lax.axis_size("expert") // CORES
    cols = weight.shape[2] // chips
    half = cols // CORES

    def kernel(where, token_ref, gate_ref, hidden_ref, weight_ref, keep_ref, send_ref, by_token, turned):
        @pl.when(pl.program_id(0) == 0)
        def _():
            for local in range(local_count):
                hot = hot_rows(token_ref[local], gate_ref[local], tokens)
                made = dot(hot, hidden_ref[local], 1, 0).astype(jnp.bfloat16)
                by_token[:, local * width_in : (local + 1) * width_in] = made

        stacked = weight_ref[...].reshape(local_count * width_in, cols)
        turned[...] = dot(by_token[...], stacked, 1, 0).astype(jnp.bfloat16).T
        keep_ref[0] = turned[pl.ds(pl.multiple_of(where[1] * half, half), half), :]
        send_ref[0] = turned[pl.ds(pl.multiple_of((1 - where[1]) * half, half), half), :]

    shape = jax.ShapeDtypeStruct((chips, half, tokens), jnp.bfloat16)
    out_spec = pl.BlockSpec((1, half, tokens), lambda k, where: (k, 0, 0))
    return call(
        kernel,
        where,
        (chips,),
        [
            whole((local_count, 1, slots)),
            whole((local_count, 1, slots)),
            whole(hidden_rows.shape),
            pl.BlockSpec((local_count, width_in, cols), lambda k, where: (0, 0, k)),
        ],
        (out_spec, out_spec),
        (shape, shape),
        [
            pltpu.VMEM((tokens, local_count * width_in), jnp.bfloat16),
            pltpu.VMEM((cols, tokens), jnp.bfloat16),
        ],
        (token_rows[:, None], row_gate[:, None], hidden_rows, in_hbm(weight)),
        32 * MIB,
    )


def resident(kernel, scalars, operands, out_shapes, scratch=(), distant=(), passed=None):
    held = [pltpu.with_memory_space_constraint(array, pltpu.VMEM) for array in operands]
    in_vmem, anywhere = pl.BlockSpec(memory_space=pltpu.VMEM), pl.BlockSpec(memory_space=pl.ANY)
    far_off = [in_hbm(array) for array in distant] + ([] if passed is None else [passed])
    return pl.pallas_call(
        kernel,
        in_specs=[pl.BlockSpec(memory_space=pltpu.SMEM)] + [in_vmem] * len(held) + [anywhere] * len(far_off),
        out_specs=[anywhere if isinstance(shape, jax.ShapeDtypeStruct) else in_vmem for shape in out_shapes],
        out_shape=out_shapes,
        scratch_shapes=list(scratch),
        input_output_aliases={} if passed is None else {len(held) + len(far_off): 0},
        compiler_params=pltpu.CompilerParams(vmem_limit_bytes=20 * MIB),
    )(scalars, *held, *far_off)


def shares_by_token(where, payloads, slots, tokens):
    local_count, _, share = payloads[0].shape
    groups = len(payloads)

    def kernel(where, *refs):
        sources, (out_ref, held, sem) = refs[:groups], refs[groups:]
        loads = [pltpu.make_async_copy(ref, held.at[i], sem.at[i]) for i, ref in enumerate(sources)]
        for load in loads:
            load.start()

        def row(group, local, first):
            wide = [held[group, local, slots + first + i : slots + first + i + 1, :] for i in range(2)]
            return jnp.concatenate(wide, axis=1)[:, :slots].astype(jnp.float32)

        for group in range(groups):
            loads[group].wait()
            for local in range(local_count):
                token = (row(group, local, 0) * 2.0 + row(group, local, 2)).astype(jnp.int32)
                hot = hot_rows(token, row(group, local, 4), tokens)
                by_token = dot(hot, held[group, local, :slots, :], 1, 0).astype(jnp.bfloat16)
                out_ref[local * share : (local + 1) * share, group * tokens : (group + 1) * tokens] = by_token.T

    shape = (local_count * share, groups * tokens)
    scratch = [pltpu.VMEM((groups, *payloads[0].shape), jnp.bfloat16), pltpu.SemaphoreType.DMA((groups,))]
    return resident(kernel, where, [], [pltpu.VMEM(shape, jnp.bfloat16)], scratch, payloads)[0]


def blocks_of(where, gathered, steps, parts):
    chips, rows, tokens = gathered.shape
    part = rows // parts

    def kernel(where, gathered_ref, *refs):
        sem = refs[-1]
        copies = []
        for place, step in enumerate(steps):
            chip = lax.rem(where[0] + step, chips)
            for index, out_ref in enumerate(refs[:-1]):
                source = gathered_ref.at[chip, pl.ds(index * part, part)]
                copies.append(pltpu.make_async_copy(source, out_ref.at[place], sem.at[len(copies)]))
        for copy in copies:
            copy.start()
        for copy in copies:
            copy.wait()

    return pl.pallas_call(
        kernel,
        in_specs=[pl.BlockSpec(memory_space=pltpu.SMEM), pl.BlockSpec(memory_space=pl.ANY)],
        out_specs=[pl.BlockSpec(memory_space=pltpu.VMEM)] * parts,
        out_shape=[pltpu.VMEM((len(steps), part, tokens), gathered.dtype)] * parts,
        scratch_shapes=[pltpu.SemaphoreType.DMA((len(steps) * parts,))],
    )(where, in_hbm(gathered))


def hidden_grads(where, token_rows, row_gate, gathered, weight):
    local_count, width_in, width = weight.shape
    slots = token_rows.shape[1]
    chips, half, tokens = gathered[0].shape
    depth = width_in // 2

    def kernel(where, token_ref, gate_ref, mine_ref, other_ref, weight_ref, out_ref, group_cot, sem):
        local = pl.program_id(0)

        @pl.when((local == 0) & (pl.program_id(1) == 0))
        def _():
            loads = []
            for side, ref in enumerate((mine_ref, other_ref)):
                for chip in range(chips):
                    start = (chip * CORES + jnp.bitwise_xor(where[1], side)) * half
                    rows = group_cot.at[pl.ds(pl.multiple_of(start, half), half)]
                    loads.append(pltpu.make_async_copy(ref.at[chip], rows, sem.at[len(loads)]))
            for load in loads:
                load.start()
            for load in loads:
                load.wait()

        sums = dot(weight_ref[0], group_cot[...], 1, 0).astype(jnp.bfloat16)
        hot = hot_rows(token_ref[local], gate_ref[local], tokens)
        out_ref[0] = dot(hot, sums, 0, 1).astype(jnp.bfloat16)

    return call(
        kernel,
        where,
        (local_count, width_in // depth),
        [whole((local_count, 1, slots))] * 2
        + [pl.BlockSpec(memory_space=pl.ANY)] * CORES
        + [pl.BlockSpec((1, depth, width), lambda e, h, where: (e, h, 0))],
        pl.BlockSpec((1, slots, depth), lambda e, h, where: (e, 0, h)),
        jax.ShapeDtypeStruct((local_count, slots, width_in), jnp.bfloat16),
        [pltpu.VMEM((width, tokens), jnp.bfloat16), pltpu.SemaphoreType.DMA((CORES * chips,))],
        (token_rows[:, None], row_gate[:, None], *map(in_hbm, gathered), in_hbm(weight)),
        28 * MIB,
    )


def group_products(where, shares, groups, refs, chip):
    total, at = None, 0
    for place, sides in groups:
        loaded = []
        for pieces in sides:
            loaded.append([ref[first + chip] for ref, (_, first) in zip(refs[at:], pieces)])
            at += len(pieces)
        mine, other = [jnp.concatenate(pieces, axis=0) if len(pieces) > 1 else pieces[0] for pieces in loaded]
        low = jnp.where(where[1] == 0, mine, other)
        high = jnp.where(where[1] == 0, other, mine)
        block = jnp.concatenate([low, high], axis=0)
        tokens = block.shape[1]
        product = dot(shares[:, place * tokens : (place + 1) * tokens], block, 1, 1)
        total = product if total is None else total + product
    return total


def halves(parts):
    return [(part, 0) for part in parts]


def weight_cols(
    where, first, count, shares, groups, local_count, width, gathered=None, so_far=None, passed=None, keep=False
):
    chips = lax.axis_size("expert") // CORES
    cols = width // chips
    share = shares.shape[0] // local_count
    flat = [array for _, sides in groups for pieces in sides for array, _ in pieces]
    tokens = flat[0].shape[-1]
    kept = (count, shares.shape[0], cols)
    distant = [*(gathered or []), *([] if so_far is None else [so_far])]

    def kernel(where, shares_ref, *refs):
        refs = list(refs)
        pieces = [refs.pop(0) for _ in flat]
        sources = [refs.pop(0) for _ in gathered or []]
        added = refs.pop(0) if so_far is not None else None
        if passed is not None:
            refs.pop(0)
        out_ref, total_ref, sem = refs[:3]
        refs = refs[3:]
        place = [lax.rem(where[0] + first + chip, chips) for chip in range(count)]
        loads, stores = [], []
        for chip in range(count):
            loads.append([])
            for side, source in enumerate(sources):
                target = refs[0].at[chip, jnp.bitwise_xor(where[1], side)]
                loads[chip].append(pltpu.make_async_copy(source.at[place[chip]], target, refs[1].at[chip, side]))
            if added is not None:
                loads[chip].append(pltpu.make_async_copy(added.at[first - 1 + chip], refs[-2].at[chip], refs[-1].at[chip]))
            for load in loads[chip]:
                load.start()
        for chip in range(count):
            total = group_products(where, shares_ref, groups, pieces, chip)
            for load in loads[chip]:
                load.wait()
            if sources:
                total = total + dot(shares_ref[:, :tokens], refs[0][chip].reshape(cols, tokens), 1, 1)
            if added is not None:
                total = total + refs[-2][chip].astype(jnp.float32)
            if keep:
                total_ref[chip] = total.astype(jnp.bfloat16)
                target = out_ref.at[chip]
            else:
                for local in range(local_count):
                    total_ref[chip, local] = total[local * share : (local + 1) * share]
                target = out_ref.at[:, :, pl.ds(pl.multiple_of(place[chip] * cols, LANES), cols)]
            stores.append(pltpu.make_async_copy(total_ref.at[chip], target, sem.at[chip]))
            stores[-1].start()
        for store in stores:
            store.wait()

    if keep:
        scratch = [pltpu.VMEM(kept, jnp.bfloat16)]
        out_shape = jax.ShapeDtypeStruct(kept, jnp.bfloat16)
    else:
        scratch = [pltpu.VMEM((count, local_count, share, cols), jnp.float32)]
        out_shape = jax.ShapeDtypeStruct((local_count, share, width), jnp.float32)
    scratch.append(pltpu.SemaphoreType.DMA((count,)))
    if gathered is not None:
        scratch += [pltpu.VMEM((count, CORES, cols // CORES, tokens), jnp.bfloat16)]
        scratch.append(pltpu.SemaphoreType.DMA((count, CORES)))
    if so_far is not None:
        scratch += [pltpu.VMEM(kept, jnp.bfloat16), pltpu.SemaphoreType.DMA((count,))]
    return resident(kernel, where, [shares, *flat], [out_shape], scratch, distant, passed)[0]


def planned_body(hidden, down_weight, cotangent, expert_ids, gate_weights, row_token, tile_count):
    local_count, width_in, width = down_weight.shape
    tokens = cotangent.shape[0]
    slots = hidden.shape[2]
    groups = lax.axis_size("dp")
    chips = lax.axis_size("expert") // CORES
    share = width_in // groups
    group = lax.axis_index("dp")
    expert_place = lax.axis_index("expert")
    chip = expert_place // CORES
    core = expert_place % CORES
    where = jnp.stack([chip, core])

    own = cotangent.T
    middle = own.shape[0] // 2
    gathered = exchanged(jnp.broadcast_to(own[None], (chips, *own.shape)))
    x_own, y_own = across_dp(own, 1), across_dp(own, 2)

    slot_index = jnp.arange(slots, dtype=jnp.int32)
    token_index = jnp.arange(tokens, dtype=jnp.int32)
    live = (row_token[0] >= 0) & (slot_index[None] < tile_count[0][:, None] * TILE)
    token_rows = jnp.where(live, row_token[0], -1)
    experts = expert_place * local_count + jnp.arange(local_count, dtype=jnp.int32)
    named = expert_ids[None] == experts[:, None, None]
    token_gate = jnp.sum(jnp.where(named, gate_weights[None].astype(jnp.float32), 0.0), axis=2)
    at_token = token_rows[:, :, None] == token_index[None, None, :]
    row_gate = jnp.sum(jnp.where(at_token, token_gate[:, None, :], 0.0), axis=2)

    def as_rows(values):
        padded = jnp.pad(values.astype(jnp.bfloat16), ((0, 0), (0, 2 * share - slots)))
        return padded.reshape(local_count, 2, share)

    extra = jnp.concatenate(
        [as_rows(token_rows >> 1), as_rows(token_rows & 1), as_rows(row_gate)], axis=1
    )
    extra = jnp.pad(extra, ((0, 0), (0, EXTRA_ROWS - extra.shape[1]), (0, 0)))
    payloads = []
    for mask in range(groups):
        rows = lax.dynamic_slice_in_dim(hidden[0], (group ^ mask) * share, share, 2)
        payloads.append(jnp.concatenate([rows, extra], axis=1))
    x_own, y_own, token_rows, row_gate, *payloads = joined(
        x_own, y_own, token_rows, row_gate, *payloads
    )

    payloads = [across_dp(payload, mask) if mask else payload for mask, payload in enumerate(payloads)]
    far_own = [across_dp(x_own[:middle], 2), across_dp(y_own[middle:], 1)]
    keep, send = expert_sums(where, token_rows, row_gate, hidden[0], down_weight, tokens)
    x_own, y_own, keep, send, *sent = joined(x_own, y_own, keep, send, *far_own, *payloads)
    far_own, payloads = sent[:2], sent[2:]

    steps = list(range(1, chips))
    near = blocks_of(where, gathered, steps, 2)
    x_near, y_near = [None, None], [None, None]
    x_near[0], y_near[1] = across_dp(near[0], 1), across_dp(near[1], 2)
    x_near[1], y_near[0] = across_dp(near[1], 1), across_dp(near[0], 2)

    from_other = across_cores(send)
    own_far = jnp.stack([x_own, y_own, jnp.concatenate(far_own, axis=0)])
    from_other, own_far, *payloads = joined(from_other, own_far, *payloads)
    own_far_other = across_cores(own_far)
    sums = (keep.astype(jnp.float32) + from_other.astype(jnp.float32)).astype(jnp.bfloat16)
    mixed = exchanged(sums)
    gathered = [gathered, across_cores(gathered)]
    shares = shares_by_token(where, payloads, slots, tokens)
    hidden_grad = hidden_grads(where, token_rows, row_gate, gathered, down_weight)
    rest = (local_count, width)
    own_groups = [(place + 1, ([(own_far, place)], [(own_far_other, place)])) for place in range(groups - 1)]
    weight_grad = weight_cols(where, 0, 1, shares, own_groups, *rest, gathered)
    hidden_grad, shares, weight_grad, _, *sent = joined(
        hidden_grad, shares, weight_grad, sums, *x_near, *y_near
    )
    x_near, y_near = sent[:2], sent[2:]

    early = chips - 2
    spans = [slice(0, early), slice(early, early + 1)]
    far = [[across_dp(x_near[0][span], 2), across_dp(y_near[1][span], 1)] for span in spans]
    x_other = [across_cores(part) for part in x_near]
    y_other = [across_cores(part) for part in y_near]
    two = [(place, tuple(map(halves, pair))) for place, pair in ((1, (x_near, x_other)), (2, (y_near, y_other)))]
    so_far = weight_cols(where, 1, chips - 1, shares, two, *rest, gathered, keep=True)
    for first, count, pieces in ((1, early, far[0]), (1 + early, 1, far[1])):
        if first == 1:
            so_far, *pieces = joined(so_far, *pieces)
        else:
            weight_grad, mixed, *pieces = joined(weight_grad, mixed, *pieces)
        last = [(groups - 1, (halves(pieces), halves([across_cores(part) for part in pieces])))]
        weight_grad = weight_cols(where, first, count, shares, last, *rest, None, so_far, weight_grad)
    mixed = jnp.sum(mixed.astype(jnp.float32), axis=0).astype(jnp.bfloat16)
    return (mixed.T, hidden_grad[None], weight_grad)


def tile_products(rows_in, weight_mat, count, contract_dim):
    rows_cap = rows_in.shape[0]
    width_out = weight_mat.shape[1 - contract_dim]

    def one_tile(tile_index, outputs):
        block = lax.dynamic_slice_in_dim(rows_in, tile_index * TILE, TILE, 0)
        product = lax.dot_general(
            block,
            weight_mat,
            (((1,), (contract_dim,)), ((), ())),
            preferred_element_type=jnp.float32,
        )
        return lax.dynamic_update_slice_in_dim(
            outputs, product.astype(jnp.bfloat16), tile_index * TILE, 0
        )

    return lax.fori_loop(0, count, one_tile, jnp.zeros((rows_cap, width_out), jnp.bfloat16))


def general_body(hidden, down_weight, cotangent, expert_ids, gate_weights, row_token, tile_count):
    local_count = down_weight.shape[0]
    group_size = cotangent.shape[0]
    expert_index = jnp.arange(EXPERTS, dtype=jnp.int32)
    named_cols = expert_ids[:, :, None] == expert_index[None, None, :]
    gate_cols = jnp.sum(
        jnp.where(named_cols, gate_weights[:, :, None].astype(jnp.float32), 0.0), axis=1
    ).astype(jnp.bfloat16)
    group_cot = lax.all_gather(cotangent, "expert", axis=1, tiled=True)
    width = group_cot.shape[1]
    first_expert = lax.axis_index("expert") * local_count
    slot_index = jnp.arange(hidden.shape[2], dtype=jnp.int32)
    share_rows = down_weight.shape[1] // lax.axis_size("dp")
    partial_value = jnp.zeros((group_size, width), jnp.float32)
    grad_list = []
    weight_list = []
    for local in range(local_count):
        token_rows = row_token[0, local]
        count = tile_count[0, local]
        live_rows = (token_rows >= 0) & (slot_index < count * TILE)
        safe_rows = jnp.where(live_rows, token_rows, 0)
        column = lax.dynamic_index_in_dim(gate_cols, first_expert + local, 1, keepdims=False)
        row_gate = jnp.where(live_rows, column[safe_rows].astype(jnp.float32), 0.0)
        target = jnp.where(live_rows, token_rows, group_size)
        hidden_rows = hidden[0, local]
        weight_mat = down_weight[local]
        out_rows = tile_products(hidden_rows, weight_mat, count, 0)
        partial_value = partial_value.at[target].add(
            row_gate[:, None] * out_rows.astype(jnp.float32), mode="drop"
        )
        routed = (row_gate[:, None] * group_cot[safe_rows].astype(jnp.float32)).astype(jnp.bfloat16)
        grad_list.append(tile_products(routed, weight_mat, count, 1))

        def weight_rows(start, rows_count, hidden_rows=hidden_rows, routed_rows=routed):
            return lax.dot_general(
                hidden_rows,
                routed_rows,
                (((0,), (0,)), ((), ())),
                preferred_element_type=jnp.float32,
            )

        weight_list.append(
            lax.psum_scatter(
                weight_rows(jnp.int32(0), share_rows * lax.axis_size("dp")).astype(jnp.bfloat16),
                "dp",
                scatter_dimension=0,
                tiled=True,
            ).astype(jnp.float32)
        )
    merged = partial_value
    top_bit = lax.axis_size("expert").bit_length() - 1
    axis_index = lax.axis_index("expert")
    for bit_index in reversed(range(top_bit)):
        half_cols = merged.shape[1] // 2
        lower_half = merged[:, :half_cols]
        upper_half = merged[:, half_cols:]
        high_side = axis_index // 2**bit_index % 2 == 1
        sending = jnp.where(high_side, lower_half, upper_half)
        keeping = jnp.where(high_side, upper_half, lower_half)
        merged = keeping + swapped(sending.astype(jnp.bfloat16), "expert", bit_index).astype(
            sending.dtype
        )
    mixed_out = merged.astype(jnp.bfloat16)
    hidden_grad = jnp.stack(grad_list, axis=0)[None]
    weight_grad = jnp.stack(weight_list, axis=0)
    return (mixed_out, hidden_grad, weight_grad)


def solution(mesh):
    placed = (
        P("dp", "expert", None, None),
        P("expert", None, None),
        P("dp", "expert"),
        P("dp", None),
        P("dp", None),
        P("dp", "expert", None),
        P("dp", "expert"),
    )

    def body(*shards):
        width = shards[1].shape[2]
        chips = mesh.shape["expert"] // CORES
        fits = mesh.shape["dp"] == 4 and chips > 2 and width % (chips * LANES) == 0
        return planned_body(*shards) if fits else general_body(*shards)

    return jax.shard_map(
        body,
        mesh=mesh,
        in_specs=placed,
        out_specs=(P("dp", "expert"), P("dp", "expert", None, None), P("expert", "dp", None)),
        check_vma=False,
    )
```

```python
import jax
import jax.numpy as jnp
from jax import lax
from jax.experimental import pallas as pl
from jax.experimental.pallas import tpu as pltpu
from jax.sharding import PartitionSpec as P

EXPERTS = 16
TILE = 128
LANES = 128
CORES = 2
EXTRA_ROWS = 16
MIB = 1024 * 1024


def swapped(shard, axis, bit):
    return lax.ppermute(shard, axis, [(i, i ^ 1 << bit) for i in range(lax.axis_size(axis))])


def across_dp(shard, mask):
    return lax.ppermute(shard, "dp", [(i, i ^ mask) for i in range(lax.axis_size("dp"))])


def across_cores(shard):
    return swapped(shard, "expert", 0)


def z_lines():
    size = lax.axis_size("expert")
    return [list(range(core, size, CORES)) for core in range(CORES)]


def exchanged(parts):
    return lax.all_to_all(parts, "expert", 0, 0, axis_index_groups=z_lines(), tiled=True)


def joined(*values):
    return lax.optimization_barrier(values)


def dot(lhs, rhs, lhs_dim, rhs_dim):
    return lax.dot_general(
        lhs, rhs, (((lhs_dim,), (rhs_dim,)), ((), ())), preferred_element_type=jnp.float32
    )


def hot_rows(token_row, gate_row, tokens):
    slots = token_row.shape[1]
    token_index = lax.broadcasted_iota(jnp.int32, (tokens, slots), 0)
    spread = jnp.broadcast_to(gate_row, (tokens, slots))
    return jnp.where(token_index == token_row, spread, 0.0).astype(jnp.bfloat16)


def in_hbm(array):
    return pltpu.with_memory_space_constraint(array, pltpu.HBM)


def whole(shape):
    return pl.BlockSpec(shape, lambda *_: (0,) * len(shape))


def call(kernel, scalars, grid, in_specs, out_specs, out_shape, scratch, operands, vmem):
    return pl.pallas_call(
        kernel,
        grid_spec=pltpu.PrefetchScalarGridSpec(
            num_scalar_prefetch=1,
            grid=grid,
            in_specs=in_specs,
            out_specs=out_specs,
            scratch_shapes=scratch,
        ),
        out_shape=out_shape,
        compiler_params=pltpu.CompilerParams(
            dimension_semantics=("arbitrary",) * len(grid), vmem_limit_bytes=vmem
        ),
    )(scalars, *operands)


def expert_sums(where, token_rows, row_gate, hidden_rows, weight, tokens):
    local_count, slots, width_in = hidden_rows.shape
    chips = lax.axis_size("expert") // CORES
    cols = weight.shape[2] // chips
    half = cols // CORES

    def kernel(where, token_ref, gate_ref, hidden_ref, weight_ref, keep_ref, send_ref, by_token, turned):
        @pl.when(pl.program_id(0) == 0)
        def _():
            for local in range(local_count):
                hot = hot_rows(token_ref[local], gate_ref[local], tokens)
                made = dot(hot, hidden_ref[local], 1, 0).astype(jnp.bfloat16)
                by_token[:, local * width_in : (local + 1) * width_in] = made

        stacked = weight_ref[...].reshape(local_count * width_in, cols)
        turned[...] = dot(by_token[...], stacked, 1, 0).astype(jnp.bfloat16).T
        keep_ref[0] = turned[pl.ds(pl.multiple_of(where[1] * half, half), half), :]
        send_ref[0] = turned[pl.ds(pl.multiple_of((1 - where[1]) * half, half), half), :]

    shape = jax.ShapeDtypeStruct((chips, half, tokens), jnp.bfloat16)
    out_spec = pl.BlockSpec((1, half, tokens), lambda k, where: (k, 0, 0))
    return call(
        kernel,
        where,
        (chips,),
        [
            whole((local_count, 1, slots)),
            whole((local_count, 1, slots)),
            whole(hidden_rows.shape),
            pl.BlockSpec((local_count, width_in, cols), lambda k, where: (0, 0, k)),
        ],
        (out_spec, out_spec),
        (shape, shape),
        [
            pltpu.VMEM((tokens, local_count * width_in), jnp.bfloat16),
            pltpu.VMEM((cols, tokens), jnp.bfloat16),
        ],
        (token_rows[:, None], row_gate[:, None], hidden_rows, in_hbm(weight)),
        32 * MIB,
    )


def resident(kernel, scalars, operands, out_shapes, scratch=(), distant=(), passed=None):
    held = [pltpu.with_memory_space_constraint(array, pltpu.VMEM) for array in operands]
    in_vmem, anywhere = pl.BlockSpec(memory_space=pltpu.VMEM), pl.BlockSpec(memory_space=pl.ANY)
    far_off = [in_hbm(array) for array in distant] + ([] if passed is None else [passed])
    return pl.pallas_call(
        kernel,
        in_specs=[pl.BlockSpec(memory_space=pltpu.SMEM)] + [in_vmem] * len(held) + [anywhere] * len(far_off),
        out_specs=[anywhere if isinstance(shape, jax.ShapeDtypeStruct) else in_vmem for shape in out_shapes],
        out_shape=out_shapes,
        scratch_shapes=list(scratch),
        input_output_aliases={} if passed is None else {len(held) + len(far_off): 0},
        compiler_params=pltpu.CompilerParams(vmem_limit_bytes=20 * MIB),
    )(scalars, *held, *far_off)


def shares_by_token(where, payloads, slots, tokens):
    local_count, _, share = payloads[0].shape
    groups = len(payloads)

    def kernel(where, *refs):
        sources, (out_ref, held, sem) = refs[:groups], refs[groups:]
        loads = [pltpu.make_async_copy(ref, held.at[i], sem.at[i]) for i, ref in enumerate(sources)]
        for load in loads:
            load.start()

        def row(group, local, first):
            wide = [held[group, local, slots + first + i : slots + first + i + 1, :] for i in range(2)]
            return jnp.concatenate(wide, axis=1)[:, :slots].astype(jnp.float32)

        for group in range(groups):
            loads[group].wait()
            for local in range(local_count):
                token = (row(group, local, 0) * 2.0 + row(group, local, 2)).astype(jnp.int32)
                hot = hot_rows(token, row(group, local, 4), tokens)
                by_token = dot(hot, held[group, local, :slots, :], 1, 0).astype(jnp.bfloat16)
                out_ref[local * share : (local + 1) * share, group * tokens : (group + 1) * tokens] = by_token.T

    shape = (local_count * share, groups * tokens)
    scratch = [pltpu.VMEM((groups, *payloads[0].shape), jnp.bfloat16), pltpu.SemaphoreType.DMA((groups,))]
    return resident(kernel, where, [], [pltpu.VMEM(shape, jnp.bfloat16)], scratch, payloads)[0]


def blocks_of(where, gathered, steps, parts):
    chips, rows, tokens = gathered.shape
    part = rows // parts

    def kernel(where, gathered_ref, *refs):
        sem = refs[-1]
        copies = []
        for place, step in enumerate(steps):
            chip = lax.rem(where[0] + step, chips)
            for index, out_ref in enumerate(refs[:-1]):
                source = gathered_ref.at[chip, pl.ds(index * part, part)]
                copies.append(pltpu.make_async_copy(source, out_ref.at[place], sem.at[len(copies)]))
        for copy in copies:
            copy.start()
        for copy in copies:
            copy.wait()

    return pl.pallas_call(
        kernel,
        in_specs=[pl.BlockSpec(memory_space=pltpu.SMEM), pl.BlockSpec(memory_space=pl.ANY)],
        out_specs=[pl.BlockSpec(memory_space=pltpu.VMEM)] * parts,
        out_shape=[pltpu.VMEM((len(steps), part, tokens), gathered.dtype)] * parts,
        scratch_shapes=[pltpu.SemaphoreType.DMA((len(steps) * parts,))],
    )(where, in_hbm(gathered))


def hidden_grads(where, token_rows, row_gate, gathered, weight):
    local_count, width_in, width = weight.shape
    slots = token_rows.shape[1]
    chips, half, tokens = gathered[0].shape
    depth = width_in // 2

    def kernel(where, token_ref, gate_ref, mine_ref, other_ref, weight_ref, out_ref, group_cot, sem):
        local = pl.program_id(0)

        @pl.when((local == 0) & (pl.program_id(1) == 0))
        def _():
            loads = []
            for side, ref in enumerate((mine_ref, other_ref)):
                for chip in range(chips):
                    start = (chip * CORES + jnp.bitwise_xor(where[1], side)) * half
                    rows = group_cot.at[pl.ds(pl.multiple_of(start, half), half)]
                    loads.append(pltpu.make_async_copy(ref.at[chip], rows, sem.at[len(loads)]))
            for load in loads:
                load.start()
            for load in loads:
                load.wait()

        sums = dot(weight_ref[0], group_cot[...], 1, 0).astype(jnp.bfloat16)
        hot = hot_rows(token_ref[local], gate_ref[local], tokens)
        out_ref[0] = dot(hot, sums, 0, 1).astype(jnp.bfloat16)

    return call(
        kernel,
        where,
        (local_count, width_in // depth),
        [whole((local_count, 1, slots))] * 2
        + [pl.BlockSpec(memory_space=pl.ANY)] * CORES
        + [pl.BlockSpec((1, depth, width), lambda e, h, where: (e, h, 0))],
        pl.BlockSpec((1, slots, depth), lambda e, h, where: (e, 0, h)),
        jax.ShapeDtypeStruct((local_count, slots, width_in), jnp.bfloat16),
        [pltpu.VMEM((width, tokens), jnp.bfloat16), pltpu.SemaphoreType.DMA((CORES * chips,))],
        (token_rows[:, None], row_gate[:, None], *map(in_hbm, gathered), in_hbm(weight)),
        28 * MIB,
    )


def group_products(where, shares, groups, refs, chip):
    total, at = None, 0
    for place, sides in groups:
        loaded = []
        for pieces in sides:
            loaded.append([ref[first + chip] for ref, (_, first) in zip(refs[at:], pieces)])
            at += len(pieces)
        mine, other = [jnp.concatenate(pieces, axis=0) if len(pieces) > 1 else pieces[0] for pieces in loaded]
        low = jnp.where(where[1] == 0, mine, other)
        high = jnp.where(where[1] == 0, other, mine)
        block = jnp.concatenate([low, high], axis=0)
        tokens = block.shape[1]
        product = dot(shares[:, place * tokens : (place + 1) * tokens], block, 1, 1)
        total = product if total is None else total + product
    return total


def halves(parts):
    return [(part, 0) for part in parts]


def weight_cols(
    where, first, count, shares, groups, local_count, width, gathered=None, so_far=None, passed=None, keep=False
):
    chips = lax.axis_size("expert") // CORES
    cols = width // chips
    share = shares.shape[0] // local_count
    flat = [array for _, sides in groups for pieces in sides for array, _ in pieces]
    tokens = flat[0].shape[-1]
    kept = (count, shares.shape[0], cols)
    distant = [*(gathered or []), *([] if so_far is None else [so_far])]

    def kernel(where, shares_ref, *refs):
        refs = list(refs)
        pieces = [refs.pop(0) for _ in flat]
        sources = [refs.pop(0) for _ in gathered or []]
        added = refs.pop(0) if so_far is not None else None
        if passed is not None:
            refs.pop(0)
        out_ref, total_ref, sem = refs[:3]
        refs = refs[3:]
        place = [lax.rem(where[0] + first + chip, chips) for chip in range(count)]
        loads, stores = [], []
        for chip in range(count):
            loads.append([])
            for side, source in enumerate(sources):
                target = refs[0].at[chip, jnp.bitwise_xor(where[1], side)]
                loads[chip].append(pltpu.make_async_copy(source.at[place[chip]], target, refs[1].at[chip, side]))
            if added is not None:
                loads[chip].append(pltpu.make_async_copy(added.at[first - 1 + chip], refs[-2].at[chip], refs[-1].at[chip]))
            for load in loads[chip]:
                load.start()
        for chip in range(count):
            total = group_products(where, shares_ref, groups, pieces, chip)
            for load in loads[chip]:
                load.wait()
            if sources:
                total = total + dot(shares_ref[:, :tokens], refs[0][chip].reshape(cols, tokens), 1, 1)
            if added is not None:
                total = total + refs[-2][chip].astype(jnp.float32)
            if keep:
                total_ref[chip] = total.astype(jnp.bfloat16)
                target = out_ref.at[chip]
            else:
                for local in range(local_count):
                    total_ref[chip, local] = total[local * share : (local + 1) * share]
                target = out_ref.at[:, :, pl.ds(pl.multiple_of(place[chip] * cols, LANES), cols)]
            stores.append(pltpu.make_async_copy(total_ref.at[chip], target, sem.at[chip]))
            stores[-1].start()
        for store in stores:
            store.wait()

    if keep:
        scratch = [pltpu.VMEM(kept, jnp.bfloat16)]
        out_shape = jax.ShapeDtypeStruct(kept, jnp.bfloat16)
    else:
        scratch = [pltpu.VMEM((count, local_count, share, cols), jnp.float32)]
        out_shape = jax.ShapeDtypeStruct((local_count, share, width), jnp.float32)
    scratch.append(pltpu.SemaphoreType.DMA((count,)))
    if gathered is not None:
        scratch += [pltpu.VMEM((count, CORES, cols // CORES, tokens), jnp.bfloat16)]
        scratch.append(pltpu.SemaphoreType.DMA((count, CORES)))
    if so_far is not None:
        scratch += [pltpu.VMEM(kept, jnp.bfloat16), pltpu.SemaphoreType.DMA((count,))]
    return resident(kernel, where, [shares, *flat], [out_shape], scratch, distant, passed)[0]


def planned_body(hidden, down_weight, cotangent, expert_ids, gate_weights, row_token, tile_count):
    local_count, width_in, width = down_weight.shape
    tokens = cotangent.shape[0]
    slots = hidden.shape[2]
    groups = lax.axis_size("dp")
    chips = lax.axis_size("expert") // CORES
    share = width_in // groups
    group = lax.axis_index("dp")
    expert_place = lax.axis_index("expert")
    chip = expert_place // CORES
    core = expert_place % CORES
    where = jnp.stack([chip, core])

    own = cotangent.T
    middle = own.shape[0] // 2
    gathered = exchanged(jnp.broadcast_to(own[None], (chips, *own.shape)))
    x_own, y_own = across_dp(own, 1), across_dp(own, 2)
    own_other = across_cores(own)

    slot_index = jnp.arange(slots, dtype=jnp.int32)
    token_index = jnp.arange(tokens, dtype=jnp.int32)
    live = (row_token[0] >= 0) & (slot_index[None] < tile_count[0][:, None] * TILE)
    token_rows = jnp.where(live, row_token[0], -1)
    experts = expert_place * local_count + jnp.arange(local_count, dtype=jnp.int32)
    named = expert_ids[None] == experts[:, None, None]
    token_gate = jnp.sum(jnp.where(named, gate_weights[None].astype(jnp.float32), 0.0), axis=2)
    at_token = token_rows[:, :, None] == token_index[None, None, :]
    row_gate = jnp.sum(jnp.where(at_token, token_gate[:, None, :], 0.0), axis=2)

    def as_rows(values):
        padded = jnp.pad(values.astype(jnp.bfloat16), ((0, 0), (0, 2 * share - slots)))
        return padded.reshape(local_count, 2, share)

    extra = jnp.concatenate(
        [as_rows(token_rows >> 1), as_rows(token_rows & 1), as_rows(row_gate)], axis=1
    )
    extra = jnp.pad(extra, ((0, 0), (0, EXTRA_ROWS - extra.shape[1]), (0, 0)))
    payloads = []
    for mask in range(groups):
        rows = lax.dynamic_slice_in_dim(hidden[0], (group ^ mask) * share, share, 2)
        payloads.append(jnp.concatenate([rows, extra], axis=1))
    x_own, y_own, own_other, token_rows, row_gate, *payloads = joined(
        x_own, y_own, own_other, token_rows, row_gate, *payloads
    )

    payloads = [across_dp(payload, mask) if mask else payload for mask, payload in enumerate(payloads)]
    far_own = [across_dp(x_own[:middle], 2), across_dp(y_own[middle:], 1)]
    keep, send = expert_sums(where, token_rows, row_gate, hidden[0], down_weight, tokens)
    x_own, y_own, keep, send, *sent = joined(x_own, y_own, keep, send, *far_own, *payloads)
    far_own, payloads = sent[:2], sent[2:]

    steps = list(range(1, chips))
    near = blocks_of(where, gathered, steps, 2)
    x_near, y_near = [None, None], [None, None]
    x_near[0], y_near[1] = across_dp(near[0], 1), across_dp(near[1], 2)
    x_near[1], y_near[0] = across_dp(near[1], 1), across_dp(near[0], 2)

    from_other = across_cores(send)
    shares = shares_by_token(where, payloads, slots, tokens)
    from_other, shares, x_own, y_own, *far_own = joined(from_other, shares, x_own, y_own, *far_own)
    sums = (keep.astype(jnp.float32) + from_other.astype(jnp.float32)).astype(jnp.bfloat16)
    mixed = exchanged(sums)
    own_far = jnp.stack([x_own, y_own, jnp.concatenate(far_own, axis=0)])
    own_far_other = across_cores(own_far)
    _, *gathered = joined(sums, gathered, across_cores(gathered))
    hidden_grad = hidden_grads(where, token_rows, row_gate, gathered, down_weight)
    hidden_grad, shares, _, *sent = joined(hidden_grad, shares, sums, *x_near, *y_near)
    x_near, y_near = sent[:2], sent[2:]

    rest = (local_count, width)
    far = [across_dp(x_near[0], 2), across_dp(y_near[1], 1)]
    x_other = [across_cores(part) for part in x_near]
    y_other = [across_cores(part) for part in y_near]
    own_groups = [(0, (halves([own[None]]), halves([own_other[None]])))]
    own_groups += [(place + 1, ([(own_far, place)], [(own_far_other, place)])) for place in range(groups - 1)]
    weight_grad = weight_cols(where, 0, 1, shares, own_groups, *rest)
    two = [(place, tuple(map(halves, pair))) for place, pair in ((1, (x_near, x_other)), (2, (y_near, y_other)))]
    so_far = weight_cols(where, 1, chips - 1, shares, two, *rest, gathered, keep=True)
    so_far, weight_grad, *far = joined(so_far, weight_grad, *far)
    last = [(groups - 1, (halves(far), halves([across_cores(part) for part in far])))]
    weight_grad = weight_cols(where, 1, chips - 1, shares, last, *rest, None, so_far, weight_grad)
    mixed = jnp.sum(mixed.astype(jnp.float32), axis=0).astype(jnp.bfloat16)
    return (mixed.T, hidden_grad[None], weight_grad)


def tile_products(rows_in, weight_mat, count, contract_dim):
    rows_cap = rows_in.shape[0]
    width_out = weight_mat.shape[1 - contract_dim]

    def one_tile(tile_index, outputs):
        block = lax.dynamic_slice_in_dim(rows_in, tile_index * TILE, TILE, 0)
        product = lax.dot_general(
            block,
            weight_mat,
            (((1,), (contract_dim,)), ((), ())),
            preferred_element_type=jnp.float32,
        )
        return lax.dynamic_update_slice_in_dim(
            outputs, product.astype(jnp.bfloat16), tile_index * TILE, 0
        )

    return lax.fori_loop(0, count, one_tile, jnp.zeros((rows_cap, width_out), jnp.bfloat16))


def general_body(hidden, down_weight, cotangent, expert_ids, gate_weights, row_token, tile_count):
    local_count = down_weight.shape[0]
    group_size = cotangent.shape[0]
    expert_index = jnp.arange(EXPERTS, dtype=jnp.int32)
    named_cols = expert_ids[:, :, None] == expert_index[None, None, :]
    gate_cols = jnp.sum(
        jnp.where(named_cols, gate_weights[:, :, None].astype(jnp.float32), 0.0), axis=1
    ).astype(jnp.bfloat16)
    group_cot = lax.all_gather(cotangent, "expert", axis=1, tiled=True)
    width = group_cot.shape[1]
    first_expert = lax.axis_index("expert") * local_count
    slot_index = jnp.arange(hidden.shape[2], dtype=jnp.int32)
    share_rows = down_weight.shape[1] // lax.axis_size("dp")
    partial_value = jnp.zeros((group_size, width), jnp.float32)
    grad_list = []
    weight_list = []
    for local in range(local_count):
        token_rows = row_token[0, local]
        count = tile_count[0, local]
        live_rows = (token_rows >= 0) & (slot_index < count * TILE)
        safe_rows = jnp.where(live_rows, token_rows, 0)
        column = lax.dynamic_index_in_dim(gate_cols, first_expert + local, 1, keepdims=False)
        row_gate = jnp.where(live_rows, column[safe_rows].astype(jnp.float32), 0.0)
        target = jnp.where(live_rows, token_rows, group_size)
        hidden_rows = hidden[0, local]
        weight_mat = down_weight[local]
        out_rows = tile_products(hidden_rows, weight_mat, count, 0)
        partial_value = partial_value.at[target].add(
            row_gate[:, None] * out_rows.astype(jnp.float32), mode="drop"
        )
        routed = (row_gate[:, None] * group_cot[safe_rows].astype(jnp.float32)).astype(jnp.bfloat16)
        grad_list.append(tile_products(routed, weight_mat, count, 1))

        def weight_rows(start, rows_count, hidden_rows=hidden_rows, routed_rows=routed):
            return lax.dot_general(
                hidden_rows,
                routed_rows,
                (((0,), (0,)), ((), ())),
                preferred_element_type=jnp.float32,
            )

        weight_list.append(
            lax.psum_scatter(
                weight_rows(jnp.int32(0), share_rows * lax.axis_size("dp")).astype(jnp.bfloat16),
                "dp",
                scatter_dimension=0,
                tiled=True,
            ).astype(jnp.float32)
        )
    merged = partial_value
    top_bit = lax.axis_size("expert").bit_length() - 1
    axis_index = lax.axis_index("expert")
    for bit_index in reversed(range(top_bit)):
        half_cols = merged.shape[1] // 2
        lower_half = merged[:, :half_cols]
        upper_half = merged[:, half_cols:]
        high_side = axis_index // 2**bit_index % 2 == 1
        sending = jnp.where(high_side, lower_half, upper_half)
        keeping = jnp.where(high_side, upper_half, lower_half)
        merged = keeping + swapped(sending.astype(jnp.bfloat16), "expert", bit_index).astype(
            sending.dtype
        )
    mixed_out = merged.astype(jnp.bfloat16)
    hidden_grad = jnp.stack(grad_list, axis=0)[None]
    weight_grad = jnp.stack(weight_list, axis=0)
    return (mixed_out, hidden_grad, weight_grad)


def solution(mesh):
    placed = (
        P("dp", "expert", None, None),
        P("expert", None, None),
        P("dp", "expert"),
        P("dp", None),
        P("dp", None),
        P("dp", "expert", None),
        P("dp", "expert"),
    )

    def body(*shards):
        width = shards[1].shape[2]
        chips = mesh.shape["expert"] // CORES
        fits = mesh.shape["dp"] == 4 and chips > 2 and width % (chips * LANES) == 0
        return planned_body(*shards) if fits else general_body(*shards)

    return jax.shard_map(
        body,
        mesh=mesh,
        in_specs=placed,
        out_specs=(P("dp", "expert"), P("dp", "expert", None, None), P("expert", "dp", None)),
        check_vma=False,
    )
```

```python
import jax
import jax.numpy as jnp
from jax import lax
from jax.experimental import pallas as pl
from jax.experimental.pallas import tpu as pltpu
from jax.sharding import PartitionSpec as P

EXPERTS = 16
TILE = 128
LANES = 128
CORES = 2
EXTRA_ROWS = 16
MIB = 1024 * 1024


def swapped(shard, axis, bit):
    return lax.ppermute(shard, axis, [(i, i ^ 1 << bit) for i in range(lax.axis_size(axis))])


def across_dp(shard, mask):
    return lax.ppermute(shard, "dp", [(i, i ^ mask) for i in range(lax.axis_size("dp"))])


def across_cores(shard):
    return swapped(shard, "expert", 0)


def z_lines():
    size = lax.axis_size("expert")
    return [list(range(core, size, CORES)) for core in range(CORES)]


def exchanged(parts):
    return lax.all_to_all(parts, "expert", 0, 0, axis_index_groups=z_lines(), tiled=True)


def joined(*values):
    return lax.optimization_barrier(values)


def dot(lhs, rhs, lhs_dim, rhs_dim):
    return lax.dot_general(
        lhs, rhs, (((lhs_dim,), (rhs_dim,)), ((), ())), preferred_element_type=jnp.float32
    )


def hot_rows(token_row, gate_row, tokens):
    slots = token_row.shape[1]
    token_index = lax.broadcasted_iota(jnp.int32, (tokens, slots), 0)
    spread = jnp.broadcast_to(gate_row, (tokens, slots))
    return jnp.where(token_index == token_row, spread, 0.0).astype(jnp.bfloat16)


def in_hbm(array):
    return pltpu.with_memory_space_constraint(array, pltpu.HBM)


def whole(shape):
    return pl.BlockSpec(shape, lambda *_: (0,) * len(shape))


def call(kernel, scalars, grid, in_specs, out_specs, out_shape, scratch, operands, vmem):
    return pl.pallas_call(
        kernel,
        grid_spec=pltpu.PrefetchScalarGridSpec(
            num_scalar_prefetch=1,
            grid=grid,
            in_specs=in_specs,
            out_specs=out_specs,
            scratch_shapes=scratch,
        ),
        out_shape=out_shape,
        compiler_params=pltpu.CompilerParams(
            dimension_semantics=("arbitrary",) * len(grid), vmem_limit_bytes=vmem
        ),
    )(scalars, *operands)


def expert_sums(where, token_rows, row_gate, hidden_rows, weight, tokens):
    local_count, slots, width_in = hidden_rows.shape
    chips = lax.axis_size("expert") // CORES
    cols = weight.shape[2] // chips
    half = cols // CORES

    def kernel(where, token_ref, gate_ref, hidden_ref, weight_ref, keep_ref, send_ref, by_token, turned):
        @pl.when(pl.program_id(0) == 0)
        def _():
            for local in range(local_count):
                hot = hot_rows(token_ref[local], gate_ref[local], tokens)
                made = dot(hot, hidden_ref[local], 1, 0).astype(jnp.bfloat16)
                by_token[:, local * width_in : (local + 1) * width_in] = made

        stacked = weight_ref[...].reshape(local_count * width_in, cols)
        turned[...] = dot(by_token[...], stacked, 1, 0).astype(jnp.bfloat16).T
        keep_ref[0] = turned[pl.ds(pl.multiple_of(where[1] * half, half), half), :]
        send_ref[0] = turned[pl.ds(pl.multiple_of((1 - where[1]) * half, half), half), :]

    shape = jax.ShapeDtypeStruct((chips, half, tokens), jnp.bfloat16)
    out_spec = pl.BlockSpec((1, half, tokens), lambda k, where: (k, 0, 0))
    return call(
        kernel,
        where,
        (chips,),
        [
            whole((local_count, 1, slots)),
            whole((local_count, 1, slots)),
            whole(hidden_rows.shape),
            pl.BlockSpec((local_count, width_in, cols), lambda k, where: (0, 0, k)),
        ],
        (out_spec, out_spec),
        (shape, shape),
        [
            pltpu.VMEM((tokens, local_count * width_in), jnp.bfloat16),
            pltpu.VMEM((cols, tokens), jnp.bfloat16),
        ],
        (token_rows[:, None], row_gate[:, None], hidden_rows, in_hbm(weight)),
        32 * MIB,
    )


def resident(kernel, scalars, operands, out_shapes, scratch=(), distant=(), passed=None):
    held = [pltpu.with_memory_space_constraint(array, pltpu.VMEM) for array in operands]
    in_vmem, anywhere = pl.BlockSpec(memory_space=pltpu.VMEM), pl.BlockSpec(memory_space=pl.ANY)
    far_off = [in_hbm(array) for array in distant] + ([] if passed is None else [passed])
    return pl.pallas_call(
        kernel,
        in_specs=[pl.BlockSpec(memory_space=pltpu.SMEM)] + [in_vmem] * len(held) + [anywhere] * len(far_off),
        out_specs=[in_vmem if shape.memory_space == pltpu.VMEM else anywhere for shape in out_shapes],
        out_shape=out_shapes,
        scratch_shapes=list(scratch),
        input_output_aliases={} if passed is None else {len(held) + len(far_off): 0},
        compiler_params=pltpu.CompilerParams(vmem_limit_bytes=20 * MIB),
    )(scalars, *held, *far_off)


def shares_by_token(where, payloads, slots, tokens):
    local_count, _, share = payloads[0].shape
    groups = len(payloads)

    def kernel(where, *refs):
        sources, (out_ref, held, sem) = refs[:groups], refs[groups:]
        loads = [pltpu.make_async_copy(ref, held.at[i], sem.at[i]) for i, ref in enumerate(sources)]
        for load in loads:
            load.start()

        def row(group, local, first):
            wide = [held[group, local, slots + first + i : slots + first + i + 1, :] for i in range(2)]
            return jnp.concatenate(wide, axis=1)[:, :slots].astype(jnp.float32)

        for group in range(groups):
            loads[group].wait()
            for local in range(local_count):
                token = (row(group, local, 0) * 2.0 + row(group, local, 2)).astype(jnp.int32)
                hot = hot_rows(token, row(group, local, 4), tokens)
                by_token = dot(hot, held[group, local, :slots, :], 1, 0).astype(jnp.bfloat16)
                out_ref[local * share : (local + 1) * share, group * tokens : (group + 1) * tokens] = by_token.T

    shape = (local_count * share, groups * tokens)
    scratch = [pltpu.VMEM((groups, *payloads[0].shape), jnp.bfloat16), pltpu.SemaphoreType.DMA((groups,))]
    return resident(kernel, where, [], [pltpu.VMEM(shape, jnp.bfloat16)], scratch, payloads)[0]


def blocks_of(where, gathered, steps, parts):
    chips, rows, tokens = gathered.shape
    part = rows // parts

    def kernel(where, gathered_ref, *refs):
        sem = refs[-1]
        copies = []
        for place, step in enumerate(steps):
            chip = lax.rem(where[0] + step, chips)
            for index, out_ref in enumerate(refs[:-1]):
                source = gathered_ref.at[chip, pl.ds(index * part, part)]
                copies.append(pltpu.make_async_copy(source, out_ref.at[place], sem.at[len(copies)]))
        for copy in copies:
            copy.start()
        for copy in copies:
            copy.wait()

    return pl.pallas_call(
        kernel,
        in_specs=[pl.BlockSpec(memory_space=pltpu.SMEM), pl.BlockSpec(memory_space=pl.ANY)],
        out_specs=[pl.BlockSpec(memory_space=pltpu.VMEM)] * parts,
        out_shape=[pltpu.VMEM((len(steps), part, tokens), gathered.dtype)] * parts,
        scratch_shapes=[pltpu.SemaphoreType.DMA((len(steps) * parts,))],
    )(where, in_hbm(gathered))


def hidden_grads(where, token_rows, row_gate, gathered, weight):
    local_count, width_in, width = weight.shape
    slots = token_rows.shape[1]
    chips, half, tokens = gathered[0].shape
    depth = width_in // 2

    def kernel(where, token_ref, gate_ref, mine_ref, other_ref, weight_ref, out_ref, group_cot, sem):
        local = pl.program_id(0)

        @pl.when((local == 0) & (pl.program_id(1) == 0))
        def _():
            loads = []
            for side, ref in enumerate((mine_ref, other_ref)):
                for chip in range(chips):
                    start = (chip * CORES + jnp.bitwise_xor(where[1], side)) * half
                    rows = group_cot.at[pl.ds(pl.multiple_of(start, half), half)]
                    loads.append(pltpu.make_async_copy(ref.at[chip], rows, sem.at[len(loads)]))
            for load in loads:
                load.start()
            for load in loads:
                load.wait()

        sums = dot(weight_ref[0], group_cot[...], 1, 0).astype(jnp.bfloat16)
        hot = hot_rows(token_ref[local], gate_ref[local], tokens)
        out_ref[0] = dot(hot, sums, 0, 1).astype(jnp.bfloat16)

    return call(
        kernel,
        where,
        (local_count, width_in // depth),
        [whole((local_count, 1, slots))] * 2
        + [pl.BlockSpec(memory_space=pl.ANY)] * CORES
        + [pl.BlockSpec((1, depth, width), lambda e, h, where: (e, h, 0))],
        pl.BlockSpec((1, slots, depth), lambda e, h, where: (e, 0, h)),
        jax.ShapeDtypeStruct((local_count, slots, width_in), jnp.bfloat16),
        [pltpu.VMEM((width, tokens), jnp.bfloat16), pltpu.SemaphoreType.DMA((CORES * chips,))],
        (token_rows[:, None], row_gate[:, None], *map(in_hbm, gathered), in_hbm(weight)),
        28 * MIB,
    )


def group_products(where, shares, groups, refs, chip):
    total, at = None, 0
    for place, sides in groups:
        loaded = []
        for pieces in sides:
            loaded.append([ref[first + chip] for ref, (_, first) in zip(refs[at:], pieces)])
            at += len(pieces)
        mine, other = [jnp.concatenate(pieces, axis=0) if len(pieces) > 1 else pieces[0] for pieces in loaded]
        low = jnp.where(where[1] == 0, mine, other)
        high = jnp.where(where[1] == 0, other, mine)
        block = jnp.concatenate([low, high], axis=0)
        tokens = block.shape[1]
        product = dot(shares[:, place * tokens : (place + 1) * tokens], block, 1, 1)
        total = product if total is None else total + product
    return total


def halves(parts):
    return [(part, 0) for part in parts]


def weight_cols(where, shares, own_groups, groups, local_count, width, gathered=None, so_far=None, passed=None):
    chips = lax.axis_size("expert") // CORES
    cols = width // chips
    half = cols // CORES
    share = shares.shape[0] // local_count
    own_flat, flat = [
        [array for _, sides in listed for pieces in sides for array, _ in pieces]
        for listed in (own_groups, groups)
    ]
    tokens = flat[0].shape[-1]
    count = chips - 1
    kept = (count, shares.shape[0], cols)
    distant = [so_far] if gathered is None else gathered
    stored = count if gathered is None else 1

    def kernel(where, shares_ref, *refs):
        refs = list(refs)
        own_pieces = [refs.pop(0) for _ in own_flat]
        pieces = [refs.pop(0) for _ in flat]
        sources = [refs.pop(0) for _ in distant]
        if passed is not None:
            refs.pop(0)
        out_ref = refs.pop(0)
        kept_ref = None if gathered is None else refs.pop(0)
        total_ref, total_sem, loaded_ref, load_sem = refs[:4]
        place = [lax.rem(where[0] + step, chips) for step in range(chips)]
        loads, stores = [], []
        for chip in range(count):
            if gathered is None:
                loads.append([pltpu.make_async_copy(sources[0].at[chip], loaded_ref.at[chip], load_sem.at[chip, 0])])
            else:
                loads.append([])
                for side, source in enumerate(sources):
                    target = loaded_ref.at[chip, jnp.bitwise_xor(where[1], side)]
                    loads[chip].append(
                        pltpu.make_async_copy(source.at[place[chip + 1]], target, load_sem.at[chip, side])
                    )
            for load in loads[chip]:
                load.start()

        def store(total, index, step):
            for local in range(local_count):
                total_ref[index, local] = total[local * share : (local + 1) * share]
            columns = pl.ds(pl.multiple_of(place[step] * cols, LANES), cols)
            stores.append(pltpu.make_async_copy(total_ref.at[index], out_ref.at[:, :, columns], total_sem.at[index]))
            stores[-1].start()

        if own_groups:
            store(group_products(where, shares_ref, own_groups, own_pieces, 0), 0, 0)
        for chip in range(count):
            total = group_products(where, shares_ref, groups, pieces, chip)
            for load in loads[chip]:
                load.wait()
            if gathered is None:
                store(total + loaded_ref[chip].astype(jnp.float32), chip, chip + 1)
                continue
            block = loaded_ref[chip].reshape(cols, tokens)
            staged_ref, staged_sem = refs[4:]
            staged_ref[chip] = (total + dot(shares_ref[:, :tokens], block, 1, 1)).astype(jnp.bfloat16)
            stores.append(pltpu.make_async_copy(staged_ref.at[chip], kept_ref.at[chip], staged_sem.at[chip]))
            stores[-1].start()
        for copy in stores:
            copy.wait()

    scratch = [
        pltpu.VMEM((stored, local_count, share, cols), jnp.float32),
        pltpu.SemaphoreType.DMA((stored,)),
        pltpu.VMEM(kept if gathered is None else (count, CORES, half, tokens), jnp.bfloat16),
        pltpu.SemaphoreType.DMA((count, CORES)),
    ]
    out_shapes = [pltpu.HBM((local_count, share, width), jnp.float32)]
    if gathered is not None:
        scratch += [pltpu.VMEM(kept, jnp.bfloat16), pltpu.SemaphoreType.DMA((count,))]
        out_shapes.append(pltpu.HBM(kept, jnp.bfloat16))
    return resident(kernel, where, [shares, *own_flat, *flat], out_shapes, scratch, distant, passed)


def planned_body(hidden, down_weight, cotangent, expert_ids, gate_weights, row_token, tile_count):
    local_count, width_in, width = down_weight.shape
    tokens = cotangent.shape[0]
    slots = hidden.shape[2]
    groups = lax.axis_size("dp")
    chips = lax.axis_size("expert") // CORES
    share = width_in // groups
    group = lax.axis_index("dp")
    expert_place = lax.axis_index("expert")
    chip = expert_place // CORES
    core = expert_place % CORES
    where = jnp.stack([chip, core])

    own = cotangent.T
    middle = own.shape[0] // 2
    gathered = exchanged(jnp.broadcast_to(own[None], (chips, *own.shape)))
    x_own, y_own = across_dp(own, 1), across_dp(own, 2)
    own_other = across_cores(own)

    slot_index = jnp.arange(slots, dtype=jnp.int32)
    token_index = jnp.arange(tokens, dtype=jnp.int32)
    live = (row_token[0] >= 0) & (slot_index[None] < tile_count[0][:, None] * TILE)
    token_rows = jnp.where(live, row_token[0], -1)
    experts = expert_place * local_count + jnp.arange(local_count, dtype=jnp.int32)
    named = expert_ids[None] == experts[:, None, None]
    token_gate = jnp.sum(jnp.where(named, gate_weights[None].astype(jnp.float32), 0.0), axis=2)
    at_token = token_rows[:, :, None] == token_index[None, None, :]
    row_gate = jnp.sum(jnp.where(at_token, token_gate[:, None, :], 0.0), axis=2)

    def as_rows(values):
        padded = jnp.pad(values.astype(jnp.bfloat16), ((0, 0), (0, 2 * share - slots)))
        return padded.reshape(local_count, 2, share)

    extra = jnp.concatenate(
        [as_rows(token_rows >> 1), as_rows(token_rows & 1), as_rows(row_gate)], axis=1
    )
    extra = jnp.pad(extra, ((0, 0), (0, EXTRA_ROWS - extra.shape[1]), (0, 0)))
    payloads = []
    for mask in range(groups):
        rows = lax.dynamic_slice_in_dim(hidden[0], (group ^ mask) * share, share, 2)
        payloads.append(jnp.concatenate([rows, extra], axis=1))
    x_own, y_own, own_other, token_rows, row_gate, *payloads = joined(
        x_own, y_own, own_other, token_rows, row_gate, *payloads
    )

    payloads = [across_dp(payload, mask) if mask else payload for mask, payload in enumerate(payloads)]
    far_own = [across_dp(x_own[:middle], 2), across_dp(y_own[middle:], 1)]
    keep, send = expert_sums(where, token_rows, row_gate, hidden[0], down_weight, tokens)
    x_own, y_own, keep, send, *sent = joined(x_own, y_own, keep, send, *far_own, *payloads)
    far_own, payloads = sent[:2], sent[2:]

    gathered, send = joined(gathered, send)
    steps = list(range(1, chips))
    near = blocks_of(where, gathered, steps, 2)
    x_near, y_near = [None, None], [None, None]
    x_near[0], y_near[1] = across_dp(near[0], 1), across_dp(near[1], 2)
    x_near[1], y_near[0] = across_dp(near[1], 1), across_dp(near[0], 2)

    from_other = across_cores(send)
    gathered_other = across_cores(gathered)
    gathered_other, from_other, *payloads = joined(gathered_other, from_other, *payloads)
    shares = shares_by_token(where, payloads, slots, tokens)
    from_other, shares = joined(from_other, shares)
    sums = (keep.astype(jnp.float32) + from_other.astype(jnp.float32)).astype(jnp.bfloat16)
    mixed = exchanged(sums)
    _, gathered_other, x_own, y_own, *far_own = joined(sums, gathered_other, x_own, y_own, *far_own)
    gathered = [gathered, gathered_other]
    own_far = jnp.stack([x_own, y_own, jnp.concatenate(far_own, axis=0)])
    own_far_other = across_cores(own_far)
    hidden_grad = hidden_grads(where, token_rows, row_gate, gathered, down_weight)
    hidden_grad, shares, _, *sent = joined(hidden_grad, shares, sums, *x_near, *y_near)
    x_near, y_near = sent[:2], sent[2:]

    rest = (local_count, width)
    far = [across_dp(x_near[0], 2), across_dp(y_near[1], 1)]
    x_other = [across_cores(part) for part in x_near]
    y_other = [across_cores(part) for part in y_near]
    own_groups = [(0, (halves([own[None]]), halves([own_other[None]])))]
    own_groups += [(place + 1, ([(own_far, place)], [(own_far_other, place)])) for place in range(groups - 1)]
    two = [(place, tuple(map(halves, pair))) for place, pair in ((1, (x_near, x_other)), (2, (y_near, y_other)))]
    weight_grad, so_far = weight_cols(where, shares, own_groups, two, *rest, gathered)
    so_far, weight_grad, *far = joined(so_far, weight_grad, *far)
    last = [(groups - 1, (halves(far), halves([across_cores(part) for part in far])))]
    weight_grad = weight_cols(where, shares, [], last, *rest, None, so_far, weight_grad)[0]
    mixed = jnp.sum(mixed.astype(jnp.float32), axis=0).astype(jnp.bfloat16)
    return (mixed.T, hidden_grad[None], weight_grad)


def tile_products(rows_in, weight_mat, count, contract_dim):
    rows_cap = rows_in.shape[0]
    width_out = weight_mat.shape[1 - contract_dim]

    def one_tile(tile_index, outputs):
        block = lax.dynamic_slice_in_dim(rows_in, tile_index * TILE, TILE, 0)
        product = lax.dot_general(
            block,
            weight_mat,
            (((1,), (contract_dim,)), ((), ())),
            preferred_element_type=jnp.float32,
        )
        return lax.dynamic_update_slice_in_dim(
            outputs, product.astype(jnp.bfloat16), tile_index * TILE, 0
        )

    return lax.fori_loop(0, count, one_tile, jnp.zeros((rows_cap, width_out), jnp.bfloat16))


def general_body(hidden, down_weight, cotangent, expert_ids, gate_weights, row_token, tile_count):
    local_count = down_weight.shape[0]
    group_size = cotangent.shape[0]
    expert_index = jnp.arange(EXPERTS, dtype=jnp.int32)
    named_cols = expert_ids[:, :, None] == expert_index[None, None, :]
    gate_cols = jnp.sum(
        jnp.where(named_cols, gate_weights[:, :, None].astype(jnp.float32), 0.0), axis=1
    ).astype(jnp.bfloat16)
    group_cot = lax.all_gather(cotangent, "expert", axis=1, tiled=True)
    width = group_cot.shape[1]
    first_expert = lax.axis_index("expert") * local_count
    slot_index = jnp.arange(hidden.shape[2], dtype=jnp.int32)
    share_rows = down_weight.shape[1] // lax.axis_size("dp")
    partial_value = jnp.zeros((group_size, width), jnp.float32)
    grad_list = []
    weight_list = []
    for local in range(local_count):
        token_rows = row_token[0, local]
        count = tile_count[0, local]
        live_rows = (token_rows >= 0) & (slot_index < count * TILE)
        safe_rows = jnp.where(live_rows, token_rows, 0)
        column = lax.dynamic_index_in_dim(gate_cols, first_expert + local, 1, keepdims=False)
        row_gate = jnp.where(live_rows, column[safe_rows].astype(jnp.float32), 0.0)
        target = jnp.where(live_rows, token_rows, group_size)
        hidden_rows = hidden[0, local]
        weight_mat = down_weight[local]
        out_rows = tile_products(hidden_rows, weight_mat, count, 0)
        partial_value = partial_value.at[target].add(
            row_gate[:, None] * out_rows.astype(jnp.float32), mode="drop"
        )
        routed = (row_gate[:, None] * group_cot[safe_rows].astype(jnp.float32)).astype(jnp.bfloat16)
        grad_list.append(tile_products(routed, weight_mat, count, 1))

        def weight_rows(start, rows_count, hidden_rows=hidden_rows, routed_rows=routed):
            return lax.dot_general(
                hidden_rows,
                routed_rows,
                (((0,), (0,)), ((), ())),
                preferred_element_type=jnp.float32,
            )

        weight_list.append(
            lax.psum_scatter(
                weight_rows(jnp.int32(0), share_rows * lax.axis_size("dp")).astype(jnp.bfloat16),
                "dp",
                scatter_dimension=0,
                tiled=True,
            ).astype(jnp.float32)
        )
    merged = partial_value
    top_bit = lax.axis_size("expert").bit_length() - 1
    axis_index = lax.axis_index("expert")
    for bit_index in reversed(range(top_bit)):
        half_cols = merged.shape[1] // 2
        lower_half = merged[:, :half_cols]
        upper_half = merged[:, half_cols:]
        high_side = axis_index // 2**bit_index % 2 == 1
        sending = jnp.where(high_side, lower_half, upper_half)
        keeping = jnp.where(high_side, upper_half, lower_half)
        merged = keeping + swapped(sending.astype(jnp.bfloat16), "expert", bit_index).astype(
            sending.dtype
        )
    mixed_out = merged.astype(jnp.bfloat16)
    hidden_grad = jnp.stack(grad_list, axis=0)[None]
    weight_grad = jnp.stack(weight_list, axis=0)
    return (mixed_out, hidden_grad, weight_grad)


def solution(mesh):
    placed = (
        P("dp", "expert", None, None),
        P("expert", None, None),
        P("dp", "expert"),
        P("dp", None),
        P("dp", None),
        P("dp", "expert", None),
        P("dp", "expert"),
    )

    def body(*shards):
        width = shards[1].shape[2]
        chips = mesh.shape["expert"] // CORES
        fits = mesh.shape["dp"] == 4 and chips > 2 and width % (chips * LANES) == 0
        return planned_body(*shards) if fits else general_body(*shards)

    return jax.shard_map(
        body,
        mesh=mesh,
        in_specs=placed,
        out_specs=(P("dp", "expert"), P("dp", "expert", None, None), P("expert", "dp", None)),
        check_vma=False,
    )
```

```python
import jax
import jax.numpy as jnp
from jax import lax
from jax.experimental import pallas as pl
from jax.experimental.pallas import tpu as pltpu
from jax.sharding import PartitionSpec as P

EXPERTS = 16
TILE = 128
LANES = 128
CORES = 2
EXTRA_ROWS = 16
MIB = 1024 * 1024


def swapped(shard, axis, bit):
    return lax.ppermute(shard, axis, [(i, i ^ 1 << bit) for i in range(lax.axis_size(axis))])


def across_dp(shard, mask):
    return lax.ppermute(shard, "dp", [(i, i ^ mask) for i in range(lax.axis_size("dp"))])


def across_cores(shard):
    return swapped(shard, "expert", 0)


def z_lines():
    size = lax.axis_size("expert")
    return [list(range(core, size, CORES)) for core in range(CORES)]


def exchanged(parts):
    return lax.all_to_all(parts, "expert", 0, 0, axis_index_groups=z_lines(), tiled=True)


def joined(*values):
    return lax.optimization_barrier(values)


def dot(lhs, rhs, lhs_dim, rhs_dim):
    return lax.dot_general(
        lhs, rhs, (((lhs_dim,), (rhs_dim,)), ((), ())), preferred_element_type=jnp.float32
    )


def hot_rows(token_row, gate_row, tokens):
    slots = token_row.shape[1]
    token_index = lax.broadcasted_iota(jnp.int32, (tokens, slots), 0)
    spread = jnp.broadcast_to(gate_row, (tokens, slots))
    return jnp.where(token_index == token_row, spread, 0.0).astype(jnp.bfloat16)


def in_hbm(array):
    return pltpu.with_memory_space_constraint(array, pltpu.HBM)


def whole(shape):
    return pl.BlockSpec(shape, lambda *_: (0,) * len(shape))


def call(kernel, scalars, grid, in_specs, out_specs, out_shape, scratch, operands, vmem):
    return pl.pallas_call(
        kernel,
        grid_spec=pltpu.PrefetchScalarGridSpec(
            num_scalar_prefetch=1,
            grid=grid,
            in_specs=in_specs,
            out_specs=out_specs,
            scratch_shapes=scratch,
        ),
        out_shape=out_shape,
        compiler_params=pltpu.CompilerParams(
            dimension_semantics=("arbitrary",) * len(grid), vmem_limit_bytes=vmem
        ),
    )(scalars, *operands)


def expert_sums(where, token_rows, row_gate, hidden_rows, weight, tokens):
    local_count, slots, width_in = hidden_rows.shape
    chips = lax.axis_size("expert") // CORES
    cols = weight.shape[2] // chips
    half = cols // CORES

    def kernel(where, token_ref, gate_ref, hidden_ref, weight_ref, keep_ref, send_ref, by_token, turned):
        @pl.when(pl.program_id(0) == 0)
        def _():
            for local in range(local_count):
                hot = hot_rows(token_ref[local], gate_ref[local], tokens)
                made = dot(hot, hidden_ref[local], 1, 0).astype(jnp.bfloat16)
                by_token[:, local * width_in : (local + 1) * width_in] = made

        stacked = weight_ref[...].reshape(local_count * width_in, cols)
        turned[...] = dot(by_token[...], stacked, 1, 0).astype(jnp.bfloat16).T
        keep_ref[0] = turned[pl.ds(pl.multiple_of(where[1] * half, half), half), :]
        send_ref[0] = turned[pl.ds(pl.multiple_of((1 - where[1]) * half, half), half), :]

    shape = jax.ShapeDtypeStruct((chips, half, tokens), jnp.bfloat16)
    out_spec = pl.BlockSpec((1, half, tokens), lambda k, where: (k, 0, 0))
    return call(
        kernel,
        where,
        (chips,),
        [
            whole((local_count, 1, slots)),
            whole((local_count, 1, slots)),
            whole(hidden_rows.shape),
            pl.BlockSpec((local_count, width_in, cols), lambda k, where: (0, 0, k)),
        ],
        (out_spec, out_spec),
        (shape, shape),
        [
            pltpu.VMEM((tokens, local_count * width_in), jnp.bfloat16),
            pltpu.VMEM((cols, tokens), jnp.bfloat16),
        ],
        (token_rows[:, None], row_gate[:, None], hidden_rows, in_hbm(weight)),
        32 * MIB,
    )


def resident(kernel, scalars, operands, out_shapes, scratch=(), distant=(), passed=None):
    held = [pltpu.with_memory_space_constraint(array, pltpu.VMEM) for array in operands]
    in_vmem, anywhere = pl.BlockSpec(memory_space=pltpu.VMEM), pl.BlockSpec(memory_space=pl.ANY)
    far_off = [in_hbm(array) for array in distant] + ([] if passed is None else [passed])
    return pl.pallas_call(
        kernel,
        in_specs=[pl.BlockSpec(memory_space=pltpu.SMEM)] + [in_vmem] * len(held) + [anywhere] * len(far_off),
        out_specs=[in_vmem if shape.memory_space == pltpu.VMEM else anywhere for shape in out_shapes],
        out_shape=out_shapes,
        scratch_shapes=list(scratch),
        input_output_aliases={} if passed is None else {len(held) + len(far_off): 0},
        compiler_params=pltpu.CompilerParams(vmem_limit_bytes=20 * MIB),
    )(scalars, *held, *far_off)


def shares_by_token(where, payloads, slots, tokens):
    local_count, _, share = payloads[0].shape
    groups = len(payloads)

    def kernel(where, *refs):
        sources, (out_ref, held, sem) = refs[:groups], refs[groups:]
        loads = [pltpu.make_async_copy(ref, held.at[i], sem.at[i]) for i, ref in enumerate(sources)]
        for load in loads:
            load.start()

        def row(group, local, first):
            wide = [held[group, local, slots + first + i : slots + first + i + 1, :] for i in range(2)]
            return jnp.concatenate(wide, axis=1)[:, :slots].astype(jnp.float32)

        for group in range(groups):
            loads[group].wait()
            for local in range(local_count):
                token = (row(group, local, 0) * 2.0 + row(group, local, 2)).astype(jnp.int32)
                hot = hot_rows(token, row(group, local, 4), tokens)
                by_token = dot(hot, held[group, local, :slots, :], 1, 0).astype(jnp.bfloat16)
                out_ref[local * share : (local + 1) * share, group * tokens : (group + 1) * tokens] = by_token.T

    shape = (local_count * share, groups * tokens)
    scratch = [pltpu.VMEM((groups, *payloads[0].shape), jnp.bfloat16), pltpu.SemaphoreType.DMA((groups,))]
    return resident(kernel, where, [], [pltpu.VMEM(shape, jnp.bfloat16)], scratch, payloads)[0]


def blocks_of(where, gathered, steps, parts):
    chips, rows, tokens = gathered.shape
    part = rows // parts

    def kernel(where, gathered_ref, *refs):
        sem = refs[-1]
        copies = []
        for place, step in enumerate(steps):
            chip = lax.rem(where[0] + step, chips)
            for index, out_ref in enumerate(refs[:-1]):
                source = gathered_ref.at[chip, pl.ds(index * part, part)]
                copies.append(pltpu.make_async_copy(source, out_ref.at[place], sem.at[len(copies)]))
        for copy in copies:
            copy.start()
        for copy in copies:
            copy.wait()

    return pl.pallas_call(
        kernel,
        in_specs=[pl.BlockSpec(memory_space=pltpu.SMEM), pl.BlockSpec(memory_space=pl.ANY)],
        out_specs=[pl.BlockSpec(memory_space=pltpu.VMEM)] * parts,
        out_shape=[pltpu.VMEM((len(steps), part, tokens), gathered.dtype)] * parts,
        scratch_shapes=[pltpu.SemaphoreType.DMA((len(steps) * parts,))],
    )(where, in_hbm(gathered))


def hidden_grads(where, token_rows, row_gate, gathered, weight):
    local_count, width_in, width = weight.shape
    slots = token_rows.shape[1]
    chips, half, tokens = gathered[0].shape
    depth = width_in // 2

    def kernel(where, token_ref, gate_ref, mine_ref, other_ref, weight_ref, out_ref, group_cot, sem):
        local = pl.program_id(0)

        @pl.when((local == 0) & (pl.program_id(1) == 0))
        def _():
            loads = []
            for side, ref in enumerate((mine_ref, other_ref)):
                for chip in range(chips):
                    start = (chip * CORES + jnp.bitwise_xor(where[1], side)) * half
                    rows = group_cot.at[pl.ds(pl.multiple_of(start, half), half)]
                    loads.append(pltpu.make_async_copy(ref.at[chip], rows, sem.at[len(loads)]))
            for load in loads:
                load.start()
            for load in loads:
                load.wait()

        sums = dot(weight_ref[0], group_cot[...], 1, 0).astype(jnp.bfloat16)
        hot = hot_rows(token_ref[local], gate_ref[local], tokens)
        out_ref[0] = dot(hot, sums, 0, 1).astype(jnp.bfloat16)

    return call(
        kernel,
        where,
        (local_count, width_in // depth),
        [whole((local_count, 1, slots))] * 2
        + [pl.BlockSpec(memory_space=pl.ANY)] * CORES
        + [pl.BlockSpec((1, depth, width), lambda e, h, where: (e, h, 0))],
        pl.BlockSpec((1, slots, depth), lambda e, h, where: (e, 0, h)),
        jax.ShapeDtypeStruct((local_count, slots, width_in), jnp.bfloat16),
        [pltpu.VMEM((width, tokens), jnp.bfloat16), pltpu.SemaphoreType.DMA((CORES * chips,))],
        (token_rows[:, None], row_gate[:, None], *map(in_hbm, gathered), in_hbm(weight)),
        28 * MIB,
    )


def group_products(where, shares, groups, refs, chip):
    total, at = None, 0
    for place, sides in groups:
        loaded = []
        for pieces in sides:
            loaded.append([ref[first + chip] for ref, (_, first) in zip(refs[at:], pieces)])
            at += len(pieces)
        mine, other = [jnp.concatenate(pieces, axis=0) if len(pieces) > 1 else pieces[0] for pieces in loaded]
        low = jnp.where(where[1] == 0, mine, other)
        high = jnp.where(where[1] == 0, other, mine)
        block = jnp.concatenate([low, high], axis=0)
        tokens = block.shape[1]
        product = dot(shares[:, place * tokens : (place + 1) * tokens], block, 1, 1)
        total = product if total is None else total + product
    return total


def halves(parts):
    return [(part, 0) for part in parts]


def weight_cols(where, shares, own_groups, groups, local_count, width, gathered=None, so_far=None, passed=None):
    chips = lax.axis_size("expert") // CORES
    cols = width // chips
    half = cols // CORES
    share = shares.shape[0] // local_count
    own_flat, flat = [
        [array for _, sides in listed for pieces in sides for array, _ in pieces]
        for listed in (own_groups, groups)
    ]
    tokens = flat[0].shape[-1]
    count = chips - 1
    kept = (count, shares.shape[0], cols)
    distant = [so_far] if gathered is None else gathered
    stored = count if gathered is None else 1

    def kernel(where, shares_ref, *refs):
        refs = list(refs)
        own_pieces = [refs.pop(0) for _ in own_flat]
        pieces = [refs.pop(0) for _ in flat]
        sources = [refs.pop(0) for _ in distant]
        if passed is not None:
            refs.pop(0)
        out_ref = refs.pop(0)
        kept_ref = None if gathered is None else refs.pop(0)
        total_ref, total_sem, loaded_ref, load_sem = refs[:4]
        place = [lax.rem(where[0] + step, chips) for step in range(chips)]
        loads, stores = [], []
        for chip in range(count):
            if gathered is None:
                loads.append([pltpu.make_async_copy(sources[0].at[chip], loaded_ref.at[chip], load_sem.at[chip, 0])])
            else:
                loads.append([])
                for side, source in enumerate(sources):
                    target = loaded_ref.at[chip, jnp.bitwise_xor(where[1], side)]
                    loads[chip].append(
                        pltpu.make_async_copy(source.at[place[chip + 1]], target, load_sem.at[chip, side])
                    )
            for load in loads[chip]:
                load.start()

        def store(total, index, step):
            for local in range(local_count):
                total_ref[index, local] = total[local * share : (local + 1) * share]
            columns = pl.ds(pl.multiple_of(place[step] * cols, LANES), cols)
            stores.append(pltpu.make_async_copy(total_ref.at[index], out_ref.at[:, :, columns], total_sem.at[index]))
            stores[-1].start()

        if own_groups:
            store(group_products(where, shares_ref, own_groups, own_pieces, 0), 0, 0)
        for chip in range(count):
            total = group_products(where, shares_ref, groups, pieces, chip)
            for load in loads[chip]:
                load.wait()
            if gathered is None:
                store(total + loaded_ref[chip].astype(jnp.float32), chip, chip + 1)
                continue
            block = loaded_ref[chip].reshape(cols, tokens)
            staged_ref, staged_sem = refs[4:]
            staged_ref[chip] = (total + dot(shares_ref[:, :tokens], block, 1, 1)).astype(jnp.bfloat16)
            stores.append(pltpu.make_async_copy(staged_ref.at[chip], kept_ref.at[chip], staged_sem.at[chip]))
            stores[-1].start()
        for copy in stores:
            copy.wait()

    scratch = [
        pltpu.VMEM((stored, local_count, share, cols), jnp.float32),
        pltpu.SemaphoreType.DMA((stored,)),
        pltpu.VMEM(kept if gathered is None else (count, CORES, half, tokens), jnp.bfloat16),
        pltpu.SemaphoreType.DMA((count, CORES)),
    ]
    out_shapes = [pltpu.HBM((local_count, share, width), jnp.float32)]
    if gathered is not None:
        scratch += [pltpu.VMEM(kept, jnp.bfloat16), pltpu.SemaphoreType.DMA((count,))]
        out_shapes.append(pltpu.HBM(kept, jnp.bfloat16))
    return resident(kernel, where, [shares, *own_flat, *flat], out_shapes, scratch, distant, passed)


def planned_body(hidden, down_weight, cotangent, expert_ids, gate_weights, row_token, tile_count):
    local_count, width_in, width = down_weight.shape
    tokens = cotangent.shape[0]
    slots = hidden.shape[2]
    groups = lax.axis_size("dp")
    chips = lax.axis_size("expert") // CORES
    share = width_in // groups
    group = lax.axis_index("dp")
    expert_place = lax.axis_index("expert")
    chip = expert_place // CORES
    core = expert_place % CORES
    where = jnp.stack([chip, core])

    own = cotangent.T
    middle = own.shape[0] // 2
    gathered = exchanged(jnp.broadcast_to(own[None], (chips, *own.shape)))
    x_own, y_own = across_dp(own, 1), across_dp(own, 2)
    own_other = across_cores(own)

    slot_index = jnp.arange(slots, dtype=jnp.int32)
    token_index = jnp.arange(tokens, dtype=jnp.int32)
    live = (row_token[0] >= 0) & (slot_index[None] < tile_count[0][:, None] * TILE)
    token_rows = jnp.where(live, row_token[0], -1)
    experts = expert_place * local_count + jnp.arange(local_count, dtype=jnp.int32)
    named = expert_ids[None] == experts[:, None, None]
    token_gate = jnp.sum(jnp.where(named, gate_weights[None].astype(jnp.float32), 0.0), axis=2)
    at_token = token_rows[:, :, None] == token_index[None, None, :]
    row_gate = jnp.sum(jnp.where(at_token, token_gate[:, None, :], 0.0), axis=2)

    def as_rows(values):
        padded = jnp.pad(values.astype(jnp.bfloat16), ((0, 0), (0, 2 * share - slots)))
        return padded.reshape(local_count, 2, share)

    extra = jnp.concatenate(
        [as_rows(token_rows >> 1), as_rows(token_rows & 1), as_rows(row_gate)], axis=1
    )
    extra = jnp.pad(extra, ((0, 0), (0, EXTRA_ROWS - extra.shape[1]), (0, 0)))
    payloads = []
    for mask in range(groups):
        rows = lax.dynamic_slice_in_dim(hidden[0], (group ^ mask) * share, share, 2)
        payloads.append(jnp.concatenate([rows, extra], axis=1))
    x_own, y_own, own_other, token_rows, row_gate, *payloads = joined(
        x_own, y_own, own_other, token_rows, row_gate, *payloads
    )

    payloads = [across_dp(payload, mask) if mask else payload for mask, payload in enumerate(payloads)]
    far_own = [across_dp(x_own[:middle], 2), across_dp(y_own[middle:], 1)]
    keep, send = expert_sums(where, token_rows, row_gate, hidden[0], down_weight, tokens)
    x_own, y_own, keep, send, *sent = joined(x_own, y_own, keep, send, *far_own, *payloads)
    far_own, payloads = sent[:2], sent[2:]

    own_far = jnp.stack([x_own, y_own, jnp.concatenate(far_own, axis=0)])
    gathered, send, own_far = joined(gathered, send, own_far)
    own_far_other = across_cores(own_far)
    steps = list(range(1, chips))
    near = blocks_of(where, gathered, steps, 2)
    x_near, y_near = [None, None], [None, None]
    x_near[0], y_near[1] = across_dp(near[0], 1), across_dp(near[1], 2)
    x_near[1], y_near[0] = across_dp(near[1], 1), across_dp(near[0], 2)

    from_other = across_cores(send)
    gathered_other = across_cores(gathered)
    gathered_other, from_other, *payloads = joined(gathered_other, from_other, *payloads)
    shares = shares_by_token(where, payloads, slots, tokens)
    from_other, shares = joined(from_other, shares)
    sums = (keep.astype(jnp.float32) + from_other.astype(jnp.float32)).astype(jnp.bfloat16)
    mixed = exchanged(sums)
    _, gathered_other = joined(sums, gathered_other)
    gathered = [gathered, gathered_other]
    hidden_grad = hidden_grads(where, token_rows, row_gate, gathered, down_weight)
    hidden_grad, shares, own_far_other, _, *sent = joined(
        hidden_grad, shares, own_far_other, sums, *x_near, *y_near
    )
    x_near, y_near = sent[:2], sent[2:]

    rest = (local_count, width)
    far = [across_dp(x_near[0], 2), across_dp(y_near[1], 1)]
    x_other = [across_cores(part) for part in x_near]
    y_other = [across_cores(part) for part in y_near]
    own_groups = [(0, (halves([own[None]]), halves([own_other[None]])))]
    own_groups += [(place + 1, ([(own_far, place)], [(own_far_other, place)])) for place in range(groups - 1)]
    two = [(place, tuple(map(halves, pair))) for place, pair in ((1, (x_near, x_other)), (2, (y_near, y_other)))]
    weight_grad, so_far = weight_cols(where, shares, own_groups, two, *rest, gathered)
    so_far, weight_grad, *far = joined(so_far, weight_grad, *far)
    mixed = jnp.sum(mixed.astype(jnp.float32), axis=0).astype(jnp.bfloat16)
    mixed, *far_other = joined(mixed, *[across_cores(part) for part in far])
    last = [(groups - 1, (halves(far), halves(far_other)))]
    weight_grad = weight_cols(where, shares, [], last, *rest, None, so_far, weight_grad)[0]
    return (mixed.T, hidden_grad[None], weight_grad)


def tile_products(rows_in, weight_mat, count, contract_dim):
    rows_cap = rows_in.shape[0]
    width_out = weight_mat.shape[1 - contract_dim]

    def one_tile(tile_index, outputs):
        block = lax.dynamic_slice_in_dim(rows_in, tile_index * TILE, TILE, 0)
        product = lax.dot_general(
            block,
            weight_mat,
            (((1,), (contract_dim,)), ((), ())),
            preferred_element_type=jnp.float32,
        )
        return lax.dynamic_update_slice_in_dim(
            outputs, product.astype(jnp.bfloat16), tile_index * TILE, 0
        )

    return lax.fori_loop(0, count, one_tile, jnp.zeros((rows_cap, width_out), jnp.bfloat16))


def general_body(hidden, down_weight, cotangent, expert_ids, gate_weights, row_token, tile_count):
    local_count = down_weight.shape[0]
    group_size = cotangent.shape[0]
    expert_index = jnp.arange(EXPERTS, dtype=jnp.int32)
    named_cols = expert_ids[:, :, None] == expert_index[None, None, :]
    gate_cols = jnp.sum(
        jnp.where(named_cols, gate_weights[:, :, None].astype(jnp.float32), 0.0), axis=1
    ).astype(jnp.bfloat16)
    group_cot = lax.all_gather(cotangent, "expert", axis=1, tiled=True)
    width = group_cot.shape[1]
    first_expert = lax.axis_index("expert") * local_count
    slot_index = jnp.arange(hidden.shape[2], dtype=jnp.int32)
    share_rows = down_weight.shape[1] // lax.axis_size("dp")
    partial_value = jnp.zeros((group_size, width), jnp.float32)
    grad_list = []
    weight_list = []
    for local in range(local_count):
        token_rows = row_token[0, local]
        count = tile_count[0, local]
        live_rows = (token_rows >= 0) & (slot_index < count * TILE)
        safe_rows = jnp.where(live_rows, token_rows, 0)
        column = lax.dynamic_index_in_dim(gate_cols, first_expert + local, 1, keepdims=False)
        row_gate = jnp.where(live_rows, column[safe_rows].astype(jnp.float32), 0.0)
        target = jnp.where(live_rows, token_rows, group_size)
        hidden_rows = hidden[0, local]
        weight_mat = down_weight[local]
        out_rows = tile_products(hidden_rows, weight_mat, count, 0)
        partial_value = partial_value.at[target].add(
            row_gate[:, None] * out_rows.astype(jnp.float32), mode="drop"
        )
        routed = (row_gate[:, None] * group_cot[safe_rows].astype(jnp.float32)).astype(jnp.bfloat16)
        grad_list.append(tile_products(routed, weight_mat, count, 1))

        def weight_rows(start, rows_count, hidden_rows=hidden_rows, routed_rows=routed):
            return lax.dot_general(
                hidden_rows,
                routed_rows,
                (((0,), (0,)), ((), ())),
                preferred_element_type=jnp.float32,
            )

        weight_list.append(
            lax.psum_scatter(
                weight_rows(jnp.int32(0), share_rows * lax.axis_size("dp")).astype(jnp.bfloat16),
                "dp",
                scatter_dimension=0,
                tiled=True,
            ).astype(jnp.float32)
        )
    merged = partial_value
    top_bit = lax.axis_size("expert").bit_length() - 1
    axis_index = lax.axis_index("expert")
    for bit_index in reversed(range(top_bit)):
        half_cols = merged.shape[1] // 2
        lower_half = merged[:, :half_cols]
        upper_half = merged[:, half_cols:]
        high_side = axis_index // 2**bit_index % 2 == 1
        sending = jnp.where(high_side, lower_half, upper_half)
        keeping = jnp.where(high_side, upper_half, lower_half)
        merged = keeping + swapped(sending.astype(jnp.bfloat16), "expert", bit_index).astype(
            sending.dtype
        )
    mixed_out = merged.astype(jnp.bfloat16)
    hidden_grad = jnp.stack(grad_list, axis=0)[None]
    weight_grad = jnp.stack(weight_list, axis=0)
    return (mixed_out, hidden_grad, weight_grad)


def solution(mesh):
    placed = (
        P("dp", "expert", None, None),
        P("expert", None, None),
        P("dp", "expert"),
        P("dp", None),
        P("dp", None),
        P("dp", "expert", None),
        P("dp", "expert"),
    )

    def body(*shards):
        width = shards[1].shape[2]
        chips = mesh.shape["expert"] // CORES
        fits = mesh.shape["dp"] == 4 and chips > 2 and width % (chips * LANES) == 0
        return planned_body(*shards) if fits else general_body(*shards)

    return jax.shard_map(
        body,
        mesh=mesh,
        in_specs=placed,
        out_specs=(P("dp", "expert"), P("dp", "expert", None, None), P("expert", "dp", None)),
        check_vma=False,
    )
```

```python
import jax
import jax.numpy as jnp
from jax import lax
from jax.experimental import pallas as pl
from jax.experimental.pallas import tpu as pltpu
from jax.sharding import PartitionSpec as P

EXPERTS = 16
TILE = 128
LANES = 128
CORES = 2
EXTRA_ROWS = 16
MIB = 1024 * 1024


def swapped(shard, axis, bit):
    return lax.ppermute(shard, axis, [(i, i ^ 1 << bit) for i in range(lax.axis_size(axis))])


def across_dp(shard, mask):
    return lax.ppermute(shard, "dp", [(i, i ^ mask) for i in range(lax.axis_size("dp"))])


def across_cores(shard):
    return swapped(shard, "expert", 0)


def z_lines():
    size = lax.axis_size("expert")
    return [list(range(core, size, CORES)) for core in range(CORES)]


def exchanged(parts):
    return lax.all_to_all(parts, "expert", 0, 0, axis_index_groups=z_lines(), tiled=True)


def joined(*values):
    return lax.optimization_barrier(values)


def dot(lhs, rhs, lhs_dim, rhs_dim):
    return lax.dot_general(
        lhs, rhs, (((lhs_dim,), (rhs_dim,)), ((), ())), preferred_element_type=jnp.float32
    )


def hot_rows(token_row, gate_row, tokens):
    slots = token_row.shape[1]
    token_index = lax.broadcasted_iota(jnp.int32, (tokens, slots), 0)
    spread = jnp.broadcast_to(gate_row, (tokens, slots))
    return jnp.where(token_index == token_row, spread, 0.0).astype(jnp.bfloat16)


def in_hbm(array):
    return pltpu.with_memory_space_constraint(array, pltpu.HBM)


def whole(shape):
    return pl.BlockSpec(shape, lambda *_: (0,) * len(shape))


def call(kernel, scalars, grid, in_specs, out_specs, out_shape, scratch, operands, vmem):
    return pl.pallas_call(
        kernel,
        grid_spec=pltpu.PrefetchScalarGridSpec(
            num_scalar_prefetch=1,
            grid=grid,
            in_specs=in_specs,
            out_specs=out_specs,
            scratch_shapes=scratch,
        ),
        out_shape=out_shape,
        compiler_params=pltpu.CompilerParams(
            dimension_semantics=("arbitrary",) * len(grid), vmem_limit_bytes=vmem
        ),
    )(scalars, *operands)


def expert_sums(where, token_rows, row_gate, hidden_rows, weight, tokens):
    local_count, slots, width_in = hidden_rows.shape
    chips = lax.axis_size("expert") // CORES
    cols = weight.shape[2] // chips
    half = cols // CORES

    def kernel(where, token_ref, gate_ref, hidden_ref, weight_ref, keep_ref, send_ref, by_token, turned):
        @pl.when(pl.program_id(0) == 0)
        def _():
            for local in range(local_count):
                hot = hot_rows(token_ref[local], gate_ref[local], tokens)
                made = dot(hot, hidden_ref[local], 1, 0).astype(jnp.bfloat16)
                by_token[:, local * width_in : (local + 1) * width_in] = made

        stacked = weight_ref[...].reshape(local_count * width_in, cols)
        turned[...] = dot(by_token[...], stacked, 1, 0).astype(jnp.bfloat16).T
        keep_ref[0] = turned[pl.ds(pl.multiple_of(where[1] * half, half), half), :]
        send_ref[0] = turned[pl.ds(pl.multiple_of((1 - where[1]) * half, half), half), :]

    shape = jax.ShapeDtypeStruct((chips, half, tokens), jnp.bfloat16)
    out_spec = pl.BlockSpec((1, half, tokens), lambda k, where: (k, 0, 0))
    return call(
        kernel,
        where,
        (chips,),
        [
            whole((local_count, 1, slots)),
            whole((local_count, 1, slots)),
            whole(hidden_rows.shape),
            pl.BlockSpec((local_count, width_in, cols), lambda k, where: (0, 0, k)),
        ],
        (out_spec, out_spec),
        (shape, shape),
        [
            pltpu.VMEM((tokens, local_count * width_in), jnp.bfloat16),
            pltpu.VMEM((cols, tokens), jnp.bfloat16),
        ],
        (token_rows[:, None], row_gate[:, None], hidden_rows, in_hbm(weight)),
        32 * MIB,
    )


def resident(kernel, scalars, operands, out_shapes, scratch=(), distant=(), passed=None):
    held = [pltpu.with_memory_space_constraint(array, pltpu.VMEM) for array in operands]
    in_vmem, anywhere = pl.BlockSpec(memory_space=pltpu.VMEM), pl.BlockSpec(memory_space=pl.ANY)
    far_off = [in_hbm(array) for array in distant] + ([] if passed is None else [passed])
    return pl.pallas_call(
        kernel,
        in_specs=[pl.BlockSpec(memory_space=pltpu.SMEM)] + [in_vmem] * len(held) + [anywhere] * len(far_off),
        out_specs=[in_vmem if shape.memory_space == pltpu.VMEM else anywhere for shape in out_shapes],
        out_shape=out_shapes,
        scratch_shapes=list(scratch),
        input_output_aliases={} if passed is None else {len(held) + len(far_off): 0},
        compiler_params=pltpu.CompilerParams(vmem_limit_bytes=20 * MIB),
    )(scalars, *held, *far_off)


def shares_by_token(where, payloads, slots, tokens):
    local_count, _, share = payloads[0].shape
    groups = len(payloads)

    def kernel(where, *refs):
        sources, (out_ref, held, sem) = refs[:groups], refs[groups:]
        loads = [pltpu.make_async_copy(ref, held.at[i], sem.at[i]) for i, ref in enumerate(sources)]
        for load in loads:
            load.start()

        def row(group, local, first):
            wide = [held[group, local, slots + first + i : slots + first + i + 1, :] for i in range(2)]
            return jnp.concatenate(wide, axis=1)[:, :slots].astype(jnp.float32)

        for group in range(groups):
            loads[group].wait()
            for local in range(local_count):
                token = (row(group, local, 0) * 2.0 + row(group, local, 2)).astype(jnp.int32)
                hot = hot_rows(token, row(group, local, 4), tokens)
                by_token = dot(hot, held[group, local, :slots, :], 1, 0).astype(jnp.bfloat16)
                out_ref[local * share : (local + 1) * share, group * tokens : (group + 1) * tokens] = by_token.T

    shape = (local_count * share, groups * tokens)
    scratch = [pltpu.VMEM((groups, *payloads[0].shape), jnp.bfloat16), pltpu.SemaphoreType.DMA((groups,))]
    return resident(kernel, where, [], [pltpu.VMEM(shape, jnp.bfloat16)], scratch, payloads)[0]


def blocks_of(where, gathered, steps, parts):
    chips, rows, tokens = gathered.shape
    part = rows // parts

    def kernel(where, gathered_ref, *refs):
        sem = refs[-1]
        copies = []
        for place, step in enumerate(steps):
            chip = lax.rem(where[0] + step, chips)
            for index, out_ref in enumerate(refs[:-1]):
                source = gathered_ref.at[chip, pl.ds(index * part, part)]
                copies.append(pltpu.make_async_copy(source, out_ref.at[place], sem.at[len(copies)]))
        for copy in copies:
            copy.start()
        for copy in copies:
            copy.wait()

    return pl.pallas_call(
        kernel,
        in_specs=[pl.BlockSpec(memory_space=pltpu.SMEM), pl.BlockSpec(memory_space=pl.ANY)],
        out_specs=[pl.BlockSpec(memory_space=pltpu.VMEM)] * parts,
        out_shape=[pltpu.VMEM((len(steps), part, tokens), gathered.dtype)] * parts,
        scratch_shapes=[pltpu.SemaphoreType.DMA((len(steps) * parts,))],
    )(where, in_hbm(gathered))


def hidden_grads(where, token_rows, row_gate, gathered, weight):
    local_count, width_in, width = weight.shape
    slots = token_rows.shape[1]
    chips, half, tokens = gathered[0].shape
    depth = width_in // 2

    def kernel(where, token_ref, gate_ref, mine_ref, other_ref, weight_ref, out_ref, group_cot, sem):
        local = pl.program_id(0)

        @pl.when((local == 0) & (pl.program_id(1) == 0))
        def _():
            loads = []
            for side, ref in enumerate((mine_ref, other_ref)):
                for chip in range(chips):
                    start = (chip * CORES + jnp.bitwise_xor(where[1], side)) * half
                    rows = group_cot.at[pl.ds(pl.multiple_of(start, half), half)]
                    loads.append(pltpu.make_async_copy(ref.at[chip], rows, sem.at[len(loads)]))
            for load in loads:
                load.start()
            for load in loads:
                load.wait()

        sums = dot(weight_ref[0], group_cot[...], 1, 0).astype(jnp.bfloat16)
        hot = hot_rows(token_ref[local], gate_ref[local], tokens)
        out_ref[0] = dot(hot, sums, 0, 1).astype(jnp.bfloat16)

    return call(
        kernel,
        where,
        (local_count, width_in // depth),
        [whole((local_count, 1, slots))] * 2
        + [pl.BlockSpec(memory_space=pl.ANY)] * CORES
        + [pl.BlockSpec((1, depth, width), lambda e, h, where: (e, h, 0))],
        pl.BlockSpec((1, slots, depth), lambda e, h, where: (e, 0, h)),
        jax.ShapeDtypeStruct((local_count, slots, width_in), jnp.bfloat16),
        [pltpu.VMEM((width, tokens), jnp.bfloat16), pltpu.SemaphoreType.DMA((CORES * chips,))],
        (token_rows[:, None], row_gate[:, None], *map(in_hbm, gathered), in_hbm(weight)),
        28 * MIB,
    )


def group_products(where, shares, groups, refs, chip):
    total, at = None, 0
    for place, sides in groups:
        loaded = []
        for pieces in sides:
            loaded.append([ref[first + chip] for ref, (_, first) in zip(refs[at:], pieces)])
            at += len(pieces)
        mine, other = [jnp.concatenate(pieces, axis=0) if len(pieces) > 1 else pieces[0] for pieces in loaded]
        low = jnp.where(where[1] == 0, mine, other)
        high = jnp.where(where[1] == 0, other, mine)
        block = jnp.concatenate([low, high], axis=0)
        tokens = block.shape[1]
        product = dot(shares[:, place * tokens : (place + 1) * tokens], block, 1, 1)
        total = product if total is None else total + product
    return total


def halves(parts):
    return [(part, 0) for part in parts]


def weight_cols(where, shares, own_groups, groups, local_count, width, gathered=None, so_far=None, passed=None):
    chips = lax.axis_size("expert") // CORES
    cols = width // chips
    half = cols // CORES
    share = shares.shape[0] // local_count
    own_flat, flat = [
        [array for _, sides in listed for pieces in sides for array, _ in pieces]
        for listed in (own_groups, groups)
    ]
    tokens = flat[0].shape[-1]
    count = chips - 1
    kept = (count, shares.shape[0], cols)
    distant = [so_far] if gathered is None else gathered
    stored = count if gathered is None else 1

    def kernel(where, shares_ref, *refs):
        refs = list(refs)
        own_pieces = [refs.pop(0) for _ in own_flat]
        pieces = [refs.pop(0) for _ in flat]
        sources = [refs.pop(0) for _ in distant]
        if passed is not None:
            refs.pop(0)
        out_ref = refs.pop(0)
        kept_ref = None if gathered is None else refs.pop(0)
        total_ref, total_sem, loaded_ref, load_sem = refs[:4]
        place = [lax.rem(where[0] + step, chips) for step in range(chips)]
        loads, stores = [], []
        for chip in range(count):
            if gathered is None:
                loads.append([pltpu.make_async_copy(sources[0].at[chip], loaded_ref.at[chip], load_sem.at[chip, 0])])
            else:
                loads.append([])
                for side, source in enumerate(sources):
                    target = loaded_ref.at[chip, jnp.bitwise_xor(where[1], side)]
                    loads[chip].append(
                        pltpu.make_async_copy(source.at[place[chip + 1]], target, load_sem.at[chip, side])
                    )
            for load in loads[chip]:
                load.start()

        def store(total, index, step):
            for local in range(local_count):
                total_ref[index, local] = total[local * share : (local + 1) * share]
            columns = pl.ds(pl.multiple_of(place[step] * cols, LANES), cols)
            stores.append(pltpu.make_async_copy(total_ref.at[index], out_ref.at[:, :, columns], total_sem.at[index]))
            stores[-1].start()

        if own_groups:
            store(group_products(where, shares_ref, own_groups, own_pieces, 0), 0, 0)
        for chip in range(count):
            total = group_products(where, shares_ref, groups, pieces, chip)
            for load in loads[chip]:
                load.wait()
            if gathered is None:
                store(total + loaded_ref[chip].astype(jnp.float32), chip, chip + 1)
                continue
            block = loaded_ref[chip].reshape(cols, tokens)
            staged_ref, staged_sem = refs[4:]
            staged_ref[chip] = (total + dot(shares_ref[:, :tokens], block, 1, 1)).astype(jnp.bfloat16)
            stores.append(pltpu.make_async_copy(staged_ref.at[chip], kept_ref.at[chip], staged_sem.at[chip]))
            stores[-1].start()
        for copy in stores:
            copy.wait()

    scratch = [
        pltpu.VMEM((stored, local_count, share, cols), jnp.float32),
        pltpu.SemaphoreType.DMA((stored,)),
        pltpu.VMEM(kept if gathered is None else (count, CORES, half, tokens), jnp.bfloat16),
        pltpu.SemaphoreType.DMA((count, CORES)),
    ]
    out_shapes = [pltpu.HBM((local_count, share, width), jnp.float32)]
    if gathered is not None:
        scratch += [pltpu.VMEM(kept, jnp.bfloat16), pltpu.SemaphoreType.DMA((count,))]
        out_shapes.append(pltpu.HBM(kept, jnp.bfloat16))
    return resident(kernel, where, [shares, *own_flat, *flat], out_shapes, scratch, distant, passed)


def planned_body(hidden, down_weight, cotangent, expert_ids, gate_weights, row_token, tile_count):
    local_count, width_in, width = down_weight.shape
    tokens = cotangent.shape[0]
    slots = hidden.shape[2]
    groups = lax.axis_size("dp")
    chips = lax.axis_size("expert") // CORES
    share = width_in // groups
    group = lax.axis_index("dp")
    expert_place = lax.axis_index("expert")
    chip = expert_place // CORES
    core = expert_place % CORES
    where = jnp.stack([chip, core])

    own = cotangent.T
    middle = own.shape[0] // 2
    gathered = exchanged(jnp.broadcast_to(own[None], (chips, *own.shape)))
    x_own, y_own = across_dp(own, 1), across_dp(own, 2)
    own_other = across_cores(own)

    slot_index = jnp.arange(slots, dtype=jnp.int32)
    token_index = jnp.arange(tokens, dtype=jnp.int32)
    live = (row_token[0] >= 0) & (slot_index[None] < tile_count[0][:, None] * TILE)
    token_rows = jnp.where(live, row_token[0], -1)
    experts = expert_place * local_count + jnp.arange(local_count, dtype=jnp.int32)
    named = expert_ids[None] == experts[:, None, None]
    token_gate = jnp.sum(jnp.where(named, gate_weights[None].astype(jnp.float32), 0.0), axis=2)
    at_token = token_rows[:, :, None] == token_index[None, None, :]
    row_gate = jnp.sum(jnp.where(at_token, token_gate[:, None, :], 0.0), axis=2)

    def as_rows(values):
        padded = jnp.pad(values.astype(jnp.bfloat16), ((0, 0), (0, 2 * share - slots)))
        return padded.reshape(local_count, 2, share)

    extra = jnp.concatenate(
        [as_rows(token_rows >> 1), as_rows(token_rows & 1), as_rows(row_gate)], axis=1
    )
    extra = jnp.pad(extra, ((0, 0), (0, EXTRA_ROWS - extra.shape[1]), (0, 0)))
    payloads = []
    for mask in range(groups):
        rows = lax.dynamic_slice_in_dim(hidden[0], (group ^ mask) * share, share, 2)
        payloads.append(jnp.concatenate([rows, extra], axis=1))
    x_own, y_own, own_other, token_rows, row_gate, *payloads = joined(
        x_own, y_own, own_other, token_rows, row_gate, *payloads
    )

    payloads = [across_dp(payload, mask) if mask else payload for mask, payload in enumerate(payloads)]
    far_own = [across_dp(x_own[:middle], 2), across_dp(y_own[middle:], 1)]
    keep, send = expert_sums(where, token_rows, row_gate, hidden[0], down_weight, tokens)
    x_own, y_own, keep, send, *sent = joined(x_own, y_own, keep, send, *far_own, *payloads)
    far_own, payloads = sent[:2], sent[2:]

    own_far = jnp.stack([x_own, y_own, jnp.concatenate(far_own, axis=0)])
    gathered, own_far = joined(gathered, own_far)
    own_far_other = across_cores(own_far)
    steps = list(range(1, chips))
    near = blocks_of(where, gathered, steps, 2)
    x_near, y_near = [None, None], [None, None]
    x_near[0], y_near[1] = across_dp(near[0], 1), across_dp(near[1], 2)
    x_near[1], y_near[0] = across_dp(near[1], 1), across_dp(near[0], 2)

    from_other = across_cores(send)
    gathered_other = across_cores(gathered)
    from_other, *_ = joined(from_other, *near)
    sums = (keep.astype(jnp.float32) + from_other.astype(jnp.float32)).astype(jnp.bfloat16)
    mixed = exchanged(sums)
    _, gathered_other, *payloads = joined(sums, gathered_other, *payloads)
    shares = shares_by_token(where, payloads, slots, tokens)
    gathered = [gathered, gathered_other]
    hidden_grad = hidden_grads(where, token_rows, row_gate, gathered, down_weight)
    hidden_grad, shares, own_far_other, _, *sent = joined(
        hidden_grad, shares, own_far_other, sums, *x_near, *y_near
    )
    x_near, y_near = sent[:2], sent[2:]

    rest = (local_count, width)
    far = [across_dp(x_near[0], 2), across_dp(y_near[1], 1)]
    x_other = [across_cores(part) for part in x_near]
    y_other = [across_cores(part) for part in y_near]
    own_groups = [(0, (halves([own[None]]), halves([own_other[None]])))]
    own_groups += [(place + 1, ([(own_far, place)], [(own_far_other, place)])) for place in range(groups - 1)]
    two = [(place, tuple(map(halves, pair))) for place, pair in ((1, (x_near, x_other)), (2, (y_near, y_other)))]
    weight_grad, so_far = weight_cols(where, shares, own_groups, two, *rest, gathered)
    so_far, weight_grad, *far = joined(so_far, weight_grad, *far)
    mixed = jnp.sum(mixed.astype(jnp.float32), axis=0).astype(jnp.bfloat16)
    mixed, *far_other = joined(mixed, *[across_cores(part) for part in far])
    last = [(groups - 1, (halves(far), halves(far_other)))]
    weight_grad = weight_cols(where, shares, [], last, *rest, None, so_far, weight_grad)[0]
    return (mixed.T, hidden_grad[None], weight_grad)


def tile_products(rows_in, weight_mat, count, contract_dim):
    rows_cap = rows_in.shape[0]
    width_out = weight_mat.shape[1 - contract_dim]

    def one_tile(tile_index, outputs):
        block = lax.dynamic_slice_in_dim(rows_in, tile_index * TILE, TILE, 0)
        product = lax.dot_general(
            block,
            weight_mat,
            (((1,), (contract_dim,)), ((), ())),
            preferred_element_type=jnp.float32,
        )
        return lax.dynamic_update_slice_in_dim(
            outputs, product.astype(jnp.bfloat16), tile_index * TILE, 0
        )

    return lax.fori_loop(0, count, one_tile, jnp.zeros((rows_cap, width_out), jnp.bfloat16))


def general_body(hidden, down_weight, cotangent, expert_ids, gate_weights, row_token, tile_count):
    local_count = down_weight.shape[0]
    group_size = cotangent.shape[0]
    expert_index = jnp.arange(EXPERTS, dtype=jnp.int32)
    named_cols = expert_ids[:, :, None] == expert_index[None, None, :]
    gate_cols = jnp.sum(
        jnp.where(named_cols, gate_weights[:, :, None].astype(jnp.float32), 0.0), axis=1
    ).astype(jnp.bfloat16)
    group_cot = lax.all_gather(cotangent, "expert", axis=1, tiled=True)
    width = group_cot.shape[1]
    first_expert = lax.axis_index("expert") * local_count
    slot_index = jnp.arange(hidden.shape[2], dtype=jnp.int32)
    share_rows = down_weight.shape[1] // lax.axis_size("dp")
    partial_value = jnp.zeros((group_size, width), jnp.float32)
    grad_list = []
    weight_list = []
    for local in range(local_count):
        token_rows = row_token[0, local]
        count = tile_count[0, local]
        live_rows = (token_rows >= 0) & (slot_index < count * TILE)
        safe_rows = jnp.where(live_rows, token_rows, 0)
        column = lax.dynamic_index_in_dim(gate_cols, first_expert + local, 1, keepdims=False)
        row_gate = jnp.where(live_rows, column[safe_rows].astype(jnp.float32), 0.0)
        target = jnp.where(live_rows, token_rows, group_size)
        hidden_rows = hidden[0, local]
        weight_mat = down_weight[local]
        out_rows = tile_products(hidden_rows, weight_mat, count, 0)
        partial_value = partial_value.at[target].add(
            row_gate[:, None] * out_rows.astype(jnp.float32), mode="drop"
        )
        routed = (row_gate[:, None] * group_cot[safe_rows].astype(jnp.float32)).astype(jnp.bfloat16)
        grad_list.append(tile_products(routed, weight_mat, count, 1))

        def weight_rows(start, rows_count, hidden_rows=hidden_rows, routed_rows=routed):
            return lax.dot_general(
                hidden_rows,
                routed_rows,
                (((0,), (0,)), ((), ())),
                preferred_element_type=jnp.float32,
            )

        weight_list.append(
            lax.psum_scatter(
                weight_rows(jnp.int32(0), share_rows * lax.axis_size("dp")).astype(jnp.bfloat16),
                "dp",
                scatter_dimension=0,
                tiled=True,
            ).astype(jnp.float32)
        )
    merged = partial_value
    top_bit = lax.axis_size("expert").bit_length() - 1
    axis_index = lax.axis_index("expert")
    for bit_index in reversed(range(top_bit)):
        half_cols = merged.shape[1] // 2
        lower_half = merged[:, :half_cols]
        upper_half = merged[:, half_cols:]
        high_side = axis_index // 2**bit_index % 2 == 1
        sending = jnp.where(high_side, lower_half, upper_half)
        keeping = jnp.where(high_side, upper_half, lower_half)
        merged = keeping + swapped(sending.astype(jnp.bfloat16), "expert", bit_index).astype(
            sending.dtype
        )
    mixed_out = merged.astype(jnp.bfloat16)
    hidden_grad = jnp.stack(grad_list, axis=0)[None]
    weight_grad = jnp.stack(weight_list, axis=0)
    return (mixed_out, hidden_grad, weight_grad)


def solution(mesh):
    placed = (
        P("dp", "expert", None, None),
        P("expert", None, None),
        P("dp", "expert"),
        P("dp", None),
        P("dp", None),
        P("dp", "expert", None),
        P("dp", "expert"),
    )

    def body(*shards):
        width = shards[1].shape[2]
        chips = mesh.shape["expert"] // CORES
        fits = mesh.shape["dp"] == 4 and chips > 2 and width % (chips * LANES) == 0
        return planned_body(*shards) if fits else general_body(*shards)

    return jax.shard_map(
        body,
        mesh=mesh,
        in_specs=placed,
        out_specs=(P("dp", "expert"), P("dp", "expert", None, None), P("expert", "dp", None)),
        check_vma=False,
    )
```

```python
import jax
import jax.numpy as jnp
from jax import lax
from jax.experimental import pallas as pl
from jax.experimental.pallas import tpu as pltpu
from jax.sharding import PartitionSpec as P

EXPERTS = 16
TILE = 128
LANES = 128
CORES = 2
EXTRA_ROWS = 16
MIB = 1024 * 1024


def swapped(shard, axis, bit):
    return lax.ppermute(shard, axis, [(i, i ^ 1 << bit) for i in range(lax.axis_size(axis))])


def across_dp(shard, mask):
    return lax.ppermute(shard, "dp", [(i, i ^ mask) for i in range(lax.axis_size("dp"))])


def across_cores(shard):
    return swapped(shard, "expert", 0)


def z_lines():
    size = lax.axis_size("expert")
    return [list(range(core, size, CORES)) for core in range(CORES)]


def exchanged(parts):
    return lax.all_to_all(parts, "expert", 0, 0, axis_index_groups=z_lines(), tiled=True)


def joined(*values):
    return lax.optimization_barrier(values)


def dot(lhs, rhs, lhs_dim, rhs_dim):
    return lax.dot_general(
        lhs, rhs, (((lhs_dim,), (rhs_dim,)), ((), ())), preferred_element_type=jnp.float32
    )


def hot_rows(token_row, gate_row, tokens):
    slots = token_row.shape[1]
    token_index = lax.broadcasted_iota(jnp.int32, (tokens, slots), 0)
    spread = jnp.broadcast_to(gate_row, (tokens, slots))
    return jnp.where(token_index == token_row, spread, 0.0).astype(jnp.bfloat16)


def in_hbm(array):
    return pltpu.with_memory_space_constraint(array, pltpu.HBM)


def whole(shape):
    return pl.BlockSpec(shape, lambda *_: (0,) * len(shape))


def call(kernel, scalars, grid, in_specs, out_specs, out_shape, scratch, operands, vmem):
    return pl.pallas_call(
        kernel,
        grid_spec=pltpu.PrefetchScalarGridSpec(
            num_scalar_prefetch=1,
            grid=grid,
            in_specs=in_specs,
            out_specs=out_specs,
            scratch_shapes=scratch,
        ),
        out_shape=out_shape,
        compiler_params=pltpu.CompilerParams(
            dimension_semantics=("arbitrary",) * len(grid), vmem_limit_bytes=vmem
        ),
    )(scalars, *operands)


def expert_sums(where, token_rows, row_gate, hidden_rows, weight, tokens):
    local_count, slots, width_in = hidden_rows.shape
    chips = lax.axis_size("expert") // CORES
    cols = weight.shape[2] // chips
    half = cols // CORES

    def kernel(where, token_ref, gate_ref, hidden_ref, weight_ref, keep_ref, send_ref, by_token, turned):
        @pl.when(pl.program_id(0) == 0)
        def _():
            for local in range(local_count):
                hot = hot_rows(token_ref[local], gate_ref[local], tokens)
                made = dot(hot, hidden_ref[local], 1, 0).astype(jnp.bfloat16)
                by_token[:, local * width_in : (local + 1) * width_in] = made

        stacked = weight_ref[...].reshape(local_count * width_in, cols)
        turned[...] = dot(by_token[...], stacked, 1, 0).astype(jnp.bfloat16).T
        keep_ref[0] = turned[pl.ds(pl.multiple_of(where[1] * half, half), half), :]
        send_ref[0] = turned[pl.ds(pl.multiple_of((1 - where[1]) * half, half), half), :]

    shape = jax.ShapeDtypeStruct((chips, half, tokens), jnp.bfloat16)
    out_spec = pl.BlockSpec((1, half, tokens), lambda k, where: (k, 0, 0))
    return call(
        kernel,
        where,
        (chips,),
        [
            whole((local_count, 1, slots)),
            whole((local_count, 1, slots)),
            whole(hidden_rows.shape),
            pl.BlockSpec((local_count, width_in, cols), lambda k, where: (0, 0, k)),
        ],
        (out_spec, out_spec),
        (shape, shape),
        [
            pltpu.VMEM((tokens, local_count * width_in), jnp.bfloat16),
            pltpu.VMEM((cols, tokens), jnp.bfloat16),
        ],
        (token_rows[:, None], row_gate[:, None], hidden_rows, in_hbm(weight)),
        32 * MIB,
    )


def resident(kernel, scalars, operands, out_shapes, scratch=(), distant=(), passed=None):
    held = [pltpu.with_memory_space_constraint(array, pltpu.VMEM) for array in operands]
    in_vmem, anywhere = pl.BlockSpec(memory_space=pltpu.VMEM), pl.BlockSpec(memory_space=pl.ANY)
    far_off = [in_hbm(array) for array in distant] + ([] if passed is None else [passed])
    return pl.pallas_call(
        kernel,
        in_specs=[pl.BlockSpec(memory_space=pltpu.SMEM)] + [in_vmem] * len(held) + [anywhere] * len(far_off),
        out_specs=[in_vmem if shape.memory_space == pltpu.VMEM else anywhere for shape in out_shapes],
        out_shape=out_shapes,
        scratch_shapes=list(scratch),
        input_output_aliases={} if passed is None else {len(held) + len(far_off): 0},
        compiler_params=pltpu.CompilerParams(vmem_limit_bytes=20 * MIB),
    )(scalars, *held, *far_off)


def shares_by_token(where, payloads, slots, tokens):
    local_count, _, share = payloads[0].shape
    groups = len(payloads)

    def kernel(where, *refs):
        sources, (out_ref, held, sem) = refs[:groups], refs[groups:]
        loads = [pltpu.make_async_copy(ref, held.at[i], sem.at[i]) for i, ref in enumerate(sources)]
        for load in loads:
            load.start()

        def row(group, local, first):
            wide = [held[group, local, slots + first + i : slots + first + i + 1, :] for i in range(2)]
            return jnp.concatenate(wide, axis=1)[:, :slots].astype(jnp.float32)

        for group in range(groups):
            loads[group].wait()
            for local in range(local_count):
                token = (row(group, local, 0) * 2.0 + row(group, local, 2)).astype(jnp.int32)
                hot = hot_rows(token, row(group, local, 4), tokens)
                by_token = dot(hot, held[group, local, :slots, :], 1, 0).astype(jnp.bfloat16)
                out_ref[local * share : (local + 1) * share, group * tokens : (group + 1) * tokens] = by_token.T

    shape = (local_count * share, groups * tokens)
    scratch = [pltpu.VMEM((groups, *payloads[0].shape), jnp.bfloat16), pltpu.SemaphoreType.DMA((groups,))]
    return resident(kernel, where, [], [pltpu.VMEM(shape, jnp.bfloat16)], scratch, payloads)[0]


def blocks_of(where, gathered, steps, parts):
    chips, rows, tokens = gathered.shape
    part = rows // parts

    def kernel(where, gathered_ref, *refs):
        sem = refs[-1]
        copies = []
        for place, step in enumerate(steps):
            chip = lax.rem(where[0] + step, chips)
            for index, out_ref in enumerate(refs[:-1]):
                source = gathered_ref.at[chip, pl.ds(index * part, part)]
                copies.append(pltpu.make_async_copy(source, out_ref.at[place], sem.at[len(copies)]))
        for copy in copies:
            copy.start()
        for copy in copies:
            copy.wait()

    return pl.pallas_call(
        kernel,
        in_specs=[pl.BlockSpec(memory_space=pltpu.SMEM), pl.BlockSpec(memory_space=pl.ANY)],
        out_specs=[pl.BlockSpec(memory_space=pl.ANY)] * parts,
        out_shape=[pltpu.HBM((len(steps), part, tokens), gathered.dtype)] * parts,
        scratch_shapes=[pltpu.SemaphoreType.DMA((len(steps) * parts,))],
    )(where, in_hbm(gathered))


def hidden_grads(where, token_rows, row_gate, gathered, weight):
    local_count, width_in, width = weight.shape
    slots = token_rows.shape[1]
    chips, half, tokens = gathered[0].shape
    depth = width_in // 2

    def kernel(where, token_ref, gate_ref, mine_ref, other_ref, weight_ref, out_ref, group_cot, sem):
        local = pl.program_id(0)

        @pl.when((local == 0) & (pl.program_id(1) == 0))
        def _():
            loads = []
            for side, ref in enumerate((mine_ref, other_ref)):
                for chip in range(chips):
                    start = (chip * CORES + jnp.bitwise_xor(where[1], side)) * half
                    rows = group_cot.at[pl.ds(pl.multiple_of(start, half), half)]
                    loads.append(pltpu.make_async_copy(ref.at[chip], rows, sem.at[len(loads)]))
            for load in loads:
                load.start()
            for load in loads:
                load.wait()

        sums = dot(weight_ref[0], group_cot[...], 1, 0).astype(jnp.bfloat16)
        hot = hot_rows(token_ref[local], gate_ref[local], tokens)
        out_ref[0] = dot(hot, sums, 0, 1).astype(jnp.bfloat16)

    return call(
        kernel,
        where,
        (local_count, width_in // depth),
        [whole((local_count, 1, slots))] * 2
        + [pl.BlockSpec(memory_space=pl.ANY)] * CORES
        + [pl.BlockSpec((1, depth, width), lambda e, h, where: (e, h, 0))],
        pl.BlockSpec((1, slots, depth), lambda e, h, where: (e, 0, h)),
        jax.ShapeDtypeStruct((local_count, slots, width_in), jnp.bfloat16),
        [pltpu.VMEM((width, tokens), jnp.bfloat16), pltpu.SemaphoreType.DMA((CORES * chips,))],
        (token_rows[:, None], row_gate[:, None], *map(in_hbm, gathered), in_hbm(weight)),
        28 * MIB,
    )


def group_products(where, shares, groups, refs, chip):
    total, at = None, 0
    for place, sides in groups:
        loaded = []
        for pieces in sides:
            loaded.append([ref[first + chip] for ref, (_, first) in zip(refs[at:], pieces)])
            at += len(pieces)
        mine, other = [jnp.concatenate(pieces, axis=0) if len(pieces) > 1 else pieces[0] for pieces in loaded]
        low = jnp.where(where[1] == 0, mine, other)
        high = jnp.where(where[1] == 0, other, mine)
        block = jnp.concatenate([low, high], axis=0)
        tokens = block.shape[1]
        product = dot(shares[:, place * tokens : (place + 1) * tokens], block, 1, 1)
        total = product if total is None else total + product
    return total


def halves(parts):
    return [(part, 0) for part in parts]


def weight_cols(where, shares, own_groups, groups, local_count, width, gathered=None, so_far=None, passed=None):
    chips = lax.axis_size("expert") // CORES
    cols = width // chips
    half = cols // CORES
    share = shares.shape[0] // local_count
    own_flat, flat = [
        [array for _, sides in listed for pieces in sides for array, _ in pieces]
        for listed in (own_groups, groups)
    ]
    tokens = flat[0].shape[-1]
    count = chips - 1
    kept = (count, shares.shape[0], cols)
    distant = [so_far] if gathered is None else gathered
    stored = count if gathered is None else 1

    def kernel(where, shares_ref, *refs):
        refs = list(refs)
        own_pieces = [refs.pop(0) for _ in own_flat]
        pieces = [refs.pop(0) for _ in flat]
        sources = [refs.pop(0) for _ in distant]
        if passed is not None:
            refs.pop(0)
        out_ref = refs.pop(0)
        kept_ref = None if gathered is None else refs.pop(0)
        total_ref, total_sem, loaded_ref, load_sem = refs[:4]
        place = [lax.rem(where[0] + step, chips) for step in range(chips)]
        loads, stores = [], []
        for chip in range(count):
            if gathered is None:
                loads.append([pltpu.make_async_copy(sources[0].at[chip], loaded_ref.at[chip], load_sem.at[chip, 0])])
            else:
                loads.append([])
                for side, source in enumerate(sources):
                    target = loaded_ref.at[chip, jnp.bitwise_xor(where[1], side)]
                    loads[chip].append(
                        pltpu.make_async_copy(source.at[place[chip + 1]], target, load_sem.at[chip, side])
                    )
            for load in loads[chip]:
                load.start()

        def store(total, index, step):
            for local in range(local_count):
                total_ref[index, local] = total[local * share : (local + 1) * share]
            columns = pl.ds(pl.multiple_of(place[step] * cols, LANES), cols)
            stores.append(pltpu.make_async_copy(total_ref.at[index], out_ref.at[:, :, columns], total_sem.at[index]))
            stores[-1].start()

        if own_groups:
            store(group_products(where, shares_ref, own_groups, own_pieces, 0), 0, 0)
        for chip in range(count):
            total = group_products(where, shares_ref, groups, pieces, chip)
            for load in loads[chip]:
                load.wait()
            if gathered is None:
                store(total + loaded_ref[chip].astype(jnp.float32), chip, chip + 1)
                continue
            block = loaded_ref[chip].reshape(cols, tokens)
            staged_ref, staged_sem = refs[4:]
            staged_ref[chip] = (total + dot(shares_ref[:, :tokens], block, 1, 1)).astype(jnp.bfloat16)
            stores.append(pltpu.make_async_copy(staged_ref.at[chip], kept_ref.at[chip], staged_sem.at[chip]))
            stores[-1].start()
        for copy in stores:
            copy.wait()

    scratch = [
        pltpu.VMEM((stored, local_count, share, cols), jnp.float32),
        pltpu.SemaphoreType.DMA((stored,)),
        pltpu.VMEM(kept if gathered is None else (count, CORES, half, tokens), jnp.bfloat16),
        pltpu.SemaphoreType.DMA((count, CORES)),
    ]
    out_shapes = [pltpu.HBM((local_count, share, width), jnp.float32)]
    if gathered is not None:
        scratch += [pltpu.VMEM(kept, jnp.bfloat16), pltpu.SemaphoreType.DMA((count,))]
        out_shapes.append(pltpu.HBM(kept, jnp.bfloat16))
    return resident(kernel, where, [shares, *own_flat, *flat], out_shapes, scratch, distant, passed)


def planned_body(hidden, down_weight, cotangent, expert_ids, gate_weights, row_token, tile_count):
    local_count, width_in, width = down_weight.shape
    tokens = cotangent.shape[0]
    slots = hidden.shape[2]
    groups = lax.axis_size("dp")
    chips = lax.axis_size("expert") // CORES
    share = width_in // groups
    group = lax.axis_index("dp")
    expert_place = lax.axis_index("expert")
    chip = expert_place // CORES
    core = expert_place % CORES
    where = jnp.stack([chip, core])

    own = cotangent.T
    middle = own.shape[0] // 2
    gathered = exchanged(jnp.broadcast_to(own[None], (chips, *own.shape)))
    x_own, y_own = across_dp(own, 1), across_dp(own, 2)
    own_other = across_cores(own)

    slot_index = jnp.arange(slots, dtype=jnp.int32)
    token_index = jnp.arange(tokens, dtype=jnp.int32)
    live = (row_token[0] >= 0) & (slot_index[None] < tile_count[0][:, None] * TILE)
    token_rows = jnp.where(live, row_token[0], -1)
    experts = expert_place * local_count + jnp.arange(local_count, dtype=jnp.int32)
    named = expert_ids[None] == experts[:, None, None]
    token_gate = jnp.sum(jnp.where(named, gate_weights[None].astype(jnp.float32), 0.0), axis=2)
    at_token = token_rows[:, :, None] == token_index[None, None, :]
    row_gate = jnp.sum(jnp.where(at_token, token_gate[:, None, :], 0.0), axis=2)

    def as_rows(values):
        padded = jnp.pad(values.astype(jnp.bfloat16), ((0, 0), (0, 2 * share - slots)))
        return padded.reshape(local_count, 2, share)

    extra = jnp.concatenate(
        [as_rows(token_rows >> 1), as_rows(token_rows & 1), as_rows(row_gate)], axis=1
    )
    extra = jnp.pad(extra, ((0, 0), (0, EXTRA_ROWS - extra.shape[1]), (0, 0)))
    payloads = []
    for mask in range(groups):
        rows = lax.dynamic_slice_in_dim(hidden[0], (group ^ mask) * share, share, 2)
        payloads.append(jnp.concatenate([rows, extra], axis=1))
    x_own, y_own, own_other, token_rows, row_gate, *payloads = joined(
        x_own, y_own, own_other, token_rows, row_gate, *payloads
    )

    payloads = [across_dp(payload, mask) if mask else payload for mask, payload in enumerate(payloads)]
    far_own = [across_dp(x_own[:middle], 2), across_dp(y_own[middle:], 1)]
    keep, send = expert_sums(where, token_rows, row_gate, hidden[0], down_weight, tokens)
    x_own, y_own, keep, send, *sent = joined(x_own, y_own, keep, send, *far_own, *payloads)
    far_own, payloads = sent[:2], sent[2:]

    own_far = jnp.stack([x_own, y_own, jnp.concatenate(far_own, axis=0)])
    gathered, own_far = joined(gathered, own_far)
    own_far_other = across_cores(own_far)
    steps = list(range(1, chips))
    near = blocks_of(where, gathered, steps, 2)
    x_near, y_near = [None, None], [None, None]
    x_near[0], y_near[1] = across_dp(near[0], 1), across_dp(near[1], 2)
    x_near[1], y_near[0] = across_dp(near[1], 1), across_dp(near[0], 2)

    from_other = across_cores(send)
    gathered_other = across_cores(gathered)
    from_other, *_ = joined(from_other, *near)
    sums = (keep.astype(jnp.float32) + from_other.astype(jnp.float32)).astype(jnp.bfloat16)
    mixed = exchanged(sums)
    _, gathered_other, *payloads = joined(sums, gathered_other, *payloads)
    shares = shares_by_token(where, payloads, slots, tokens)
    gathered = [gathered, gathered_other]
    hidden_grad = hidden_grads(where, token_rows, row_gate, gathered, down_weight)
    hidden_grad, shares, own_far_other, _, *sent = joined(
        hidden_grad, shares, own_far_other, sums, *x_near, *y_near
    )
    x_near, y_near = sent[:2], sent[2:]

    rest = (local_count, width)
    far = [across_dp(x_near[0], 2), across_dp(y_near[1], 1)]
    x_other = [across_cores(part) for part in x_near]
    y_other = [across_cores(part) for part in y_near]
    own_groups = [(0, (halves([own[None]]), halves([own_other[None]])))]
    own_groups += [(place + 1, ([(own_far, place)], [(own_far_other, place)])) for place in range(groups - 1)]
    two = [(place, tuple(map(halves, pair))) for place, pair in ((1, (x_near, x_other)), (2, (y_near, y_other)))]
    weight_grad, so_far = weight_cols(where, shares, own_groups, two, *rest, gathered)
    so_far, weight_grad, *far = joined(so_far, weight_grad, *far)
    mixed = jnp.sum(mixed.astype(jnp.float32), axis=0).astype(jnp.bfloat16)
    mixed, *far_other = joined(mixed, *[across_cores(part) for part in far])
    last = [(groups - 1, (halves(far), halves(far_other)))]
    weight_grad = weight_cols(where, shares, [], last, *rest, None, so_far, weight_grad)[0]
    return (mixed.T, hidden_grad[None], weight_grad)


def tile_products(rows_in, weight_mat, count, contract_dim):
    rows_cap = rows_in.shape[0]
    width_out = weight_mat.shape[1 - contract_dim]

    def one_tile(tile_index, outputs):
        block = lax.dynamic_slice_in_dim(rows_in, tile_index * TILE, TILE, 0)
        product = lax.dot_general(
            block,
            weight_mat,
            (((1,), (contract_dim,)), ((), ())),
            preferred_element_type=jnp.float32,
        )
        return lax.dynamic_update_slice_in_dim(
            outputs, product.astype(jnp.bfloat16), tile_index * TILE, 0
        )

    return lax.fori_loop(0, count, one_tile, jnp.zeros((rows_cap, width_out), jnp.bfloat16))


def general_body(hidden, down_weight, cotangent, expert_ids, gate_weights, row_token, tile_count):
    local_count = down_weight.shape[0]
    group_size = cotangent.shape[0]
    expert_index = jnp.arange(EXPERTS, dtype=jnp.int32)
    named_cols = expert_ids[:, :, None] == expert_index[None, None, :]
    gate_cols = jnp.sum(
        jnp.where(named_cols, gate_weights[:, :, None].astype(jnp.float32), 0.0), axis=1
    ).astype(jnp.bfloat16)
    group_cot = lax.all_gather(cotangent, "expert", axis=1, tiled=True)
    width = group_cot.shape[1]
    first_expert = lax.axis_index("expert") * local_count
    slot_index = jnp.arange(hidden.shape[2], dtype=jnp.int32)
    share_rows = down_weight.shape[1] // lax.axis_size("dp")
    partial_value = jnp.zeros((group_size, width), jnp.float32)
    grad_list = []
    weight_list = []
    for local in range(local_count):
        token_rows = row_token[0, local]
        count = tile_count[0, local]
        live_rows = (token_rows >= 0) & (slot_index < count * TILE)
        safe_rows = jnp.where(live_rows, token_rows, 0)
        column = lax.dynamic_index_in_dim(gate_cols, first_expert + local, 1, keepdims=False)
        row_gate = jnp.where(live_rows, column[safe_rows].astype(jnp.float32), 0.0)
        target = jnp.where(live_rows, token_rows, group_size)
        hidden_rows = hidden[0, local]
        weight_mat = down_weight[local]
        out_rows = tile_products(hidden_rows, weight_mat, count, 0)
        partial_value = partial_value.at[target].add(
            row_gate[:, None] * out_rows.astype(jnp.float32), mode="drop"
        )
        routed = (row_gate[:, None] * group_cot[safe_rows].astype(jnp.float32)).astype(jnp.bfloat16)
        grad_list.append(tile_products(routed, weight_mat, count, 1))

        def weight_rows(start, rows_count, hidden_rows=hidden_rows, routed_rows=routed):
            return lax.dot_general(
                hidden_rows,
                routed_rows,
                (((0,), (0,)), ((), ())),
                preferred_element_type=jnp.float32,
            )

        weight_list.append(
            lax.psum_scatter(
                weight_rows(jnp.int32(0), share_rows * lax.axis_size("dp")).astype(jnp.bfloat16),
                "dp",
                scatter_dimension=0,
                tiled=True,
            ).astype(jnp.float32)
        )
    merged = partial_value
    top_bit = lax.axis_size("expert").bit_length() - 1
    axis_index = lax.axis_index("expert")
    for bit_index in reversed(range(top_bit)):
        half_cols = merged.shape[1] // 2
        lower_half = merged[:, :half_cols]
        upper_half = merged[:, half_cols:]
        high_side = axis_index // 2**bit_index % 2 == 1
        sending = jnp.where(high_side, lower_half, upper_half)
        keeping = jnp.where(high_side, upper_half, lower_half)
        merged = keeping + swapped(sending.astype(jnp.bfloat16), "expert", bit_index).astype(
            sending.dtype
        )
    mixed_out = merged.astype(jnp.bfloat16)
    hidden_grad = jnp.stack(grad_list, axis=0)[None]
    weight_grad = jnp.stack(weight_list, axis=0)
    return (mixed_out, hidden_grad, weight_grad)


def solution(mesh):
    placed = (
        P("dp", "expert", None, None),
        P("expert", None, None),
        P("dp", "expert"),
        P("dp", None),
        P("dp", None),
        P("dp", "expert", None),
        P("dp", "expert"),
    )

    def body(*shards):
        width = shards[1].shape[2]
        chips = mesh.shape["expert"] // CORES
        fits = mesh.shape["dp"] == 4 and chips > 2 and width % (chips * LANES) == 0
        return planned_body(*shards) if fits else general_body(*shards)

    return jax.shard_map(
        body,
        mesh=mesh,
        in_specs=placed,
        out_specs=(P("dp", "expert"), P("dp", "expert", None, None), P("expert", "dp", None)),
        check_vma=False,
    )
```

```python
import jax
import jax.numpy as jnp
from jax import lax
from jax.experimental import pallas as pl
from jax.experimental.pallas import tpu as pltpu
from jax.sharding import PartitionSpec as P

EXPERTS = 16
TILE = 128
LANES = 128
CORES = 2
EXTRA_ROWS = 16
MIB = 1024 * 1024


def swapped(shard, axis, bit):
    return lax.ppermute(shard, axis, [(i, i ^ 1 << bit) for i in range(lax.axis_size(axis))])


def across_dp(shard, mask):
    return lax.ppermute(shard, "dp", [(i, i ^ mask) for i in range(lax.axis_size("dp"))])


def across_cores(shard):
    return swapped(shard, "expert", 0)


def z_lines():
    size = lax.axis_size("expert")
    return [list(range(core, size, CORES)) for core in range(CORES)]


def exchanged(parts):
    return lax.all_to_all(parts, "expert", 0, 0, axis_index_groups=z_lines(), tiled=True)


def joined(*values):
    return lax.optimization_barrier(values)


def dot(lhs, rhs, lhs_dim, rhs_dim):
    return lax.dot_general(
        lhs, rhs, (((lhs_dim,), (rhs_dim,)), ((), ())), preferred_element_type=jnp.float32
    )


def hot_rows(token_row, gate_row, tokens):
    slots = token_row.shape[1]
    token_index = lax.broadcasted_iota(jnp.int32, (tokens, slots), 0)
    spread = jnp.broadcast_to(gate_row, (tokens, slots))
    return jnp.where(token_index == token_row, spread, 0.0).astype(jnp.bfloat16)


def in_hbm(array):
    return pltpu.with_memory_space_constraint(array, pltpu.HBM)


def whole(shape):
    return pl.BlockSpec(shape, lambda *_: (0,) * len(shape))


def call(kernel, scalars, grid, in_specs, out_specs, out_shape, scratch, operands, vmem):
    return pl.pallas_call(
        kernel,
        grid_spec=pltpu.PrefetchScalarGridSpec(
            num_scalar_prefetch=1,
            grid=grid,
            in_specs=in_specs,
            out_specs=out_specs,
            scratch_shapes=scratch,
        ),
        out_shape=out_shape,
        compiler_params=pltpu.CompilerParams(
            dimension_semantics=("arbitrary",) * len(grid), vmem_limit_bytes=vmem
        ),
    )(scalars, *operands)


def expert_sums(where, token_rows, row_gate, hidden_rows, weight, tokens):
    local_count, slots, width_in = hidden_rows.shape
    chips = lax.axis_size("expert") // CORES
    cols = weight.shape[2] // chips
    half = cols // CORES

    def kernel(where, token_ref, gate_ref, hidden_ref, weight_ref, keep_ref, send_ref, by_token, turned):
        @pl.when(pl.program_id(0) == 0)
        def _():
            for local in range(local_count):
                hot = hot_rows(token_ref[local], gate_ref[local], tokens)
                made = dot(hot, hidden_ref[local], 1, 0).astype(jnp.bfloat16)
                by_token[:, local * width_in : (local + 1) * width_in] = made

        stacked = weight_ref[...].reshape(local_count * width_in, cols)
        turned[...] = dot(by_token[...], stacked, 1, 0).astype(jnp.bfloat16).T
        keep_ref[0] = turned[pl.ds(pl.multiple_of(where[1] * half, half), half), :]
        send_ref[0] = turned[pl.ds(pl.multiple_of((1 - where[1]) * half, half), half), :]

    shape = jax.ShapeDtypeStruct((chips, half, tokens), jnp.bfloat16)
    out_spec = pl.BlockSpec((1, half, tokens), lambda k, where: (k, 0, 0))
    return call(
        kernel,
        where,
        (chips,),
        [
            whole((local_count, 1, slots)),
            whole((local_count, 1, slots)),
            whole(hidden_rows.shape),
            pl.BlockSpec((local_count, width_in, cols), lambda k, where: (0, 0, k)),
        ],
        (out_spec, out_spec),
        (shape, shape),
        [
            pltpu.VMEM((tokens, local_count * width_in), jnp.bfloat16),
            pltpu.VMEM((cols, tokens), jnp.bfloat16),
        ],
        (token_rows[:, None], row_gate[:, None], hidden_rows, in_hbm(weight)),
        32 * MIB,
    )


def resident(kernel, scalars, operands, out_shapes, scratch=(), distant=(), passed=None):
    held = [pltpu.with_memory_space_constraint(array, pltpu.VMEM) for array in operands]
    in_vmem, anywhere = pl.BlockSpec(memory_space=pltpu.VMEM), pl.BlockSpec(memory_space=pl.ANY)
    far_off = [in_hbm(array) for array in distant] + ([] if passed is None else [passed])
    return pl.pallas_call(
        kernel,
        in_specs=[pl.BlockSpec(memory_space=pltpu.SMEM)] + [in_vmem] * len(held) + [anywhere] * len(far_off),
        out_specs=[in_vmem if shape.memory_space == pltpu.VMEM else anywhere for shape in out_shapes],
        out_shape=out_shapes,
        scratch_shapes=list(scratch),
        input_output_aliases={} if passed is None else {len(held) + len(far_off): 0},
        compiler_params=pltpu.CompilerParams(vmem_limit_bytes=20 * MIB),
    )(scalars, *held, *far_off)


def shares_by_token(where, payloads, slots, tokens):
    local_count, _, share = payloads[0].shape
    groups = len(payloads)

    def kernel(where, *refs):
        sources, (out_ref, held, sem) = refs[:groups], refs[groups:]
        loads = [pltpu.make_async_copy(ref, held.at[i], sem.at[i]) for i, ref in enumerate(sources)]
        for load in loads:
            load.start()

        def row(group, local, first):
            wide = [held[group, local, slots + first + i : slots + first + i + 1, :] for i in range(2)]
            return jnp.concatenate(wide, axis=1)[:, :slots].astype(jnp.float32)

        for group in range(groups):
            loads[group].wait()
            for local in range(local_count):
                token = (row(group, local, 0) * 2.0 + row(group, local, 2)).astype(jnp.int32)
                hot = hot_rows(token, row(group, local, 4), tokens)
                by_token = dot(hot, held[group, local, :slots, :], 1, 0).astype(jnp.bfloat16)
                out_ref[local * share : (local + 1) * share, group * tokens : (group + 1) * tokens] = by_token.T

    shape = (local_count * share, groups * tokens)
    scratch = [pltpu.VMEM((groups, *payloads[0].shape), jnp.bfloat16), pltpu.SemaphoreType.DMA((groups,))]
    return resident(kernel, where, [], [pltpu.VMEM(shape, jnp.bfloat16)], scratch, payloads)[0]


def blocks_of(where, gathered, steps, parts):
    chips, rows, tokens = gathered.shape
    part = rows // parts

    def kernel(where, gathered_ref, *refs):
        sem = refs[-1]
        copies = []
        for place, step in enumerate(steps):
            chip = lax.rem(where[0] + step, chips)
            for index, out_ref in enumerate(refs[:-1]):
                source = gathered_ref.at[chip, pl.ds(index * part, part)]
                copies.append(pltpu.make_async_copy(source, out_ref.at[place], sem.at[len(copies)]))
        for copy in copies:
            copy.start()
        for copy in copies:
            copy.wait()

    return pl.pallas_call(
        kernel,
        in_specs=[pl.BlockSpec(memory_space=pltpu.SMEM), pl.BlockSpec(memory_space=pl.ANY)],
        out_specs=[pl.BlockSpec(memory_space=pltpu.VMEM)] * parts,
        out_shape=[pltpu.VMEM((len(steps), part, tokens), gathered.dtype)] * parts,
        scratch_shapes=[pltpu.SemaphoreType.DMA((len(steps) * parts,))],
    )(where, in_hbm(gathered))


def hidden_grads(where, token_rows, row_gate, gathered, weight):
    local_count, width_in, width = weight.shape
    slots = token_rows.shape[1]
    chips, half, tokens = gathered[0].shape
    depth = width_in // 2

    def kernel(where, token_ref, gate_ref, mine_ref, other_ref, weight_ref, out_ref, group_cot, sem):
        local = pl.program_id(0)

        @pl.when((local == 0) & (pl.program_id(1) == 0))
        def _():
            loads = []
            for side, ref in enumerate((mine_ref, other_ref)):
                for chip in range(chips):
                    start = (chip * CORES + jnp.bitwise_xor(where[1], side)) * half
                    rows = group_cot.at[pl.ds(pl.multiple_of(start, half), half)]
                    loads.append(pltpu.make_async_copy(ref.at[chip], rows, sem.at[len(loads)]))
            for load in loads:
                load.start()
            for load in loads:
                load.wait()

        sums = dot(weight_ref[0], group_cot[...], 1, 0).astype(jnp.bfloat16)
        hot = hot_rows(token_ref[local], gate_ref[local], tokens)
        out_ref[0] = dot(hot, sums, 0, 1).astype(jnp.bfloat16)

    return call(
        kernel,
        where,
        (local_count, width_in // depth),
        [whole((local_count, 1, slots))] * 2
        + [pl.BlockSpec(memory_space=pl.ANY)] * CORES
        + [pl.BlockSpec((1, depth, width), lambda e, h, where: (e, h, 0))],
        pl.BlockSpec((1, slots, depth), lambda e, h, where: (e, 0, h)),
        jax.ShapeDtypeStruct((local_count, slots, width_in), jnp.bfloat16),
        [pltpu.VMEM((width, tokens), jnp.bfloat16), pltpu.SemaphoreType.DMA((CORES * chips,))],
        (token_rows[:, None], row_gate[:, None], *map(in_hbm, gathered), in_hbm(weight)),
        28 * MIB,
    )


def group_products(where, shares, groups, refs, chip):
    total, at = None, 0
    for place, sides in groups:
        loaded = []
        for pieces in sides:
            loaded.append([ref[first + chip] for ref, (_, first) in zip(refs[at:], pieces)])
            at += len(pieces)
        mine, other = [jnp.concatenate(pieces, axis=0) if len(pieces) > 1 else pieces[0] for pieces in loaded]
        low = jnp.where(where[1] == 0, mine, other)
        high = jnp.where(where[1] == 0, other, mine)
        block = jnp.concatenate([low, high], axis=0)
        tokens = block.shape[1]
        product = dot(shares[:, place * tokens : (place + 1) * tokens], block, 1, 1)
        total = product if total is None else total + product
    return total


def halves(parts):
    return [(part, 0) for part in parts]


def weight_cols(where, shares, own_groups, groups, local_count, width, gathered=None, so_far=None, passed=None):
    chips = lax.axis_size("expert") // CORES
    cols = width // chips
    half = cols // CORES
    share = shares.shape[0] // local_count
    own_flat, flat = [
        [array for _, sides in listed for pieces in sides for array, _ in pieces]
        for listed in (own_groups, groups)
    ]
    tokens = flat[0].shape[-1]
    count = chips - 1
    kept = (count, shares.shape[0], cols)
    distant = gathered or []
    added = [] if so_far is None else [so_far]
    stored = count if gathered is None else 1

    def kernel(where, shares_ref, *refs):
        refs = list(refs)
        own_pieces = [refs.pop(0) for _ in own_flat]
        pieces = [refs.pop(0) for _ in flat]
        so_far_ref = refs.pop(0) if added else None
        sources = [refs.pop(0) for _ in distant]
        if passed is not None:
            refs.pop(0)
        out_ref = refs.pop(0)
        kept_ref = None if gathered is None else refs.pop(0)
        total_ref, total_sem = refs[:2]
        place = [lax.rem(where[0] + step, chips) for step in range(chips)]
        loads, stores = [], []
        for chip in range(count):
            loads.append([])
            for side, source in enumerate(sources):
                target = refs[2].at[chip, jnp.bitwise_xor(where[1], side)]
                loads[chip].append(pltpu.make_async_copy(source.at[place[chip + 1]], target, refs[3].at[chip, side]))
            for load in loads[chip]:
                load.start()

        def store(total, index, step):
            for local in range(local_count):
                total_ref[index, local] = total[local * share : (local + 1) * share]
            columns = pl.ds(pl.multiple_of(place[step] * cols, LANES), cols)
            stores.append(pltpu.make_async_copy(total_ref.at[index], out_ref.at[:, :, columns], total_sem.at[index]))
            stores[-1].start()

        if own_groups:
            store(group_products(where, shares_ref, own_groups, own_pieces, 0), 0, 0)
        for chip in range(count):
            total = group_products(where, shares_ref, groups, pieces, chip)
            for load in loads[chip]:
                load.wait()
            if gathered is None:
                store(total + so_far_ref[chip].astype(jnp.float32), chip, chip + 1)
                continue
            block = refs[2][chip].reshape(cols, tokens)
            kept_ref[chip] = (total + dot(shares_ref[:, :tokens], block, 1, 1)).astype(jnp.bfloat16)
        for copy in stores:
            copy.wait()

    scratch = [
        pltpu.VMEM((stored, local_count, share, cols), jnp.float32),
        pltpu.SemaphoreType.DMA((stored,)),
    ]
    out_shapes = [pltpu.HBM((local_count, share, width), jnp.float32)]
    if gathered is not None:
        scratch += [pltpu.VMEM((count, CORES, half, tokens), jnp.bfloat16), pltpu.SemaphoreType.DMA((count, CORES))]
        out_shapes.append(pltpu.VMEM(kept, jnp.bfloat16))
    return resident(kernel, where, [shares, *own_flat, *flat, *added], out_shapes, scratch, distant, passed)


def planned_body(hidden, down_weight, cotangent, expert_ids, gate_weights, row_token, tile_count):
    local_count, width_in, width = down_weight.shape
    tokens = cotangent.shape[0]
    slots = hidden.shape[2]
    groups = lax.axis_size("dp")
    chips = lax.axis_size("expert") // CORES
    share = width_in // groups
    group = lax.axis_index("dp")
    expert_place = lax.axis_index("expert")
    chip = expert_place // CORES
    core = expert_place % CORES
    where = jnp.stack([chip, core])

    own = cotangent.T
    middle = own.shape[0] // 2
    gathered = exchanged(jnp.broadcast_to(own[None], (chips, *own.shape)))
    x_own, y_own = across_dp(own, 1), across_dp(own, 2)
    own_other = across_cores(own)

    slot_index = jnp.arange(slots, dtype=jnp.int32)
    token_index = jnp.arange(tokens, dtype=jnp.int32)
    live = (row_token[0] >= 0) & (slot_index[None] < tile_count[0][:, None] * TILE)
    token_rows = jnp.where(live, row_token[0], -1)
    experts = expert_place * local_count + jnp.arange(local_count, dtype=jnp.int32)
    named = expert_ids[None] == experts[:, None, None]
    token_gate = jnp.sum(jnp.where(named, gate_weights[None].astype(jnp.float32), 0.0), axis=2)
    at_token = token_rows[:, :, None] == token_index[None, None, :]
    row_gate = jnp.sum(jnp.where(at_token, token_gate[:, None, :], 0.0), axis=2)

    def as_rows(values):
        padded = jnp.pad(values.astype(jnp.bfloat16), ((0, 0), (0, 2 * share - slots)))
        return padded.reshape(local_count, 2, share)

    extra = jnp.concatenate(
        [as_rows(token_rows >> 1), as_rows(token_rows & 1), as_rows(row_gate)], axis=1
    )
    extra = jnp.pad(extra, ((0, 0), (0, EXTRA_ROWS - extra.shape[1]), (0, 0)))
    payloads = []
    for mask in range(groups):
        rows = lax.dynamic_slice_in_dim(hidden[0], (group ^ mask) * share, share, 2)
        payloads.append(jnp.concatenate([rows, extra], axis=1))
    x_own, y_own, own_other, token_rows, row_gate, *payloads = joined(
        x_own, y_own, own_other, token_rows, row_gate, *payloads
    )

    payloads = [across_dp(payload, mask) if mask else payload for mask, payload in enumerate(payloads)]
    far_own = [across_dp(x_own[:middle], 2), across_dp(y_own[middle:], 1)]
    keep, send = expert_sums(where, token_rows, row_gate, hidden[0], down_weight, tokens)
    x_own, y_own, keep, send, *sent = joined(x_own, y_own, keep, send, *far_own, *payloads)
    far_own, payloads = sent[:2], sent[2:]

    own_far = jnp.stack([x_own, y_own, jnp.concatenate(far_own, axis=0)])
    gathered, own_far = joined(gathered, own_far)
    own_far_other = across_cores(own_far)
    steps = list(range(1, chips))
    near = blocks_of(where, gathered, steps, 2)
    x_near, y_near = [None, None], [None, None]
    x_near[0], y_near[1] = across_dp(near[0], 1), across_dp(near[1], 2)
    x_near[1], y_near[0] = across_dp(near[1], 1), across_dp(near[0], 2)

    from_other = across_cores(send)
    gathered_other = across_cores(gathered)
    from_other, *_ = joined(from_other, *near)
    sums = (keep.astype(jnp.float32) + from_other.astype(jnp.float32)).astype(jnp.bfloat16)
    mixed = exchanged(sums)
    _, gathered_other, *payloads = joined(sums, gathered_other, *payloads)
    shares = shares_by_token(where, payloads, slots, tokens)
    gathered = [gathered, gathered_other]
    hidden_grad = hidden_grads(where, token_rows, row_gate, gathered, down_weight)
    hidden_grad, shares, own_far_other, _, *sent = joined(
        hidden_grad, shares, own_far_other, sums, *x_near, *y_near
    )
    x_near, y_near = sent[:2], sent[2:]

    rest = (local_count, width)
    far = [across_dp(x_near[0], 2), across_dp(y_near[1], 1)]
    x_other = [across_cores(part) for part in x_near]
    y_other = [across_cores(part) for part in y_near]
    own_groups = [(0, (halves([own[None]]), halves([own_other[None]])))]
    own_groups += [(place + 1, ([(own_far, place)], [(own_far_other, place)])) for place in range(groups - 1)]
    two = [(place, tuple(map(halves, pair))) for place, pair in ((1, (x_near, x_other)), (2, (y_near, y_other)))]
    weight_grad, so_far = weight_cols(where, shares, own_groups, two, *rest, gathered)
    so_far, weight_grad, *far = joined(so_far, weight_grad, *far)
    mixed = jnp.sum(mixed.astype(jnp.float32), axis=0).astype(jnp.bfloat16)
    mixed, *far_other = joined(mixed, *[across_cores(part) for part in far])
    last = [(groups - 1, (halves(far), halves(far_other)))]
    weight_grad = weight_cols(where, shares, [], last, *rest, None, so_far, weight_grad)[0]
    return (mixed.T, hidden_grad[None], weight_grad)


def tile_products(rows_in, weight_mat, count, contract_dim):
    rows_cap = rows_in.shape[0]
    width_out = weight_mat.shape[1 - contract_dim]

    def one_tile(tile_index, outputs):
        block = lax.dynamic_slice_in_dim(rows_in, tile_index * TILE, TILE, 0)
        product = lax.dot_general(
            block,
            weight_mat,
            (((1,), (contract_dim,)), ((), ())),
            preferred_element_type=jnp.float32,
        )
        return lax.dynamic_update_slice_in_dim(
            outputs, product.astype(jnp.bfloat16), tile_index * TILE, 0
        )

    return lax.fori_loop(0, count, one_tile, jnp.zeros((rows_cap, width_out), jnp.bfloat16))


def general_body(hidden, down_weight, cotangent, expert_ids, gate_weights, row_token, tile_count):
    local_count = down_weight.shape[0]
    group_size = cotangent.shape[0]
    expert_index = jnp.arange(EXPERTS, dtype=jnp.int32)
    named_cols = expert_ids[:, :, None] == expert_index[None, None, :]
    gate_cols = jnp.sum(
        jnp.where(named_cols, gate_weights[:, :, None].astype(jnp.float32), 0.0), axis=1
    ).astype(jnp.bfloat16)
    group_cot = lax.all_gather(cotangent, "expert", axis=1, tiled=True)
    width = group_cot.shape[1]
    first_expert = lax.axis_index("expert") * local_count
    slot_index = jnp.arange(hidden.shape[2], dtype=jnp.int32)
    share_rows = down_weight.shape[1] // lax.axis_size("dp")
    partial_value = jnp.zeros((group_size, width), jnp.float32)
    grad_list = []
    weight_list = []
    for local in range(local_count):
        token_rows = row_token[0, local]
        count = tile_count[0, local]
        live_rows = (token_rows >= 0) & (slot_index < count * TILE)
        safe_rows = jnp.where(live_rows, token_rows, 0)
        column = lax.dynamic_index_in_dim(gate_cols, first_expert + local, 1, keepdims=False)
        row_gate = jnp.where(live_rows, column[safe_rows].astype(jnp.float32), 0.0)
        target = jnp.where(live_rows, token_rows, group_size)
        hidden_rows = hidden[0, local]
        weight_mat = down_weight[local]
        out_rows = tile_products(hidden_rows, weight_mat, count, 0)
        partial_value = partial_value.at[target].add(
            row_gate[:, None] * out_rows.astype(jnp.float32), mode="drop"
        )
        routed = (row_gate[:, None] * group_cot[safe_rows].astype(jnp.float32)).astype(jnp.bfloat16)
        grad_list.append(tile_products(routed, weight_mat, count, 1))

        def weight_rows(start, rows_count, hidden_rows=hidden_rows, routed_rows=routed):
            return lax.dot_general(
                hidden_rows,
                routed_rows,
                (((0,), (0,)), ((), ())),
                preferred_element_type=jnp.float32,
            )

        weight_list.append(
            lax.psum_scatter(
                weight_rows(jnp.int32(0), share_rows * lax.axis_size("dp")).astype(jnp.bfloat16),
                "dp",
                scatter_dimension=0,
                tiled=True,
            ).astype(jnp.float32)
        )
    merged = partial_value
    top_bit = lax.axis_size("expert").bit_length() - 1
    axis_index = lax.axis_index("expert")
    for bit_index in reversed(range(top_bit)):
        half_cols = merged.shape[1] // 2
        lower_half = merged[:, :half_cols]
        upper_half = merged[:, half_cols:]
        high_side = axis_index // 2**bit_index % 2 == 1
        sending = jnp.where(high_side, lower_half, upper_half)
        keeping = jnp.where(high_side, upper_half, lower_half)
        merged = keeping + swapped(sending.astype(jnp.bfloat16), "expert", bit_index).astype(
            sending.dtype
        )
    mixed_out = merged.astype(jnp.bfloat16)
    hidden_grad = jnp.stack(grad_list, axis=0)[None]
    weight_grad = jnp.stack(weight_list, axis=0)
    return (mixed_out, hidden_grad, weight_grad)


def solution(mesh):
    placed = (
        P("dp", "expert", None, None),
        P("expert", None, None),
        P("dp", "expert"),
        P("dp", None),
        P("dp", None),
        P("dp", "expert", None),
        P("dp", "expert"),
    )

    def body(*shards):
        width = shards[1].shape[2]
        chips = mesh.shape["expert"] // CORES
        fits = mesh.shape["dp"] == 4 and chips > 2 and width % (chips * LANES) == 0
        return planned_body(*shards) if fits else general_body(*shards)

    return jax.shard_map(
        body,
        mesh=mesh,
        in_specs=placed,
        out_specs=(P("dp", "expert"), P("dp", "expert", None, None), P("expert", "dp", None)),
        check_vma=False,
    )
```
